32 devices in a mesh: dp: 8 (over z, x), blk: 4 (over y, core).
Axes of the slice: x: 2, y: 2, z: 4, core: 2. Of those that a mesh axis runs over, the one named last changes fastest.
Arguments:
- block_input: bfloat16 [2, 8, 1024, 960], P(None, 'dp', 'blk'), may hold values from -6 to 6
- cotangent: bfloat16 [2, 8, 1024, 960], P(None, 'dp', 'blk'), may hold values from -6 to 6
- seq_lengths: int32 [2, 8], P(None, 'dp'), may hold values from 512 to 1024, as said below
- routes_two: int32 [2, 8, 256], P(None, 'dp'), may hold values from 0 to 1023, as said below
- routes_three: int32 [2, 8, 128], P(None, 'dp'), may hold values from 0 to 1023, as said below
- query_weight: bfloat16 [960, 960], P('dp'), may hold values from -0.1875 to 0.1875
- key_weight: bfloat16 [960, 320], P('dp'), may hold values from -0.1875 to 0.1875
- value_weight: bfloat16 [960, 320], P('dp'), may hold values from -0.1875 to 0.1875
- output_weight: bfloat16 [960, 960], P('dp'), may hold values from -1.5 to 1.5
- gate_weight: bfloat16 [960, 2560], P('dp'), may hold values from -0.1875 to 0.1875
- up_weight: bfloat16 [960, 2560], P('dp'), may hold values from -0.1875 to 0.1875
- down_weight: bfloat16 [2560, 960], P('dp'), may hold values from -0.125 to 0.125
- first_gain: bfloat16 [960], P('dp'), may hold values from 0.099609375 to 1.8984375
- second_gain: bfloat16 [960], P('dp'), may hold values from 0.099609375 to 1.8984375
- router_weight: bfloat16 [960, 3], P('dp'), may hold values from -0.125 to 0.125
Outputs:
- block_output: bfloat16 [2, 8, 1024, 960], P(None, 'dp', 'blk')
- input_grad: float32 [2, 8, 1024, 960], P(None, 'dp', 'blk')
- grad_query: float32 [960, 960], P('dp')
- grad_key: float32 [960, 320], P('dp')
- grad_value: float32 [960, 320], P('dp')
- grad_output: float32 [960, 960], P('dp')
- grad_gate: float32 [960, 2560], P('dp')
- grad_up: float32 [960, 2560], P('dp')
- grad_down: float32 [2560, 960], P('dp')
- grad_first: float32 [960], P('dp')
- grad_second: float32 [960], P('dp')
- grad_router: float32 [960, 3], P('dp')
The draws below stay inside these ranges and needn't reach their ends.
Inputs may be any that keep to these rules, and one draw needn't show every extreme that they name: `seq_lengths`: in each micro-batch, each group of 1 sequence holds one sequence (drawn from the seed) longer than 768; some sequence has length exactly 1024. `routes_two`: for each sequence: 256 distinct positions below its length, in increasing order; at most 128 of them lie in any aligned block of 256 positions, and some block of every sequence holds exactly 128. `routes_three`: for each sequence: 128 distinct positions taken from its routes_two, in increasing order; at most 64 of them lie in any aligned block of 256 positions, and some block of every sequence holds exactly 64.
All inputs are finite; a program needn't handle non-finite values.
Results may differ from the reference program's by a relative error of at most 0.033.
Values may be sent and summed in bfloat16 or wider, within the bound.
A program may use at most 192 MiB of HBM per device.

```python
import math
import jax
import jax.numpy as jnp
from jax import lax

D = 960
HEADS = 15
KV_HEADS = 5
HEAD_DIM = 64
FF = 2560
RECUR = 3
LEN = 1024
MICRO = 2
SEQS = 1
NSEQ = 8
BLOCK_LEN = 256
CAP_TWO = 128
CAP_THREE = 64
TOP_TWO = 256
TOP_THREE = 128
N_BLK = 4


def block_rank(priority, eligible):
    priority_grid = priority.reshape(N_BLK, BLOCK_LEN)
    open_grid = eligible.reshape(N_BLK, BLOCK_LEN)
    higher = (priority_grid[:, None, :] > priority_grid[:, :, None]) & open_grid[:, None, :]
    return jnp.sum(higher.astype(jnp.int32), axis=2).reshape(LEN)


def route_one(seed_key, seq_length):
    perm_key, block_key = jax.random.split(seed_key)
    priority = jax.random.permutation(perm_key, LEN).astype(jnp.int32)
    places = jnp.arange(LEN, dtype=jnp.int32)
    forced = jax.random.randint(block_key, (), 0, N_BLK // 2)
    in_forced = (places // BLOCK_LEN == forced).astype(jnp.int32)
    is_valid = places < seq_length
    open_two = is_valid & (block_rank(priority, is_valid) < CAP_TWO)
    score_two = open_two.astype(jnp.int32) * (4 * LEN) + in_forced * (2 * LEN) + priority
    picked_two = lax.top_k(score_two, TOP_TWO)[1]
    member_two = jnp.zeros(LEN, jnp.int32).at[picked_two].set(1) > 0
    open_three = member_two & (block_rank(priority, member_two) < CAP_THREE)
    score_three = open_three.astype(jnp.int32) * (4 * LEN) + in_forced * (2 * LEN) + priority
    picked_three = lax.top_k(score_three, TOP_THREE)[1]
    return (jnp.sort(picked_two).astype(jnp.int32), jnp.sort(picked_three).astype(jnp.int32))


def route_plan(seed_key):
    length_key, choose_key, order_key, reach_key = jax.random.split(seed_key, 4)
    lengths = jax.random.randint(length_key, (MICRO, NSEQ), LEN // 2, LEN + 1)
    reaching = LEN - jax.random.randint(reach_key, (MICRO, NSEQ), 0, BLOCK_LEN)
    chosen = jax.random.randint(choose_key, (MICRO, NSEQ // SEQS), 0, SEQS)
    member_ids = jnp.arange(SEQS, dtype=jnp.int32)
    full_one = (member_ids[None, None, :] == chosen[:, :, None]).reshape(MICRO, NSEQ)
    lengths = jnp.where(full_one, reaching, lengths).astype(jnp.int32)
    lengths = lengths.at[0, chosen[0, 0]].set(LEN)
    order_keys = jax.random.split(order_key, MICRO * NSEQ)
    two_sets, three_sets = jax.vmap(route_one)(order_keys, lengths.reshape(MICRO * NSEQ))
    return (lengths, two_sets.reshape(MICRO, NSEQ, TOP_TWO), three_sets.reshape(MICRO, NSEQ, TOP_THREE))


def draw_seq_lengths(key, part):
    return route_plan(key)[0]


def draw_routes_two(key, part):
    return route_plan(key)[1]


def draw_routes_three(key, part):
    return route_plan(key)[2]


def shard_levels(key, dims, pieces, smallest, top_value):
    def one(position, shards_of):
        heights = jax.random.uniform(jax.random.fold_in(jax.random.fold_in(key, 6), position), (shards_of,), jnp.float32, smallest / len(pieces), top_value / len(pieces))
        return jnp.repeat(jnp.exp(heights), dims[position] // shards_of).reshape((-1,) + (1,) * (len(dims) - position - 1))

    level = one(*pieces[0])
    for cut in pieces[1:]:
        level = level * one(*cut)
    return level


def centred(own_key, dims, scale, reach, shards=(), kind=jnp.bfloat16):
    loudness = shard_levels(own_key, dims, shards, -0.22, 0.18) if shards else 1.0
    values = jax.random.normal(own_key, dims, jnp.float32) * scale * loudness
    return jnp.minimum(jnp.maximum(values, -reach), reach).astype(kind)


def setup_inputs(seed: int = 0) -> dict:
    streams_of = jax.random.split(jax.random.key(seed), 16)
    return {
        "block_input": centred(streams_of[0], (MICRO, NSEQ, LEN, D), 1.0, 6.0, ((1, 8), (2, 4))),
        "cotangent": centred(streams_of[1], (MICRO, NSEQ, LEN, D), 1.0, 6.0, ((1, 8), (2, 4))),
        "seq_lengths": draw_seq_lengths(jax.random.fold_in(streams_of[15], 71), 0),
        "routes_two": draw_routes_two(jax.random.fold_in(streams_of[15], 71), 0),
        "routes_three": draw_routes_three(jax.random.fold_in(streams_of[15], 71), 0),
        "query_weight": centred(streams_of[5], (D, HEADS * HEAD_DIM), D ** -0.5, 0.1875, ((0, 8),)),
        "key_weight": centred(streams_of[6], (D, KV_HEADS * HEAD_DIM), D ** -0.5, 0.1875, ((0, 8),)),
        "value_weight": centred(streams_of[7], (D, KV_HEADS * HEAD_DIM), D ** -0.5, 0.1875, ((0, 8),)),
        "output_weight": centred(streams_of[8], (HEADS * HEAD_DIM, D), (max(1, HEADS * HEAD_DIM // 64)) ** -0.5, 1.5, ((0, 8),)),
        "gate_weight": centred(streams_of[9], (D, FF), D ** -0.5, 0.1875, ((0, 8),)),
        "up_weight": centred(streams_of[10], (D, FF), D ** -0.5, 0.1875, ((0, 8),)),
        "down_weight": centred(streams_of[11], (FF, D), FF ** -0.5, 0.125, ((0, 8),)),
        "first_gain": jnp.clip(1.0 + 0.18 * jax.random.normal(streams_of[12], (D,), jnp.float32), 0.099609375, 1.8984375).astype(jnp.bfloat16),
        "second_gain": jnp.clip(1.0 + 0.18 * jax.random.normal(streams_of[13], (D,), jnp.float32), 0.099609375, 1.8984375).astype(jnp.bfloat16),
        "router_weight": centred(streams_of[14], (D, RECUR), (2 * D) ** -0.5, 0.125, ((0, 8),)),
    }


@jax.custom_vjp
def low(v):
    return lax.optimization_barrier(v.astype(jnp.bfloat16)).astype(jnp.float32)

@jax.custom_vjp
def low_back(v):
    return v

def low_keep(v):
    return (low(v), None)

def low_pass(kept, grad):
    return (grad,)

def back_keep(v):
    return (v, None)

def back_low(kept, grad):
    return (low(grad),)
low.defvjp(low_keep, low_pass)
low_back.defvjp(back_keep, back_low)
eps = 1e-05
rope_base = 10000.0
masked_fill = -1e+30

def highest_precision(pattern, left_side, right_side):
    return jnp.einsum(pattern, left_side, right_side, precision=lax.Precision.HIGHEST)

def rotate(values, cosine, sine_part):
    half_dim = values.shape[-1] // 2
    turned = jnp.concatenate([-values[..., half_dim:], values[..., :half_dim]], axis=-1)
    return values * cosine + turned * sine_part

def angles(positions):
    frequency = rope_base ** (-(jnp.arange(HEAD_DIM // 2, dtype=jnp.float32) * 2.0) / HEAD_DIM)
    frequency = jnp.concatenate([frequency, frequency])
    phases = positions.astype(jnp.float32)[..., None] * frequency
    return (jnp.cos(phases)[..., None, :], jnp.sin(phases)[..., None, :])

def attend_one(packed):
    queries, keyset, value_collection, active = packed
    places = jnp.arange(LEN, dtype=jnp.int32)
    allowed = active[None, :] & (places[None, :] <= places[:, None])
    scores = low_back(highest_precision('qgcd,kgd->gcqk', queries, keyset) * (1.0 / math.sqrt(HEAD_DIM)))
    scores = jnp.where(allowed[None, None], scores, masked_fill)
    chances = low(jax.nn.softmax(scores, axis=-1))
    return highest_precision('gcqk,kgd->qgcd', chances, value_collection)

def forward(tokens, weights, member):
    query_projection, key_projection, value_projection, output_projection, gate_projection, up_projection, down_projection, gain_one, gain_two, router_matrix = weights
    seq_count = tokens.shape[0]
    groups = HEADS // KV_HEADS
    cosine, sine_part = angles(jnp.arange(LEN, dtype=jnp.int32))
    current = tokens
    for recursion in range(RECUR):
        first_scale = lax.rsqrt(lax.optimization_barrier(jnp.mean(current * current, axis=-1, keepdims=True)) + eps)
        normalized_input = low(current * first_scale * gain_one)
        query_unrotated = low_back(highest_precision('gip,pm->gim', normalized_input, query_projection))
        queries = low(rotate(query_unrotated.reshape(seq_count, LEN, HEADS, HEAD_DIM), cosine, sine_part))
        key_unrotated = low_back(highest_precision('tfu,uc->tfc', normalized_input, key_projection))
        keyset = low(rotate(key_unrotated.reshape(seq_count, LEN, KV_HEADS, HEAD_DIM), cosine, sine_part))
        value_collection = low(low_back(highest_precision('tfu,uc->tfc', normalized_input, value_projection)))
        value_collection = value_collection.reshape(seq_count, LEN, KV_HEADS, HEAD_DIM)
        attended = lax.map(jax.checkpoint(attend_one), (queries.reshape(seq_count, LEN, KV_HEADS, groups, HEAD_DIM), keyset, value_collection, member[recursion]))
        attention_reduced = low(low_back(attended.reshape(seq_count, LEN, HEADS * HEAD_DIM)))
        branch_result = low_back(highest_precision('buw,wp->bup', attention_reduced, output_projection))
        middle = current + branch_result
        second_scale = lax.rsqrt(lax.optimization_barrier(jnp.mean(middle * middle, axis=-1, keepdims=True)) + eps)
        normalized_second = low(middle * second_scale * gain_two)
        gate_preactivation = low_back(highest_precision('bro,on->brn', normalized_second, gate_projection))
        up_preactivation = low_back(highest_precision('bro,on->brn', normalized_second, up_projection))
        hidden_activation = low(jax.nn.silu(gate_preactivation) * up_preactivation)
        feedforward_output = low_back(highest_precision('nhz,zm->nhm', hidden_activation, down_projection))
        router_gate = jax.nn.sigmoid(lax.optimization_barrier(jnp.sum(current * router_matrix[:, recursion], axis=-1)))[..., None]
        current = jnp.where(member[recursion][..., None], current + router_gate * (branch_result + feedforward_output), current)
    return current

def reference(block_input, cotangent, seq_lengths, routes_two, routes_three, query_weight, key_weight, value_weight, output_weight, gate_weight, up_weight, down_weight, first_gain, second_gain, router_weight):
    weights = tuple((matrix.astype(jnp.float32) for matrix in (query_weight, key_weight, value_weight, output_weight, gate_weight, up_weight, down_weight, first_gain, second_gain, router_weight)))
    places = jnp.arange(LEN, dtype=jnp.int32)
    outputs = []
    input_grads = []
    totals = tuple((jnp.zeros(matrix.shape, jnp.float32) for matrix in weights))
    for microbatch in range(MICRO):
        member = jnp.stack([places[None, :] < seq_lengths[microbatch][:, None], jnp.any(places[None, :, None] == routes_two[microbatch][:, None, :], axis=-1), jnp.any(places[None, :, None] == routes_three[microbatch][:, None, :], axis=-1)])

        def run_block(tokens, params):
            return forward(tokens, params, member)
        result, pullback = jax.vjp(run_block, block_input[microbatch].astype(jnp.float32), weights)
        token_grad, weight_grads = pullback(cotangent[microbatch].astype(jnp.float32))
        outputs.append(result.astype(jnp.bfloat16))
        input_grads.append(token_grad)
        totals = tuple((earlier + latest for earlier, latest in zip(totals, weight_grads)))
    return (jnp.stack(outputs), jnp.stack(input_grads), totals[0], totals[1], totals[2], totals[3], totals[4], totals[5], totals[6], totals[7], totals[8], totals[9])
```

```python
import functools
import math

import jax
import jax.numpy as jnp
from jax import lax
from jax.experimental import pallas as pl
from jax.experimental.pallas import tpu as pltpu
from jax.sharding import PartitionSpec as P


HEADS = 15
KV_HEADS = 5
HEAD_DIM = 64
RECUR = 3


eps = 1e-05
rope_base = 10000.0
masked_fill = -1e30


def as_sent(shard):

    def short(part):
        return part.astype(jnp.bfloat16) if part.dtype == jnp.float32 else part

    return jax.tree.map(short, shard)


def rotate(values, cosine, sine_part):
    half_dim = values.shape[-1] // 2
    turned = jnp.concatenate([-values[..., half_dim:], values[..., :half_dim]], axis=-1)
    return values * cosine + turned * sine_part


def rotate_back(gradient, cosine, sine_part):
    half_dim = gradient.shape[-1] // 2
    scaled = gradient * sine_part
    turned = jnp.concatenate([scaled[..., half_dim:], -scaled[..., :half_dim]], axis=-1)
    return gradient * cosine + turned


def angles(positions):
    frequency = rope_base ** (-(jnp.arange(HEAD_DIM // 2, dtype=jnp.float32) * 2.0) / HEAD_DIM)
    frequency = jnp.concatenate([frequency, frequency])
    phases = positions.astype(jnp.float32)[..., None] * frequency
    return (jnp.cos(phases)[..., None, :], jnp.sin(phases)[..., None, :])


def routed_slots(routes, blocks, block_len, slot_count):
    total_routes = routes.shape[1]
    block_starts = jnp.arange(blocks, dtype=jnp.int32) * block_len
    before = jnp.sum((routes[:, None, :] < block_starts[None, :, None]).astype(jnp.int32), axis=2)
    first_pick = jnp.minimum(before, total_routes - slot_count)
    pick_index = first_pick[:, :, None] + jnp.arange(slot_count, dtype=jnp.int32)[None, None, :]
    found_places = jnp.take_along_axis(
        routes, pick_index.reshape(routes.shape[0], blocks * slot_count), axis=1
    )
    found_places = found_places.reshape(routes.shape[0], blocks, slot_count)
    inside = (found_places >= block_starts[None, :, None]) & (
        found_places < block_starts[None, :, None] + block_len
    )
    return jnp.where(inside, found_places, -1).reshape(routes.shape[0], blocks * slot_count)


def pick_rows(block_vals, index_vals):
    return block_vals[index_vals]


def place_rows(block_vals, index_vals, new_vals):
    return block_vals.at[index_vals].set(new_vals, mode="drop")


def attention_mask(query_places, key_places):
    key_side = key_places[:, None, None, None, :]
    return (key_side >= 0) & (key_side <= query_places[:, None, None, :, None])


def block_forward(tokens, positions, all_slots, gathered, recursion):
    (
        query_projection,
        key_projection,
        value_projection,
        output_projection,
        gate_projection,
        up_projection,
        down_projection,
        gain_one,
        gain_two,
        router_matrix,
    ) = gathered
    seq_count, slot_count, model_width = tokens.shape
    groups = HEADS // KV_HEADS
    attn_scale = 1.0 / math.sqrt(HEAD_DIM)
    first_scale = lax.rsqrt(jnp.mean(tokens * tokens, axis=-1, keepdims=True) + eps)
    normalized_input = (tokens * first_scale * gain_one.astype(jnp.float32)).astype(jnp.bfloat16)
    cosine, sine_part = angles(positions)
    query_unrotated = jnp.dot(
        normalized_input, query_projection, preferred_element_type=jnp.float32
    )
    queries = rotate(
        query_unrotated.reshape(seq_count, slot_count, HEADS, HEAD_DIM), cosine, sine_part
    )
    queries = queries.astype(jnp.bfloat16).reshape(
        seq_count, slot_count, KV_HEADS, groups, HEAD_DIM
    )
    key_unrotated = jnp.dot(normalized_input, key_projection, preferred_element_type=jnp.float32)
    keyset = rotate(
        key_unrotated.reshape(seq_count, slot_count, KV_HEADS, HEAD_DIM), cosine, sine_part
    )
    keyset = keyset.astype(jnp.bfloat16).reshape(seq_count, slot_count, KV_HEADS * HEAD_DIM)
    value_collection = jnp.dot(
        normalized_input, value_projection, preferred_element_type=jnp.float32
    ).astype(jnp.bfloat16)
    key_all, value_all = (
        lax.all_gather(keyset, "blk", axis=1, tiled=True),
        lax.all_gather(value_collection, "blk", axis=1, tiled=True),
    )
    key_all = key_all.reshape(seq_count, -1, KV_HEADS, HEAD_DIM)
    value_all = value_all.reshape(seq_count, -1, KV_HEADS, HEAD_DIM)
    allowed = attention_mask(positions, all_slots)
    scores = (
        jnp.einsum("sqgcd,skgd->sgcqk", queries, key_all, preferred_element_type=jnp.float32)
        * attn_scale
    )
    scores = jnp.where(allowed, scores, masked_fill)
    row_max = jnp.max(scores, axis=-1)
    raised = jnp.where(allowed, jnp.exp(scores - row_max[..., None]), 0.0)
    total = jnp.sum(raised, axis=-1)
    safe_sum = jnp.where(total > 0, total, 1.0)
    chances = (raised / safe_sum[..., None]).astype(jnp.bfloat16)
    attended = jnp.einsum(
        "sgcqk,skgd->sqgcd", chances, value_all, preferred_element_type=jnp.float32
    )
    attended = attended.reshape(seq_count, slot_count, HEADS * HEAD_DIM)
    summary = row_max + jnp.log(safe_sum)
    attention_reduced = attended.astype(jnp.bfloat16)
    branch_result = jnp.dot(
        attention_reduced, output_projection, preferred_element_type=jnp.float32
    )
    middle = tokens + branch_result
    second_scale = lax.rsqrt(jnp.mean(middle * middle, axis=-1, keepdims=True) + eps)
    normalized_second = (middle * second_scale * gain_two.astype(jnp.float32)).astype(jnp.bfloat16)
    gate_preactivation = jnp.dot(
        normalized_second, gate_projection, preferred_element_type=jnp.float32
    )
    up_preactivation = jnp.dot(normalized_second, up_projection, preferred_element_type=jnp.float32)
    hidden_activation = (jax.nn.silu(gate_preactivation) * up_preactivation).astype(jnp.bfloat16)
    feedforward_output = jnp.dot(
        hidden_activation, down_projection, preferred_element_type=jnp.float32
    )
    router_gate = jax.nn.sigmoid(
        jnp.sum(tokens * router_matrix[:, recursion].astype(jnp.float32), axis=-1)
    )
    result = tokens + router_gate[..., None] * (branch_result + feedforward_output)
    stored = (
        tokens,
        positions,
        cosine,
        sine_part,
        first_scale,
        normalized_input,
        queries,
        keyset,
        value_collection,
        attention_reduced,
        summary,
        branch_result,
        middle,
        second_scale,
        normalized_second,
        gate_preactivation.astype(jnp.bfloat16),
        up_preactivation.astype(jnp.bfloat16),
        hidden_activation,
        feedforward_output,
        router_gate,
    )
    return (result, stored)


def block_backward(incoming, stored, gathered, recursion, all_slots):
    (
        query_projection,
        key_projection,
        value_projection,
        output_projection,
        gate_projection,
        up_projection,
        down_projection,
        gain_one,
        gain_two,
        router_matrix,
    ) = gathered
    (
        tokens,
        positions,
        cosine,
        sine_part,
        first_scale,
        normalized_input,
        queries,
        keyset,
        value_collection,
        attention_reduced,
        summary,
        branch_result,
        middle,
        second_scale,
        normalized_second,
        gate_preactivation,
        up_preactivation,
        hidden_activation,
        feedforward_output,
        router_gate,
    ) = stored
    seq_count, slot_count, model_width = tokens.shape
    groups = HEADS // KV_HEADS
    attn_scale = 1.0 / math.sqrt(HEAD_DIM)
    router_column = router_matrix[:, recursion].astype(jnp.float32)
    branches = branch_result + feedforward_output
    gate_grad = jnp.sum(incoming * branches, axis=-1)
    logit_grad = gate_grad * router_gate * (1.0 - router_gate)
    token_grad = incoming + logit_grad[..., None] * router_column
    router_grad = jnp.einsum("sr,srd->d", logit_grad, tokens, precision=lax.Precision.HIGHEST)
    scaled_grad = router_gate[..., None] * incoming
    feed_grad = scaled_grad.astype(jnp.bfloat16)
    grad_down = jnp.einsum(
        "srf,srd->fd", hidden_activation, feed_grad, preferred_element_type=jnp.float32
    )
    hidden_grad = jnp.einsum(
        "srd,fd->srf", feed_grad, down_projection, preferred_element_type=jnp.float32
    )
    gate_preactivation = gate_preactivation.astype(jnp.float32)
    up_preactivation = up_preactivation.astype(jnp.float32)
    gate_sigmoid = jax.nn.sigmoid(gate_preactivation)
    up_grad = (hidden_grad * gate_preactivation * gate_sigmoid).astype(jnp.bfloat16)
    gate_pre_grad = (
        hidden_grad
        * up_preactivation
        * gate_sigmoid
        * (1.0 + gate_preactivation * (1.0 - gate_sigmoid))
    ).astype(jnp.bfloat16)
    grad_gate = jnp.einsum(
        "srd,srf->df", normalized_second, gate_pre_grad, preferred_element_type=jnp.float32
    )
    grad_up = jnp.einsum(
        "srd,srf->df", normalized_second, up_grad, preferred_element_type=jnp.float32
    )
    normed_two_grad = jnp.einsum(
        "srf,df->srd", gate_pre_grad, gate_projection, preferred_element_type=jnp.float32
    ) + jnp.einsum("srf,df->srd", up_grad, up_projection, preferred_element_type=jnp.float32)
    grad_second = jnp.sum(normed_two_grad * middle * second_scale, axis=(0, 1))
    shaped = normed_two_grad * gain_two.astype(jnp.float32)
    middle_grad = second_scale * shaped - second_scale**3 * middle * jnp.mean(
        shaped * middle, axis=-1, keepdims=True
    )
    token_grad = token_grad + middle_grad
    branch_grad = (scaled_grad + middle_grad).astype(jnp.bfloat16)
    grad_output = jnp.einsum(
        "srq,srd->qd", attention_reduced, branch_grad, preferred_element_type=jnp.float32
    )
    attn_grad = jnp.einsum(
        "srd,qd->srq", branch_grad, output_projection, preferred_element_type=jnp.float32
    )
    attn_grad = attn_grad.astype(jnp.bfloat16).reshape(
        seq_count, slot_count, KV_HEADS, groups, HEAD_DIM
    )
    key_all, value_all = (
        lax.all_gather(as_sent(keyset), "blk", axis=1, tiled=True).astype(keyset.dtype),
        lax.all_gather(as_sent(value_collection), "blk", axis=1, tiled=True).astype(
            value_collection.dtype
        ),
    )
    key_all = key_all.reshape(seq_count, -1, KV_HEADS, HEAD_DIM)
    value_all = value_all.reshape(seq_count, -1, KV_HEADS, HEAD_DIM)
    def one_sequence(queries, key_all, value_all, attn_grad, summary, positions, all_slots):
        allowed = attention_mask(positions, all_slots)
        scores = (
            jnp.einsum("sqgcd,skgd->sgcqk", queries, key_all, preferred_element_type=jnp.float32)
            * attn_scale
        )
        chances = jnp.where(allowed, jnp.exp(scores - summary[..., None]), 0.0)
        chance_grad = jnp.einsum(
            "sqgcd,skgd->sgcqk", attn_grad, value_all, preferred_element_type=jnp.float32
        )
        row_dots = jnp.sum(chances * chance_grad, axis=-1)
        score_grad = (chances * (chance_grad - row_dots[..., None])).astype(jnp.bfloat16)
        query_grad = (
            jnp.einsum("sgcqk,skgd->sqgcd", score_grad, key_all, preferred_element_type=jnp.float32)
            * attn_scale
        )
        key_grad_all = (
            jnp.einsum("sgcqk,sqgcd->skgd", score_grad, queries, preferred_element_type=jnp.float32)
            * attn_scale
        )
        value_grad_all = jnp.einsum(
            "sgcqk,sqgcd->skgd",
            chances.astype(jnp.bfloat16),
            attn_grad,
            preferred_element_type=jnp.float32,
        )

        return query_grad, key_grad_all.astype(jnp.bfloat16), value_grad_all.astype(jnp.bfloat16)

    pieces, token = [], None
    for s in range(seq_count):
        args = tuple(v[s:s + 1] for v in (queries, key_all, value_all, attn_grad, summary, positions, all_slots))
        if pieces:
            args, last = lax.optimization_barrier((args, pieces[-1]))
            pieces[-1] = last
        pieces.append(one_sequence(*args))
    query_grad, key_grad_all, value_grad_all = (jnp.concatenate(v, axis=0) for v in zip(*pieces))
    key_grad, value_grad = (
        lax.psum_scatter(
            key_grad_all.reshape(seq_count, -1, KV_HEADS * HEAD_DIM).astype(jnp.bfloat16),
            "blk",
            scatter_dimension=1,
            tiled=True,
        ).astype(jnp.float32),
        lax.psum_scatter(
            value_grad_all.reshape(seq_count, -1, KV_HEADS * HEAD_DIM).astype(jnp.bfloat16),
            "blk",
            scatter_dimension=1,
            tiled=True,
        ).astype(jnp.float32),
    )
    query_raw_grad = rotate_back(
        query_grad.reshape(seq_count, slot_count, HEADS, HEAD_DIM), cosine, sine_part
    )
    query_raw_grad = query_raw_grad.astype(jnp.bfloat16).reshape(
        seq_count, slot_count, HEADS * HEAD_DIM
    )
    key_raw_grad = rotate_back(
        key_grad.reshape(seq_count, slot_count, KV_HEADS, HEAD_DIM), cosine, sine_part
    )
    key_raw_grad = key_raw_grad.astype(jnp.bfloat16).reshape(
        seq_count, slot_count, KV_HEADS * HEAD_DIM
    )
    value_low = value_grad.astype(jnp.bfloat16)
    grad_query = jnp.einsum(
        "srd,srq->dq", normalized_input, query_raw_grad, preferred_element_type=jnp.float32
    )
    grad_key = jnp.einsum(
        "srd,srk->dk", normalized_input, key_raw_grad, preferred_element_type=jnp.float32
    )
    grad_value = jnp.einsum(
        "srd,srk->dk", normalized_input, value_low, preferred_element_type=jnp.float32
    )
    normed_grad = (
        jnp.einsum(
            "srq,dq->srd", query_raw_grad, query_projection, preferred_element_type=jnp.float32
        )
        + jnp.einsum(
            "srk,dk->srd", key_raw_grad, key_projection, preferred_element_type=jnp.float32
        )
        + jnp.einsum("srk,dk->srd", value_low, value_projection, preferred_element_type=jnp.float32)
    )
    grad_first = jnp.sum(normed_grad * tokens * first_scale, axis=(0, 1))
    shaped_one = normed_grad * gain_one.astype(jnp.float32)
    token_grad = (
        token_grad
        + first_scale * shaped_one
        - first_scale**3 * tokens * jnp.mean(shaped_one * tokens, axis=-1, keepdims=True)
    )
    matrices = (
        grad_query,
        grad_key,
        grad_value,
        grad_output,
        grad_gate,
        grad_up,
        grad_down,
        grad_first,
        grad_second,
    )
    return (token_grad, matrices, router_grad)


MESH = pl.DeviceIdType.MESH

NZ, NX = 4, 2
G = NZ * NX


def gather_kernel(chunks, nslab, *refs):
    ins, outs = refs[:nslab], refs[nslab:2 * nslab]
    ls, zs, zr, xs, xr, ys, yr, cs, cr = refs[2 * nslab:]
    dp, blk = lax.axis_index("dp"), lax.axis_index("blk")
    z, x = dp // NX, lax.rem(dp, NX)
    y, c = blk // 2, lax.rem(blk, 2)
    left, right = (dp - NX, blk), (dp + NX, blk)
    xm, ym, cm = (dp + 1 - 2 * x, blk), (dp, lax.rem(blk + 2, 4)), (dp, blk + 1 - 2 * c)
    bar = pltpu.get_barrier_semaphore()
    for t in (xm, ym, cm):
        pl.semaphore_signal(bar, inc=1, device_id=t, device_id_type=MESH)

    @pl.when(z > 0)
    def _():
        pl.semaphore_signal(bar, inc=1, device_id=left, device_id_type=MESH)

    @pl.when(z < NZ - 1)
    def _():
        pl.semaphore_signal(bar, inc=1, device_id=right, device_id_type=MESH)

    pl.semaphore_wait(bar, 3 + jnp.where(z > 0, 1, 0) + jnp.where(z < NZ - 1, 1, 0))

    locs = [pltpu.make_async_copy(ins[s], outs[s].at[dp], ls.at[s]) for s in range(nslab)]
    for l in locs:
        l.start()

    def piece(i, g, q):
        s, c0, n, split = chunks[i]
        return outs[s].at[g, q, :, pl.ds(c0, n)]

    def myq(i):
        return blk if chunks[i][3] == 4 else c

    def rem(src, dst, a, b, to):
        return pltpu.make_async_remote_copy(src_ref=src, dst_ref=dst, send_sem=a, recv_sem=b, device_id=to, device_id_type=MESH)

    def own(i):
        s, c0, n, split = chunks[i]
        return ins[s].at[myq(i), :, pl.ds(c0, n)]

    def zcopy(i, d, s, src_own):
        zz = z - s if d == 0 else z + s
        p = piece(i, zz * NX + x, myq(i))
        return rem(own(i) if src_own else p, p, zs.at[i, d, s], zr.at[i, d, s], right if d == 0 else left)

    def zrecv(i, d, s):
        zz = z - 1 - s if d == 0 else z + 1 + s
        p = piece(i, zz * NX + x, myq(i))
        return rem(p, p, zs.at[i, d, s], zr.at[i, d, s], right if d == 0 else left)

    def xcopy(i, zz, src_own=False):
        p = piece(i, zz * NX + x, myq(i))
        return rem(own(i) if src_own else p, p, xs.at[i, zz], xr.at[i, zz], xm)

    def xrecv(i, zz):
        p = piece(i, zz * NX + 1 - x, myq(i))
        return rem(p, p, xs.at[i, zz], xr.at[i, zz], xm)

    def ycopy(i, g):
        p = piece(i, g, blk)
        return rem(p, p, ys.at[i, g], yr.at[i, g], ym)

    def yrecv(i, g):
        p = piece(i, g, lax.rem(blk + 2, 4))
        return rem(p, p, ys.at[i, g], yr.at[i, g], ym)

    def ccopy(i, k, g):
        q = myq(i) if k == 0 else lax.rem(blk + 2, 4)
        p = piece(i, g, q)
        return rem(p, p, cs.at[i, k, g], cr.at[i, k, g], cm)

    def crecv(i, k, g):
        if chunks[i][3] == 4:
            mate = blk + 1 - 2 * c
            q = mate if k == 0 else lax.rem(mate + 2, 4)
        else:
            q = 1 - c
        p = piece(i, g, q)
        return rem(p, p, cs.at[i, k, g], cr.at[i, k, g], cm)

    def spread(i, g):
        if chunks[i][3] == 4:
            ycopy(i, g).start()
        ccopy(i, 0, g).start()

    nch = len(chunks)

    def begin(i):
        @pl.when(z < NZ - 1)
        def _():
            zcopy(i, 0, 0, True).start()

        @pl.when(z > 0)
        def _():
            zcopy(i, 1, 0, True).start()
        xcopy(i, z, True).start()

    def zstep(i, s):
        @pl.when(z - 1 - s >= 0)
        def _():
            zrecv(i, 0, s).wait_recv()
            if s < NZ - 2:
                @pl.when(z < NZ - 1)
                def _():
                    zcopy(i, 0, s + 1, False).start()
            xcopy(i, z - 1 - s).start()
            spread(i, (z - 1 - s) * NX + x)

        @pl.when(z + 1 + s < NZ)
        def _():
            zrecv(i, 1, s).wait_recv()
            if s < NZ - 2:
                @pl.when(z > 0)
                def _():
                    zcopy(i, 1, s + 1, False).start()
            xcopy(i, z + 1 + s).start()
            spread(i, (z + 1 + s) * NX + x)

    def xstep(i, k):
        def one(zz):
            xrecv(i, zz).wait_recv()
            spread(i, zz * NX + 1 - x)
        if k == 0:
            one(z)
        else:
            pl.when(z - k >= 0)(lambda: one(z - k))
            pl.when(z + k < NZ)(lambda: one(z + k))

    def ystep(i, k):
        g = lax.rem(dp + k, G)
        yrecv(i, g).wait_recv()
        ccopy(i, 1, g).start()

    def cstep(i, k):
        g = lax.rem(dp + k, G)
        crecv(i, 0, g).wait_recv()
        if chunks[i][3] == 4:
            crecv(i, 1, g).wait_recv()

    def sent(i):
        @pl.when(z < NZ - 1)
        def _():
            zcopy(i, 0, 0, True).wait_send()

        @pl.when(z > 0)
        def _():
            zcopy(i, 1, 0, True).wait_send()
        for s in range(NZ - 1):
            if s < NZ - 2:
                @pl.when((z - 1 - s >= 0) & (z < NZ - 1))
                def _():
                    zcopy(i, 0, s + 1, False).wait_send()

                @pl.when((z + 1 + s < NZ) & (z > 0))
                def _():
                    zcopy(i, 1, s + 1, False).wait_send()
        xcopy(i, z, True).wait_send()
        for k in range(1, NZ):
            xcopy(i, lax.rem(z + k, NZ)).wait_send()
        for k in range(1, G):
            g = lax.rem(dp + k, G)
            ccopy(i, 0, g).wait_send()
            if chunks[i][3] == 4:
                ycopy(i, g).wait_send()
                ccopy(i, 1, g).wait_send()

    stages = [begin] + [functools.partial(lambda i, s: (zstep(i, s), xstep(i, s)), s=s) for s in range(NZ - 1)]
    stages.append(lambda i: xstep(i, NZ - 1))
    stages.append(lambda i: [ystep(i, k) for k in range(1, G)] if chunks[i][3] == 4 else None)
    stages.append(lambda i: [cstep(i, k) for k in range(1, G)])
    stages.append(sent)
    for t in range(nch + len(stages) - 1):
        for s in reversed(range(len(stages))):
            i = t - s
            if 0 <= i < nch:
                stages[s](i)
    for l in locs:
        l.wait()


def gather(slabs, chunks):
    n, nch = len(slabs), len(chunks)
    dma = pltpu.SemaphoreType.DMA
    return pl.pallas_call(
        functools.partial(gather_kernel, chunks, n),
        out_shape=[jax.ShapeDtypeStruct((G,) + s.shape, s.dtype) for s in slabs],
        in_specs=[pl.BlockSpec(memory_space=pl.ANY)] * n,
        out_specs=[pl.BlockSpec(memory_space=pl.ANY)] * n,
        scratch_shapes=[dma((n,)), dma((nch, 2, NZ - 1)), dma((nch, 2, NZ - 1)), dma((nch, NZ)), dma((nch, NZ)),
                        dma((nch, G)), dma((nch, G)), dma((nch, 2, G)), dma((nch, 2, G))],
        compiler_params=pltpu.CompilerParams(collective_id=1, has_side_effects=True),
        name="gather_weights",
    )(*slabs)


def add_into(dst, other, n):
    def body(k, _):
        dst[k] = (dst[k].astype(jnp.float32) + other(k).astype(jnp.float32)).astype(dst.dtype)
        return 0
    lax.fori_loop(0, n, body, 0)


def reduce_kernel(chunks, nslab, *refs):
    nch = len(chunks)
    ins, outs = refs[:nslab], refs[nslab:2 * nslab]
    bufs = refs[2 * nslab:]
    own, crv, yrv, xrv, zrv, fin, s4b = (bufs[k * nch:(k + 1) * nch] for k in range(7))
    ls, cs, cr, ys, yr, xs, xr, zs, zr, fs, fr = bufs[7 * nch:]
    dp, blk = lax.axis_index("dp"), lax.axis_index("blk")
    z, x = dp // NX, lax.rem(dp, NX)
    y, c = blk // 2, lax.rem(blk, 2)
    left, right = (dp - NX, blk), (dp + NX, blk)
    xm, ym, cm = (dp + 1 - 2 * x, blk), (dp, lax.rem(blk + 2, 4)), (dp, blk + 1 - 2 * c)
    bar = pltpu.get_barrier_semaphore()
    for t in (xm, ym, cm):
        pl.semaphore_signal(bar, inc=1, device_id=t, device_id_type=MESH)

    @pl.when(z > 0)
    def _():
        pl.semaphore_signal(bar, inc=1, device_id=left, device_id_type=MESH)

    @pl.when(z < NZ - 1)
    def _():
        pl.semaphore_signal(bar, inc=1, device_id=right, device_id_type=MESH)

    pl.semaphore_wait(bar, 3 + jnp.where(z > 0, 1, 0) + jnp.where(z < NZ - 1, 1, 0))

    def rem(src, dst, a, b, to):
        return pltpu.make_async_remote_copy(src_ref=src, dst_ref=dst, send_sem=a, recv_sem=b, device_id=to, device_id_type=MESH)

    def four(i):
        return chunks[i][3] == 4

    def part(i, core):
        s, c0, n, split = chunks[i]
        cols = pl.ds(c0, n)
        return ins[s].at[:, :, :, core, :, cols] if split == 4 else ins[s].at[:, :, core, :, cols]

    def load(i):
        return pltpu.make_async_copy(part(i, c), own[i], ls.at[i])

    def core_send(i):
        return rem(part(i, 1 - c), crv[i], cs.at[i, 0], cr.at[i, 0], cm)

    def y_send(i):
        return rem(own[i].at[:, :, 1 - y], yrv[i], ys.at[i], yr.at[i], ym)

    def s2(i):
        return yrv[i] if four(i) else own[i]

    def x_send(i):
        return rem(s2(i).at[:, 1 - x], xrv[i], xs.at[i], xr.at[i], xm)

    def z_copy(i, d, lo, hi, first, to):
        src = xrv[i].at[pl.ds(lo, hi - lo)] if first else zrv[i].at[d, pl.ds(lo, hi - lo)]
        return rem(src, zrv[i].at[d, pl.ds(lo, hi - lo)], zs.at[i, d], zr.at[i, d], to)

    def right_send(i, k):
        return z_copy(i, 0, k + 1, NZ, k == 0, right)

    def left_send(i, k):
        return z_copy(i, 1, 0, k, k == NZ - 1, left)

    def st0(i):
        load(i).start()
        core_send(i).start()

    def st1(i):
        load(i).wait()
        core_send(i).wait_recv()

        def body(g, _):
            zz, xx = g // NX, lax.rem(g, NX)
            for yy in ((0, 1) if four(i) else (None,)):
                at = (zz, xx) if yy is None else (zz, xx, yy)
                own[i][at] = (own[i][at].astype(jnp.float32) + crv[i][at].astype(jnp.float32)).astype(jnp.bfloat16)
            return 0
        lax.fori_loop(0, G, body, 0)
        if four(i):
            y_send(i).start()

    def st2(i):
        if four(i):
            y_send(i).wait_recv()

            def body(g, _):
                zz, xx = g // NX, lax.rem(g, NX)
                yrv[i][zz, xx] = (yrv[i][zz, xx].astype(jnp.float32) + own[i][zz, xx, y].astype(jnp.float32)).astype(jnp.bfloat16)
                return 0
            lax.fori_loop(0, G, body, 0)
        x_send(i).start()

    def zstep(i, s):
        if s < NZ - 1:
            @pl.when(z == s)
            def _():
                if s > 0:
                    z_copy(i, 0, s, NZ, False, right).wait_recv()
                    for k in range(s + 1, NZ):
                        zrv[i][0, k] = (zrv[i][0, k].astype(jnp.float32) + xrv[i][k].astype(jnp.float32)).astype(jnp.bfloat16)
                right_send(i, s).start()

            @pl.when(z == NZ - 1 - s)
            def _():
                k0 = NZ - 1 - s
                if s > 0:
                    z_copy(i, 1, 0, k0 + 1, False, left).wait_recv()
                    for k in range(k0):
                        zrv[i][1, k] = (zrv[i][1, k].astype(jnp.float32) + xrv[i][k].astype(jnp.float32)).astype(jnp.bfloat16)
                left_send(i, k0).start()

    def st3(i):
        x_send(i).wait_recv()
        add_into(xrv[i], lambda k: s2(i)[k, x], NZ)
        zstep(i, 0)

    def finish(i):
        q = blk if four(i) else c
        dst = fin[i].at[q] if four(i) else s4b[i]

        def put(v):
            if four(i):
                fin[i][blk] = v.astype(jnp.bfloat16)
            else:
                s4b[i][...] = v.astype(jnp.bfloat16)

        @pl.when(z == 0)
        def _():
            z_copy(i, 1, 0, 1, False, left).wait_recv()
            put(xrv[i][0].astype(jnp.float32) + zrv[i][1, 0].astype(jnp.float32))

        @pl.when(z == NZ - 1)
        def _():
            z_copy(i, 0, NZ - 1, NZ, False, right).wait_recv()
            put(xrv[i][NZ - 1].astype(jnp.float32) + zrv[i][0, NZ - 1].astype(jnp.float32))

        @pl.when((z > 0) & (z < NZ - 1))
        def _():
            put(xrv[i][z].astype(jnp.float32) + zrv[i][0, z].astype(jnp.float32) + zrv[i][1, z].astype(jnp.float32))
        if four(i):
            fin_send(i, 0).start()
            fin_send(i, 1).start()
        else:
            fin_send(i, 0).start()

    def fin_send(i, k):
        if four(i):
            q = blk if k < 2 else lax.rem(blk + 2, 4)
            return rem(fin[i].at[q], fin[i].at[q], fs.at[i, k], fr.at[i, k], ym if k == 0 else cm)
        if k == 0:
            return rem(s4b[i], fin[i].at[2], fs.at[i, 0], fr.at[i, 0], ym)
        return rem(fin[i].at[c], fin[i].at[c], fs.at[i, 1], fr.at[i, 1], cm)

    def fin_recv(i, k):
        if four(i):
            mate = blk + 1 - 2 * c
            q = lax.rem(blk + 2, 4) if k == 0 else mate if k == 1 else lax.rem(mate + 2, 4)
            return rem(fin[i].at[q], fin[i].at[q], fs.at[i, k], fr.at[i, k], cm)
        if k == 0:
            return fin_send(i, 0)
        return rem(fin[i].at[1 - c], fin[i].at[1 - c], fs.at[i, 1], fr.at[i, 1], cm)

    def st8(i):
        fin_recv(i, 0).wait_recv()
        if four(i):
            fin_send(i, 2).start()
        else:
            fin[i][c] = (fin[i][2].astype(jnp.float32) + s4b[i][...].astype(jnp.float32)).astype(jnp.bfloat16)
            fin_send(i, 1).start()

    def st9(i):
        s, c0, n, split = chunks[i]
        for k in ((1, 2) if four(i) else (1,)):
            fin_recv(i, k).wait_recv()
        for q in range(split):
            outs[s][q, :, pl.ds(c0, n)] = fin[i][q].astype(jnp.float32)

    def sent(i):
        core_send(i).wait_send()
        if four(i):
            y_send(i).wait_send()
        x_send(i).wait_send()
        for k in range(NZ - 1):
            pl.when(z == k)(lambda k=k: right_send(i, k).wait_send())
            pl.when(z == k + 1)(lambda k=k: left_send(i, k + 1).wait_send())
        for k in range(3 if four(i) else 2):
            fin_send(i, k).wait_send()

    stages = [st1, st2, st3] + [functools.partial(lambda i, s: zstep(i, s), s=s) for s in range(1, NZ - 1)] + [finish, st8, st9, sent]
    for i in range(nch):
        st0(i)
    for t in range(nch + len(stages) - 1):
        for s in reversed(range(len(stages))):
            i = t - s
            if 0 <= i < nch:
                stages[s](i)


def reduce(slabs, chunks):
    n, nch = len(slabs), len(chunks)
    dma = pltpu.SemaphoreType.DMA
    bf = jnp.bfloat16

    def shapes(kind):
        out = []
        for s, c0, nc, split in chunks:
            h = slabs[s].shape[-2]
            lead = (NZ, NX, 2) if split == 4 else (NZ, NX)
            tiny = (1, 16, 128)
            shape = dict(own=lead + (h, nc), crv=lead + (h, nc), yrv=(NZ, NX, h, nc) if split == 4 else tiny,
                         xrv=(NZ, h, nc), zrv=(2, NZ, h, nc), fin=(4 if split == 4 else 3, h, nc),
                         s4b=(h, nc) if split == 2 else tiny)[kind]
            out.append(pltpu.VMEM(shape, bf))
        return out
    scratch = sum([shapes(k) for k in ("own", "crv", "yrv", "xrv", "zrv", "fin", "s4b")], [])
    sems = [dma((nch,)), dma((nch, 1)), dma((nch, 1)), dma((nch,)), dma((nch,)), dma((nch,)), dma((nch,)),
            dma((nch, 2)), dma((nch, 2)), dma((nch, 3)), dma((nch, 3))]
    outs = []
    for k, s in enumerate(slabs):
        split = next(ch[3] for ch in chunks if ch[0] == k)
        outs.append(jax.ShapeDtypeStruct((split,) + s.shape[-2:], jnp.float32))
    return pl.pallas_call(
        functools.partial(reduce_kernel, chunks, n),
        out_shape=outs,
        in_specs=[pl.BlockSpec(memory_space=pl.ANY)] * n,
        out_specs=[pl.BlockSpec(memory_space=pltpu.VMEM)] * n,
        scratch_shapes=scratch + sems,
        compiler_params=pltpu.CompilerParams(collective_id=2, has_side_effects=True, vmem_limit_bytes=60 << 20),
        name="reduce_grads",
    )(*slabs)

AG_CHUNKS = [(0, 0, 1664, 4), (1, 0, 1024, 2), (2, 0, 1280, 4), (2, 1280, 1280, 4), (3, 0, 512, 2), (2, 2560, 1280, 4),
             (2, 3840, 1280, 4), (3, 512, 512, 2)]
RS_CHUNKS = [(2, 0, 1280, 4), (3, 0, 512, 2), (2, 1280, 1280, 4), (2, 2560, 1280, 4), (3, 512, 512, 2), (2, 3840, 1280, 4),
             (1, 0, 1024, 2), (0, 0, 896, 4), (0, 896, 768, 4)]


def pad_to(v, shape):
    return jnp.pad(v, [(0, b - a) for a, b in zip(v.shape, shape)])


def gather_weights(weights):
    n_dp, n_blk = lax.axis_size("dp"), lax.axis_size("blk")
    if (n_dp, n_blk) != (G, 4):
        return tuple(lax.all_gather(w, "dp", axis=0, tiled=True) for w in weights)
    q, k, v, o, g, u, d, g1, g2, rt = weights
    a = jnp.concatenate([q, k, v, g1[:, None], g2[:, None], rt], axis=1)
    gu = jnp.concatenate([g, u], axis=1)
    slabs = [pad_to(a, (128, 1664)).reshape(4, 32, 1664), pad_to(o, (128, 1024)).reshape(2, 64, 1024),
             pad_to(gu, (128, 5120)).reshape(4, 32, 5120), pad_to(d, (320, 1024)).reshape(2, 160, 1024)]
    a, o, gu, d = gather(slabs, AG_CHUNKS)
    rows = q.shape[0]
    a = a.reshape(G, 128, 1664)[:, :rows].reshape(G * rows, 1664)
    o = o.reshape(G, 128, 1024)[:, :rows].reshape(G * rows, 1024)[:, :960]
    gu = gu.reshape(G, 128, 5120)[:, :rows].reshape(G * rows, 5120)
    d = d.reshape(2560, 1024)[:, :960]
    return (a[:, :960], a[:, 960:1280], a[:, 1280:1600], o, gu[:, :2560], gu[:, 2560:], d,
            a[:, 1600], a[:, 1601], a[:, 1602:1605])


def reduce_grads(grads):
    n_dp, n_blk = lax.axis_size("dp"), lax.axis_size("blk")
    bf = jnp.bfloat16
    if (n_dp, n_blk) != (G, 4):
        shares = [lax.psum_scatter(v.astype(bf), "dp", scatter_dimension=0, tiled=True) for v in grads]
        return tuple(lax.psum(v, "blk").astype(jnp.float32) for v in shares)
    q, k, v, o, g, u, d, g1, g2, rt = grads
    rows = q.shape[0] // G
    a = jnp.concatenate([q, k, v, g1[:, None], g2[:, None], rt], axis=1).astype(bf)
    gu = jnp.concatenate([g, u], axis=1).astype(bf)
    a = pad_to(a.reshape(G, rows, -1), (G, 128, 1664)).reshape(NZ, NX, 2, 2, 32, 1664)
    o = pad_to(o.astype(bf).reshape(G, rows, -1), (G, 128, 1024)).reshape(NZ, NX, 2, 64, 1024)
    gu = pad_to(gu.reshape(G, rows, -1), (G, 128, 5120)).reshape(NZ, NX, 2, 2, 32, 5120)
    d = pad_to(d.astype(bf), (2560, 1024)).reshape(NZ, NX, 2, 160, 1024)
    a, o, gu, d = reduce([a, o, gu, d], RS_CHUNKS)
    a = a.reshape(128, 1664)[:rows]
    o = o.reshape(128, 1024)[:rows, :960]
    gu = gu.reshape(128, 5120)[:rows]
    d = d.reshape(320, 1024)[:, :960]
    return (a[:, :960], a[:, 960:1280], a[:, 1280:1600], o, gu[:, :2560], gu[:, 2560:], d,
            a[:, 1600], a[:, 1601], a[:, 1602:1605])


def per_device(
    block_input,
    cotangent,
    seq_lengths,
    routes_two,
    routes_three,
    query_weight,
    key_weight,
    value_weight,
    output_weight,
    gate_weight,
    up_weight,
    down_weight,
    first_gain,
    second_gain,
    router_weight,
):
    micro_count, seq_count, block_len, model_width = block_input.shape
    blocks = lax.axis_size("blk")
    device = lax.axis_index("blk")
    capacity = (block_len, block_len // 2, block_len // 4)
    all_places = jnp.arange(block_len * blocks, dtype=jnp.int32)
    gathered = gather_weights((query_weight, key_weight, value_weight, output_weight, gate_weight, up_weight, down_weight,
                               first_gain, second_gain, router_weight))
    flat = lambda v: v.reshape((micro_count * seq_count,) + v.shape[2:])

    def whole(inputs):
        micro_input, micro_cotangent, lengths_now, routes_now_two, routes_now_three = inputs
        slot_sets = (
            jnp.where(all_places[None, :] < lengths_now[:, None], all_places[None, :], -1),
            routed_slots(routes_now_two, blocks, block_len, capacity[1]),
            routed_slots(routes_now_three, blocks, block_len, capacity[2]),
        )
        current = micro_input.astype(jnp.float32)
        records = []
        for recursion in range(RECUR):
            slot_count = capacity[recursion]
            own_slots = lax.dynamic_slice_in_dim(
                slot_sets[recursion], device * slot_count, slot_count, 1
            )
            present = own_slots >= 0
            local_index = jnp.where(present, own_slots - device * block_len, 0)
            if recursion == 0:
                tokens = current
            else:
                tokens = jax.vmap(pick_rows)(current, local_index)
            result, stored = block_forward(
                tokens, own_slots, slot_sets[recursion], gathered, recursion
            )
            target = jnp.where(present, local_index, block_len)
            current = jax.vmap(place_rows)(current, target, result)
            records.append((stored, local_index, target, present))
        upstream = micro_cotangent.astype(jnp.float32)
        matrix_sums = None
        router_columns = [None] * RECUR
        for recursion in range(RECUR - 1, -1, -1):
            stored, local_index, target, present = records[recursion]
            incoming = jnp.where(
                present[..., None], jax.vmap(pick_rows)(upstream, local_index), 0.0
            )
            token_grad, matrices, router_grad = block_backward(
                incoming, stored, gathered, recursion, slot_sets[recursion]
            )
            upstream = jax.vmap(place_rows)(upstream, target, token_grad)
            router_columns[recursion] = router_grad
            if matrix_sums is None:
                matrix_sums = matrices
            else:
                matrix_sums = tuple(
                    (earlier + latest for earlier, latest in zip(matrix_sums, matrices))
                )
        full_grads = matrix_sums + (jnp.stack(router_columns, axis=1),)
        return (full_grads, current.astype(jnp.bfloat16), upstream)

    full_grads, outputs, input_grads = whole(tuple(map(flat, (block_input, cotangent, seq_lengths, routes_two, routes_three))))
    unflat = lambda v: v.reshape(block_input.shape)
    return (unflat(outputs), unflat(input_grads)) + reduce_grads(full_grads)


def solution(mesh):
    in_specs = (
        P(None, "dp", "blk", None),
        P(None, "dp", "blk", None),
        P(None, "dp"),
        P(None, "dp", None),
        P(None, "dp", None),
        P("dp", None),
        P("dp", None),
        P("dp", None),
        P("dp", None),
        P("dp", None),
        P("dp", None),
        P("dp", None),
        P("dp"),
        P("dp"),
        P("dp", None),
    )
    out_specs = (
        P(None, "dp", "blk", None),
        P(None, "dp", "blk", None),
        P("dp", None),
        P("dp", None),
        P("dp", None),
        P("dp", None),
        P("dp", None),
        P("dp", None),
        P("dp", None),
        P("dp"),
        P("dp"),
        P("dp", None),
    )
    return jax.shard_map(
        per_device, mesh=mesh, in_specs=in_specs, out_specs=out_specs, check_vma=False
    )
```

```python
import functools
import math
import types

import jax
import jax.numpy as jnp
import numpy as np
from jax import lax
from jax.experimental import pallas as pl
from jax.experimental.pallas import tpu as pltpu
from jax.sharding import PartitionSpec as P

HEADS, KV_HEADS, HEAD_DIM, RECUR = 15, 5, 64, 3
GROUP = HEADS // KV_HEADS
eps = 1e-05
rope_base = 10000.0
masked_fill = -1e30
BF, F32 = jnp.bfloat16, jnp.float32
COLS_A = 1664
FT = 512


def dot(a, b):
    return lax.dot_general(a, b, (((1,), (0,)), ((), ())), preferred_element_type=F32)


def dot_nt(a, b):
    return lax.dot_general(a, b, (((1,), (1,)), ((), ())), preferred_element_type=F32)


def dot_tn(a, b):
    return lax.dot_general(a, b, (((0,), (0,)), ((), ())), preferred_element_type=F32)


def halves(v):
    high = v.astype(BF)
    return high, (v - high.astype(F32)).astype(BF)


def pick(choice, v):
    high, low = halves(v)
    return dot(choice, high) + dot(choice, low)


def put_back(choice, v):
    high, low = halves(v)
    return dot_tn(choice, high) + dot_tn(choice, low)


def lanes(shape):
    return lax.broadcasted_iota(jnp.int32, shape, len(shape) - 1)


def rowid(shape):
    return lax.broadcasted_iota(jnp.int32, shape, len(shape) - 2)


def swapped(x):
    first = lax.rem(lanes(x.shape), 64) < 32
    return jnp.where(first, pltpu.roll(x, 96, 1), pltpu.roll(x, 32, 1))


def call(name, body, ins, outs, scratch=None, limit=63, hbm=()):
    scratch = scratch or {}
    names = list(ins) + list(outs) + list(scratch)

    def kernel(*refs):
        body(types.SimpleNamespace(**dict(zip(names, refs))))

    vm, anyw = pl.BlockSpec(memory_space=pltpu.VMEM), pl.BlockSpec(memory_space=pl.ANY)
    got = pl.pallas_call(
        kernel,
        out_shape=[jax.ShapeDtypeStruct(s, d) for s, d in outs.values()],
        in_specs=[anyw if k in hbm else pl.BlockSpec(memory_space=pltpu.SMEM) if k == "lens" else vm for k in ins],
        out_specs=[anyw if k in hbm else vm for k in outs],
        scratch_shapes=list(scratch.values()),
        compiler_params=pltpu.CompilerParams(vmem_limit_bytes=limit << 20),
        name=name,
    )(*ins.values())
    return dict(zip(outs, got))


class Geo:
    def __init__(self, ns, bl, n_dp, n_blk, d, ff, tops):
        self.ns, self.bl, self.n_dp, self.n_blk, self.d, self.ff = ns, bl, n_dp, n_blk, d, ff
        self.gw = d // n_dp
        self.gp = -(-self.gw // 16) * 16
        self.dp = n_dp * self.gp
        self.slots = (bl, bl // 2, bl // 4)
        self.tops = tops

    def rows(self, r):
        return self.ns * self.slots[r]

    def keys(self, r):
        return self.n_blk * self.slots[r]

    def spread(self):
        e = np.zeros((1024, self.dp), np.float32)
        f = np.arange(self.d)
        e[f, f // self.gw * self.gp + f % self.gw] = 1
        return jnp.asarray(e, BF)

    def tables(self):
        f = rope_base ** (-(np.arange(32, dtype=np.float64) * 2.0) / 64)
        f32 = np.asarray(f, np.float32)
        ph = (np.arange(self.bl * self.n_blk, dtype=np.float32)[:, None] * f32).astype(np.float32).astype(np.float64)
        c, s = np.cos(ph), np.sin(ph)
        cos = np.concatenate([c, c, c, c], 1).astype(np.float32)
        sin = np.concatenate([-s, s, -s, s], 1).astype(np.float32)
        return jnp.asarray(cos), jnp.asarray(sin)


def gains(wa):
    sel = (lanes((8, 128)) == rowid((8, 128)) + 64).astype(BF)
    return dot_nt(sel, wa[:, 896:1024])


def choose(geo, r, routes, blk):
    s, t, bl = geo.slots[r], geo.tops[r], geo.bl
    before = jnp.sum((routes < blk * bl).astype(F32), axis=1, keepdims=True).astype(jnp.int32)
    shift = ((lanes((s, t)) - rowid((s, t))) == before).astype(BF)
    here = (routes == rowid((bl, t)) + blk * bl).astype(BF)
    return dot_nt(shift, here).astype(BF)


def allowed(geo, r, routes, blk, turned):
    s, kn, bl = geo.slots[r], geo.keys(r), geo.bl
    shape = (kn, s) if turned else (s, kn)
    key = rowid(shape) if turned else lanes(shape)
    query = lanes(shape) if turned else rowid(shape)
    ok = key <= blk * s + query
    if r > 0:
        t = geo.tops[r]
        inside = (routes // bl == rowid((kn, t)) // s)
        if turned:
            count = jnp.sum(inside.astype(F32), axis=1, keepdims=True)
        else:
            count = dot_nt(jnp.ones((8, t), BF), inside.astype(BF))[0:1]
        ok = ok & (lax.rem(key, s).astype(F32) < count)
    return jnp.where(ok, 0.0, masked_fill)


def project(geo, r, k):
    a = k.a[...].astype(F32)
    n1 = lax.rsqrt(jnp.sum(a * a, axis=-1, keepdims=True) * (1.0 / geo.d) + eps)
    k.u[...] = (a * n1 * k.gn[0:1]).astype(BF)
    k.st[...] = jnp.where(lanes(k.st.shape) == 0, n1, 0.0)
    u = k.u[...]
    cos, sin = k.cos[...], k.sin[...]
    left = lanes(cos.shape) < 64
    for t in range(4):
        both = dot(u, k.wa[:, 256 * t:256 * t + 256])
        for j in range(2):
            x = both[:, 128 * j:128 * j + 128]
            x = (x * cos + swapped(x) * sin).astype(BF).astype(F32) * 0.125
            h = 4 * t + 2 * j
            k.q16[h] = jnp.where(left, x, 0.0).astype(BF)
            if h + 1 < HEADS:
                k.q16[h + 1] = jnp.where(left, pltpu.roll(x, 64, 1), 0.0).astype(BF)
    ckv, skv = jnp.where(left, cos, 1.0), jnp.where(left, sin, 0.0)
    for c0, n in ((1024, 256), (1280, 256), (1536, 128)):
        some = dot(u, k.wa[:, c0:c0 + n])
        for j in range(n // 128):
            x = some[:, 128 * j:128 * j + 128]
            k.kv[:, c0 - 1024 + 128 * j:c0 - 1024 + 128 * j + 128] = (x * ckv + swapped(x) * skv).astype(BF)


def select_rows(geo, r, k, blk):
    s, bl = geo.slots[r], geo.bl
    for m in range(geo.ns):
        ch = choose(geo, r, k.routes[m:m + 1], blk)
        k.choice[m] = ch
        k.a[m * s:m * s + s] = pick(ch, k.h[m * bl:m * bl + bl])
        k.cos[m * s:m * s + s] = pick(ch, k.cosb[...])
        k.sin[m * s:m * s + s] = pick(ch, k.sinb[...])


def attend(geo, r, k, blk):
    s, kn = geo.slots[r], geo.keys(r)

    def seq(m, _):
        kv = k.kvall[:, m]
        k.kvg[...] = kv.reshape(kn, KV_HEADS * 128)
        k.bias[...] = allowed(geo, r, k.routes[pl.ds(m, 1)] if r else None, blk, False)
        row0 = pl.multiple_of(m * s, s)
        k.col[...] = jnp.zeros(k.col.shape, F32)

        def head(h, _):
            kvh = k.kvg[:, pl.ds(pl.multiple_of(h // GROUP * 128, 128), 128)]
            sc = dot_nt(k.q16[h, pl.ds(row0, s)], kvh) + k.bias[...]
            top = jnp.max(sc, axis=-1, keepdims=True)
            p = jnp.exp(sc - top)
            total = jnp.sum(p, axis=-1, keepdims=True)
            o2 = dot(p.astype(BF), kvh) * (1.0 / total)
            k.o16[h] = o2
            k.col[...] = jnp.where(lanes(k.col.shape) == h, top + jnp.log(total), k.col[...])
            return 0
        lax.fori_loop(0, HEADS, head, 0)
        left = lanes((s, 128)) < 64
        for t in range(8):
            odd = k.o16[2 * t + 1] if 2 * t + 1 < HEADS else 0.0
            k.o[pl.ds(row0, s), 128 * t:128 * t + 128] = jnp.where(left, pltpu.roll(k.o16[2 * t], 64, 1), odd).astype(BF)
        k.lse[m] = k.col[...].T[0:16]
        return 0
    lax.fori_loop(0, geo.ns, seq, 0)


class Tiles:
    def __init__(self, geo, k, pre=None):
        self.k, self.n, self.ff, self.pre = k, geo.ff // FT, geo.ff, pre

    def parts(self, t, slot):
        k, c0 = self.k, t * FT
        if not isinstance(t, int):
            c0 = pl.multiple_of(c0, FT)
        cu = c0 + self.ff
        return [pltpu.make_async_copy(k.gu.at[:, pl.ds(c0, FT)], k.gbuf.at[slot], k.tsem.at[slot, 0]),
                pltpu.make_async_copy(k.gu.at[:, pl.ds(cu, FT)], k.ubuf.at[slot], k.tsem.at[slot, 1]),
                pltpu.make_async_copy(k.wd.at[pl.ds(c0, FT)], k.dbuf.at[slot], k.tsem.at[slot, 2])] + [
                    pltpu.make_async_copy(v.at[:, pl.ds(c0, FT)], k.pre.at[slot, j], k.tsem.at[slot, 3 + j])
                    for j, v in enumerate(self.pre or ())]

    def start(self, t, slot):
        for c in self.parts(t, slot):
            c.start()

    def loop(self, step):
        def body(t, _):
            slot = lax.rem(t, 2)

            @pl.when(t + 1 < self.n)
            def _():
                self.start(t + 1, 1 - slot)
            for c in self.parts(t, slot):
                c.wait()
            step(t, slot)
            return 0
        lax.fori_loop(0, self.n, body, 0)

    @staticmethod
    def scratch(geo):
        return dict(gbuf=pltpu.VMEM((2, geo.dp, FT), BF), ubuf=pltpu.VMEM((2, geo.dp, FT), BF),
                    dbuf=pltpu.VMEM((2, FT, geo.dp), BF), tsem=pltpu.SemaphoreType.DMA((2, 5)))


def feed(geo, r, k, blk, tiles):
    s, bl = geo.slots[r], geo.bl
    y = dot(k.o[...], k.wou[...])
    a = k.a[...].astype(F32)
    b = a + y
    n2 = lax.rsqrt(jnp.sum(b * b, axis=-1, keepdims=True) * (1.0 / geo.d) + eps)
    gate = jax.nn.sigmoid(jnp.sum(a * k.gn[2 + r:3 + r], axis=-1, keepdims=True))
    k.b[...] = b.astype(BF)
    k.w[...] = (b * n2 * k.gn[1:2]).astype(BF)
    lane = lanes((geo.rows(r), 128))
    k.sx[...] = jnp.where(lane == 0, n2, jnp.where(lane == 1, gate, 0.0))
    k.acc[...] = y

    def wide(t, slot):
        c0 = t * FT if isinstance(t, int) else pl.multiple_of(t * FT, FT)
        return [pltpu.make_async_copy(k.keep.at[slot, j], ref.at[:, pl.ds(c0, FT)], k.ksem.at[slot, j])
                for j, ref in enumerate((k.gp, k.up))]

    def step(t, slot):
        @pl.when(t >= 2)
        def _():
            for c in wide(t - 2, slot):
                c.wait()
        gp = dot(k.w[...], k.gbuf[slot])
        up = dot(k.w[...], k.ubuf[slot])
        k.keep[slot, 0] = gp.astype(BF)
        k.keep[slot, 1] = up.astype(BF)
        z = (gp * jax.nn.sigmoid(gp) * up).astype(BF)
        k.acc[...] += dot(z, k.dbuf[slot])
        for c in wide(t, slot):
            c.start()
    tiles.loop(step)
    for t in range(max(tiles.n - 2, 0), tiles.n):
        for c in wide(t, t % 2):
            c.wait()
    yf = k.acc[...]
    k.yf[...] = yf.astype(BF)
    delta = yf * k.sx[:, 1:2]
    for m in range(geo.ns):
        if r == 0:
            here = rowid((bl, 1)) + blk * bl < k.lens[m]
            rows = slice(m * bl, m * bl + bl)
            k.h2[rows] = k.a[rows].astype(F32) + jnp.where(here, delta[rows], 0.0)
        else:
            k.h2[m * bl:m * bl + bl] = k.h[m * bl:m * bl + bl] + put_back(k.choice[m], delta[m * s:m * s + s])


def back_feed(geo, r, k, blk, tiles):
    s, bl, rows = geo.slots[r], geo.bl, geo.rows(r)
    k.small[2 + r:3 + r] = jnp.zeros((1, geo.dp), F32)
    k.small[1:2] = jnp.zeros((1, geo.dp), F32)

    def incoming(m):
        here = slice(m * s, m * s + s)
        if r == 0:
            return jnp.where(rowid((bl, 1)) + blk * bl < k.lens[m], k.dh[here], 0.0)
        return k.inc[here]
    for m in range(geo.ns):
        here = slice(m * s, m * s + s)
        if r > 0:
            k.inc[here] = pick(k.choice[m], k.dh[m * bl:m * bl + bl])
        inc = incoming(m)
        gate = k.sx[here, 1:2]
        dg = jnp.sum(inc * k.yf[here].astype(F32), axis=-1, keepdims=True)
        dl = dg * gate * (1.0 - gate)
        k.tok[here] = inc + dl * k.gn[2 + r:3 + r]
        k.small[2 + r:3 + r] += jnp.sum(k.a[here].astype(F32) * dl, axis=0, keepdims=True)
        k.df[here] = (gate * inc).astype(BF)
    k.acc[...] = jnp.zeros(k.acc.shape, F32)

    def wide(t, slot):
        c0 = t * FT if isinstance(t, int) else pl.multiple_of(t * FT, FT)
        return [pltpu.make_async_copy(k.wide.at[slot, j], ref.at[:, pl.ds(c0, FT)], k.wsem.at[slot, j])
                for j, ref in enumerate((k.dgp, k.dup, k.z))]

    def step(t, slot):
        @pl.when(t >= 2)
        def _():
            for c in wide(t - 2, slot):
                c.wait()
        dz = dot_nt(k.df[...], k.dbuf[slot])
        gp = k.pre[slot, 0].astype(F32)
        up = k.pre[slot, 1].astype(F32)
        sig = jax.nn.sigmoid(gp)
        silu = gp * sig
        k.wide[slot, 2] = (silu * up).astype(BF)
        dup = (dz * silu).astype(BF)
        dgp = (dz * up * (sig * (1.0 + gp * (1.0 - sig)))).astype(BF)
        k.wide[slot, 1] = dup
        k.wide[slot, 0] = dgp
        k.acc[...] += dot_nt(dgp, k.gbuf[slot]) + dot_nt(dup, k.ubuf[slot])
        for c in wide(t, slot):
            c.start()
    tiles.loop(step)
    for t in range(max(tiles.n - 2, 0), tiles.n):
        for c in wide(t, t % 2):
            c.wait()
    for m in range(geo.ns):
        here = slice(m * s, m * s + s)
        n2, gate = k.sx[here, 0:1], k.sx[here, 1:2]
        dw = k.acc[here]
        b = k.b[here].astype(F32)
        k.small[1:2] += jnp.sum(dw * (b * n2), axis=0, keepdims=True)
        t = dw * k.gn[1:2]
        db = n2 * t - n2 * n2 * n2 * b * (jnp.sum(t * b, axis=-1, keepdims=True) * (1.0 / geo.d))
        k.tok[here] += db
        k.dy[here] = (gate * incoming(m) + db).astype(BF)


def back_attend(geo, r, k, blk):
    s, kn = geo.slots[r], geo.keys(r)
    rows = geo.rows(r)
    left = lanes((rows, 128)) < 64
    lane = lanes((rows, 128))
    dcol = jnp.zeros((rows, 128), F32)
    for t in range(8):
        x = dot_nt(k.dy[...], k.wou[128 * t:128 * t + 128])
        x = x.astype(BF).astype(F32)
        prod = x * k.o[:, 128 * t:128 * t + 128].astype(F32)
        even = jnp.sum(jnp.where(left, prod, 0.0), axis=-1, keepdims=True)
        dcol = jnp.where(lane == 2 * t, even, dcol)
        k.do16[2 * t] = jnp.where(left, 0.0, pltpu.roll(x, 64, 1)).astype(BF)
        if 2 * t + 1 < HEADS:
            odd = jnp.sum(jnp.where(left, 0.0, prod), axis=-1, keepdims=True)
            dcol = jnp.where(lane == 2 * t + 1, odd, dcol)
            k.do16[2 * t + 1] = jnp.where(left, 0.0, x).astype(BF)
    k.dcol[...] = dcol

    def seq(m, _):
        row0 = pl.multiple_of(m * s, s)
        k.kvg[...] = k.kvall[:, m].reshape(kn, KV_HEADS * 128)
        for g in range(KV_HEADS):
            k.kvt[g] = k.kvg[:, 128 * g:128 * g + 128].astype(F32).T.astype(BF)
        k.bias[...] = allowed(geo, r, k.routes[pl.ds(m, 1)] if r else None, blk, True)
        k.dt[...] = k.dcol[pl.ds(row0, s)].T[0:16]
        k.ct[0] = k.cos[pl.ds(row0, s)].T[0:32] * 0.125
        k.ct[1] = k.sin[pl.ds(row0, s)].T[32:64] * 0.125

        def group(g, _):
            kvh = k.kvg[:, pl.ds(pl.multiple_of(g * 128, 128), 128)]
            total = None
            for j in range(GROUP):
                h = g * GROUP + j
                qh, doh = k.q16[h, pl.ds(row0, s)], k.do16[h, pl.ds(row0, s)]
                p = jnp.exp(dot_nt(kvh, qh) + k.bias[...] - k.lse[m, pl.ds(h, 1)])
                ds = (p * (dot_nt(kvh, doh) - k.dt[pl.ds(h, 1)])).astype(BF)
                part = dot(ds, qh) + dot(p.astype(BF), doh)
                total = part if total is None else total + part
                dqt = dot(k.kvt[g], ds)
                y1, y2 = dqt[0:32], dqt[32:64]
                c, sn = k.ct[0], k.ct[1]
                k.dqt[h, 0:32] = (y1 * c + y2 * sn)
                k.dqt[h, 32:64] = (y2 * c - y1 * sn)
            k.dkv[:, m, :, pl.ds(pl.multiple_of(g * 128, 128), 128)] = total.astype(BF).reshape(geo.n_blk, s, 128)
            return 0
        lax.fori_loop(0, KV_HEADS, group, 0)
        for t in range(8):
            if 2 * t + 1 < HEADS:
                x = k.dqt[2 * t:2 * t + 2].reshape(128, s).T
            else:
                x = jnp.concatenate([k.dqt[2 * t], jnp.zeros((64, s), F32)], axis=0).T
            k.da[pl.ds(row0, s), 128 * t:128 * t + 128] = x.astype(BF)
        return 0
    lax.fori_loop(0, geo.ns, seq, 0)


def back_project(geo, r, k, blk):
    s, bl, rows = geo.slots[r], geo.bl, geo.rows(r)
    cos, sin = k.cos[...], k.sin[...]
    left = lanes(cos.shape) < 64
    ckv, skv = jnp.where(left, cos, 1.0), jnp.where(left, sin, 0.0)
    k.da2[:, 0:1024] = k.da[...]
    for g in range(KV_HEADS):
        x = k.dkvown[:, 128 * g:128 * g + 128].astype(F32)
        k.da2[:, 1024 + 128 * g:1152 + 128 * g] = (x * ckv - swapped(x) * skv).astype(BF)
    for m in range(geo.ns):
        here = slice(m * bl, m * bl + bl)
        mine = slice(m * s, m * s + s)
        du = dot_nt(k.da2[mine], k.wa[...])
        a = k.a[mine].astype(F32)
        n1 = k.st[mine, 0:1]
        k.first[0:1] += jnp.sum(du * (a * n1), axis=0, keepdims=True)
        t1 = du * k.gn[0:1]
        tok = k.tok[mine] + n1 * t1 - n1 * n1 * n1 * a * (jnp.sum(t1 * a, axis=-1, keepdims=True) * (1.0 / geo.d))
        if r == 0:
            ok = rowid((bl, 1)) + blk * bl < k.lens[m]
            k.dh2[here] = jnp.where(ok, tok, k.dh[here])
        else:
            k.dh2[here] = k.dh[here] + put_back(k.choice[m], tok - k.inc[mine])


def ns(**kw):
    return types.SimpleNamespace(**kw)


def block(geo, x, cot, lens, routes, wa, wo, gu, wd, share, give_back):
    blk_of = lambda: lax.axis_index("blk")
    bl, d, dp, ff, nsq, nb = geo.bl, geo.d, geo.dp, geo.ff, geo.ns, geo.n_blk
    full = nsq * bl
    cos_all, sin_all = geo.tables()
    b0 = lax.axis_index("blk") * bl
    cosb = lax.dynamic_slice_in_dim(cos_all, b0, bl, 0)
    sinb = lax.dynamic_slice_in_dim(sin_all, b0, bl, 0)
    spread = geo.spread()
    R, S, KN = [geo.rows(r) for r in range(3)], geo.slots, [geo.keys(r) for r in range(3)]
    V = pltpu.VMEM

    def proj_outs(r):
        return {f"a{r}": ((R[r], dp), BF if r == 0 else F32), f"u{r}": ((R[r], dp), BF), f"q16{r}": ((HEADS, R[r], 128), BF),
                f"kv{r}": ((R[r], 640), BF), f"st{r}": ((R[r], 128), F32),
                f"cos{r}": ((R[r], 128), F32), f"sin{r}": ((R[r], 128), F32)}

    def feed_outs(r):
        return {f"o{r}": ((R[r], 1024), BF), f"lse{r}": ((nsq, 16, S[r]), F32), f"b{r}": ((R[r], dp), BF),
                f"w{r}": ((R[r], dp), BF), f"gp{r}": ((R[r], ff), BF), f"up{r}": ((R[r], ff), BF),
                f"yf{r}": ((R[r], dp), BF), f"sx{r}": ((R[r], 128), F32), f"h{r + 1}": ((full, dp), F32)}

    def attn_scratch(r):
        return dict(kvg=V((KN[r], 640), BF), bias=V((S[r], KN[r]), F32), col=V((S[r], 128), F32),
                    o16=V((HEADS, S[r], 128), F32), acc=V((R[r], dp), F32), keep=V((2, 2, R[r], FT), BF),
                    ksem=pltpu.SemaphoreType.DMA((2, 2)))

    def view(k, r, **more):
        names = ("a", "u", "q16", "kv", "st", "cos", "sin", "o", "lse", "b", "w", "gp", "up", "yf", "sx", "kvall", "routes",
                 "choice", "df", "dgp", "dup", "z", "dy", "tok", "inc", "da", "da2", "dkv", "dkvown")
        out = {n: getattr(k, f"{n}{r}") for n in names if hasattr(k, f"{n}{r}")}
        for n, v in vars(k).items():
            out.setdefault(n, v)
        out.update(more)
        return types.SimpleNamespace(**out)

    env = {}

    def need(*names):
        return {n: env[n] for n in names}

    def k_first(k):
        k.gn = gains(k.wa)
        k.a0[...] = dot(k.x[...], k.spread[0:d]).astype(BF)
        for m in range(nsq):
            k.cos0[m * bl:m * bl + bl] = k.cosb[...]
            k.sin0[m * bl:m * bl + bl] = k.sinb[...]
        project(geo, 0, view(k, 0))

    env.update(x=x, cot=cot, lens=lens, routes1=routes[0], routes2=routes[1], wa=wa, wo=wo, gu=gu, wd=wd, spread=spread,
               cosb=cosb, sinb=sinb)
    env.update(call("first_project", k_first, need("x", "spread", "wa", "cosb", "sinb"), proj_outs(0)))
    env["kvall0"] = share(env["kv0"].reshape(nsq, S[0], 640))

    def k_mid(r, k):
        blk = blk_of()
        tiles = Tiles(geo, k)
        tiles.start(0, 0)
        k.gn = gains(k.wa)
        if r == 0:
            k.wou[...] = dot(k.spread[...], k.wo[...]).astype(BF)
        v = view(k, r, h=getattr(k, f"h{r}", None), h2=getattr(k, f"h{r + 1}"))
        attend(geo, r, v, blk)
        feed(geo, r, v, blk, tiles)
        n = view(k, r + 1, h=getattr(k, f"h{r + 1}"))
        select_rows(geo, r + 1, n, blk)
        project(geo, r + 1, n)

    for r in range(2):
        ins = need("wa", "gu", "wd", f"a{r}", f"q16{r}", f"kvall{r}", "cosb", "sinb", f"routes{r + 1}",
                   *(("wo", "spread", "lens") if r == 0 else ("wou", f"routes{r}", f"choice{r}", f"h{r}")))
        outs = {**feed_outs(r), **proj_outs(r + 1), f"choice{r + 1}": ((nsq, S[r + 1], bl), BF)}
        if r == 0:
            outs["wou"] = ((1024, dp), BF)
        env.update(call(f"forward_{r}", functools.partial(k_mid, r), ins, outs, {**attn_scratch(r), **Tiles.scratch(geo)},
                        hbm=("gu", "wd", f"gp{r}", f"up{r}")))
        env[f"kvall{r + 1}"] = share(env[f"kv{r + 1}"].reshape(nsq, S[r + 1], 640))

    def back_outs(r):
        more = {f"inc{r}": ((R[r], dp), F32), **attend_outs(r)} if r else {}
        return {**more, f"tok{r}": ((R[r], dp), F32), f"df{r}": ((R[r], dp), BF),
                f"dgp{r}": ((R[r], ff), BF), f"dup{r}": ((R[r], ff), BF), f"z{r}": ((R[r], ff), BF),
                f"dy{r}": ((R[r], dp), BF), f"small{r}": ((8, dp), F32)}

    def attend_outs(r):
        return {f"da{r}": ((R[r], 1024), BF), f"dkv{r}": ((nb, nsq, S[r], 640), BF)}

    def back_scratch(r):
        return {**feed_scratch(r), **(turned_scratch(r) if r else {})}

    def turned_scratch(r):
        return dict(kvg=V((KN[r], 640), BF), kvt=V((KV_HEADS, 128, KN[r]), BF), bias=V((KN[r], S[r]), F32),
                    dcol=V((R[r], 128), F32), dt=V((16, S[r]), F32), ct=V((2, 32, S[r]), F32),
                    do16=V((HEADS, R[r], 128), BF), dqt=V((HEADS, 64, S[r]), F32))

    def feed_scratch(r):
        return dict(acc=V((R[r], dp), F32), pre=V((2, 2, R[r], FT), BF), wide=V((2, 3, R[r], FT), BF), wsem=pltpu.SemaphoreType.DMA((2, 3)))

    def back_one(r, k, blk, tiles, dh):
        v = view(k, r, dh=dh, small=getattr(k, f"small{r}"))
        v.small[...] = jnp.zeros(v.small.shape, F32)
        back_feed(geo, r, v, blk, tiles)
        if r > 0:
            back_attend(geo, r, v, blk)

    def k_turn(k):
        blk = blk_of()
        tiles = Tiles(geo, k)
        tiles.start(0, 0)
        k.gn = gains(k.wa)
        v = view(k, 2, h=k.h2, h2=k.h3, acc=k.acc)
        attend(geo, 2, v, blk)
        feed(geo, 2, v, blk, tiles)
        tiles = Tiles(geo, k, (k.gp2, k.up2))
        tiles.start(0, 0)
        k.out[...] = dot_nt(k.h3[...].astype(BF), k.spread[0:d]).astype(BF)
        k.dhe[...] = dot(k.cot[...], k.spread[0:d])
        back_one(2, view(k, 2, bias=k.biast), blk, tiles, k.dhe)

    ins = need("wa", "gu", "wd", "wou", "a2", "q162", "kvall2", "routes2", "choice2", "h2", "spread", "cot", "cos2", "sin2")
    sc = {**attn_scratch(2), **Tiles.scratch(geo)}
    bs = back_scratch(2)
    bs["biast"] = bs.pop("bias")
    outs = {**feed_outs(2), **back_outs(2), "out": ((full, d), BF), "dhe": ((full, dp), F32)}
    env.update(call("turn", k_turn, ins, outs, {**bs, **sc}, hbm=("gu", "wd", "gp2", "up2", "dgp2", "dup2", "z2")))
    env["dh3"] = env["dhe"]

    saved = ("a", "b", "gp", "up", "yf", "sx")
    kept = ("q16", "kvall", "o", "lse", "cos", "sin")
    for r in (1, 0):
        env[f"dkvown{r + 1}"] = give_back(env[f"dkv{r + 1}"]).reshape(R[r + 1], 640)

        def k_back(r, k):
            blk = blk_of()
            tiles = Tiles(geo, k, (getattr(k, f"gp{r}"), getattr(k, f"up{r}")))
            tiles.start(0, 0)
            k.gn = gains(k.wa)
            p = view(k, r + 1, a=getattr(k, f"a{r + 1}"), dh=getattr(k, f"dh{r + 2}"), dh2=getattr(k, f"dh{r + 1}"),
                     first=getattr(k, f"first{r + 1}"))
            p.first[...] = jnp.zeros(p.first.shape, F32)
            back_project(geo, r + 1, p, blk)
            back_one(r, k, blk, tiles, getattr(k, f"dh{r + 1}"))
        n = r + 1
        ins = need("wa", "gu", "wd", f"dkvown{n}", f"da{n}", f"tok{n}", f"inc{n}", f"dh{n + 1}", f"choice{n}", f"st{n}",
                   f"a{n}", f"cos{n}", f"sin{n}", *[s + str(r) for s in saved], *(("lens",) if r == 0 else ("wou", "routes1", "choice1", *[s + str(r) for s in kept])))
        outs = {**back_outs(r), f"da2{n}": ((R[n], COLS_A), BF), f"first{n}": ((8, dp), F32), f"dh{n}": ((full, dp), F32)}
        env.update(call(f"backward_{r}", functools.partial(k_back, r), ins, outs, {**back_scratch(r), **Tiles.scratch(geo)},
                        hbm=("gu", "wd", *[v + str(r) for v in ("gp", "up", "dgp", "dup", "z")])))
    env.update(call("backward_attend_0", lambda k: back_attend(geo, 0, view(k, 0), blk_of()),
                    need("wou", "dy0", *[s + "0" for s in kept]), attend_outs(0), turned_scratch(0)))
    env["dkvown0"] = give_back(env["dkv0"]).reshape(R[0], 640)

    def k_last(k):
        blk = blk_of()
        k.gn = gains(k.wa)
        k.first0[...] = jnp.zeros(k.first0.shape, F32)
        back_project(geo, 0, view(k, 0, dh=k.dh1, dh2=k.dh0, first=k.first0), blk)
        high, low = halves(k.dh0[...])
        k.grad[...] = dot_nt(high, k.spread[0:d]) + dot_nt(low, k.spread[0:d])
    ins = need("wa", "dkvown0", "da0", "tok0", "dh1", "lens", "st0", "a0", "cos0", "sin0", "spread")
    env.update(call("last_project", k_last, ins, {"da20": ((R[0], COLS_A), BF), "first0": ((8, dp), F32), "grad": ((full, d), F32)},
                    dict(dh0=V((full, dp), F32))))
    return env


def weight_grads(geo, env, h):
    R = [geo.rows(r) for r in range(3)]
    dp, ff = geo.dp, geo.ff

    def products(name, lefts, rights, width, tile, rows, spread=None, extra=None):
        ins, hbm = {}, []
        nl = len(lefts)
        for i, v in enumerate(lefts):
            ins[f"l{i}"] = v
        for j, group in enumerate(rights):
            for i, v in enumerate(group):
                ins[f"r{j}{i}"] = v
        if spread is not None:
            ins["spread"] = spread
        if extra is not None:
            ins.update(extra)
        total = sum(R)

        def body(k):
            at = 0
            for i in range(3):
                v = getattr(k, f"l{i}")
                if spread is not None:
                    k.left[at:at + R[i]] = dot(v[...], k.spread[...]).astype(BF)
                else:
                    k.left[at:at + R[i]] = v[...]
                at += R[i]
            c0 = 0
            for j in range(len(rights)):
                n = rights[j][0].shape[1]
                refs = [getattr(k, f"r{j}{i}") for i in range(3)]
                for t in range(0, n, tile):
                    w = min(tile, n - t)
                    right = jnp.concatenate([v[:, t:t + w] for v in refs], axis=0)
                    res = dot_tn(k.left[...], right)
                    k.res[:, c0 + t:c0 + t + w] = res.astype(BF)
                c0 += n
            if extra is not None:
                small = k.small0[...] + k.small1[...] + k.small2[...]
                f = k.first0[...] + k.first1[...] + k.first2[...]
                small = jnp.where(rowid(small.shape) == 0, f, small)
                cols = jnp.concatenate([small, jnp.zeros((120, dp), F32)], axis=0).T
                cols = pltpu.roll(cols, 64, 1)
                k.res[:, 896:1024] = jnp.where(lanes(cols.shape) < 64, k.res[:, 896:1024].astype(F32), cols).astype(BF)
        return call(name, body, ins, {"res": ((rows, width), BF)}, dict(left=pltpu.VMEM((total, rows), BF)))["res"]

    three = lambda n: [env[f"{n}{r}"] for r in range(3)]
    if h == "gu":
        return products("grad_gate_up", three("w"), [three("dgp"), three("dup")], 2 * ff, 512, dp)
    if h == "d":
        return products("grad_down", three("z"), [three("df")], dp, 256, ff)
    if h == "o":
        return products("grad_output", three("o"), [three("dy")], dp, 512, dp, spread=env["spread"])
    return products("grad_query_kv", three("u"), [three("da2")], COLS_A, 512, dp,
                    extra={f"{n}{r}": env[f"{n}{r}"] for n in ("small", "first") for r in range(3)})


MESH = pl.DeviceIdType.MESH

NZ, NX = 4, 2
G = NZ * NX


def gather_kernel(chunks, nslab, *refs):
    ins, outs = refs[:nslab], refs[nslab:2 * nslab]
    ls, zs, zr, xs, xr, ys, yr, cs, cr = refs[2 * nslab:]
    dp, blk = lax.axis_index("dp"), lax.axis_index("blk")
    z, x = dp // NX, lax.rem(dp, NX)
    y, c = blk // 2, lax.rem(blk, 2)
    left, right = (dp - NX, blk), (dp + NX, blk)
    xm, ym, cm = (dp + 1 - 2 * x, blk), (dp, lax.rem(blk + 2, 4)), (dp, blk + 1 - 2 * c)
    bar = pltpu.get_barrier_semaphore()
    for t in (xm, ym, cm):
        pl.semaphore_signal(bar, inc=1, device_id=t, device_id_type=MESH)

    @pl.when(z > 0)
    def _():
        pl.semaphore_signal(bar, inc=1, device_id=left, device_id_type=MESH)

    @pl.when(z < NZ - 1)
    def _():
        pl.semaphore_signal(bar, inc=1, device_id=right, device_id_type=MESH)

    pl.semaphore_wait(bar, 3 + jnp.where(z > 0, 1, 0) + jnp.where(z < NZ - 1, 1, 0))

    locs = [pltpu.make_async_copy(ins[s], outs[s].at[dp], ls.at[s]) for s in range(nslab)]
    for l in locs:
        l.start()

    def piece(i, g, q):
        s, c0, n, split = chunks[i]
        return outs[s].at[g, q, :, pl.ds(c0, n)]

    def myq(i):
        return blk if chunks[i][3] == 4 else c

    def rem(src, dst, a, b, to):
        return pltpu.make_async_remote_copy(src_ref=src, dst_ref=dst, send_sem=a, recv_sem=b, device_id=to, device_id_type=MESH)

    def own(i):
        s, c0, n, split = chunks[i]
        return ins[s].at[myq(i), :, pl.ds(c0, n)]

    def zcopy(i, d, s, src_own):
        zz = z - s if d == 0 else z + s
        p = piece(i, zz * NX + x, myq(i))
        return rem(own(i) if src_own else p, p, zs.at[i, d, s], zr.at[i, d, s], right if d == 0 else left)

    def zrecv(i, d, s):
        zz = z - 1 - s if d == 0 else z + 1 + s
        p = piece(i, zz * NX + x, myq(i))
        return rem(p, p, zs.at[i, d, s], zr.at[i, d, s], right if d == 0 else left)

    def xcopy(i, zz, src_own=False):
        p = piece(i, zz * NX + x, myq(i))
        return rem(own(i) if src_own else p, p, xs.at[i, zz], xr.at[i, zz], xm)

    def xrecv(i, zz):
        p = piece(i, zz * NX + 1 - x, myq(i))
        return rem(p, p, xs.at[i, zz], xr.at[i, zz], xm)

    def ycopy(i, g):
        p = piece(i, g, blk)
        return rem(p, p, ys.at[i, g], yr.at[i, g], ym)

    def yrecv(i, g):
        p = piece(i, g, lax.rem(blk + 2, 4))
        return rem(p, p, ys.at[i, g], yr.at[i, g], ym)

    def ccopy(i, k, g):
        q = myq(i) if k == 0 else lax.rem(blk + 2, 4)
        p = piece(i, g, q)
        return rem(p, p, cs.at[i, k, g], cr.at[i, k, g], cm)

    def crecv(i, k, g):
        if chunks[i][3] == 4:
            mate = blk + 1 - 2 * c
            q = mate if k == 0 else lax.rem(mate + 2, 4)
        else:
            q = 1 - c
        p = piece(i, g, q)
        return rem(p, p, cs.at[i, k, g], cr.at[i, k, g], cm)

    def spread(i, g):
        if chunks[i][3] == 4:
            ycopy(i, g).start()
        ccopy(i, 0, g).start()

    nch = len(chunks)

    def begin(i):
        @pl.when(z < NZ - 1)
        def _():
            zcopy(i, 0, 0, True).start()

        @pl.when(z > 0)
        def _():
            zcopy(i, 1, 0, True).start()
        xcopy(i, z, True).start()

    def zstep(i, s):
        @pl.when(z - 1 - s >= 0)
        def _():
            zrecv(i, 0, s).wait_recv()
            if s < NZ - 2:
                @pl.when(z < NZ - 1)
                def _():
                    zcopy(i, 0, s + 1, False).start()
            xcopy(i, z - 1 - s).start()
            spread(i, (z - 1 - s) * NX + x)

        @pl.when(z + 1 + s < NZ)
        def _():
            zrecv(i, 1, s).wait_recv()
            if s < NZ - 2:
                @pl.when(z > 0)
                def _():
                    zcopy(i, 1, s + 1, False).start()
            xcopy(i, z + 1 + s).start()
            spread(i, (z + 1 + s) * NX + x)

    def xstep(i, k):
        def one(zz):
            xrecv(i, zz).wait_recv()
            spread(i, zz * NX + 1 - x)
        if k == 0:
            one(z)
        else:
            pl.when(z - k >= 0)(lambda: one(z - k))
            pl.when(z + k < NZ)(lambda: one(z + k))

    def ystep(i, k):
        g = lax.rem(dp + k, G)
        yrecv(i, g).wait_recv()
        ccopy(i, 1, g).start()

    def cstep(i, k):
        g = lax.rem(dp + k, G)
        crecv(i, 0, g).wait_recv()
        if chunks[i][3] == 4:
            crecv(i, 1, g).wait_recv()

    def sent(i):
        @pl.when(z < NZ - 1)
        def _():
            zcopy(i, 0, 0, True).wait_send()

        @pl.when(z > 0)
        def _():
            zcopy(i, 1, 0, True).wait_send()
        for s in range(NZ - 1):
            if s < NZ - 2:
                @pl.when((z - 1 - s >= 0) & (z < NZ - 1))
                def _():
                    zcopy(i, 0, s + 1, False).wait_send()

                @pl.when((z + 1 + s < NZ) & (z > 0))
                def _():
                    zcopy(i, 1, s + 1, False).wait_send()
        xcopy(i, z, True).wait_send()
        for k in range(1, NZ):
            xcopy(i, lax.rem(z + k, NZ)).wait_send()
        for k in range(1, G):
            g = lax.rem(dp + k, G)
            ccopy(i, 0, g).wait_send()
            if chunks[i][3] == 4:
                ycopy(i, g).wait_send()
                ccopy(i, 1, g).wait_send()

    stages = [begin] + [functools.partial(lambda i, s: (zstep(i, s), xstep(i, s)), s=s) for s in range(NZ - 1)]
    stages.append(lambda i: xstep(i, NZ - 1))
    stages.append(lambda i: [ystep(i, k) for k in range(1, G)] if chunks[i][3] == 4 else None)
    stages.append(lambda i: [cstep(i, k) for k in range(1, G)])
    stages.append(sent)
    for t in range(nch + len(stages) - 1):
        for s in reversed(range(len(stages))):
            i = t - s
            if 0 <= i < nch:
                stages[s](i)
    for l in locs:
        l.wait()


def gather(slabs, chunks):
    n, nch = len(slabs), len(chunks)
    dma = pltpu.SemaphoreType.DMA
    return pl.pallas_call(
        functools.partial(gather_kernel, chunks, n),
        out_shape=[jax.ShapeDtypeStruct((G,) + s.shape, s.dtype) for s in slabs],
        in_specs=[pl.BlockSpec(memory_space=pl.ANY)] * n,
        out_specs=[pl.BlockSpec(memory_space=pl.ANY)] * n,
        scratch_shapes=[dma((n,)), dma((nch, 2, NZ - 1)), dma((nch, 2, NZ - 1)), dma((nch, NZ)), dma((nch, NZ)),
                        dma((nch, G)), dma((nch, G)), dma((nch, 2, G)), dma((nch, 2, G))],
        compiler_params=pltpu.CompilerParams(collective_id=1, has_side_effects=True),
        name="gather_weights",
    )(*slabs)


def add_into(dst, other, n):
    def body(k, _):
        dst[k] = (dst[k].astype(jnp.float32) + other(k).astype(jnp.float32)).astype(dst.dtype)
        return 0
    lax.fori_loop(0, n, body, 0)


def reduce_kernel(chunks, nslab, *refs):
    nch = len(chunks)
    ins, outs = refs[:nslab], refs[nslab:2 * nslab]
    bufs = refs[2 * nslab:]
    own, crv, yrv, xrv, zrv, fin, s4b = (bufs[k * nch:(k + 1) * nch] for k in range(7))
    ls, cs, cr, ys, yr, xs, xr, zs, zr, fs, fr = bufs[7 * nch:]
    dp, blk = lax.axis_index("dp"), lax.axis_index("blk")
    z, x = dp // NX, lax.rem(dp, NX)
    y, c = blk // 2, lax.rem(blk, 2)
    left, right = (dp - NX, blk), (dp + NX, blk)
    xm, ym, cm = (dp + 1 - 2 * x, blk), (dp, lax.rem(blk + 2, 4)), (dp, blk + 1 - 2 * c)
    bar = pltpu.get_barrier_semaphore()
    for t in (xm, ym, cm):
        pl.semaphore_signal(bar, inc=1, device_id=t, device_id_type=MESH)

    @pl.when(z > 0)
    def _():
        pl.semaphore_signal(bar, inc=1, device_id=left, device_id_type=MESH)

    @pl.when(z < NZ - 1)
    def _():
        pl.semaphore_signal(bar, inc=1, device_id=right, device_id_type=MESH)

    pl.semaphore_wait(bar, 3 + jnp.where(z > 0, 1, 0) + jnp.where(z < NZ - 1, 1, 0))

    def rem(src, dst, a, b, to):
        return pltpu.make_async_remote_copy(src_ref=src, dst_ref=dst, send_sem=a, recv_sem=b, device_id=to, device_id_type=MESH)

    def four(i):
        return chunks[i][3] == 4

    def part(i, core):
        s, c0, n, split = chunks[i]
        cols = pl.ds(c0, n)
        return ins[s].at[:, :, :, core, :, cols] if split == 4 else ins[s].at[:, :, core, :, cols]

    def load(i):
        return pltpu.make_async_copy(part(i, c), own[i], ls.at[i])

    def core_send(i):
        return rem(part(i, 1 - c), crv[i], cs.at[i, 0], cr.at[i, 0], cm)

    def y_send(i):
        return rem(own[i].at[:, :, 1 - y], yrv[i], ys.at[i], yr.at[i], ym)

    def s2(i):
        return yrv[i] if four(i) else own[i]

    def x_send(i):
        return rem(s2(i).at[:, 1 - x], xrv[i], xs.at[i], xr.at[i], xm)

    def z_copy(i, d, lo, hi, first, to):
        src = xrv[i].at[pl.ds(lo, hi - lo)] if first else zrv[i].at[d, pl.ds(lo, hi - lo)]
        return rem(src, zrv[i].at[d, pl.ds(lo, hi - lo)], zs.at[i, d], zr.at[i, d], to)

    def right_send(i, k):
        return z_copy(i, 0, k + 1, NZ, k == 0, right)

    def left_send(i, k):
        return z_copy(i, 1, 0, k, k == NZ - 1, left)

    def st0(i):
        load(i).start()
        core_send(i).start()

    def st1(i):
        load(i).wait()
        core_send(i).wait_recv()

        def body(g, _):
            zz, xx = g // NX, lax.rem(g, NX)
            for yy in ((0, 1) if four(i) else (None,)):
                at = (zz, xx) if yy is None else (zz, xx, yy)
                own[i][at] = (own[i][at].astype(jnp.float32) + crv[i][at].astype(jnp.float32)).astype(jnp.bfloat16)
            return 0
        lax.fori_loop(0, G, body, 0)
        if four(i):
            y_send(i).start()

    def st2(i):
        if four(i):
            y_send(i).wait_recv()

            def body(g, _):
                zz, xx = g // NX, lax.rem(g, NX)
                yrv[i][zz, xx] = (yrv[i][zz, xx].astype(jnp.float32) + own[i][zz, xx, y].astype(jnp.float32)).astype(jnp.bfloat16)
                return 0
            lax.fori_loop(0, G, body, 0)
        x_send(i).start()

    def zstep(i, s):
        if s < NZ - 1:
            @pl.when(z == s)
            def _():
                if s > 0:
                    z_copy(i, 0, s, NZ, False, right).wait_recv()
                    for k in range(s + 1, NZ):
                        zrv[i][0, k] = (zrv[i][0, k].astype(jnp.float32) + xrv[i][k].astype(jnp.float32)).astype(jnp.bfloat16)
                right_send(i, s).start()

            @pl.when(z == NZ - 1 - s)
            def _():
                k0 = NZ - 1 - s
                if s > 0:
                    z_copy(i, 1, 0, k0 + 1, False, left).wait_recv()
                    for k in range(k0):
                        zrv[i][1, k] = (zrv[i][1, k].astype(jnp.float32) + xrv[i][k].astype(jnp.float32)).astype(jnp.bfloat16)
                left_send(i, k0).start()

    def st3(i):
        x_send(i).wait_recv()
        add_into(xrv[i], lambda k: s2(i)[k, x], NZ)
        zstep(i, 0)

    def finish(i):
        q = blk if four(i) else c
        dst = fin[i].at[q] if four(i) else s4b[i]

        def put(v):
            if four(i):
                fin[i][blk] = v.astype(jnp.bfloat16)
            else:
                s4b[i][...] = v.astype(jnp.bfloat16)

        @pl.when(z == 0)
        def _():
            z_copy(i, 1, 0, 1, False, left).wait_recv()
            put(xrv[i][0].astype(jnp.float32) + zrv[i][1, 0].astype(jnp.float32))

        @pl.when(z == NZ - 1)
        def _():
            z_copy(i, 0, NZ - 1, NZ, False, right).wait_recv()
            put(xrv[i][NZ - 1].astype(jnp.float32) + zrv[i][0, NZ - 1].astype(jnp.float32))

        @pl.when((z > 0) & (z < NZ - 1))
        def _():
            put(xrv[i][z].astype(jnp.float32) + zrv[i][0, z].astype(jnp.float32) + zrv[i][1, z].astype(jnp.float32))
        if four(i):
            fin_send(i, 0).start()
            fin_send(i, 1).start()
        else:
            fin_send(i, 0).start()

    def fin_send(i, k):
        if four(i):
            q = blk if k < 2 else lax.rem(blk + 2, 4)
            return rem(fin[i].at[q], fin[i].at[q], fs.at[i, k], fr.at[i, k], ym if k == 0 else cm)
        if k == 0:
            return rem(s4b[i], fin[i].at[2], fs.at[i, 0], fr.at[i, 0], ym)
        return rem(fin[i].at[c], fin[i].at[c], fs.at[i, 1], fr.at[i, 1], cm)

    def fin_recv(i, k):
        if four(i):
            mate = blk + 1 - 2 * c
            q = lax.rem(blk + 2, 4) if k == 0 else mate if k == 1 else lax.rem(mate + 2, 4)
            return rem(fin[i].at[q], fin[i].at[q], fs.at[i, k], fr.at[i, k], cm)
        if k == 0:
            return fin_send(i, 0)
        return rem(fin[i].at[1 - c], fin[i].at[1 - c], fs.at[i, 1], fr.at[i, 1], cm)

    def st8(i):
        fin_recv(i, 0).wait_recv()
        if four(i):
            fin_send(i, 2).start()
        else:
            fin[i][c] = (fin[i][2].astype(jnp.float32) + s4b[i][...].astype(jnp.float32)).astype(jnp.bfloat16)
            fin_send(i, 1).start()

    def st9(i):
        s, c0, n, split = chunks[i]
        for k in ((1, 2) if four(i) else (1,)):
            fin_recv(i, k).wait_recv()
        for q in range(split):
            outs[s][q, :, pl.ds(c0, n)] = fin[i][q].astype(jnp.float32)

    def sent(i):
        core_send(i).wait_send()
        if four(i):
            y_send(i).wait_send()
        x_send(i).wait_send()
        for k in range(NZ - 1):
            pl.when(z == k)(lambda k=k: right_send(i, k).wait_send())
            pl.when(z == k + 1)(lambda k=k: left_send(i, k + 1).wait_send())
        for k in range(3 if four(i) else 2):
            fin_send(i, k).wait_send()

    stages = [st1, st2, st3] + [functools.partial(lambda i, s: zstep(i, s), s=s) for s in range(1, NZ - 1)] + [finish, st8, st9, sent]
    for i in range(nch):
        st0(i)
    for t in range(nch + len(stages) - 1):
        for s in reversed(range(len(stages))):
            i = t - s
            if 0 <= i < nch:
                stages[s](i)


def reduce(slabs, chunks):
    n, nch = len(slabs), len(chunks)
    dma = pltpu.SemaphoreType.DMA
    bf = jnp.bfloat16

    def shapes(kind):
        out = []
        for s, c0, nc, split in chunks:
            h = slabs[s].shape[-2]
            lead = (NZ, NX, 2) if split == 4 else (NZ, NX)
            tiny = (1, 16, 128)
            shape = dict(own=lead + (h, nc), crv=lead + (h, nc), yrv=(NZ, NX, h, nc) if split == 4 else tiny,
                         xrv=(NZ, h, nc), zrv=(2, NZ, h, nc), fin=(4 if split == 4 else 3, h, nc),
                         s4b=(h, nc) if split == 2 else tiny)[kind]
            out.append(pltpu.VMEM(shape, bf))
        return out
    scratch = sum([shapes(k) for k in ("own", "crv", "yrv", "xrv", "zrv", "fin", "s4b")], [])
    sems = [dma((nch,)), dma((nch, 1)), dma((nch, 1)), dma((nch,)), dma((nch,)), dma((nch,)), dma((nch,)),
            dma((nch, 2)), dma((nch, 2)), dma((nch, 3)), dma((nch, 3))]
    outs = []
    for k, s in enumerate(slabs):
        split = next(ch[3] for ch in chunks if ch[0] == k)
        outs.append(jax.ShapeDtypeStruct((split,) + s.shape[-2:], jnp.float32))
    return pl.pallas_call(
        functools.partial(reduce_kernel, chunks, n),
        out_shape=outs,
        in_specs=[pl.BlockSpec(memory_space=pl.ANY)] * n,
        out_specs=[pl.BlockSpec(memory_space=pltpu.VMEM)] * n,
        scratch_shapes=scratch + sems,
        compiler_params=pltpu.CompilerParams(collective_id=2, has_side_effects=True, vmem_limit_bytes=60 << 20),
        name="reduce_grads",
    )(*slabs)


AG_CHUNKS = [(0, 0, 1664, 4), (1, 0, 1024, 2), (2, 0, 1280, 4), (2, 1280, 1280, 4), (3, 0, 512, 2), (2, 2560, 1280, 4),
             (2, 3840, 1280, 4), (3, 512, 512, 2)]
RS_CHUNKS = [(2, 0, 1280, 4), (3, 0, 512, 2), (2, 1280, 1280, 4), (2, 2560, 1280, 4), (3, 512, 512, 2), (2, 3840, 1280, 4),
             (1, 0, 1024, 2), (0, 0, 896, 4), (0, 896, 768, 4)]


def pad_to(v, shape):
    return jnp.pad(v, [(0, b - a) for a, b in zip(v.shape, shape)])


def pad_cols(v, geo):
    v = v.reshape(v.shape[0], geo.n_dp, geo.gw)
    return jnp.pad(v, ((0, 0), (0, 0), (0, geo.gp - geo.gw))).reshape(v.shape[0], geo.dp)


def unpad_cols(v, geo):
    return v.reshape(v.shape[0], geo.n_dp, geo.gp)[:, :, :geo.gw].reshape(v.shape[0], geo.d)


def pack(geo, q, k, v, o, g, u, d, g1, g2, rt):
    rows = q.shape[0]
    kv = jnp.concatenate([k.reshape(rows, KV_HEADS, 64), v.reshape(rows, KV_HEADS, 64)], axis=2).reshape(rows, 640)
    small = pad_to(jnp.concatenate([g1[:, None], g2[:, None], rt], axis=1), (rows, 64))
    a = pad_to(jnp.concatenate([q, small, kv], axis=1), (geo.gp, COLS_A))
    gu = pad_to(jnp.concatenate([g, u], axis=1), (geo.gp, 2 * geo.ff))
    return a, pad_to(pad_cols(o, geo), (geo.gp, geo.dp)), gu, pad_cols(d, geo)


def whole_weights(geo, slabs):
    a, o, gu, d = slabs
    if (geo.n_dp, geo.n_blk) != (G, 4):
        return tuple(lax.all_gather(w, "dp", axis=0, tiled=True) for w in slabs)
    gp, rd = geo.gp, d.shape[0]
    got = gather([a.reshape(4, gp // 4, -1), o.reshape(2, gp // 2, -1), gu.reshape(4, gp // 4, -1), d.reshape(2, rd // 2, -1)],
                 AG_CHUNKS)
    return tuple(w.reshape(-1, w.shape[-1]) for w in got)


def summed_grads(geo, slabs):
    a, o, gu, d = slabs
    if (geo.n_dp, geo.n_blk) != (G, 4):
        shares = [lax.psum_scatter(v, "dp", scatter_dimension=0, tiled=True) for v in slabs]
        return tuple(lax.psum(v, "blk").astype(F32) for v in shares)
    gp, rd = geo.gp, d.shape[0] // G
    got = reduce([a.reshape(NZ, NX, 2, 2, gp // 4, -1), o.reshape(NZ, NX, 2, gp // 2, -1), gu.reshape(NZ, NX, 2, 2, gp // 4, -1),
                  d.reshape(NZ, NX, 2, rd // 2, -1)], RS_CHUNKS)
    return tuple(w.reshape(-1, w.shape[-1]) for w in got)


def unpack(geo, slabs):
    a, o, gu, d = slabs
    a, o, gu = a[:geo.gw], o[:geo.gw], gu[:geo.gw]
    kv = a[:, 1024:].reshape(geo.gw, KV_HEADS, 128)
    return (a[:, :960], kv[:, :, :64].reshape(geo.gw, 320), kv[:, :, 64:].reshape(geo.gw, 320), unpad_cols(o, geo),
            gu[:, :geo.ff], gu[:, geo.ff:], unpad_cols(d, geo), a[:, 960], a[:, 961], a[:, 962:965])


def meet(*others):
    bar = pltpu.get_barrier_semaphore()
    for t in others:
        pl.semaphore_signal(bar, inc=1, device_id=t, device_id_type=MESH)
    pl.semaphore_wait(bar, len(others))


def mates():
    dp, blk = lax.axis_index("dp"), lax.axis_index("blk")
    y, c = blk // 2, lax.rem(blk, 2)
    return dp, blk, y, c, (dp, lax.rem(blk + 2, 4)), (dp, blk + 1 - 2 * c)


def share_kernel(own, out, lsem, ssem, rsem):
    dp, blk, y, c, ym, cm = mates()
    meet(ym, cm)

    def rem(src, b, k, to):
        return pltpu.make_async_remote_copy(src_ref=src, dst_ref=out.at[b], send_sem=ssem.at[k], recv_sem=rsem.at[k],
                                            device_id=to, device_id_type=MESH)
    far, near = lax.rem(blk + 2, 4), blk + 1 - 2 * c
    rem(own, blk, 0, ym).start()
    rem(own, blk, 1, cm).start()
    local = pltpu.make_async_copy(own, out.at[blk], lsem)
    local.start()
    rem(out.at[far], far, 0, ym).wait_recv()
    rem(out.at[far], far, 2, cm).start()
    rem(out.at[near], near, 1, cm).wait_recv()
    both = lax.rem(near + 2, 4)
    rem(out.at[both], both, 2, cm).wait_recv()
    rem(own, blk, 0, ym).wait_send()
    rem(own, blk, 1, cm).wait_send()
    rem(out.at[far], far, 2, cm).wait_send()
    local.wait()


def share_rows(geo, ident, kv):
    if geo.n_blk != 4:
        return lax.all_gather(kv, "blk", axis=0, tiled=False)
    dma = pltpu.SemaphoreType.DMA
    return pl.pallas_call(
        share_kernel, out_shape=jax.ShapeDtypeStruct((4,) + kv.shape, kv.dtype),
        in_specs=[pl.BlockSpec(memory_space=pl.ANY)], out_specs=pl.BlockSpec(memory_space=pl.ANY),
        scratch_shapes=[dma, dma((3,)), dma((3,))],
        compiler_params=pltpu.CompilerParams(collective_id=ident, has_side_effects=True), name=f"share_rows_{ident}")(kv)


def give_kernel(dkv, out, got1, half, got2, ssem, rsem):
    dp, blk, y, c, ym, cm = mates()
    meet(ym, cm)

    def rem(src, dst, k, to):
        return pltpu.make_async_remote_copy(src_ref=src, dst_ref=dst, send_sem=ssem.at[k], recv_sem=rsem.at[k],
                                            device_id=to, device_id_type=MESH)
    first = [rem(dkv.at[yy, 1 - c], got1.at[yy], yy, cm) for yy in range(2)]
    for f in first:
        f.start()
    for f in first:
        f.wait_recv()
    half[...] = (got1[1 - y].astype(F32) + dkv[1 - y, c].astype(F32)).astype(BF)
    second = rem(half, got2, 2, ym)
    second.start()
    mine = got1[y].astype(F32) + dkv[y, c].astype(F32)
    second.wait_recv()
    out[...] = mine + got2[...].astype(F32)
    for f in first + [second]:
        f.wait_send()


def give_rows(geo, ident, dkv):
    if geo.n_blk != 4:
        return lax.psum_scatter(dkv, "blk", scatter_dimension=0, tiled=False).astype(F32)
    dma = pltpu.SemaphoreType.DMA
    piece = dkv.shape[1:]
    vm = pl.BlockSpec(memory_space=pltpu.VMEM)
    return pl.pallas_call(
        give_kernel, out_shape=jax.ShapeDtypeStruct(piece, F32), in_specs=[vm], out_specs=vm,
        scratch_shapes=[pltpu.VMEM((2,) + piece, BF), pltpu.VMEM(piece, BF), pltpu.VMEM(piece, BF), dma((3,)), dma((3,))],
        compiler_params=pltpu.CompilerParams(collective_id=ident, has_side_effects=True, vmem_limit_bytes=40 << 20),
        name=f"give_rows_{ident}")(dkv.reshape((2, 2) + piece))


def per_device(block_input, cotangent, seq_lengths, routes_two, routes_three, query_weight, key_weight, value_weight, output_weight,
               gate_weight, up_weight, down_weight, first_gain, second_gain, router_weight):
    micro, seqs, bl, d = block_input.shape
    n_dp, n_blk = lax.axis_size("dp"), lax.axis_size("blk")
    count = micro * seqs
    geo = Geo(count, bl, n_dp, n_blk, d, gate_weight.shape[1], (None, routes_two.shape[2], routes_three.shape[2]))
    slabs = pack(geo, query_weight, key_weight, value_weight, output_weight, gate_weight, up_weight, down_weight, first_gain,
                 second_gain, router_weight)
    wa, wo, gu, wd = whole_weights(geo, slabs)
    ids = iter(range(10, 30))
    env = block(geo, block_input.reshape(count * bl, d), cotangent.reshape(count * bl, d), seq_lengths.reshape(count),
                (routes_two.reshape(count, -1), routes_three.reshape(count, -1)), wa, wo, gu, wd,
                lambda kv: share_rows(geo, next(ids), kv), lambda dkv: give_rows(geo, next(ids), dkv))
    grads = [weight_grads(geo, env, h) for h in ("a", "o", "gu", "d")]
    grads = unpack(geo, summed_grads(geo, grads))
    return (env["out"].reshape(block_input.shape), env["grad"].reshape(block_input.shape)) + tuple(grads)


def solution(mesh):
    in_specs = (
        P(None, "dp", "blk", None),
        P(None, "dp", "blk", None),
        P(None, "dp"),
        P(None, "dp", None),
        P(None, "dp", None),
        P("dp", None),
        P("dp", None),
        P("dp", None),
        P("dp", None),
        P("dp", None),
        P("dp", None),
        P("dp", None),
        P("dp"),
        P("dp"),
        P("dp", None),
    )
    out_specs = (
        P(None, "dp", "blk", None),
        P(None, "dp", "blk", None),
        P("dp", None),
        P("dp", None),
        P("dp", None),
        P("dp", None),
        P("dp", None),
        P("dp", None),
        P("dp", None),
        P("dp"),
        P("dp"),
        P("dp", None),
    )
    return jax.shard_map(
        per_device, mesh=mesh, in_specs=in_specs, out_specs=out_specs, check_vma=False
    )
```

```python
import functools
import math
import types

import jax
import jax.numpy as jnp
import numpy as np
from jax import lax
from jax.experimental import pallas as pl
from jax.experimental.pallas import tpu as pltpu
from jax.sharding import PartitionSpec as P

HEADS, KV_HEADS, HEAD_DIM, RECUR = 15, 5, 64, 3
GROUP = HEADS // KV_HEADS
eps = 1e-05
rope_base = 10000.0
masked_fill = -1e30
BF, F32 = jnp.bfloat16, jnp.float32
COLS_A = 1664
FT = 512


def dot(a, b):
    return lax.dot_general(a, b, (((1,), (0,)), ((), ())), preferred_element_type=F32)


def dot_nt(a, b):
    return lax.dot_general(a, b, (((1,), (1,)), ((), ())), preferred_element_type=F32)


def dot_tn(a, b):
    return lax.dot_general(a, b, (((0,), (0,)), ((), ())), preferred_element_type=F32)


def halves(v):
    high = v.astype(BF)
    return high, (v - high.astype(F32)).astype(BF)


def pick(choice, v):
    high, low = halves(v)
    return dot(choice, high) + dot(choice, low)


def put_back(choice, v):
    high, low = halves(v)
    return dot_tn(choice, high) + dot_tn(choice, low)


def lanes(shape):
    return lax.broadcasted_iota(jnp.int32, shape, len(shape) - 1)


def rowid(shape):
    return lax.broadcasted_iota(jnp.int32, shape, len(shape) - 2)


def swapped(x):
    first = lax.rem(lanes(x.shape), 64) < 32
    return jnp.where(first, pltpu.roll(x, 96, 1), pltpu.roll(x, 32, 1))


class Far:
    def __init__(self, value):
        self.value = value


class Words:
    def __init__(self, value):
        self.value = value


class Out:
    def __init__(self, shape, dtype=F32, far=False):
        self.shape, self.dtype, self.far = shape, dtype, far


def join(*parts, **more):
    got = types.SimpleNamespace()
    for p in parts + (more,):
        vars(got).update(p if isinstance(p, dict) else vars(p))
    return got


def call(name, body, ins, outs, scratch=None, limit=63, **params):
    flat_in, tree_in = jax.tree.flatten(ins)
    flat_out, tree_out = jax.tree.flatten(outs)
    flat_scratch, tree_scratch = jax.tree.flatten(scratch or {})
    n_in, n_out = len(flat_in), len(flat_out)

    def kernel(*refs):
        body(join(tree_in.unflatten(refs[:n_in]), tree_out.unflatten(refs[n_in:n_in + n_out]),
                  tree_scratch.unflatten(refs[n_in + n_out:])))

    vm, far = pl.BlockSpec(memory_space=pltpu.VMEM), pl.BlockSpec(memory_space=pl.ANY)
    words = pl.BlockSpec(memory_space=pltpu.SMEM)
    got = pl.pallas_call(
        kernel,
        out_shape=[jax.ShapeDtypeStruct(o.shape, o.dtype) for o in flat_out],
        in_specs=[far if isinstance(v, Far) else words if isinstance(v, Words) else vm for v in flat_in],
        out_specs=[far if o.far else vm for o in flat_out],
        scratch_shapes=flat_scratch,
        compiler_params=pltpu.CompilerParams(vmem_limit_bytes=limit << 20, **params),
        name=name,
    )(*[v.value if isinstance(v, (Far, Words)) else v for v in flat_in])
    return types.SimpleNamespace(**tree_out.unflatten(got))


class Geo:
    def __init__(self, ns, bl, n_dp, n_blk, d, ff, tops):
        self.ns, self.bl, self.n_dp, self.n_blk, self.d, self.ff = ns, bl, n_dp, n_blk, d, ff
        self.gw = d // n_dp
        self.gp = -(-self.gw // 16) * 16
        self.dp = n_dp * self.gp
        self.slots = (bl, bl // 2, bl // 4)
        self.tops = tops

    def rows(self, r):
        return self.ns * self.slots[r]

    def keys(self, r):
        return self.n_blk * self.slots[r]

    def spread(self):
        e = np.zeros((1024, self.dp), np.float32)
        f = np.arange(self.d)
        e[f, f // self.gw * self.gp + f % self.gw] = 1
        return jnp.asarray(e, BF)

    def tables(self):
        f = rope_base ** (-(np.arange(32, dtype=np.float64) * 2.0) / 64)
        f32 = np.asarray(f, np.float32)
        ph = (np.arange(self.bl * self.n_blk, dtype=np.float32)[:, None] * f32).astype(np.float32).astype(np.float64)
        c, s = np.cos(ph), np.sin(ph)
        cos = np.concatenate([c, c, c, c], 1).astype(np.float32)
        sin = np.concatenate([-s, s, -s, s], 1).astype(np.float32)
        return jnp.asarray(cos), jnp.asarray(sin)


def gains(wa):
    sel = (lanes((8, 128)) == rowid((8, 128)) + 64).astype(BF)
    return dot_nt(sel, wa[:, 896:1024])


def choose(geo, r, routes, blk):
    s, t, bl = geo.slots[r], geo.tops[r], geo.bl
    before = jnp.sum((routes < blk * bl).astype(F32), axis=1, keepdims=True).astype(jnp.int32)
    shift = ((lanes((s, t)) - rowid((s, t))) == before).astype(BF)
    here = (routes == rowid((bl, t)) + blk * bl).astype(BF)
    return dot_nt(shift, here).astype(BF)


def allowed(geo, r, routes, blk, turned):
    s, kn, bl = geo.slots[r], geo.keys(r), geo.bl
    shape = (kn, GROUP * s) if turned else (GROUP * s, kn)
    key = rowid(shape) if turned else lanes(shape)
    query = lax.rem(lanes(shape) if turned else rowid(shape), s)
    ok = key <= blk * s + query
    if r > 0:
        t = geo.tops[r]
        inside = (routes // bl == rowid((kn, t)) // s)
        if turned:
            count = jnp.sum(inside.astype(F32), axis=1, keepdims=True)
        else:
            count = dot_nt(jnp.ones((8, t), BF), inside.astype(BF))[0:1]
        ok = ok & (lax.rem(key, s).astype(F32) < count)
    return jnp.where(ok, 0.0, masked_fill)


def project_kv(geo, r, k):
    a = k.a[...].astype(F32)
    n1 = lax.rsqrt(jnp.sum(a * a, axis=-1, keepdims=True) * (1.0 / geo.d) + eps)
    k.u[...] = (a * n1 * k.gn[0:1]).astype(BF)
    k.st[...] = jnp.where(lanes(k.st.shape) == 0, n1, 0.0)
    u = k.u[...]
    cos, sin = k.cos[...], k.sin[...]
    left = lanes(cos.shape) < 64
    ckv, skv = jnp.where(left, cos, 1.0), jnp.where(left, sin, 0.0)
    for c0, n in ((1024, 256), (1280, 256), (1536, 128)):
        some = dot(u, k.wa[:, c0:c0 + n])
        for j in range(n // 128):
            x = some[:, 128 * j:128 * j + 128]
            k.kv[:, c0 - 1024 + 128 * j:c0 - 1024 + 128 * j + 128] = (x * ckv + swapped(x) * skv).astype(BF)


def project_q(geo, r, k):
    u = k.u[...]
    cos, sin = k.cos[...], k.sin[...]
    left = lanes(cos.shape) < 64
    for t in range(4):
        both = dot(u, k.wa[:, 256 * t:256 * t + 256])
        for j in range(2):
            x = both[:, 128 * j:128 * j + 128]
            x = (x * cos + swapped(x) * sin).astype(BF).astype(F32) * 0.125
            h = 4 * t + 2 * j
            k.q16[h] = jnp.where(left, x, 0.0).astype(BF)
            if h + 1 < HEADS:
                k.q16[h + 1] = jnp.where(left, pltpu.roll(x, 64, 1), 0.0).astype(BF)


def project(geo, r, k):
    project_kv(geo, r, k)
    project_q(geo, r, k)


def select_rows(geo, r, k, blk):
    s, bl = geo.slots[r], geo.bl
    for m in range(geo.ns):
        ch = choose(geo, r, k.routes[m:m + 1], blk)
        k.choice[m] = ch
        k.a[m * s:m * s + s] = pick(ch, k.h[m * bl:m * bl + bl])
        k.cos[m * s:m * s + s] = pick(ch, k.cosb[...])
        k.sin[m * s:m * s + s] = pick(ch, k.sinb[...])


def attend(geo, r, k, blk, pause=None):
    s, kn = geo.slots[r], geo.keys(r)

    def seq(m, _):
        row0 = m * s if isinstance(m, int) else pl.multiple_of(m * s, s)
        k.kvg[...] = k.kvall[:, m].reshape(kn, KV_HEADS * 128)
        k.bias[...] = allowed(geo, r, k.routes[pl.ds(m, 1)] if r else None, blk, False)
        k.col[...] = jnp.zeros(k.col.shape, F32)

        def group(g, _):
            kvh = k.kvg[:, pl.ds(pl.multiple_of(g * 128, 128), 128)]
            sc = dot_nt(k.q16[pl.ds(g * GROUP, GROUP), pl.ds(row0, s)].reshape(GROUP * s, 128), kvh) + k.bias[...]
            top = jnp.max(sc, axis=-1, keepdims=True)
            p = jnp.exp(sc - top)
            total = jnp.sum(p, axis=-1, keepdims=True)
            k.o16[pl.ds(g * GROUP, GROUP)] = (dot(p.astype(BF), kvh) * (1.0 / total)).reshape(GROUP, s, 128)
            k.col[...] = jnp.where(lanes(k.col.shape) == g, top + jnp.log(total), k.col[...])
            return 0
        if pause is None:
            lax.fori_loop(0, KV_HEADS, group, 0)
        else:
            lax.fori_loop(0, 3, group, 0)
            pause()
            lax.fori_loop(3, KV_HEADS, group, 0)
        left = lanes((s, 128)) < 64
        for t in range(8):
            odd = k.o16[2 * t + 1] if 2 * t + 1 < HEADS else 0.0
            k.o[pl.ds(row0, s), 128 * t:128 * t + 128] = jnp.where(left, pltpu.roll(k.o16[2 * t], 64, 1), odd).astype(BF)
        k.lse[m] = k.col[...].T[0:8]
        return 0
    if pause is None:
        lax.fori_loop(0, geo.ns, seq, 0)
    else:
        for m in range(geo.ns):
            seq(m, 0)
            pause()


class Tiles:
    def __init__(self, geo, k, pre=None):
        self.k, self.n, self.ff, self.pre = k, geo.ff // FT, geo.ff, pre

    def parts(self, t, slot):
        k, c0 = self.k, t * FT
        if not isinstance(t, int):
            c0 = pl.multiple_of(c0, FT)
        cu = c0 + self.ff
        return [pltpu.make_async_copy(k.gu.at[:, pl.ds(c0, FT)], k.gbuf.at[slot], k.tsem.at[slot, 0]),
                pltpu.make_async_copy(k.gu.at[:, pl.ds(cu, FT)], k.ubuf.at[slot], k.tsem.at[slot, 1]),
                pltpu.make_async_copy(k.wd.at[pl.ds(c0, FT)], k.dbuf.at[slot], k.tsem.at[slot, 2])] + [
                    pltpu.make_async_copy(v.at[:, pl.ds(c0, FT)], k.pre.at[slot, j], k.tsem.at[slot, 3 + j])
                    for j, v in enumerate(self.pre or ())]

    def start(self, t, slot):
        for c in self.parts(t, slot):
            c.start()

    def loop(self, step):
        def body(t, _):
            slot = lax.rem(t, 2)

            @pl.when(t + 1 < self.n)
            def _():
                self.start(t + 1, 1 - slot)
            for c in self.parts(t, slot):
                c.wait()
            step(t, slot)
            return 0
        lax.fori_loop(0, self.n, body, 0)

    @staticmethod
    def scratch(geo):
        return dict(gbuf=pltpu.VMEM((2, geo.dp, FT), BF), ubuf=pltpu.VMEM((2, geo.dp, FT), BF),
                    dbuf=pltpu.VMEM((2, FT, geo.dp), BF), tsem=pltpu.SemaphoreType.DMA((2, 5)))


def feed(geo, r, k, blk, tiles):
    s, bl = geo.slots[r], geo.bl
    y = dot(k.o[...], k.wou[...])
    a = k.a[...].astype(F32)
    b = a + y
    n2 = lax.rsqrt(jnp.sum(b * b, axis=-1, keepdims=True) * (1.0 / geo.d) + eps)
    gate = jax.nn.sigmoid(jnp.sum(a * k.gn[2 + r:3 + r], axis=-1, keepdims=True))
    k.b[...] = b.astype(BF)
    k.w[...] = (b * n2 * k.gn[1:2]).astype(BF)
    lane = lanes((geo.rows(r), 128))
    k.sx[...] = jnp.where(lane == 0, n2, jnp.where(lane == 1, gate, 0.0))
    k.acc[...] = y

    def wide(t, slot):
        c0 = t * FT if isinstance(t, int) else pl.multiple_of(t * FT, FT)
        return [pltpu.make_async_copy(k.keep.at[slot, j], ref.at[:, pl.ds(c0, FT)], k.ksem.at[slot, j])
                for j, ref in enumerate((k.gp, k.up))]

    def step(t, slot):
        @pl.when(t >= 2)
        def _():
            for c in wide(t - 2, slot):
                c.wait()
        gp = dot(k.w[...], k.gbuf[slot])
        up = dot(k.w[...], k.ubuf[slot])
        k.keep[slot, 0] = gp.astype(BF)
        k.keep[slot, 1] = up.astype(BF)
        z = (gp * jax.nn.sigmoid(gp) * up).astype(BF)
        k.acc[...] += dot(z, k.dbuf[slot])
        for c in wide(t, slot):
            c.start()
    tiles.loop(step)
    for t in range(max(tiles.n - 2, 0), tiles.n):
        for c in wide(t, t % 2):
            c.wait()
    yf = k.acc[...]
    k.yf[...] = yf.astype(BF)
    delta = yf * k.sx[:, 1:2]
    for m in range(geo.ns):
        if r == 0:
            here = rowid((bl, 1)) + blk * bl < k.lens[m]
            rows = slice(m * bl, m * bl + bl)
            k.h2[rows] = k.a[rows].astype(F32) + jnp.where(here, delta[rows], 0.0)
        else:
            k.h2[m * bl:m * bl + bl] = k.h[m * bl:m * bl + bl] + put_back(k.choice[m], delta[m * s:m * s + s])


def back_feed(geo, r, k, blk, tiles):
    s, bl, rows = geo.slots[r], geo.bl, geo.rows(r)
    k.small[2 + r:3 + r] = jnp.zeros((1, geo.dp), F32)
    k.small[1:2] = jnp.zeros((1, geo.dp), F32)

    def incoming(m):
        here = slice(m * s, m * s + s)
        if r == 0:
            return jnp.where(rowid((bl, 1)) + blk * bl < k.lens[m], k.dh[here], 0.0)
        return k.inc[here]
    for m in range(geo.ns):
        here = slice(m * s, m * s + s)
        if r > 0:
            k.inc[here] = pick(k.choice[m], k.dh[m * bl:m * bl + bl])
        inc = incoming(m)
        gate = k.sx[here, 1:2]
        dg = jnp.sum(inc * k.yf[here].astype(F32), axis=-1, keepdims=True)
        dl = dg * gate * (1.0 - gate)
        k.tok[here] = inc + dl * k.gn[2 + r:3 + r]
        k.small[2 + r:3 + r] += jnp.sum(k.a[here].astype(F32) * dl, axis=0, keepdims=True)
        k.df[here] = (gate * inc).astype(BF)
    k.acc[...] = jnp.zeros(k.acc.shape, F32)

    def wide(t, slot):
        c0 = t * FT if isinstance(t, int) else pl.multiple_of(t * FT, FT)
        return [pltpu.make_async_copy(k.wide.at[slot, j], ref.at[:, pl.ds(c0, FT)], k.wsem.at[slot, j])
                for j, ref in enumerate((k.dgp, k.dup, k.z))]

    def step(t, slot):
        @pl.when(t >= 2)
        def _():
            for c in wide(t - 2, slot):
                c.wait()
        dz = dot_nt(k.df[...], k.dbuf[slot])
        gp = k.pre[slot, 0].astype(F32)
        up = k.pre[slot, 1].astype(F32)
        sig = jax.nn.sigmoid(gp)
        silu = gp * sig
        k.wide[slot, 2] = (silu * up).astype(BF)
        dup = (dz * silu).astype(BF)
        dgp = (dz * up * (sig * (1.0 + gp * (1.0 - sig)))).astype(BF)
        k.wide[slot, 1] = dup
        k.wide[slot, 0] = dgp
        k.acc[...] += dot_nt(dgp, k.gbuf[slot]) + dot_nt(dup, k.ubuf[slot])
        for c in wide(t, slot):
            c.start()
    tiles.loop(step)
    for t in range(max(tiles.n - 2, 0), tiles.n):
        for c in wide(t, t % 2):
            c.wait()
    for m in range(geo.ns):
        here = slice(m * s, m * s + s)
        n2, gate = k.sx[here, 0:1], k.sx[here, 1:2]
        dw = k.acc[here]
        b = k.b[here].astype(F32)
        k.small[1:2] += jnp.sum(dw * (b * n2), axis=0, keepdims=True)
        t = dw * k.gn[1:2]
        db = n2 * t - n2 * n2 * n2 * b * (jnp.sum(t * b, axis=-1, keepdims=True) * (1.0 / geo.d))
        k.tok[here] += db
        k.dy[here] = (gate * incoming(m) + db).astype(BF)


def back_attend(geo, r, k, blk):
    s, kn = geo.slots[r], geo.keys(r)
    rows = geo.rows(r)
    left = lanes((rows, 128)) < 64
    lane = lanes((rows, 128))
    dcol = jnp.zeros((rows, 128), F32)
    for t in range(8):
        x = dot_nt(k.dy[...], k.wou[128 * t:128 * t + 128])
        x = x.astype(BF).astype(F32)
        prod = x * k.o[:, 128 * t:128 * t + 128].astype(F32)
        even = jnp.sum(jnp.where(left, prod, 0.0), axis=-1, keepdims=True)
        dcol = jnp.where(lane == 2 * t, even, dcol)
        k.do16[2 * t] = jnp.where(left, 0.0, pltpu.roll(x, 64, 1)).astype(BF)
        if 2 * t + 1 < HEADS:
            odd = jnp.sum(jnp.where(left, 0.0, prod), axis=-1, keepdims=True)
            dcol = jnp.where(lane == 2 * t + 1, odd, dcol)
            k.do16[2 * t + 1] = jnp.where(left, 0.0, x).astype(BF)
    k.dcol[...] = dcol

    def seq(m, _):
        row0 = pl.multiple_of(m * s, s)
        k.kvg[...] = k.kvall[:, m].reshape(kn, KV_HEADS * 128)
        for g in range(KV_HEADS):
            k.kvt[g] = k.kvg[:, 128 * g:128 * g + 128].astype(F32).T.astype(BF)
        k.bias[...] = allowed(geo, r, k.routes[pl.ds(m, 1)] if r else None, blk, True)
        dt = k.dcol[pl.ds(row0, s)].T
        for h in range(HEADS):
            k.dt[h // GROUP:h // GROUP + 1, h % GROUP * s:(h % GROUP + 1) * s] = dt[h:h + 1]
        k.ct[0] = k.cos[pl.ds(row0, s)].T[0:32] * 0.125
        k.ct[1] = k.sin[pl.ds(row0, s)].T[32:64] * 0.125

        def group(g, _):
            kvh = k.kvg[:, pl.ds(pl.multiple_of(g * 128, 128), 128)]
            heads = (pl.ds(g * GROUP, GROUP), pl.ds(row0, s))
            qh, doh = k.q16[heads].reshape(GROUP * s, 128), k.do16[heads].reshape(GROUP * s, 128)
            p = jnp.exp(dot_nt(kvh, qh) + k.bias[...] - k.lse[m, pl.ds(g, 1)])
            ds = (p * (dot_nt(kvh, doh) - k.dt[pl.ds(g, 1)])).astype(BF)
            total = dot(ds, qh) + dot(p.astype(BF), doh)
            dqt = dot(k.kvt[g], ds)
            c, sn = k.ct[0], k.ct[1]
            for j in range(GROUP):
                y1, y2 = dqt[0:32, j * s:j * s + s], dqt[32:64, j * s:j * s + s]
                k.dqt[g * GROUP + j, 0:32] = (y1 * c + y2 * sn)
                k.dqt[g * GROUP + j, 32:64] = (y2 * c - y1 * sn)
            k.dkv[:, m, :, pl.ds(pl.multiple_of(g * 128, 128), 128)] = total.astype(BF).reshape(geo.n_blk, s, 128)
            return 0
        lax.fori_loop(0, KV_HEADS, group, 0)
        for t in range(8):
            if 2 * t + 1 < HEADS:
                x = k.dqt[2 * t:2 * t + 2].reshape(128, s).T
            else:
                x = jnp.concatenate([k.dqt[2 * t], jnp.zeros((64, s), F32)], axis=0).T
            k.da[pl.ds(row0, s), 128 * t:128 * t + 128] = x.astype(BF)
        return 0
    lax.fori_loop(0, geo.ns, seq, 0)


def back_project(geo, r, k, blk):
    s, bl, rows = geo.slots[r], geo.bl, geo.rows(r)
    cos, sin = k.cos[...], k.sin[...]
    left = lanes(cos.shape) < 64
    ckv, skv = jnp.where(left, cos, 1.0), jnp.where(left, sin, 0.0)
    k.da2[:, 0:1024] = k.da[...]
    for g in range(KV_HEADS):
        x = k.dkvown[:, 128 * g:128 * g + 128].astype(F32)
        k.da2[:, 1024 + 128 * g:1152 + 128 * g] = (x * ckv - swapped(x) * skv).astype(BF)
    for m in range(geo.ns):
        here = slice(m * bl, m * bl + bl)
        mine = slice(m * s, m * s + s)
        du = dot_nt(k.da2[mine], k.wa[...])
        a = k.a[mine].astype(F32)
        n1 = k.st[mine, 0:1]
        k.first[0:1] += jnp.sum(du * (a * n1), axis=0, keepdims=True)
        t1 = du * k.gn[0:1]
        tok = k.tok[mine] + n1 * t1 - n1 * n1 * n1 * a * (jnp.sum(t1 * a, axis=-1, keepdims=True) * (1.0 / geo.d))
        if r == 0:
            ok = rowid((bl, 1)) + blk * bl < k.lens[m]
            k.dh2[here] = jnp.where(ok, tok, k.dh[here])
        else:
            k.dh2[here] = k.dh[here] + put_back(k.choice[m], tok - k.inc[mine])


def block(geo, x, cot, lens, routes, slabs, share, give_back):
    blk_of = lambda: lax.axis_index("blk")
    bl, d, dp, ff, nsq, nb = geo.bl, geo.d, geo.dp, geo.ff, geo.ns, geo.n_blk
    full = nsq * bl
    cos_all, sin_all = geo.tables()
    b0 = lax.axis_index("blk") * bl
    cosb = lax.dynamic_slice_in_dim(cos_all, b0, bl, 0)
    sinb = lax.dynamic_slice_in_dim(sin_all, b0, bl, 0)
    spread = geo.spread()
    R, S, KN = [geo.rows(r) for r in range(3)], geo.slots, [geo.keys(r) for r in range(3)]
    V, dma = pltpu.VMEM, pltpu.SemaphoreType.DMA
    lens = Words(lens)

    def proj_outs(r, kv=True):
        more = dict(choice=Out((nsq, S[r], bl), BF)) if r else {}
        more = dict(kv=Out((R[r], 640), BF), **more) if kv else more
        return dict(a=Out((R[r], dp), F32 if r else BF), u=Out((R[r], dp), BF), q16=Out((HEADS, R[r], 128), BF), st=Out((R[r], 128)), cos=Out((R[r], 128)), sin=Out((R[r], 128)), **more)

    def seen_outs(r):
        return dict(o=Out((R[r], 1024), BF), lse=Out((nsq, 8, GROUP * S[r])))

    def fore_outs(r):
        return dict(**(seen_outs(r) if r else {}), b=Out((R[r], dp), BF), w=Out((R[r], dp), BF),
                    gp=Out((R[r], ff), BF, True), up=Out((R[r], ff), BF, True), yf=Out((R[r], dp), BF), sx=Out((R[r], 128)))

    def seen_scratch(r):
        return dict(kvg=V((KN[r], 640), BF), bias=V((GROUP * S[r], KN[r]), F32), col=V((GROUP * S[r], 128), F32),
                    o16=V((HEADS, S[r], 128), F32))

    def fore_scratch(r):
        return dict(acc=V((R[r], dp), F32), keep=V((2, 2, R[r], FT), BF), ksem=dma((2, 2)), **(seen_scratch(r) if r else {}))

    def feed_outs(r):
        more = dict(inc=Out((R[r], dp))) if r else {}
        return dict(tok=Out((R[r], dp)), df=Out((R[r], dp), BF), dgp=Out((R[r], ff), BF, True), dup=Out((R[r], ff), BF, True),
                    z=Out((R[r], ff), BF, True), dy=Out((R[r], dp), BF), small=Out((8, dp)), **more)

    def feed_scratch(r):
        return dict(acc=V((R[r], dp), F32), pre=V((2, 2, R[r], FT), BF), wide=V((2, 3, R[r], FT), BF), wsem=dma((2, 3)))

    def turned_outs(r):
        return dict(da=Out((R[r], 1024), BF), dkv=Out((nb, nsq, S[r], 640), BF))

    def turned_scratch(r):
        return dict(kvg=V((KN[r], 640), BF), kvt=V((KV_HEADS, 128, KN[r]), BF), bias=V((KN[r], GROUP * S[r]), F32),
                    dcol=V((R[r], 128), F32), dt=V((8, GROUP * S[r]), F32), ct=V((2, 32, S[r]), F32),
                    do16=V((HEADS, R[r], 128), BF), dqt=V((HEADS, 64, S[r]), F32))

    P, F, B, T, L = [None] * 3, [None] * 3, [None] * 3, [None] * 3, [None] * 3
    rt = [None] + list(routes)

    def begin(k):
        k.a[...] = dot(k.x[...], k.spread[0:d]).astype(BF)
        for m in range(nsq):
            k.cos[m * bl:m * bl + bl] = k.cosb[...]
            k.sin[m * bl:m * bl + bl] = k.sinb[...]

    ins = dict(x=x, spread=spread, cosb=cosb, sinb=sinb)
    afters = seen_outs(0)
    if (geo.n_dp, geo.n_blk) != (G, 4):
        wa, wo, gu, wd = (lax.all_gather(w, "dp", axis=0, tiled=True) for w in slabs)

        def k_first(k):
            k = join(k, k.p)
            begin(k)
            k.gn = gains(k.wa)
            project(geo, 0, k)
        P[0] = join(call("first_project", k_first, dict(wa=wa, **ins), dict(p=proj_outs(0))).p)
        P[0].kvall = share(P[0].kv.reshape(nsq, S[0], 640))
        F[0] = call("attend", lambda k: attend(geo, 0, k, blk_of()), dict(q16=P[0].q16, kvall=P[0].kvall), afters, seen_scratch(0))
    else:
        def k_head(k):
            dp_, blk, y, c, ym, cm = mates()
            z, x_ = dp_ // NX, lax.rem(dp_, NX)
            k = join(k, k.p, k.f, k.fs)
            ticks = gather_ticks(AG_CHUNKS, k.shards, k.slabs, k.sems)
            meet((dp_ + 1 - 2 * x_, blk), ym, cm, z=z)

            def tick(n=1):
                for _ in range(min(n, len(ticks))):
                    ticks.pop(0)()
            tick(2)
            begin(k)
            tick(A_TICKS - 2)
            load = pltpu.make_async_copy(k.slabs[0], k.wa, k.wsem)
            load.start()
            load.wait()
            k.gn = gains(k.wa)
            project_kv(geo, 0, k)
            sharing = Share(k.own, k.kvall, k.ssem, k.rsem)
            k.own[...] = k.kv[...].reshape(nsq, S[0], 640)
            k.kvall[blk] = k.own[...]
            sharing.start()
            tick()
            project_q(geo, 0, k)
            tick()
            sharing.forward()
            tick()
            sharing.arrive()
            attend(geo, 0, k, blk, tick)
            tick(len(ticks))
            sharing.sent()
        got = call("head", k_head, dict(shards=list(slabs), **ins),
                   dict(slabs=[Out((v.shape[0] * geo.n_dp, v.shape[1]), BF, True) for v in slabs], p=proj_outs(0, False), f=afters,
                        kvall=Out((nb, nsq, S[0], 640), BF)),
                   dict(fs=seen_scratch(0), wa=V((dp, COLS_A), BF), kv=V((R[0], 640), BF), own=V((nsq, S[0], 640), BF),
                        wsem=dma, ssem=dma((3,)), rsem=dma((3,)), sems=gather_sems(4, len(AG_CHUNKS))),
                   collective_id=1, has_side_effects=True)
        wa, wo, gu, wd = got.slabs
        P[0], F[0] = join(got.p, kvall=got.kvall), join(got.f)
    gu, wd = Far(gu), Far(wd)
    wou = h = None

    def k_fore(r, k):
        blk = blk_of()
        k = join(k, k.s, k.tl)
        tiles = Tiles(geo, k)
        tiles.start(0, 0)
        k.gn = gains(k.wa)
        if r == 0:
            k.wou[...] = dot(k.spread[...], k.wo[...]).astype(BF)
        v = join(k, k.p, k.f, k.fs)
        if r:
            attend(geo, r, v, blk)
        feed(geo, r, v, blk, tiles)
        n = join(k, k.n, h=k.h2, routes=k.routes2)
        select_rows(geo, r + 1, n, blk)
        project(geo, r + 1, n)

    for r in range(2):
        p = dict(a=P[r].a, q16=P[r].q16, kvall=P[r].kvall) if r else dict(a=P[0].a, o=F[0].o)
        more = dict(choice=P[r].choice, h=h, routes=rt[r], wou=wou) if r else dict(wo=wo, spread=spread, lens=lens)
        got = call("forward", functools.partial(k_fore, r),
                   dict(wa=wa, gu=gu, wd=wd, p=p, cosb=cosb, sinb=sinb, routes2=rt[r + 1], s=more),
                   dict(f=fore_outs(r), n=proj_outs(r + 1), h2=Out((full, dp)), **({} if r else dict(wou=Out((1024, dp), BF)))),
                   dict(fs=fore_scratch(r), tl=Tiles.scratch(geo)))
        h, F[r], P[r + 1] = got.h2, join(F[r] or {}, got.f), join(got.n)
        wou = wou if r else got.wou
        P[r + 1].kvall = share(P[r + 1].kv.reshape(nsq, S[r + 1], 640))

    def k_turn(k):
        blk = blk_of()
        k = join(k, k.tl)
        tiles = Tiles(geo, k)
        tiles.start(0, 0)
        k.gn = gains(k.wa)
        v = join(k, k.p, k.f, k.fs, h2=k.h3)
        attend(geo, 2, v, blk)
        feed(geo, 2, v, blk, tiles)
        tiles = Tiles(geo, join(k, k.bs), (v.gp, v.up))
        tiles.start(0, 0)
        k.out[...] = dot_nt(k.h3[...].astype(BF), k.spread[0:d]).astype(BF)
        k.dh[...] = dot(k.cot[...], k.spread[0:d])
        v = join(v, k.bs, k.ts, k.b, k.t)
        back_feed(geo, 2, v, blk, tiles)
        back_attend(geo, 2, v, blk)

    p = P[2]
    got = call("turn", k_turn,
               dict(wa=wa, gu=gu, wd=wd, wou=wou, h=h, spread=spread, cot=cot, routes=rt[2],
                    p=dict(a=p.a, q16=p.q16, kvall=p.kvall, choice=p.choice, cos=p.cos, sin=p.sin)),
               dict(f=fore_outs(2), b=feed_outs(2), t=turned_outs(2), out=Out((full, d), BF), dh=Out((full, dp))),
               dict(fs=fore_scratch(2), bs=feed_scratch(2), ts=turned_scratch(2), tl=Tiles.scratch(geo), h3=V((full, dp), F32)))
    F[2], B[2], T[2], out, dh = join(got.f), join(got.b), join(got.t), got.out, got.dh

    def k_back(r, k):
        blk = blk_of()
        v = join(k, k.p, k.f, k.b, k.bs, k.tl)
        tiles = Tiles(geo, v, (v.gp, v.up))
        tiles.start(0, 0)
        v.gn = k.gn = gains(k.wa)
        k.first[...] = jnp.zeros(k.first.shape, F32)
        back_project(geo, r + 1, join(k, k.n), blk)
        v.dh = k.dh2
        back_feed(geo, r, v, blk, tiles)
        if r > 0:
            back_attend(geo, r, join(v, k.t, k.ts), blk)

    for r in (1, 0):
        n, q, p, f = r + 1, P[r + 1], P[r], F[r]
        mine = give_back(T[n].dkv).reshape(R[n], 640)
        late = dict(q16=p.q16, kvall=p.kvall, cos=p.cos, sin=p.sin, choice=p.choice) if r else {}
        more = dict(o=f.o, lse=f.lse) if r else {}
        rest = dict(wou=wou, routes=rt[r]) if r else dict(lens=lens)
        got = call("backward", functools.partial(k_back, r),
                   dict(wa=wa, gu=gu, wd=wd, dh=dh, **rest,
                        n=dict(dkvown=mine, da=T[n].da, tok=B[n].tok, inc=B[n].inc, choice=q.choice, st=q.st, a=q.a,
                               cos=q.cos, sin=q.sin),
                        p=dict(a=p.a, **late),
                        f=dict(b=f.b, gp=Far(f.gp), up=Far(f.up), yf=f.yf, sx=f.sx, **more)),
                   dict(b=feed_outs(r), da2=Out((R[n], COLS_A), BF), first=Out((8, dp)), dh2=Out((full, dp)),
                        **(dict(t=turned_outs(r)) if r else {})),
                   dict(bs=feed_scratch(r), tl=Tiles.scratch(geo), **(dict(ts=turned_scratch(r)) if r else {})))
        dh, B[r], L[n] = got.dh2, join(got.b), join(da2=got.da2, first=got.first)
        if r:
            T[r] = join(got.t)
    p, f = P[0], F[0]
    T[0] = call("backward_attend", lambda k: back_attend(geo, 0, k, blk_of()),
                dict(wou=wou, dy=B[0].dy, q16=p.q16, kvall=p.kvall, o=f.o, lse=f.lse, cos=p.cos, sin=p.sin),
                turned_outs(0), turned_scratch(0))
    mine = give_back(T[0].dkv).reshape(R[0], 640)

    def k_last(k):
        blk = blk_of()
        k.gn = gains(k.wa)
        k.first[...] = jnp.zeros(k.first.shape, F32)
        back_project(geo, 0, k, blk)
        high, low = halves(k.dh2[...])
        k.grad[...] = dot_nt(high, k.spread[0:d]) + dot_nt(low, k.spread[0:d])
    L[0] = call("last_project", k_last,
                dict(wa=wa, dkvown=mine, da=T[0].da, tok=B[0].tok, dh=dh, lens=lens, st=p.st, a=p.a, cos=p.cos, sin=p.sin,
                     spread=spread),
                dict(da2=Out((R[0], COLS_A), BF), first=Out((8, dp)), grad=Out((full, d))), dict(dh2=V((full, dp), F32)))
    return out, L[0].grad, spread, [join(P[r], F[r], B[r], L[r]) for r in range(3)]


def products(geo, lefts, rights, width, tile, rows, spread=None, extra=None):
    R = [geo.rows(r) for r in range(3)]
    dp = geo.dp

    def body(k):
        at = 0
        for i in range(3):
            for c in range(0, rows, 256):
                v = k.lefts[i][:, c:c + 256] if spread is None else dot(k.lefts[i][...], k.spread[:, c:c + 256]).astype(BF)
                k.left[c:c + 256, at:at + R[i]] = v.T
            at += R[i]
        c0 = 0
        for refs in k.rights:
            n = refs[0].shape[1]
            for t in range(0, n, tile):
                w = min(tile, n - t)
                right = jnp.concatenate([v[:, t:t + w] for v in refs], axis=0)
                k.res[:, c0 + t:c0 + t + w] = dot(k.left[...], right).astype(BF)
            c0 += n
        if extra is not None:
            small = k.small[0][...] + k.small[1][...] + k.small[2][...]
            f = k.first[0][...] + k.first[1][...] + k.first[2][...]
            small = jnp.where(rowid(small.shape) == 0, f, small)
            cols = jnp.concatenate([small, jnp.zeros((120, dp), F32)], axis=0).T
            cols = pltpu.roll(cols, 64, 1)
            k.res[:, 896:1024] = jnp.where(lanes(cols.shape) < 64, k.res[:, 896:1024].astype(F32), cols).astype(BF)
    ins = dict(lefts=lefts, rights=rights, **(extra or {}), **({} if spread is None else dict(spread=spread)))
    return call("weight_grads", body, ins, dict(res=Out((rows, width), BF)), dict(left=pltpu.VMEM((rows, sum(R)), BF))).res


def weight_grads(geo, saved, spread):
    dp, ff = geo.dp, geo.ff
    a = products(geo, [v.u for v in saved], [[v.da2 for v in saved]], COLS_A, 512, dp,
                 extra=dict(small=[v.small for v in saved], first=[v.first for v in saved]))
    o = products(geo, [v.o for v in saved], [[v.dy for v in saved]], dp, 512, dp, spread=spread)
    gu = products(geo, [v.w for v in saved], [[v.dgp for v in saved], [v.dup for v in saved]], 2 * ff, 512, dp)
    d = products(geo, [v.z for v in saved], [[v.df for v in saved]], dp, 256, ff)
    return a, o, gu, d


MESH = pl.DeviceIdType.MESH

NZ, NX = 4, 2
AHEAD = 2
OFFSETS = (0, 2, 4, 6, 8, 10, 12, 13, 14)
G = NZ * NX


def meet(*others, z=None):
    dp, blk = lax.axis_index("dp"), lax.axis_index("blk")
    bar = pltpu.get_barrier_semaphore()
    for t in others:
        pl.semaphore_signal(bar, inc=1, device_id=t, device_id_type=MESH)
    count = len(others)
    if z is not None:
        @pl.when(z > 0)
        def _():
            pl.semaphore_signal(bar, inc=1, device_id=(dp - NX, blk), device_id_type=MESH)

        @pl.when(z < NZ - 1)
        def _():
            pl.semaphore_signal(bar, inc=1, device_id=(dp + NX, blk), device_id_type=MESH)
        count = count + jnp.where(z > 0, 1, 0) + jnp.where(z < NZ - 1, 1, 0)
    pl.semaphore_wait(bar, count)


def gather_ticks(chunks, ins, outs, sems):
    ls, zs, zr, xs, xr, ys, yr, cs, cr = sems
    nslab = len(ins)
    dp, blk = lax.axis_index("dp"), lax.axis_index("blk")
    z, x = dp // NX, lax.rem(dp, NX)
    y, c = blk // 2, lax.rem(blk, 2)
    left, right = (dp - NX, blk), (dp + NX, blk)
    xm, ym, cm = (dp + 1 - 2 * x, blk), (dp, lax.rem(blk + 2, 4)), (dp, blk + 1 - 2 * c)

    locs = [pltpu.make_async_copy(ins[s], outs[s].at[pl.ds(pl.multiple_of(dp * ins[s].shape[0], 16), ins[s].shape[0])], ls.at[s])
            for s in range(nslab)]

    def piece(i, g, q):
        s, c0, n, split = chunks[i]
        rows = ins[s].shape[0]
        h = rows // split
        return outs[s].at[pl.ds(pl.multiple_of(g * rows + q * h, 16), h), pl.ds(c0, n)]

    def myq(i):
        return blk if chunks[i][3] == 4 else c

    def rem(src, dst, a, b, to):
        return pltpu.make_async_remote_copy(src_ref=src, dst_ref=dst, send_sem=a, recv_sem=b, device_id=to, device_id_type=MESH)

    def own(i):
        s, c0, n, split = chunks[i]
        h = ins[s].shape[0] // split
        return ins[s].at[pl.ds(pl.multiple_of(myq(i) * h, 16), h), pl.ds(c0, n)]

    def zcopy(i, d, s, src_own):
        zz = z - s if d == 0 else z + s
        p = piece(i, zz * NX + x, myq(i))
        return rem(own(i) if src_own else p, p, zs.at[i, d, s], zr.at[i, d, s], right if d == 0 else left)

    def zrecv(i, d, s):
        zz = z - 1 - s if d == 0 else z + 1 + s
        p = piece(i, zz * NX + x, myq(i))
        return rem(p, p, zs.at[i, d, s], zr.at[i, d, s], right if d == 0 else left)

    def xcopy(i, zz, src_own=False):
        p = piece(i, zz * NX + x, myq(i))
        return rem(own(i) if src_own else p, p, xs.at[i, zz], xr.at[i, zz], xm)

    def xrecv(i, zz):
        p = piece(i, zz * NX + 1 - x, myq(i))
        return rem(p, p, xs.at[i, zz], xr.at[i, zz], xm)

    def ycopy(i, g):
        p = piece(i, g, blk)
        return rem(p, p, ys.at[i, g], yr.at[i, g], ym)

    def yrecv(i, g):
        p = piece(i, g, lax.rem(blk + 2, 4))
        return rem(p, p, ys.at[i, g], yr.at[i, g], ym)

    def ccopy(i, k, g):
        q = myq(i) if k == 0 else lax.rem(blk + 2, 4)
        p = piece(i, g, q)
        return rem(p, p, cs.at[i, k, g], cr.at[i, k, g], cm)

    def crecv(i, k, g):
        if chunks[i][3] == 4:
            mate = blk + 1 - 2 * c
            q = mate if k == 0 else lax.rem(mate + 2, 4)
        else:
            q = 1 - c
        p = piece(i, g, q)
        return rem(p, p, cs.at[i, k, g], cr.at[i, k, g], cm)

    def spread(i, g):
        if chunks[i][3] == 4:
            ycopy(i, g).start()
        ccopy(i, 0, g).start()

    def begin(i):
        @pl.when(z < NZ - 1)
        def _():
            zcopy(i, 0, 0, True).start()

        @pl.when(z > 0)
        def _():
            zcopy(i, 1, 0, True).start()
        xcopy(i, z, True).start()

    def zstep(i, s):
        @pl.when(z - 1 - s >= 0)
        def _():
            zrecv(i, 0, s).wait_recv()
            if s < NZ - 2:
                @pl.when(z < NZ - 1)
                def _():
                    zcopy(i, 0, s + 1, False).start()
            xcopy(i, z - 1 - s).start()
            spread(i, (z - 1 - s) * NX + x)

        @pl.when(z + 1 + s < NZ)
        def _():
            zrecv(i, 1, s).wait_recv()
            if s < NZ - 2:
                @pl.when(z > 0)
                def _():
                    zcopy(i, 1, s + 1, False).start()
            xcopy(i, z + 1 + s).start()
            spread(i, (z + 1 + s) * NX + x)

    def xstep(i, k):
        def one(zz):
            xrecv(i, zz).wait_recv()
            spread(i, zz * NX + 1 - x)
        if k == 0:
            one(z)
        else:
            pl.when(z - k >= 0)(lambda: one(z - k))
            pl.when(z + k < NZ)(lambda: one(z + k))

    def ystep(i, k):
        g = lax.rem(dp + k, G)
        yrecv(i, g).wait_recv()
        ccopy(i, 1, g).start()

    def cstep(i, k):
        g = lax.rem(dp + k, G)
        crecv(i, 0, g).wait_recv()
        if chunks[i][3] == 4:
            crecv(i, 1, g).wait_recv()

    def sent(i):
        @pl.when(z < NZ - 1)
        def _():
            zcopy(i, 0, 0, True).wait_send()

        @pl.when(z > 0)
        def _():
            zcopy(i, 1, 0, True).wait_send()
        for s in range(NZ - 1):
            if s < NZ - 2:
                @pl.when((z - 1 - s >= 0) & (z < NZ - 1))
                def _():
                    zcopy(i, 0, s + 1, False).wait_send()

                @pl.when((z + 1 + s < NZ) & (z > 0))
                def _():
                    zcopy(i, 1, s + 1, False).wait_send()
        xcopy(i, z, True).wait_send()
        for k in range(1, NZ):
            xcopy(i, lax.rem(z + k, NZ)).wait_send()
        for k in range(1, G):
            g = lax.rem(dp + k, G)
            ccopy(i, 0, g).wait_send()
            if chunks[i][3] == 4:
                ycopy(i, g).wait_send()
                ccopy(i, 1, g).wait_send()

    nch = len(chunks)
    stages = [begin] + [functools.partial(lambda i, s: (zstep(i, s), xstep(i, s)), s=s) for s in range(NZ - 1)]
    stages.append(lambda i: xstep(i, NZ - 1))
    stages.append(lambda i: [ystep(i, k) for k in range(1, G)] if chunks[i][3] == 4 else None)
    stages.append(lambda i: [cstep(i, k) for k in range(1, G)])
    stages.append(sent)

    def first():
        for l in locs:
            l.start()

    def tick(t):
        if t == 6:
            locs[0].wait()
        if t == nch + len(stages) - 2:
            for l in locs[1:]:
                l.wait()
        for s in reversed(range(len(stages))):
            i = t - s
            if 0 <= i < nch:
                stages[s](i)
    return [first] + [functools.partial(tick, t) for t in range(nch + len(stages) - 1)]


def gather_sems(n, nch):
    dma = pltpu.SemaphoreType.DMA
    return [dma((n,)), dma((nch, 2, NZ - 1)), dma((nch, 2, NZ - 1)), dma((nch, NZ)), dma((nch, NZ)),
            dma((nch, G)), dma((nch, G)), dma((nch, 2, G)), dma((nch, 2, G))]


def add_into(dst, other, n):
    def body(k, _):
        dst[k] = (dst[k].astype(jnp.float32) + other(k).astype(jnp.float32)).astype(dst.dtype)
        return 0
    lax.fori_loop(0, n, body, 0)


def reduce_kernel(chunks, nslab, *refs):
    nch = len(chunks)
    ins, outs = refs[:nslab], refs[nslab:2 * nslab]
    bufs = refs[2 * nslab:]
    own, crv, yrv, xrv, zrv, fin, s4b = (bufs[k * nch:(k + 1) * nch] for k in range(7))
    ls, cs, cr, ys, yr, xs, xr, zs, zr, fs, fr = bufs[7 * nch:]
    dp, blk = lax.axis_index("dp"), lax.axis_index("blk")
    z, x = dp // NX, lax.rem(dp, NX)
    y, c = blk // 2, lax.rem(blk, 2)
    left, right = (dp - NX, blk), (dp + NX, blk)
    xm, ym, cm = (dp + 1 - 2 * x, blk), (dp, lax.rem(blk + 2, 4)), (dp, blk + 1 - 2 * c)
    meet(xm, ym, cm, z=z)

    def rem(src, dst, a, b, to):
        return pltpu.make_async_remote_copy(src_ref=src, dst_ref=dst, send_sem=a, recv_sem=b, device_id=to, device_id_type=MESH)

    def four(i):
        return chunks[i][3] == 4

    def part(i, core):
        s, c0, n, split = chunks[i]
        cols = pl.ds(c0, n)
        return ins[s].at[:, :, :, core, :, cols] if split == 4 else ins[s].at[:, :, core, :, cols]

    def load(i):
        return pltpu.make_async_copy(part(i, c), own[i], ls.at[i])

    def core_send(i):
        return rem(part(i, 1 - c), crv[i], cs.at[i, 0], cr.at[i, 0], cm)

    def y_send(i):
        return rem(own[i].at[:, :, 1 - y], yrv[i], ys.at[i], yr.at[i], ym)

    def s2(i):
        return yrv[i] if four(i) else own[i]

    def x_send(i):
        return rem(s2(i).at[:, 1 - x], xrv[i], xs.at[i], xr.at[i], xm)

    def z_copy(i, d, lo, hi, first, to):
        src = xrv[i].at[pl.ds(lo, hi - lo)] if first else zrv[i].at[d, pl.ds(lo, hi - lo)]
        return rem(src, zrv[i].at[d, pl.ds(lo, hi - lo)], zs.at[i, d], zr.at[i, d], to)

    def right_send(i, k):
        return z_copy(i, 0, k + 1, NZ, k == 0, right)

    def left_send(i, k):
        return z_copy(i, 1, 0, k, k == NZ - 1, left)

    def st0(i):
        load(i).start()
        core_send(i).start()

    def st1(i):
        load(i).wait()
        core_send(i).wait_recv()

        def body(g, _):
            zz, xx = g // NX, lax.rem(g, NX)
            for yy in ((0, 1) if four(i) else (None,)):
                at = (zz, xx) if yy is None else (zz, xx, yy)
                own[i][at] = (own[i][at].astype(jnp.float32) + crv[i][at].astype(jnp.float32)).astype(jnp.bfloat16)
            return 0
        lax.fori_loop(0, G, body, 0)
        if four(i):
            y_send(i).start()

    def st2(i):
        if four(i):
            y_send(i).wait_recv()

            def body(g, _):
                zz, xx = g // NX, lax.rem(g, NX)
                yrv[i][zz, xx] = (yrv[i][zz, xx].astype(jnp.float32) + own[i][zz, xx, y].astype(jnp.float32)).astype(jnp.bfloat16)
                return 0
            lax.fori_loop(0, G, body, 0)
        x_send(i).start()

    def zstep(i, s):
        if s < NZ - 1:
            @pl.when(z == s)
            def _():
                if s > 0:
                    z_copy(i, 0, s, NZ, False, right).wait_recv()
                    for k in range(s + 1, NZ):
                        zrv[i][0, k] = (zrv[i][0, k].astype(jnp.float32) + xrv[i][k].astype(jnp.float32)).astype(jnp.bfloat16)
                right_send(i, s).start()

            @pl.when(z == NZ - 1 - s)
            def _():
                k0 = NZ - 1 - s
                if s > 0:
                    z_copy(i, 1, 0, k0 + 1, False, left).wait_recv()
                    for k in range(k0):
                        zrv[i][1, k] = (zrv[i][1, k].astype(jnp.float32) + xrv[i][k].astype(jnp.float32)).astype(jnp.bfloat16)
                left_send(i, k0).start()

    def st3(i):
        x_send(i).wait_recv()
        add_into(xrv[i], lambda k: s2(i)[k, x], NZ)
        zstep(i, 0)

    def finish(i):
        q = blk if four(i) else c
        dst = fin[i].at[q] if four(i) else s4b[i]

        def put(v):
            if four(i):
                fin[i][blk] = v.astype(jnp.bfloat16)
            else:
                s4b[i][...] = v.astype(jnp.bfloat16)

        @pl.when(z == 0)
        def _():
            z_copy(i, 1, 0, 1, False, left).wait_recv()
            put(xrv[i][0].astype(jnp.float32) + zrv[i][1, 0].astype(jnp.float32))

        @pl.when(z == NZ - 1)
        def _():
            z_copy(i, 0, NZ - 1, NZ, False, right).wait_recv()
            put(xrv[i][NZ - 1].astype(jnp.float32) + zrv[i][0, NZ - 1].astype(jnp.float32))

        @pl.when((z > 0) & (z < NZ - 1))
        def _():
            put(xrv[i][z].astype(jnp.float32) + zrv[i][0, z].astype(jnp.float32) + zrv[i][1, z].astype(jnp.float32))
        if four(i):
            fin_send(i, 0).start()
            fin_send(i, 1).start()
        else:
            fin_send(i, 0).start()

    def fin_send(i, k):
        if four(i):
            q = blk if k < 2 else lax.rem(blk + 2, 4)
            return rem(fin[i].at[q], fin[i].at[q], fs.at[i, k], fr.at[i, k], ym if k == 0 else cm)
        if k == 0:
            return rem(s4b[i], fin[i].at[2], fs.at[i, 0], fr.at[i, 0], ym)
        return rem(fin[i].at[c], fin[i].at[c], fs.at[i, 1], fr.at[i, 1], cm)

    def fin_recv(i, k):
        if four(i):
            mate = blk + 1 - 2 * c
            q = lax.rem(blk + 2, 4) if k == 0 else mate if k == 1 else lax.rem(mate + 2, 4)
            return rem(fin[i].at[q], fin[i].at[q], fs.at[i, k], fr.at[i, k], cm)
        if k == 0:
            return fin_send(i, 0)
        return rem(fin[i].at[1 - c], fin[i].at[1 - c], fs.at[i, 1], fr.at[i, 1], cm)

    def st8(i):
        fin_recv(i, 0).wait_recv()
        if four(i):
            fin_send(i, 2).start()
        else:
            fin[i][c] = (fin[i][2].astype(jnp.float32) + s4b[i][...].astype(jnp.float32)).astype(jnp.bfloat16)
            fin_send(i, 1).start()

    def st9(i):
        s, c0, n, split = chunks[i]
        for k in ((1, 2) if four(i) else (1,)):
            fin_recv(i, k).wait_recv()
        for q in range(split):
            outs[s][q, :, pl.ds(c0, n)] = fin[i][q].astype(jnp.float32)

    def sent(i):
        core_send(i).wait_send()
        if four(i):
            y_send(i).wait_send()
        x_send(i).wait_send()
        for k in range(NZ - 1):
            pl.when(z == k)(lambda k=k: right_send(i, k).wait_send())
            pl.when(z == k + 1)(lambda k=k: left_send(i, k + 1).wait_send())
        for k in range(3 if four(i) else 2):
            fin_send(i, k).wait_send()

    stages = [st1, st2, st3] + [functools.partial(lambda i, s: zstep(i, s), s=s) for s in range(1, NZ - 1)] + [finish, st8, st9, sent]
    for i in range(min(AHEAD, nch)):
        st0(i)
    for t in range(nch + max(OFFSETS)):
        if t + AHEAD < nch:
            st0(t + AHEAD)
        for s in reversed(range(len(stages))):
            i = t - OFFSETS[s]
            if 0 <= i < nch:
                stages[s](i)


def reduce(slabs, chunks):
    n, nch = len(slabs), len(chunks)
    dma = pltpu.SemaphoreType.DMA
    bf = jnp.bfloat16

    def shapes(kind):
        out = []
        for s, c0, nc, split in chunks:
            h = slabs[s].shape[-2]
            lead = (NZ, NX, 2) if split == 4 else (NZ, NX)
            tiny = (1, 16, 128)
            shape = dict(own=lead + (h, nc), crv=lead + (h, nc), yrv=(NZ, NX, h, nc) if split == 4 else tiny,
                         xrv=(NZ, h, nc), zrv=(2, NZ, h, nc), fin=(4 if split == 4 else 3, h, nc),
                         s4b=(h, nc) if split == 2 else tiny)[kind]
            out.append(pltpu.VMEM(shape, bf))
        return out
    scratch = sum([shapes(k) for k in ("own", "crv", "yrv", "xrv", "zrv", "fin", "s4b")], [])
    sems = [dma((nch,)), dma((nch, 1)), dma((nch, 1)), dma((nch,)), dma((nch,)), dma((nch,)), dma((nch,)),
            dma((nch, 2)), dma((nch, 2)), dma((nch, 3)), dma((nch, 3))]
    outs = []
    for k, s in enumerate(slabs):
        split = next(ch[3] for ch in chunks if ch[0] == k)
        outs.append(jax.ShapeDtypeStruct((split,) + s.shape[-2:], jnp.float32))
    return pl.pallas_call(
        functools.partial(reduce_kernel, chunks, n),
        out_shape=outs,
        in_specs=[pl.BlockSpec(memory_space=pl.ANY)] * n,
        out_specs=[pl.BlockSpec(memory_space=pltpu.VMEM)] * n,
        scratch_shapes=scratch + sems,
        compiler_params=pltpu.CompilerParams(collective_id=2, has_side_effects=True, vmem_limit_bytes=60 << 20),
        name="reduce_grads",
    )(*slabs)


A_TICKS = 8
AG_CHUNKS = [(0, 0, 1664, 4), (1, 0, 1024, 2), (2, 0, 2560, 4), (2, 2560, 2560, 4), (3, 0, 1024, 2)]
RS_CHUNKS = [(2, 0, 640, 4), (3, 0, 256, 2), (2, 640, 640, 4), (3, 256, 256, 2), (2, 1280, 640, 4), (3, 512, 256, 2),
             (2, 1920, 640, 4), (3, 768, 256, 2), (2, 2560, 640, 4), (0, 0, 512, 2), (2, 3200, 640, 4), (0, 512, 512, 2),
             (2, 3840, 640, 4), (0, 1024, 640, 2), (2, 4480, 640, 4), (1, 0, 512, 2), (1, 512, 512, 2)]


def pad_to(v, shape):
    return jnp.pad(v, [(0, b - a) for a, b in zip(v.shape, shape)])


def pad_cols(v, geo):
    v = v.reshape(v.shape[0], geo.n_dp, geo.gw)
    return jnp.pad(v, ((0, 0), (0, 0), (0, geo.gp - geo.gw))).reshape(v.shape[0], geo.dp)


def unpad_cols(v, geo):
    return v.reshape(v.shape[0], geo.n_dp, geo.gp)[:, :, :geo.gw].reshape(v.shape[0], geo.d)


def pack(geo, q, k, v, o, g, u, d, g1, g2, rt):
    rows = q.shape[0]
    kv = jnp.concatenate([k.reshape(rows, KV_HEADS, 64), v.reshape(rows, KV_HEADS, 64)], axis=2).reshape(rows, 640)
    small = pad_to(jnp.concatenate([g1[:, None], g2[:, None], rt], axis=1), (rows, 64))
    a = pad_to(jnp.concatenate([q, small, kv], axis=1), (geo.gp, COLS_A))
    gu = pad_to(jnp.concatenate([g, u], axis=1), (geo.gp, 2 * geo.ff))
    return a, pad_to(pad_cols(o, geo), (geo.gp, geo.dp)), gu, pad_cols(d, geo)


def summed_grads(geo, slabs):
    a, o, gu, d = slabs
    if (geo.n_dp, geo.n_blk) != (G, 4):
        shares = [lax.psum_scatter(v, "dp", scatter_dimension=0, tiled=True) for v in slabs]
        return tuple(lax.psum(v, "blk").astype(F32) for v in shares)
    gp, rd = geo.gp, d.shape[0] // G
    got = reduce([a.reshape(NZ, NX, 2, gp // 2, -1), o.reshape(NZ, NX, 2, gp // 2, -1), gu.reshape(NZ, NX, 2, 2, gp // 4, -1),
                  d.reshape(NZ, NX, 2, rd // 2, -1)], RS_CHUNKS)
    return tuple(w.reshape(-1, w.shape[-1]) for w in got)


def unpack(geo, slabs):
    a, o, gu, d = slabs
    a, o, gu = a[:geo.gw], o[:geo.gw], gu[:geo.gw]
    kv = a[:, 1024:].reshape(geo.gw, KV_HEADS, 128)
    return (a[:, :960], kv[:, :, :64].reshape(geo.gw, 320), kv[:, :, 64:].reshape(geo.gw, 320), unpad_cols(o, geo),
            gu[:, :geo.ff], gu[:, geo.ff:], unpad_cols(d, geo), a[:, 960], a[:, 961], a[:, 962:965])


def mates():
    dp, blk = lax.axis_index("dp"), lax.axis_index("blk")
    y, c = blk // 2, lax.rem(blk, 2)
    return dp, blk, y, c, (dp, lax.rem(blk + 2, 4)), (dp, blk + 1 - 2 * c)


class Share:
    def __init__(self, own, out, ssem, rsem):
        dp, blk, y, c, ym, cm = mates()

        def rem(src, b, k, to):
            return pltpu.make_async_remote_copy(src_ref=src, dst_ref=out.at[b], send_sem=ssem.at[k], recv_sem=rsem.at[k],
                                                device_id=to, device_id_type=MESH)
        far, near = lax.rem(blk + 2, 4), blk + 1 - 2 * c
        both = lax.rem(near + 2, 4)
        self.out = [rem(own, blk, 0, ym), rem(own, blk, 1, cm), rem(out.at[far], far, 2, cm)]
        self.come = [rem(out.at[far], far, 0, ym), rem(out.at[near], near, 1, cm), rem(out.at[both], both, 2, cm)]

    def start(self):
        self.out[0].start()
        self.out[1].start()

    def forward(self):
        self.come[0].wait_recv()
        self.out[2].start()

    def arrive(self):
        self.come[1].wait_recv()
        self.come[2].wait_recv()

    def sent(self):
        for v in self.out:
            v.wait_send()


def share_kernel(own, out, lsem, ssem, rsem):
    dp, blk, y, c, ym, cm = mates()
    meet(ym, cm)
    s = Share(own, out, ssem, rsem)
    s.start()
    local = pltpu.make_async_copy(own, out.at[blk], lsem)
    local.start()
    s.forward()
    s.arrive()
    s.sent()
    local.wait()


def share_rows(geo, ident, kv):
    if geo.n_blk != 4:
        return lax.all_gather(kv, "blk", axis=0, tiled=False)
    dma = pltpu.SemaphoreType.DMA
    return pl.pallas_call(
        share_kernel, out_shape=jax.ShapeDtypeStruct((4,) + kv.shape, kv.dtype),
        in_specs=[pl.BlockSpec(memory_space=pltpu.VMEM)], out_specs=pl.BlockSpec(memory_space=pl.ANY),
        scratch_shapes=[dma, dma((3,)), dma((3,))],
        compiler_params=pltpu.CompilerParams(collective_id=ident, has_side_effects=True), name="share_rows")(kv)


def give_kernel(dkv, out, got1, half, got2, ssem, rsem):
    dp, blk, y, c, ym, cm = mates()
    meet(ym, cm)

    def rem(src, dst, k, to):
        return pltpu.make_async_remote_copy(src_ref=src, dst_ref=dst, send_sem=ssem.at[k], recv_sem=rsem.at[k],
                                            device_id=to, device_id_type=MESH)
    first = [rem(dkv.at[yy, 1 - c], got1.at[yy], yy, cm) for yy in range(2)]
    for f in first:
        f.start()
    for f in first:
        f.wait_recv()
    half[...] = (got1[1 - y].astype(F32) + dkv[1 - y, c].astype(F32)).astype(BF)
    second = rem(half, got2, 2, ym)
    second.start()
    mine = got1[y].astype(F32) + dkv[y, c].astype(F32)
    second.wait_recv()
    out[...] = mine + got2[...].astype(F32)
    for f in first + [second]:
        f.wait_send()


def give_rows(geo, ident, dkv):
    if geo.n_blk != 4:
        return lax.psum_scatter(dkv, "blk", scatter_dimension=0, tiled=False).astype(F32)
    dma = pltpu.SemaphoreType.DMA
    piece = dkv.shape[1:]
    vm = pl.BlockSpec(memory_space=pltpu.VMEM)
    return pl.pallas_call(
        give_kernel, out_shape=jax.ShapeDtypeStruct(piece, F32), in_specs=[vm], out_specs=vm,
        scratch_shapes=[pltpu.VMEM((2,) + piece, BF), pltpu.VMEM(piece, BF), pltpu.VMEM(piece, BF), dma((3,)), dma((3,))],
        compiler_params=pltpu.CompilerParams(collective_id=ident, has_side_effects=True, vmem_limit_bytes=40 << 20),
        name="give_rows")(dkv.reshape((2, 2) + piece))


def per_device(block_input, cotangent, seq_lengths, routes_two, routes_three, query_weight, key_weight, value_weight, output_weight,
               gate_weight, up_weight, down_weight, first_gain, second_gain, router_weight):
    micro, seqs, bl, d = block_input.shape
    n_dp, n_blk = lax.axis_size("dp"), lax.axis_size("blk")
    count = micro * seqs
    geo = Geo(count, bl, n_dp, n_blk, d, gate_weight.shape[1], (None, routes_two.shape[2], routes_three.shape[2]))
    slabs = pack(geo, query_weight, key_weight, value_weight, output_weight, gate_weight, up_weight, down_weight, first_gain,
                 second_gain, router_weight)
    ids = iter(range(10, 30))
    out, grad, spread, saved = block(geo, block_input.reshape(count * bl, d), cotangent.reshape(count * bl, d), seq_lengths.reshape(count),
                (routes_two.reshape(count, -1), routes_three.reshape(count, -1)), slabs,
                lambda kv: share_rows(geo, next(ids), kv), lambda dkv: give_rows(geo, next(ids), dkv))
    grads = unpack(geo, summed_grads(geo, weight_grads(geo, saved, spread)))
    return (out.reshape(block_input.shape), grad.reshape(block_input.shape)) + tuple(grads)


def solution(mesh):
    in_specs = (
        P(None, "dp", "blk", None),
        P(None, "dp", "blk", None),
        P(None, "dp"),
        P(None, "dp", None),
        P(None, "dp", None),
        P("dp", None),
        P("dp", None),
        P("dp", None),
        P("dp", None),
        P("dp", None),
        P("dp", None),
        P("dp", None),
        P("dp"),
        P("dp"),
        P("dp", None),
    )
    out_specs = (
        P(None, "dp", "blk", None),
        P(None, "dp", "blk", None),
        P("dp", None),
        P("dp", None),
        P("dp", None),
        P("dp", None),
        P("dp", None),
        P("dp", None),
        P("dp", None),
        P("dp"),
        P("dp"),
        P("dp", None),
    )
    return jax.shard_map(
        per_device, mesh=mesh, in_specs=in_specs, out_specs=out_specs, check_vma=False
    )
```

```python
import functools
import math
import types

import jax
import jax.numpy as jnp
import numpy as np
from jax import lax
from jax.experimental import pallas as pl
from jax.experimental.pallas import tpu as pltpu
from jax.sharding import PartitionSpec as P

HEADS, KV_HEADS, HEAD_DIM, RECUR = 15, 5, 64, 3
GROUP = HEADS // KV_HEADS
eps = 1e-05
rope_base = 10000.0
masked_fill = -1e30
BF, F32 = jnp.bfloat16, jnp.float32
COLS_A = 1664
FT = 512


def dot(a, b):
    return lax.dot_general(a, b, (((1,), (0,)), ((), ())), preferred_element_type=F32)


def dot_nt(a, b):
    return lax.dot_general(a, b, (((1,), (1,)), ((), ())), preferred_element_type=F32)


def dot_tn(a, b):
    return lax.dot_general(a, b, (((0,), (0,)), ((), ())), preferred_element_type=F32)


def halves(v):
    high = v.astype(BF)
    return high, (v - high.astype(F32)).astype(BF)


def pick(choice, v):
    high, low = halves(v)
    return dot(choice, high) + dot(choice, low)


def put_back(choice, v):
    high, low = halves(v)
    return dot_tn(choice, high) + dot_tn(choice, low)


def lanes(shape):
    return lax.broadcasted_iota(jnp.int32, shape, len(shape) - 1)


def rowid(shape):
    return lax.broadcasted_iota(jnp.int32, shape, len(shape) - 2)


def swapped(x):
    first = lax.rem(lanes(x.shape), 64) < 32
    return jnp.where(first, pltpu.roll(x, 96, 1), pltpu.roll(x, 32, 1))


class Far:
    def __init__(self, value):
        self.value = value


class Words:
    def __init__(self, value):
        self.value = value


class Out:
    def __init__(self, shape, dtype=F32, far=False):
        self.shape, self.dtype, self.far = shape, dtype, far


def join(*parts, **more):
    got = types.SimpleNamespace()
    for p in parts + (more,):
        vars(got).update(p if isinstance(p, dict) else vars(p))
    return got


def call(name, body, ins, outs, scratch=None, limit=63, **params):
    flat_in, tree_in = jax.tree.flatten(ins)
    flat_out, tree_out = jax.tree.flatten(outs)
    flat_scratch, tree_scratch = jax.tree.flatten(scratch or {})
    n_in, n_out = len(flat_in), len(flat_out)

    def kernel(*refs):
        body(join(tree_in.unflatten(refs[:n_in]), tree_out.unflatten(refs[n_in:n_in + n_out]),
                  tree_scratch.unflatten(refs[n_in + n_out:])))

    vm, far = pl.BlockSpec(memory_space=pltpu.VMEM), pl.BlockSpec(memory_space=pl.ANY)
    words = pl.BlockSpec(memory_space=pltpu.SMEM)
    got = pl.pallas_call(
        kernel,
        out_shape=[jax.ShapeDtypeStruct(o.shape, o.dtype) for o in flat_out],
        in_specs=[far if isinstance(v, Far) else words if isinstance(v, Words) else vm for v in flat_in],
        out_specs=[far if o.far else vm for o in flat_out],
        scratch_shapes=flat_scratch,
        compiler_params=pltpu.CompilerParams(vmem_limit_bytes=limit << 20, **params),
        name=name,
    )(*[v.value if isinstance(v, (Far, Words)) else v for v in flat_in])
    return types.SimpleNamespace(**tree_out.unflatten(got))


class Geo:
    def __init__(self, ns, bl, n_dp, n_blk, d, ff, tops):
        self.ns, self.bl, self.n_dp, self.n_blk, self.d, self.ff = ns, bl, n_dp, n_blk, d, ff
        self.gw = d // n_dp
        self.gp = -(-self.gw // 16) * 16
        self.dp = n_dp * self.gp
        self.slots = (bl, bl // 2, bl // 4)
        self.tops = tops

    def rows(self, r):
        return self.ns * self.slots[r]

    def keys(self, r):
        return self.n_blk * self.slots[r]

    def spread(self):
        e = np.zeros((1024, self.dp), np.float32)
        f = np.arange(self.d)
        e[f, f // self.gw * self.gp + f % self.gw] = 1
        return jnp.asarray(e, BF)

    def tables(self):
        f = rope_base ** (-(np.arange(32, dtype=np.float64) * 2.0) / 64)
        f32 = np.asarray(f, np.float32)
        ph = (np.arange(self.bl * self.n_blk, dtype=np.float32)[:, None] * f32).astype(np.float32).astype(np.float64)
        c, s = np.cos(ph), np.sin(ph)
        cos = np.concatenate([c, c, c, c], 1).astype(np.float32)
        sin = np.concatenate([-s, s, -s, s], 1).astype(np.float32)
        return jnp.asarray(cos), jnp.asarray(sin)


def gains(wa):
    sel = (lanes((8, 128)) == rowid((8, 128)) + 64).astype(BF)
    return dot_nt(sel, wa[:, 896:1024])


def choose(geo, r, routes, blk):
    s, t, bl = geo.slots[r], geo.tops[r], geo.bl
    before = jnp.sum((routes < blk * bl).astype(F32), axis=1, keepdims=True).astype(jnp.int32)
    shift = ((lanes((s, t)) - rowid((s, t))) == before).astype(BF)
    here = (routes == rowid((bl, t)) + blk * bl).astype(BF)
    return dot_nt(shift, here).astype(BF)


def allowed(geo, r, routes, blk, turned, heads=GROUP):
    s, kn, bl = geo.slots[r], geo.keys(r), geo.bl
    shape = (kn, heads * s) if turned else (heads * s, kn)
    key = rowid(shape) if turned else lanes(shape)
    query = lax.rem(lanes(shape) if turned else rowid(shape), s)
    ok = key <= blk * s + query
    if r > 0:
        t = geo.tops[r]
        inside = (routes // bl == rowid((kn, t)) // s)
        if turned:
            count = jnp.sum(inside.astype(F32), axis=1, keepdims=True)
        else:
            count = dot_nt(jnp.ones((8, t), BF), inside.astype(BF))[0:1]
        ok = ok & (lax.rem(key, s).astype(F32) < count)
    return jnp.where(ok, 0.0, masked_fill)


def project_kv(geo, r, k):
    a = k.a[...].astype(F32)
    n1 = lax.rsqrt(jnp.sum(a * a, axis=-1, keepdims=True) * (1.0 / geo.d) + eps)
    k.u[...] = (a * n1 * k.gn[0:1]).astype(BF)
    k.st[...] = jnp.where(lanes(k.st.shape) == 0, n1, 0.0)
    u = k.u[...]
    cos, sin = k.cos[...], k.sin[...]
    left = lanes(cos.shape) < 64
    ckv, skv = jnp.where(left, cos, 1.0), jnp.where(left, sin, 0.0)
    for c0, n in ((1024, 256), (1280, 256), (1536, 128)):
        some = dot(u, k.wa[:, c0:c0 + n])
        for j in range(n // 128):
            x = some[:, 128 * j:128 * j + 128]
            k.kv[:, c0 - 1024 + 128 * j:c0 - 1024 + 128 * j + 128] = (x * ckv + swapped(x) * skv).astype(BF)


def project_q(geo, r, k):
    u = k.u[...]
    cos, sin = k.cos[...], k.sin[...]
    left = lanes(cos.shape) < 64
    for t in range(4):
        both = dot(u, k.wa[:, 256 * t:256 * t + 256])
        for j in range(2):
            x = both[:, 128 * j:128 * j + 128]
            x = (x * cos + swapped(x) * sin).astype(BF).astype(F32) * 0.125
            h = 4 * t + 2 * j
            k.q16[h] = jnp.where(left, x, 0.0).astype(BF)
            if h + 1 < HEADS:
                k.q16[h + 1] = jnp.where(left, pltpu.roll(x, 64, 1), 0.0).astype(BF)


def project(geo, r, k):
    project_kv(geo, r, k)
    project_q(geo, r, k)


def select_rows(geo, r, k, blk):
    s, bl = geo.slots[r], geo.bl
    for m in range(geo.ns):
        ch = choose(geo, r, k.routes[m:m + 1], blk)
        k.choice[m] = ch
        k.a[m * s:m * s + s] = pick(ch, k.h[m * bl:m * bl + bl])
        k.cos[m * s:m * s + s] = pick(ch, k.cosb[...])
        k.sin[m * s:m * s + s] = pick(ch, k.sinb[...])


def attend(geo, r, k, blk, pause=None):
    s, kn = geo.slots[r], geo.keys(r)

    def seq(m, _):
        row0 = m * s if isinstance(m, int) else pl.multiple_of(m * s, s)
        k.kvg[...] = k.kvall[:, m].reshape(kn, KV_HEADS * 128)
        k.bias[...] = allowed(geo, r, k.routes[pl.ds(m, 1)] if r else None, blk, False)
        k.col[...] = jnp.zeros(k.col.shape, F32)

        def group(g, _):
            kvh = k.kvg[:, pl.ds(pl.multiple_of(g * 128, 128), 128)]
            sc = dot_nt(k.q16[pl.ds(g * GROUP, GROUP), pl.ds(row0, s)].reshape(GROUP * s, 128), kvh) + k.bias[...]
            top = jnp.max(sc, axis=-1, keepdims=True)
            p = jnp.exp(sc - top)
            total = jnp.sum(p, axis=-1, keepdims=True)
            k.o16[pl.ds(g * GROUP, GROUP)] = (dot(p.astype(BF), kvh) * (1.0 / total)).reshape(GROUP, s, 128)
            k.col[...] = jnp.where(lanes(k.col.shape) == g, top + jnp.log(total), k.col[...])
            return 0
        if pause is None:
            lax.fori_loop(0, KV_HEADS, group, 0)
        else:
            lax.fori_loop(0, 3, group, 0)
            pause()
            lax.fori_loop(3, KV_HEADS, group, 0)
        left = lanes((s, 128)) < 64
        for t in range(8):
            odd = k.o16[2 * t + 1] if 2 * t + 1 < HEADS else 0.0
            k.o[pl.ds(row0, s), 128 * t:128 * t + 128] = jnp.where(left, pltpu.roll(k.o16[2 * t], 64, 1), odd).astype(BF)
        k.lse[m] = k.col[...].T[0:8]
        return 0
    if pause is None:
        lax.fori_loop(0, geo.ns, seq, 0)
    else:
        for m in range(geo.ns):
            seq(m, 0)
            pause()


class Tiles:
    def __init__(self, geo, k, pre=None):
        self.k, self.n, self.ff, self.pre = k, geo.ff // FT, geo.ff, pre

    def parts(self, t, slot):
        k, c0 = self.k, t * FT
        if not isinstance(t, int):
            c0 = pl.multiple_of(c0, FT)
        cu = c0 + self.ff
        return [pltpu.make_async_copy(k.gu.at[:, pl.ds(c0, FT)], k.gbuf.at[slot], k.tsem.at[slot, 0]),
                pltpu.make_async_copy(k.gu.at[:, pl.ds(cu, FT)], k.ubuf.at[slot], k.tsem.at[slot, 1]),
                pltpu.make_async_copy(k.wd.at[pl.ds(c0, FT)], k.dbuf.at[slot], k.tsem.at[slot, 2])] + [
                    pltpu.make_async_copy(v.at[:, pl.ds(c0, FT)], k.pre.at[slot, j], k.tsem.at[slot, 3 + j])
                    for j, v in enumerate(self.pre or ())]

    def start(self, t, slot):
        for c in self.parts(t, slot):
            c.start()

    def loop(self, step):
        def body(t, _):
            slot = lax.rem(t, 2)

            @pl.when(t + 1 < self.n)
            def _():
                self.start(t + 1, 1 - slot)
            for c in self.parts(t, slot):
                c.wait()
            step(t, slot)
            return 0
        lax.fori_loop(0, self.n, body, 0)

    @staticmethod
    def scratch(geo):
        return dict(gbuf=pltpu.VMEM((2, geo.dp, FT), BF), ubuf=pltpu.VMEM((2, geo.dp, FT), BF),
                    dbuf=pltpu.VMEM((2, FT, geo.dp), BF), tsem=pltpu.SemaphoreType.DMA((2, 5)))


def feed(geo, r, k, blk, tiles):
    s, bl = geo.slots[r], geo.bl
    y = dot(k.o[...], k.wou[...])
    a = k.a[...].astype(F32)
    b = a + y
    n2 = lax.rsqrt(jnp.sum(b * b, axis=-1, keepdims=True) * (1.0 / geo.d) + eps)
    gate = jax.nn.sigmoid(jnp.sum(a * k.gn[2 + r:3 + r], axis=-1, keepdims=True))
    k.b[...] = b.astype(BF)
    k.w[...] = (b * n2 * k.gn[1:2]).astype(BF)
    lane = lanes((geo.rows(r), 128))
    k.sx[...] = jnp.where(lane == 0, n2, jnp.where(lane == 1, gate, 0.0))
    k.acc[...] = y

    def wide(t, slot):
        c0 = t * FT if isinstance(t, int) else pl.multiple_of(t * FT, FT)
        return [pltpu.make_async_copy(k.keep.at[slot, j], ref.at[:, pl.ds(c0, FT)], k.ksem.at[slot, j])
                for j, ref in enumerate((k.gp, k.up))]

    def step(t, slot):
        @pl.when(t >= 2)
        def _():
            for c in wide(t - 2, slot):
                c.wait()
        gp = dot(k.w[...], k.gbuf[slot])
        up = dot(k.w[...], k.ubuf[slot])
        k.keep[slot, 0] = gp.astype(BF)
        k.keep[slot, 1] = up.astype(BF)
        z = (gp * jax.nn.sigmoid(gp) * up).astype(BF)
        k.acc[...] += dot(z, k.dbuf[slot])
        for c in wide(t, slot):
            c.start()
    tiles.loop(step)
    for t in range(max(tiles.n - 2, 0), tiles.n):
        for c in wide(t, t % 2):
            c.wait()
    yf = k.acc[...]
    k.yf[...] = yf.astype(BF)
    delta = yf * k.sx[:, 1:2]
    for m in range(geo.ns):
        if r == 0:
            here = rowid((bl, 1)) + blk * bl < k.lens[m]
            rows = slice(m * bl, m * bl + bl)
            k.h2[rows] = k.a[rows].astype(F32) + jnp.where(here, delta[rows], 0.0)
        else:
            k.h2[m * bl:m * bl + bl] = k.h[m * bl:m * bl + bl] + put_back(k.choice[m], delta[m * s:m * s + s])


def back_feed(geo, r, k, blk, tiles):
    s, bl, rows = geo.slots[r], geo.bl, geo.rows(r)
    k.small[2 + r:3 + r] = jnp.zeros((1, geo.dp), F32)
    k.small[1:2] = jnp.zeros((1, geo.dp), F32)

    def incoming(m):
        here = slice(m * s, m * s + s)
        if r == 0:
            return jnp.where(rowid((bl, 1)) + blk * bl < k.lens[m], k.dh[here], 0.0)
        return k.inc[here]
    for m in range(geo.ns):
        here = slice(m * s, m * s + s)
        if r > 0:
            k.inc[here] = pick(k.choice[m], k.dh[m * bl:m * bl + bl])
        inc = incoming(m)
        gate = k.sx[here, 1:2]
        dg = jnp.sum(inc * k.yf[here].astype(F32), axis=-1, keepdims=True)
        dl = dg * gate * (1.0 - gate)
        k.tok[here] = inc + dl * k.gn[2 + r:3 + r]
        k.small[2 + r:3 + r] += jnp.sum(k.a[here].astype(F32) * dl, axis=0, keepdims=True)
        k.df[here] = (gate * inc).astype(BF)
    k.acc[...] = jnp.zeros(k.acc.shape, F32)

    def wide(t, slot):
        c0 = t * FT if isinstance(t, int) else pl.multiple_of(t * FT, FT)
        return [pltpu.make_async_copy(k.wide.at[slot, j], ref.at[:, pl.ds(c0, FT)], k.wsem.at[slot, j])
                for j, ref in enumerate((k.dgp, k.dup, k.z))]

    def step(t, slot):
        @pl.when(t >= 2)
        def _():
            for c in wide(t - 2, slot):
                c.wait()
        dz = dot_nt(k.df[...], k.dbuf[slot])
        gp = k.pre[slot, 0].astype(F32)
        up = k.pre[slot, 1].astype(F32)
        sig = jax.nn.sigmoid(gp)
        silu = gp * sig
        k.wide[slot, 2] = (silu * up).astype(BF)
        dup = (dz * silu).astype(BF)
        dgp = (dz * up * (sig * (1.0 + gp * (1.0 - sig)))).astype(BF)
        k.wide[slot, 1] = dup
        k.wide[slot, 0] = dgp
        k.acc[...] += dot_nt(dgp, k.gbuf[slot]) + dot_nt(dup, k.ubuf[slot])
        for c in wide(t, slot):
            c.start()
    tiles.loop(step)
    for t in range(max(tiles.n - 2, 0), tiles.n):
        for c in wide(t, t % 2):
            c.wait()
    for m in range(geo.ns):
        here = slice(m * s, m * s + s)
        n2, gate = k.sx[here, 0:1], k.sx[here, 1:2]
        dw = k.acc[here]
        b = k.b[here].astype(F32)
        k.small[1:2] += jnp.sum(dw * (b * n2), axis=0, keepdims=True)
        t = dw * k.gn[1:2]
        db = n2 * t - n2 * n2 * n2 * b * (jnp.sum(t * b, axis=-1, keepdims=True) * (1.0 / geo.d))
        k.tok[here] += db
        k.dy[here] = (gate * incoming(m) + db).astype(BF)


def back_out(geo, r, k):
    s, kn = geo.slots[r], geo.keys(r)
    rows = geo.rows(r)
    left = lanes((rows, 128)) < 64
    lane = lanes((rows, 128))
    dcol = jnp.zeros((rows, 128), F32)
    for t in range(8):
        x = dot_nt(k.dy[...], k.wou[128 * t:128 * t + 128])
        x = x.astype(BF).astype(F32)
        prod = x * k.o[:, 128 * t:128 * t + 128].astype(F32)
        even = jnp.sum(jnp.where(left, prod, 0.0), axis=-1, keepdims=True)
        dcol = jnp.where(lane == 2 * t, even, dcol)
        k.do16[2 * t] = jnp.where(left, 0.0, pltpu.roll(x, 64, 1)).astype(BF)
        if 2 * t + 1 < HEADS:
            odd = jnp.sum(jnp.where(left, 0.0, prod), axis=-1, keepdims=True)
            dcol = jnp.where(lane == 2 * t + 1, odd, dcol)
            k.do16[2 * t + 1] = jnp.where(left, 0.0, x).astype(BF)
    k.dcol[...] = dcol


def back_attend(geo, r, k, blk, pause=None):
    s, kn = geo.slots[r], geo.keys(r)
    batch = GROUP if pause is None else 1

    def seq(m, _):
        row0 = m * s if isinstance(m, int) else pl.multiple_of(m * s, s)
        if pause is None:
            k.kvg[...] = k.kvall[:, m].reshape(kn, KV_HEADS * 128)
        else:
            loads = [pltpu.make_async_copy(k.kvall.at[b, m], k.kvg.at[pl.ds(b * s, s)], k.lsem.at[b]) for b in range(geo.n_blk)]
            for v in loads:
                v.start()
            for v in loads:
                v.wait()
        for g in range(KV_HEADS):
            k.kvt[g] = k.kvg[:, 128 * g:128 * g + 128].astype(F32).T.astype(BF)
        k.bias[...] = allowed(geo, r, k.routes[pl.ds(m, 1)] if r else None, blk, True, batch)
        dt = k.dcol[pl.ds(row0, s)].T
        for h in range(HEADS):
            k.dt[h // GROUP:h // GROUP + 1, h % GROUP * s:(h % GROUP + 1) * s] = dt[h:h + 1]
        k.ct[0] = k.cos[pl.ds(row0, s)].T[0:32] * 0.125
        k.ct[1] = k.sin[pl.ds(row0, s)].T[32:64] * 0.125

        def group(g, _):
            lane0 = pl.multiple_of(g * 128, 128)
            kvh = k.kvg[:, pl.ds(lane0, 128)]
            total = None
            for j0 in range(0, GROUP, batch):
                heads = (pl.ds(g * GROUP + j0, batch), pl.ds(row0, s))
                cols = slice(j0 * s, (j0 + batch) * s)
                qh, doh = k.q16[heads].reshape(batch * s, 128), k.do16[heads].reshape(batch * s, 128)
                p = jnp.exp(dot_nt(kvh, qh) + k.bias[...] - k.lse[m, pl.ds(g, 1), cols])
                ds = (p * (dot_nt(kvh, doh) - k.dt[pl.ds(g, 1), cols])).astype(BF)
                part = dot(ds, qh) + dot(p.astype(BF), doh)
                total = part if total is None else total + part
                dqt = dot(k.kvt[g], ds)
                c, sn = k.ct[0], k.ct[1]
                for j in range(batch):
                    y1, y2 = dqt[0:32, j * s:j * s + s], dqt[32:64, j * s:j * s + s]
                    k.dqt[g * GROUP + j0 + j, 0:32] = (y1 * c + y2 * sn)
                    k.dqt[g * GROUP + j0 + j, 32:64] = (y2 * c - y1 * sn)
            total = total.astype(BF).reshape(geo.n_blk, s, 128)
            if pause is None:
                k.dkv[:, m, :, pl.ds(lane0, 128)] = total
            else:
                k.dkvm[:, :, pl.ds(lane0, 128)] = total
            return 0
        if pause is None:
            lax.fori_loop(0, KV_HEADS, group, 0)
        else:
            lax.fori_loop(0, 3, group, 0)
            pause()
            lax.fori_loop(3, KV_HEADS, group, 0)
            store = pltpu.make_async_copy(k.dkvm, k.dkv.at[:, m], k.lsem.at[0])
            store.start()
        for t in range(8):
            if 2 * t + 1 < HEADS:
                x = k.dqt[2 * t:2 * t + 2].reshape(128, s).T
            else:
                x = jnp.concatenate([k.dqt[2 * t], jnp.zeros((64, s), F32)], axis=0).T
            k.da[pl.ds(row0, s), 128 * t:128 * t + 128] = x.astype(BF)
        if pause is not None:
            store.wait()
        return 0
    if pause is None:
        lax.fori_loop(0, geo.ns, seq, 0)
    else:
        for m in range(geo.ns):
            seq(m, 0)
            pause()


def back_project(geo, r, k, blk):
    s, bl, rows = geo.slots[r], geo.bl, geo.rows(r)
    cos, sin = k.cos[...], k.sin[...]
    left = lanes(cos.shape) < 64
    ckv, skv = jnp.where(left, cos, 1.0), jnp.where(left, sin, 0.0)
    k.da2[:, 0:1024] = k.da[...]
    for g in range(KV_HEADS):
        x = k.dkvown[:, 128 * g:128 * g + 128].astype(F32)
        k.da2[:, 1024 + 128 * g:1152 + 128 * g] = (x * ckv - swapped(x) * skv).astype(BF)
    for m in range(geo.ns):
        here = slice(m * bl, m * bl + bl)
        mine = slice(m * s, m * s + s)
        du = dot_nt(k.da2[mine], k.wa[...])
        a = k.a[mine].astype(F32)
        n1 = k.st[mine, 0:1]
        k.first[0:1] += jnp.sum(du * (a * n1), axis=0, keepdims=True)
        t1 = du * k.gn[0:1]
        tok = k.tok[mine] + n1 * t1 - n1 * n1 * n1 * a * (jnp.sum(t1 * a, axis=-1, keepdims=True) * (1.0 / geo.d))
        if r == 0:
            ok = rowid((bl, 1)) + blk * bl < k.lens[m]
            k.dh2[here] = jnp.where(ok, tok, k.dh[here])
        else:
            k.dh2[here] = k.dh[here] + put_back(k.choice[m], tok - k.inc[mine])


def block(geo, x, cot, lens, routes, slabs, share, give_back):
    blk_of = lambda: lax.axis_index("blk")
    bl, d, dp, ff, nsq, nb = geo.bl, geo.d, geo.dp, geo.ff, geo.ns, geo.n_blk
    full = nsq * bl
    cos_all, sin_all = geo.tables()
    b0 = lax.axis_index("blk") * bl
    cosb = lax.dynamic_slice_in_dim(cos_all, b0, bl, 0)
    sinb = lax.dynamic_slice_in_dim(sin_all, b0, bl, 0)
    spread = geo.spread()
    R, S, KN = [geo.rows(r) for r in range(3)], geo.slots, [geo.keys(r) for r in range(3)]
    V, dma = pltpu.VMEM, pltpu.SemaphoreType.DMA
    lens = Words(lens)

    def proj_outs(r, kv=True):
        more = dict(choice=Out((nsq, S[r], bl), BF)) if r else {}
        more = dict(kv=Out((R[r], 640), BF), **more) if kv else more
        return dict(a=Out((R[r], dp), F32 if r else BF), u=Out((R[r], dp), BF), q16=Out((HEADS, R[r], 128), BF), st=Out((R[r], 128)), cos=Out((R[r], 128)), sin=Out((R[r], 128)), **more)

    def seen_outs(r):
        return dict(o=Out((R[r], 1024), BF), lse=Out((nsq, 8, GROUP * S[r])))

    def fore_outs(r):
        return dict(**(seen_outs(r) if r else {}), b=Out((R[r], dp), BF), w=Out((R[r], dp), BF),
                    gp=Out((R[r], ff), BF, True), up=Out((R[r], ff), BF, True), yf=Out((R[r], dp), BF), sx=Out((R[r], 128)))

    def seen_scratch(r):
        return dict(kvg=V((KN[r], 640), BF), bias=V((GROUP * S[r], KN[r]), F32), col=V((GROUP * S[r], 128), F32),
                    o16=V((HEADS, S[r], 128), F32))

    def fore_scratch(r):
        return dict(acc=V((R[r], dp), F32), keep=V((2, 2, R[r], FT), BF), ksem=dma((2, 2)), **(seen_scratch(r) if r else {}))

    def feed_outs(r):
        more = dict(inc=Out((R[r], dp))) if r else {}
        return dict(tok=Out((R[r], dp)), df=Out((R[r], dp), BF), dgp=Out((R[r], ff), BF, True), dup=Out((R[r], ff), BF, True),
                    z=Out((R[r], ff), BF, True), dy=Out((R[r], dp), BF), small=Out((8, dp)), **more)

    def feed_scratch(r):
        return dict(acc=V((R[r], dp), F32), pre=V((2, 2, R[r], FT), BF), wide=V((2, 3, R[r], FT), BF), wsem=dma((2, 3)))

    def turned_outs(r):
        return dict(da=Out((R[r], 1024), BF), dkv=Out((nb, nsq, S[r], 640), BF))

    def out_parts(make, r=0):
        return dict(do16=make((HEADS, R[r], 128), BF), dcol=make((R[r], 128), F32))

    def turned_scratch(r, batch=GROUP):
        return dict(kvg=V((KN[r], 640), BF), kvt=V((KV_HEADS, 128, KN[r]), BF), bias=V((KN[r], batch * S[r]), F32), dt=V((8, GROUP * S[r]), F32), ct=V((2, 32, S[r]), F32),
                    dqt=V((HEADS, 64, S[r]), F32), **(out_parts(V, r) if r else {}))

    P, F, B, T, L = [None] * 3, [None] * 3, [None] * 3, [None] * 3, [None] * 3
    rt = [None] + list(routes)

    def begin(k):
        k.a[...] = dot(k.x[...], k.spread[0:d]).astype(BF)
        for m in range(nsq):
            k.cos[m * bl:m * bl + bl] = k.cosb[...]
            k.sin[m * bl:m * bl + bl] = k.sinb[...]

    ins = dict(x=x, spread=spread, cosb=cosb, sinb=sinb)
    afters = seen_outs(0)
    if (geo.n_dp, geo.n_blk) != (G, 4):
        wa, wo, gu, wd = (lax.all_gather(w, "dp", axis=0, tiled=True) for w in slabs)

        def k_first(k):
            k = join(k, k.p)
            begin(k)
            k.gn = gains(k.wa)
            project(geo, 0, k)
        P[0] = join(call("first_project", k_first, dict(wa=wa, **ins), dict(p=proj_outs(0))).p)
        P[0].kvall = share(P[0].kv.reshape(nsq, S[0], 640))
        F[0] = call("attend", lambda k: attend(geo, 0, k, blk_of()), dict(q16=P[0].q16, kvall=P[0].kvall), afters, seen_scratch(0))
    else:
        def k_head(k):
            dp_, blk, y, c, ym, cm = mates()
            z, x_ = dp_ // NX, lax.rem(dp_, NX)
            k = join(k, k.p, k.f, k.fs)
            ticks = gather_ticks(AG_CHUNKS, k.shards, k.slabs, k.sems)
            meet((dp_ + 1 - 2 * x_, blk), ym, cm, z=z)

            def tick(n=1):
                for _ in range(min(n, len(ticks))):
                    ticks.pop(0)()
            tick(2)
            begin(k)
            tick(A_TICKS - 2)
            load = pltpu.make_async_copy(k.slabs[0], k.wa, k.wsem)
            load.start()
            load.wait()
            k.gn = gains(k.wa)
            project_kv(geo, 0, k)
            sharing = Share(k.own, k.kvall, k.ssem, k.rsem)
            k.own[...] = k.kv[...].reshape(nsq, S[0], 640)
            k.kvall[blk] = k.own[...]
            sharing.start()
            tick()
            project_q(geo, 0, k)
            tick()
            sharing.forward()
            tick()
            sharing.arrive()
            attend(geo, 0, k, blk, tick)
            tick(len(ticks))
            sharing.sent()
        got = call("head", k_head, dict(shards=list(slabs), **ins),
                   dict(slabs=[Out((v.shape[0] * geo.n_dp, v.shape[1]), BF, True) for v in slabs], p=proj_outs(0, False), f=afters,
                        kvall=Out((nb, nsq, S[0], 640), BF)),
                   dict(fs=seen_scratch(0), wa=V((dp, COLS_A), BF), kv=V((R[0], 640), BF), own=V((nsq, S[0], 640), BF),
                        wsem=dma, ssem=dma((3,)), rsem=dma((3,)), sems=gather_sems(4, len(AG_CHUNKS))),
                   collective_id=1, has_side_effects=True)
        wa, wo, gu, wd = got.slabs
        P[0], F[0] = join(got.p, kvall=got.kvall), join(got.f)
    gu, wd = Far(gu), Far(wd)
    wou = h = None

    def k_fore(r, k):
        blk = blk_of()
        k = join(k, k.s, k.tl)
        tiles = Tiles(geo, k)
        tiles.start(0, 0)
        k.gn = gains(k.wa)
        if r == 0:
            k.wou[...] = dot(k.spread[...], k.wo[...]).astype(BF)
        v = join(k, k.p, k.f, k.fs)
        if r:
            attend(geo, r, v, blk)
        feed(geo, r, v, blk, tiles)
        n = join(k, k.n, h=k.h2, routes=k.routes2)
        select_rows(geo, r + 1, n, blk)
        project(geo, r + 1, n)

    for r in range(2):
        p = dict(a=P[r].a, q16=P[r].q16, kvall=P[r].kvall) if r else dict(a=P[0].a, o=F[0].o)
        more = dict(choice=P[r].choice, h=h, routes=rt[r], wou=wou) if r else dict(wo=wo, spread=spread, lens=lens)
        got = call("forward", functools.partial(k_fore, r),
                   dict(wa=wa, gu=gu, wd=wd, p=p, cosb=cosb, sinb=sinb, routes2=rt[r + 1], s=more),
                   dict(f=fore_outs(r), n=proj_outs(r + 1), h2=Out((full, dp)), **({} if r else dict(wou=Out((1024, dp), BF)))),
                   dict(fs=fore_scratch(r), tl=Tiles.scratch(geo)))
        h, F[r], P[r + 1] = got.h2, join(F[r] or {}, got.f), join(got.n)
        wou = wou if r else got.wou
        P[r + 1].kvall = share(P[r + 1].kv.reshape(nsq, S[r + 1], 640))

    def k_turn(k):
        blk = blk_of()
        k = join(k, k.tl)
        tiles = Tiles(geo, k)
        tiles.start(0, 0)
        k.gn = gains(k.wa)
        v = join(k, k.p, k.f, k.fs, h2=k.h3)
        attend(geo, 2, v, blk)
        feed(geo, 2, v, blk, tiles)
        tiles = Tiles(geo, join(k, k.bs), (v.gp, v.up))
        tiles.start(0, 0)
        k.out[...] = dot_nt(k.h3[...].astype(BF), k.spread[0:d]).astype(BF)
        k.dh[...] = dot(k.cot[...], k.spread[0:d])
        v = join(v, k.bs, k.ts, k.b, k.t)
        back_feed(geo, 2, v, blk, tiles)
        back_out(geo, 2, v)
        back_attend(geo, 2, v, blk)

    p = P[2]
    got = call("turn", k_turn,
               dict(wa=wa, gu=gu, wd=wd, wou=wou, h=h, spread=spread, cot=cot, routes=rt[2],
                    p=dict(a=p.a, q16=p.q16, kvall=p.kvall, choice=p.choice, cos=p.cos, sin=p.sin)),
               dict(f=fore_outs(2), b=feed_outs(2), t=turned_outs(2), out=Out((full, d), BF), dh=Out((full, dp))),
               dict(fs=fore_scratch(2), bs=feed_scratch(2), ts=turned_scratch(2), tl=Tiles.scratch(geo), h3=V((full, dp), F32)))
    F[2], B[2], T[2], out, dh = join(got.f), join(got.b), join(got.t), got.out, got.dh

    def k_back(r, k):
        blk = blk_of()
        v = join(k, k.p, k.f, k.b, k.bs, k.tl)
        tiles = Tiles(geo, v, (v.gp, v.up))
        tiles.start(0, 0)
        v.gn = k.gn = gains(k.wa)
        k.first[...] = jnp.zeros(k.first.shape, F32)
        back_project(geo, r + 1, join(k, k.n), blk)
        v.dh = k.dh2
        back_feed(geo, r, v, blk, tiles)
        if r > 0:
            v = join(v, k.t, k.ts)
        back_out(geo, r, v)
        if r > 0:
            back_attend(geo, r, v, blk)

    for r in (1, 0):
        n, q, p, f = r + 1, P[r + 1], P[r], F[r]
        mine = give_back(T[n].dkv).reshape(R[n], 640)
        late = dict(q16=p.q16, kvall=p.kvall, cos=p.cos, sin=p.sin, choice=p.choice) if r else {}
        more = dict(lse=f.lse) if r else {}
        rest = dict(wou=wou, routes=rt[r]) if r else dict(wou=wou, lens=lens)
        got = call("backward", functools.partial(k_back, r),
                   dict(wa=wa, gu=gu, wd=wd, dh=dh, **rest,
                        n=dict(dkvown=mine, da=T[n].da, tok=B[n].tok, inc=B[n].inc, choice=q.choice, st=q.st, a=q.a,
                               cos=q.cos, sin=q.sin),
                        p=dict(a=p.a, **late),
                        f=dict(o=f.o, b=f.b, gp=Far(f.gp), up=Far(f.up), yf=f.yf, sx=f.sx, **more)),
                   dict(b=feed_outs(r), da2=Out((R[n], COLS_A), BF), first=Out((8, dp)), dh2=Out((full, dp)),
                        **(dict(t=turned_outs(r)) if r else out_parts(Out))),
                   dict(bs=feed_scratch(r), tl=Tiles.scratch(geo), **(dict(ts=turned_scratch(r)) if r else {})))
        dh, B[r], L[n] = got.dh2, join(got.b), join(da2=got.da2, first=got.first)
        if r:
            T[r] = join(got.t)
    p, f = P[0], F[0]
    saved = [join(P[r], F[r], B[r], L[r] or {}) for r in range(3)]
    if (geo.n_dp, geo.n_blk) == (G, 4):
        gu_d = products(geo, saved, GU), products(geo, saved, DOWN)
        grad, shards = tail(geo, join(p, f, B[0], got, wa=wa, dh=dh, lens=lens.value, spread=spread), saved, gu_d,
                            turned_scratch(0, 1))
        return out, grad, shards
    T[0] = call("backward_attend", lambda k: back_attend(geo, 0, k, blk_of()),
                dict(do16=got.do16, dcol=got.dcol, q16=p.q16, kvall=p.kvall, lse=f.lse, cos=p.cos, sin=p.sin),
                turned_outs(0), turned_scratch(0))
    mine = give_back(T[0].dkv).reshape(R[0], 640)

    def k_last(k):
        blk = blk_of()
        k.gn = gains(k.wa)
        k.first[...] = jnp.zeros(k.first.shape, F32)
        back_project(geo, 0, k, blk)
        high, low = halves(k.dh2[...])
        k.grad[...] = dot_nt(high, k.spread[0:d]) + dot_nt(low, k.spread[0:d])
    L[0] = call("last_project", k_last,
                dict(wa=wa, dkvown=mine, da=T[0].da, tok=B[0].tok, dh=dh, lens=lens, st=p.st, a=p.a, cos=p.cos, sin=p.sin,
                     spread=spread),
                dict(da2=Out((R[0], COLS_A), BF), first=Out((8, dp)), grad=Out((full, d))), dict(dh2=V((full, dp), F32)))
    saved[0] = join(saved[0], L[0])
    slabs = [products(geo, saved, kind, spread) for kind in (QKV, OUT, GU, DOWN)]
    shards = [lax.psum(lax.psum_scatter(v, "dp", scatter_dimension=0, tiled=True), "blk") for v in slabs]
    return out, L[0].grad, shards


QKV, OUT, GU, DOWN = range(4)


def product_parts(geo, saved, kind, spread=None):
    dp, ff = geo.dp, geo.ff
    if kind == QKV:
        ins = dict(lefts=[v.u for v in saved], rights=[[v.da2 for v in saved]], small=[v.small for v in saved],
                   first=[v.first for v in saved])
        return ins, (dp, COLS_A), 512
    if kind == OUT:
        return dict(lefts=[v.o for v in saved], rights=[[v.dy for v in saved]], spread=spread), (dp, dp), 512
    if kind == GU:
        return dict(lefts=[v.w for v in saved], rights=[[v.dgp for v in saved], [v.dup for v in saved]]), (dp, 2 * ff), 512
    return dict(lefts=[v.z for v in saved], rights=[[v.df for v in saved]]), (ff, dp), 256


def product_body(geo, kind, shape, tile, k):
    R = [geo.rows(r) for r in range(3)]
    rows, dp = shape[0], geo.dp
    at = 0
    for i in range(3):
        for c in range(0, rows, 256):
            v = dot(k.lefts[i][...], k.spread[:, c:c + 256]).astype(BF) if kind == OUT else k.lefts[i][:, c:c + 256]
            k.left[c:c + 256, at:at + R[i]] = v.T
        at += R[i]
    c0 = 0
    for refs in k.rights:
        n = refs[0].shape[1]
        for t in range(0, n, tile):
            w = min(tile, n - t)
            right = jnp.concatenate([v[:, t:t + w] for v in refs], axis=0)
            k.res[:, c0 + t:c0 + t + w] = dot(k.left[...], right).astype(BF)
        c0 += n
    if kind == QKV:
        small = k.small[0][...] + k.small[1][...] + k.small[2][...]
        f = k.first[0][...] + k.first[1][...] + k.first[2][...]
        small = jnp.where(rowid(small.shape) == 0, f, small)
        cols = jnp.concatenate([small, jnp.zeros((120, dp), F32)], axis=0).T
        cols = pltpu.roll(cols, 64, 1)
        k.res[:, 896:1024] = jnp.where(lanes(cols.shape) < 64, k.res[:, 896:1024].astype(F32), cols).astype(BF)


def products(geo, saved, kind, spread=None):
    ins, shape, tile = product_parts(geo, saved, kind, spread)
    total = sum(geo.rows(r) for r in range(3))
    return call("weight_grads", functools.partial(product_body, geo, kind, shape, tile), ins, dict(res=Out(shape, BF)),
                dict(left=pltpu.VMEM((shape[0], total), BF))).res


def phase(body, ins, outs, scratch=None):
    leaf = lambda v: not isinstance(v, (dict, list, tuple))
    fi, ti = jax.tree.flatten(ins, is_leaf=leaf)
    fo, to = jax.tree.flatten(outs, is_leaf=leaf)

    def run(vi, vo, sc, sems):
        loads = [pltpu.make_async_copy(far, near, sems.at[i]) for i, (far, near) in enumerate(zip(fi, vi))]
        for v in loads:
            v.start()
        for v in loads:
            v.wait()
        body(join(ti.unflatten(vi), to.unflatten(vo), sc))
        stores = [pltpu.make_async_copy(near, far, sems.at[i]) for i, (far, near) in enumerate(zip(fo, vo))]
        for v in stores:
            v.start()
        for v in stores:
            v.wait()
    near = lambda refs: [pltpu.VMEM(v.shape, v.dtype) for v in refs]
    pl.run_scoped(run, near(fi), near(fo), scratch or {}, pltpu.SemaphoreType.DMA((max(len(fi), len(fo)),)))


def tail(geo, v, saved, gu_d, turned):
    dp, d, bl, nsq, s = geo.dp, geo.d, geo.bl, geo.ns, geo.slots[0]
    full = nsq * bl
    V, dma = pltpu.VMEM, pltpu.SemaphoreType.DMA
    total = sum(geo.rows(r) for r in range(3))
    one = Geo(1, bl, geo.n_dp, geo.n_blk, d, geo.ff, geo.tops)
    part = (nsq, s, 640)

    def body(k):
        dp_, blk, y, c, ym, cm = mates()
        z, x_ = dp_ // NX, lax.rem(dp_, NX)
        meet((dp_ + 1 - 2 * x_, blk), ym, cm, z=z)
        slabs = [k.ga, k.go, k.gu, k.gd]
        ticks = reduce_ticks(RS_CHUNKS, [slab_view(geo, i, w) for i, w in enumerate(slabs)], k.shards, k.bufs, k.sems)
        ready = RS_CHUNKS_READY

        def tick(n=1):
            nonlocal ready
            for _ in range(n):
                if ready > 0:
                    ready -= 1
                    ticks.pop(0)()
        tick(2)
        a = k.at
        phase(lambda q: back_attend(geo, 0, join(q, kvall=k.kvall, dkv=k.dkv), blk, tick),
              dict(do16=a.do16, dcol=a.dcol, q16=a.q16, lse=a.lse, cos=a.cos, sin=a.sin), dict(da=k.da),
              dict(dkvm=V((geo.n_blk, s, 640), BF), lsem=dma((geo.n_blk,)), **turned))

        def rem(src, dst, i, to):
            return pltpu.make_async_remote_copy(src_ref=src, dst_ref=dst, send_sem=k.gs.at[i], recv_sem=k.gr.at[i],
                                                device_id=to, device_id_type=MESH)
        first = [rem(k.dkv.at[2 * yy + 1 - c], k.got1.at[yy], yy, cm) for yy in range(2)]
        for f in first:
            f.start()
        tick()
        for f in first:
            f.wait_recv()

        def add(q):
            for yy, mine in enumerate((q.p0, q.p1)):
                k.got1[yy] = (k.got1[yy].astype(F32) + mine[...].astype(F32)).astype(BF)
        phase(add, dict(p0=k.dkv.at[c], p1=k.dkv.at[2 + c]), {})
        second = rem(k.got1.at[1 - y], k.got2, 2, ym)
        second.start()
        tick()
        second.wait_recv()
        tick()
        k.first[...] = jnp.zeros(k.first.shape, F32)
        for m in range(nsq):
            rows = pl.ds(m * bl, bl)

            def last(q):
                q.gn = gains(q.wa)
                q.dkvown[...] = k.got1[y, m].astype(F32) + k.got2[m].astype(F32)
                back_project(one, 0, join(q, lens=[k.lens[m]], first=k.first), blk)
                high, low = halves(q.dh2[...])
                q.grad[...] = dot_nt(high, q.spread[0:d]) + dot_nt(low, q.spread[0:d])
            phase(last, dict(wa=k.wa, da=k.da.at[rows], tok=a.tok.at[rows], dh=a.dh.at[rows], st=a.st.at[rows], a=a.a.at[rows],
                             cos=a.cos.at[rows], sin=a.sin.at[rows], spread=k.spread),
                  dict(da2=k.da2.at[rows], grad=k.grad.at[rows]),
                  dict(dkvown=V((bl, 640), F32), dh2=V((bl, dp), F32)))
            tick()
        for kind, res in ((QKV, k.ga), (OUT, k.go)):
            ins, shape, tile = product_parts(geo, [types.SimpleNamespace(**q) for q in k.saved], kind, k.spread)
            if kind == QKV:
                ins[FIRST] = ins[FIRST][1:]
                ins[RIGHTS] = [[k.da2] + ins[RIGHTS][0][1:]]

            def make(q, kind=kind, shape=shape, tile=tile):
                if kind == QKV:
                    q.first = [k.first] + q.first
                product_body(geo, kind, shape, tile, q)
            phase(make, ins, dict(res=res), dict(left=V((shape[0], total), BF)))
            tick()
        for t in ticks:
            t()
        for f in first + [second]:
            f.wait_send()

    FIRST, RIGHTS = tuple(dict(first=0, rights=0))
    keep = [dict(u=Far(q.u), o=Far(q.o), dy=Far(q.dy), small=Far(q.small),
                 **(dict(da2=Far(q.da2), first=Far(q.first)) if i else dict(da2=Far(q.u), first=Far(q.small))))
            for i, q in enumerate(saved)]
    bufs, sems = reduce_scratch(geo, RS_CHUNKS)
    got = call("tail", lambda k: body(join(k, at=join(k.at))),
               dict(at=dict(do16=Far(v.do16), dcol=Far(v.dcol), q16=Far(v.q16), lse=Far(v.lse), cos=Far(v.cos), sin=Far(v.sin),
                            tok=Far(v.tok), dh=Far(v.dh), st=Far(v.st), a=Far(v.a)),
                    kvall=Far(v.kvall), lens=Words(v.lens), wa=Far(v.wa), spread=Far(v.spread), gu=Far(gu_d[0]), gd=Far(gu_d[1]),
                    saved=keep),
               dict(shards=reduce_outs(geo), grad=Out((full, d), F32, True), ga=Out((dp, COLS_A), BF, True),
                    go=Out((dp, dp), BF, True), da=Out((full, 1024), BF, True), da2=Out((full, COLS_A), BF, True),
                    dkv=Out((geo.n_blk,) + part, BF, True)),
               dict(bufs=bufs, sems=sems, got1=V((2,) + part, BF), got2=V(part, BF), first=V((8, dp), F32),
                    gs=dma((3,)), gr=dma((3,))),
               collective_id=2, has_side_effects=True)
    return got.grad, got.shards


MESH = pl.DeviceIdType.MESH

NZ, NX = 4, 2
AHEAD = 2
OFFSETS = (0, 2, 4, 6, 8, 10, 12, 13, 14)
G = NZ * NX


def meet(*others, z=None):
    dp, blk = lax.axis_index("dp"), lax.axis_index("blk")
    bar = pltpu.get_barrier_semaphore()
    for t in others:
        pl.semaphore_signal(bar, inc=1, device_id=t, device_id_type=MESH)
    count = len(others)
    if z is not None:
        @pl.when(z > 0)
        def _():
            pl.semaphore_signal(bar, inc=1, device_id=(dp - NX, blk), device_id_type=MESH)

        @pl.when(z < NZ - 1)
        def _():
            pl.semaphore_signal(bar, inc=1, device_id=(dp + NX, blk), device_id_type=MESH)
        count = count + jnp.where(z > 0, 1, 0) + jnp.where(z < NZ - 1, 1, 0)
    pl.semaphore_wait(bar, count)


def gather_ticks(chunks, ins, outs, sems):
    ls, zs, zr, xs, xr, ys, yr, cs, cr = sems
    nslab = len(ins)
    dp, blk = lax.axis_index("dp"), lax.axis_index("blk")
    z, x = dp // NX, lax.rem(dp, NX)
    y, c = blk // 2, lax.rem(blk, 2)
    left, right = (dp - NX, blk), (dp + NX, blk)
    xm, ym, cm = (dp + 1 - 2 * x, blk), (dp, lax.rem(blk + 2, 4)), (dp, blk + 1 - 2 * c)

    locs = [pltpu.make_async_copy(ins[s], outs[s].at[pl.ds(pl.multiple_of(dp * ins[s].shape[0], 16), ins[s].shape[0])], ls.at[s])
            for s in range(nslab)]

    def piece(i, g, q):
        s, c0, n, split = chunks[i]
        rows = ins[s].shape[0]
        h = rows // split
        return outs[s].at[pl.ds(pl.multiple_of(g * rows + q * h, 16), h), pl.ds(c0, n)]

    def myq(i):
        return blk if chunks[i][3] == 4 else c

    def rem(src, dst, a, b, to):
        return pltpu.make_async_remote_copy(src_ref=src, dst_ref=dst, send_sem=a, recv_sem=b, device_id=to, device_id_type=MESH)

    def own(i):
        s, c0, n, split = chunks[i]
        h = ins[s].shape[0] // split
        return ins[s].at[pl.ds(pl.multiple_of(myq(i) * h, 16), h), pl.ds(c0, n)]

    def zcopy(i, d, s, src_own):
        zz = z - s if d == 0 else z + s
        p = piece(i, zz * NX + x, myq(i))
        return rem(own(i) if src_own else p, p, zs.at[i, d, s], zr.at[i, d, s], right if d == 0 else left)

    def zrecv(i, d, s):
        zz = z - 1 - s if d == 0 else z + 1 + s
        p = piece(i, zz * NX + x, myq(i))
        return rem(p, p, zs.at[i, d, s], zr.at[i, d, s], right if d == 0 else left)

    def xcopy(i, zz, src_own=False):
        p = piece(i, zz * NX + x, myq(i))
        return rem(own(i) if src_own else p, p, xs.at[i, zz], xr.at[i, zz], xm)

    def xrecv(i, zz):
        p = piece(i, zz * NX + 1 - x, myq(i))
        return rem(p, p, xs.at[i, zz], xr.at[i, zz], xm)

    def ycopy(i, g):
        p = piece(i, g, blk)
        return rem(p, p, ys.at[i, g], yr.at[i, g], ym)

    def yrecv(i, g):
        p = piece(i, g, lax.rem(blk + 2, 4))
        return rem(p, p, ys.at[i, g], yr.at[i, g], ym)

    def ccopy(i, k, g):
        q = myq(i) if k == 0 else lax.rem(blk + 2, 4)
        p = piece(i, g, q)
        return rem(p, p, cs.at[i, k, g], cr.at[i, k, g], cm)

    def crecv(i, k, g):
        if chunks[i][3] == 4:
            mate = blk + 1 - 2 * c
            q = mate if k == 0 else lax.rem(mate + 2, 4)
        else:
            q = 1 - c
        p = piece(i, g, q)
        return rem(p, p, cs.at[i, k, g], cr.at[i, k, g], cm)

    def spread(i, g):
        if chunks[i][3] == 4:
            ycopy(i, g).start()
        ccopy(i, 0, g).start()

    def begin(i):
        @pl.when(z < NZ - 1)
        def _():
            zcopy(i, 0, 0, True).start()

        @pl.when(z > 0)
        def _():
            zcopy(i, 1, 0, True).start()
        xcopy(i, z, True).start()

    def zstep(i, s):
        @pl.when(z - 1 - s >= 0)
        def _():
            zrecv(i, 0, s).wait_recv()
            if s < NZ - 2:
                @pl.when(z < NZ - 1)
                def _():
                    zcopy(i, 0, s + 1, False).start()
            xcopy(i, z - 1 - s).start()
            spread(i, (z - 1 - s) * NX + x)

        @pl.when(z + 1 + s < NZ)
        def _():
            zrecv(i, 1, s).wait_recv()
            if s < NZ - 2:
                @pl.when(z > 0)
                def _():
                    zcopy(i, 1, s + 1, False).start()
            xcopy(i, z + 1 + s).start()
            spread(i, (z + 1 + s) * NX + x)

    def xstep(i, k):
        def one(zz):
            xrecv(i, zz).wait_recv()
            spread(i, zz * NX + 1 - x)
        if k == 0:
            one(z)
        else:
            pl.when(z - k >= 0)(lambda: one(z - k))
            pl.when(z + k < NZ)(lambda: one(z + k))

    def ystep(i, k):
        g = lax.rem(dp + k, G)
        yrecv(i, g).wait_recv()
        ccopy(i, 1, g).start()

    def cstep(i, k):
        g = lax.rem(dp + k, G)
        crecv(i, 0, g).wait_recv()
        if chunks[i][3] == 4:
            crecv(i, 1, g).wait_recv()

    def sent(i):
        @pl.when(z < NZ - 1)
        def _():
            zcopy(i, 0, 0, True).wait_send()

        @pl.when(z > 0)
        def _():
            zcopy(i, 1, 0, True).wait_send()
        for s in range(NZ - 1):
            if s < NZ - 2:
                @pl.when((z - 1 - s >= 0) & (z < NZ - 1))
                def _():
                    zcopy(i, 0, s + 1, False).wait_send()

                @pl.when((z + 1 + s < NZ) & (z > 0))
                def _():
                    zcopy(i, 1, s + 1, False).wait_send()
        xcopy(i, z, True).wait_send()
        for k in range(1, NZ):
            xcopy(i, lax.rem(z + k, NZ)).wait_send()
        for k in range(1, G):
            g = lax.rem(dp + k, G)
            ccopy(i, 0, g).wait_send()
            if chunks[i][3] == 4:
                ycopy(i, g).wait_send()
                ccopy(i, 1, g).wait_send()

    nch = len(chunks)
    stages = [begin] + [functools.partial(lambda i, s: (zstep(i, s), xstep(i, s)), s=s) for s in range(NZ - 1)]
    stages.append(lambda i: xstep(i, NZ - 1))
    stages.append(lambda i: [ystep(i, k) for k in range(1, G)] if chunks[i][3] == 4 else None)
    stages.append(lambda i: [cstep(i, k) for k in range(1, G)])
    stages.append(sent)

    def first():
        for l in locs:
            l.start()

    def tick(t):
        if t == 6:
            locs[0].wait()
        if t == nch + len(stages) - 2:
            for l in locs[1:]:
                l.wait()
        for s in reversed(range(len(stages))):
            i = t - s
            if 0 <= i < nch:
                stages[s](i)
    return [first] + [functools.partial(tick, t) for t in range(nch + len(stages) - 1)]


def gather_sems(n, nch):
    dma = pltpu.SemaphoreType.DMA
    return [dma((n,)), dma((nch, 2, NZ - 1)), dma((nch, 2, NZ - 1)), dma((nch, NZ)), dma((nch, NZ)),
            dma((nch, G)), dma((nch, G)), dma((nch, 2, G)), dma((nch, 2, G))]


def add_into(dst, other, n):
    def body(k, _):
        dst[k] = (dst[k].astype(jnp.float32) + other(k).astype(jnp.float32)).astype(dst.dtype)
        return 0
    lax.fori_loop(0, n, body, 0)


def reduce_ticks(chunks, ins, outs, bufs, sems):
    nch = len(chunks)
    own, crv, yrv, xrv, zrv, fin, s4b = bufs
    ls, cs, cr, ys, yr, xs, xr, zs, zr, fs, fr = sems
    dp, blk = lax.axis_index("dp"), lax.axis_index("blk")
    z, x = dp // NX, lax.rem(dp, NX)
    y, c = blk // 2, lax.rem(blk, 2)
    left, right = (dp - NX, blk), (dp + NX, blk)
    xm, ym, cm = (dp + 1 - 2 * x, blk), (dp, lax.rem(blk + 2, 4)), (dp, blk + 1 - 2 * c)

    def rem(src, dst, a, b, to):
        return pltpu.make_async_remote_copy(src_ref=src, dst_ref=dst, send_sem=a, recv_sem=b, device_id=to, device_id_type=MESH)

    def four(i):
        return chunks[i][3] == 4

    def part(i, core):
        s, c0, n, split = chunks[i]
        cols = pl.ds(c0, n)
        return ins[s].at[:, :, :, core, :, cols] if split == 4 else ins[s].at[:, :, core, :, cols]

    def load(i):
        return pltpu.make_async_copy(part(i, c), own[i], ls.at[i])

    def core_send(i):
        return rem(part(i, 1 - c), crv[i], cs.at[i, 0], cr.at[i, 0], cm)

    def y_send(i):
        return rem(own[i].at[:, :, 1 - y], yrv[i], ys.at[i], yr.at[i], ym)

    def s2(i):
        return yrv[i] if four(i) else own[i]

    def x_send(i):
        return rem(s2(i).at[:, 1 - x], xrv[i], xs.at[i], xr.at[i], xm)

    def z_copy(i, d, lo, hi, first, to):
        src = xrv[i].at[pl.ds(lo, hi - lo)] if first else zrv[i].at[d, pl.ds(lo, hi - lo)]
        return rem(src, zrv[i].at[d, pl.ds(lo, hi - lo)], zs.at[i, d], zr.at[i, d], to)

    def right_send(i, k):
        return z_copy(i, 0, k + 1, NZ, k == 0, right)

    def left_send(i, k):
        return z_copy(i, 1, 0, k, k == NZ - 1, left)

    def st0(i):
        load(i).start()
        core_send(i).start()

    def st1(i):
        load(i).wait()
        core_send(i).wait_recv()

        def body(g, _):
            zz, xx = g // NX, lax.rem(g, NX)
            for yy in ((0, 1) if four(i) else (None,)):
                at = (zz, xx) if yy is None else (zz, xx, yy)
                own[i][at] = (own[i][at].astype(jnp.float32) + crv[i][at].astype(jnp.float32)).astype(jnp.bfloat16)
            return 0
        lax.fori_loop(0, G, body, 0)
        if four(i):
            y_send(i).start()

    def st2(i):
        if four(i):
            y_send(i).wait_recv()

            def body(g, _):
                zz, xx = g // NX, lax.rem(g, NX)
                yrv[i][zz, xx] = (yrv[i][zz, xx].astype(jnp.float32) + own[i][zz, xx, y].astype(jnp.float32)).astype(jnp.bfloat16)
                return 0
            lax.fori_loop(0, G, body, 0)
        x_send(i).start()

    def zstep(i, s):
        if s < NZ - 1:
            @pl.when(z == s)
            def _():
                if s > 0:
                    z_copy(i, 0, s, NZ, False, right).wait_recv()
                    for k in range(s + 1, NZ):
                        zrv[i][0, k] = (zrv[i][0, k].astype(jnp.float32) + xrv[i][k].astype(jnp.float32)).astype(jnp.bfloat16)
                right_send(i, s).start()

            @pl.when(z == NZ - 1 - s)
            def _():
                k0 = NZ - 1 - s
                if s > 0:
                    z_copy(i, 1, 0, k0 + 1, False, left).wait_recv()
                    for k in range(k0):
                        zrv[i][1, k] = (zrv[i][1, k].astype(jnp.float32) + xrv[i][k].astype(jnp.float32)).astype(jnp.bfloat16)
                left_send(i, k0).start()

    def st3(i):
        x_send(i).wait_recv()
        add_into(xrv[i], lambda k: s2(i)[k, x], NZ)
        zstep(i, 0)

    def finish(i):
        q = blk if four(i) else c
        dst = fin[i].at[q] if four(i) else s4b[i]

        def put(v):
            if four(i):
                fin[i][blk] = v.astype(jnp.bfloat16)
            else:
                s4b[i][...] = v.astype(jnp.bfloat16)

        @pl.when(z == 0)
        def _():
            z_copy(i, 1, 0, 1, False, left).wait_recv()
            put(xrv[i][0].astype(jnp.float32) + zrv[i][1, 0].astype(jnp.float32))

        @pl.when(z == NZ - 1)
        def _():
            z_copy(i, 0, NZ - 1, NZ, False, right).wait_recv()
            put(xrv[i][NZ - 1].astype(jnp.float32) + zrv[i][0, NZ - 1].astype(jnp.float32))

        @pl.when((z > 0) & (z < NZ - 1))
        def _():
            put(xrv[i][z].astype(jnp.float32) + zrv[i][0, z].astype(jnp.float32) + zrv[i][1, z].astype(jnp.float32))
        if four(i):
            fin_send(i, 0).start()
            fin_send(i, 1).start()
        else:
            fin_send(i, 0).start()

    def fin_send(i, k):
        if four(i):
            q = blk if k < 2 else lax.rem(blk + 2, 4)
            return rem(fin[i].at[q], fin[i].at[q], fs.at[i, k], fr.at[i, k], ym if k == 0 else cm)
        if k == 0:
            return rem(s4b[i], fin[i].at[2], fs.at[i, 0], fr.at[i, 0], ym)
        return rem(fin[i].at[c], fin[i].at[c], fs.at[i, 1], fr.at[i, 1], cm)

    def fin_recv(i, k):
        if four(i):
            mate = blk + 1 - 2 * c
            q = lax.rem(blk + 2, 4) if k == 0 else mate if k == 1 else lax.rem(mate + 2, 4)
            return rem(fin[i].at[q], fin[i].at[q], fs.at[i, k], fr.at[i, k], cm)
        if k == 0:
            return fin_send(i, 0)
        return rem(fin[i].at[1 - c], fin[i].at[1 - c], fs.at[i, 1], fr.at[i, 1], cm)

    def st8(i):
        fin_recv(i, 0).wait_recv()
        if four(i):
            fin_send(i, 2).start()
        else:
            fin[i][c] = (fin[i][2].astype(jnp.float32) + s4b[i][...].astype(jnp.float32)).astype(jnp.bfloat16)
            fin_send(i, 1).start()

    def st9(i):
        s, c0, n, split = chunks[i]
        for k in ((1, 2) if four(i) else (1,)):
            fin_recv(i, k).wait_recv()
        for q in range(split):
            outs[s][q, :, pl.ds(c0, n)] = fin[i][q]

    def sent(i):
        core_send(i).wait_send()
        if four(i):
            y_send(i).wait_send()
        x_send(i).wait_send()
        for k in range(NZ - 1):
            pl.when(z == k)(lambda k=k: right_send(i, k).wait_send())
            pl.when(z == k + 1)(lambda k=k: left_send(i, k + 1).wait_send())
        for k in range(3 if four(i) else 2):
            fin_send(i, k).wait_send()

    stages = [st1, st2, st3] + [functools.partial(lambda i, s: zstep(i, s), s=s) for s in range(1, NZ - 1)] + [finish, st8, st9, sent]
    def tick(t):
        if t < 0:
            for i in range(min(AHEAD, nch)):
                st0(i)
            return
        if t + AHEAD < nch:
            st0(t + AHEAD)
        for s in reversed(range(len(stages))):
            i = t - OFFSETS[s]
            if 0 <= i < nch:
                stages[s](i)
    return [functools.partial(tick, t) for t in range(-1, nch + max(OFFSETS))]


def slab_split(k):
    return next(ch[3] for ch in RS_CHUNKS if ch[0] == k)


def slab_rows(geo, k):
    return (geo.ff // geo.n_dp if k == 3 else geo.gp) // slab_split(k)


def slab_view(geo, k, ref):
    lead = (NZ, NX, 2, 2) if slab_split(k) == 4 else (NZ, NX, 2)
    return ref.reshape(*lead, slab_rows(geo, k), ref.shape[1])


def reduce_scratch(geo, chunks):
    nch = len(chunks)
    dma = pltpu.SemaphoreType.DMA

    def shapes(kind):
        out = []
        for s, c0, nc, split in chunks:
            h = slab_rows(geo, s)
            lead = (NZ, NX, 2) if split == 4 else (NZ, NX)
            tiny = (1, 16, 128)
            shape = (lead + (h, nc), lead + (h, nc), (NZ, NX, h, nc) if split == 4 else tiny, (NZ, h, nc), (2, NZ, h, nc),
                     (4 if split == 4 else 3, h, nc), (h, nc) if split == 2 else tiny)[kind]
            out.append(pltpu.VMEM(shape, jnp.bfloat16))
        return out
    sems = [dma((nch,)), dma((nch, 1)), dma((nch, 1)), dma((nch,)), dma((nch,)), dma((nch,)), dma((nch,)),
            dma((nch, 2)), dma((nch, 2)), dma((nch, 3)), dma((nch, 3))]
    return [shapes(k) for k in range(7)], sems


def reduce_outs(geo):
    cols = (COLS_A, geo.dp, 2 * geo.ff, geo.dp)
    return [Out((slab_split(k), slab_rows(geo, k), cols[k]), BF) for k in range(4)]


A_TICKS = 8
AG_CHUNKS = [(0, 0, 1664, 4), (1, 0, 1024, 2), (2, 0, 2560, 4), (2, 2560, 2560, 4), (3, 0, 1024, 2)]
RS_CHUNKS = [(2, 0, 640, 4), (3, 0, 256, 2), (2, 640, 640, 4), (2, 1280, 640, 4), (3, 256, 256, 2), (2, 1920, 640, 4),
             (2, 2560, 640, 4), (3, 512, 256, 2), (2, 3200, 640, 4), (2, 3840, 640, 4), (3, 768, 256, 2), (2, 4480, 640, 4),
             (0, 0, 896, 4), (1, 0, 512, 2), (0, 896, 768, 4), (1, 512, 512, 2)]
RS_CHUNKS_READY = 12 - AHEAD + 1


def pad_to(v, shape):
    return jnp.pad(v, [(0, b - a) for a, b in zip(v.shape, shape)])


def pad_cols(v, geo):
    v = v.reshape(v.shape[0], geo.n_dp, geo.gw)
    return jnp.pad(v, ((0, 0), (0, 0), (0, geo.gp - geo.gw))).reshape(v.shape[0], geo.dp)


def unpad_cols(v, geo):
    return v.reshape(v.shape[0], geo.n_dp, geo.gp)[:, :, :geo.gw].reshape(v.shape[0], geo.d)


def pack(geo, q, k, v, o, g, u, d, g1, g2, rt):
    rows = q.shape[0]
    kv = jnp.concatenate([k.reshape(rows, KV_HEADS, 64), v.reshape(rows, KV_HEADS, 64)], axis=2).reshape(rows, 640)
    small = pad_to(jnp.concatenate([g1[:, None], g2[:, None], rt], axis=1), (rows, 64))
    a = pad_to(jnp.concatenate([q, small, kv], axis=1), (geo.gp, COLS_A))
    gu = pad_to(jnp.concatenate([g, u], axis=1), (geo.gp, 2 * geo.ff))
    return a, pad_to(pad_cols(o, geo), (geo.gp, geo.dp)), gu, pad_cols(d, geo)


def unpack(geo, slabs):
    a, o, gu, d = (w.reshape(-1, w.shape[-1]) for w in slabs)
    a, o, gu = a[:geo.gw], o[:geo.gw], gu[:geo.gw]
    kv = a[:, 1024:].reshape(geo.gw, KV_HEADS, 128)
    return tuple(w.astype(F32) for w in (a[:, :960], kv[:, :, :64].reshape(geo.gw, 320), kv[:, :, 64:].reshape(geo.gw, 320), unpad_cols(o, geo),
            gu[:, :geo.ff], gu[:, geo.ff:], unpad_cols(d, geo), a[:, 960], a[:, 961], a[:, 962:965]))


def mates():
    dp, blk = lax.axis_index("dp"), lax.axis_index("blk")
    y, c = blk // 2, lax.rem(blk, 2)
    return dp, blk, y, c, (dp, lax.rem(blk + 2, 4)), (dp, blk + 1 - 2 * c)


class Share:
    def __init__(self, own, out, ssem, rsem):
        dp, blk, y, c, ym, cm = mates()

        def rem(src, b, k, to):
            return pltpu.make_async_remote_copy(src_ref=src, dst_ref=out.at[b], send_sem=ssem.at[k], recv_sem=rsem.at[k],
                                                device_id=to, device_id_type=MESH)
        far, near = lax.rem(blk + 2, 4), blk + 1 - 2 * c
        both = lax.rem(near + 2, 4)
        self.out = [rem(own, blk, 0, ym), rem(own, blk, 1, cm), rem(out.at[far], far, 2, cm)]
        self.come = [rem(out.at[far], far, 0, ym), rem(out.at[near], near, 1, cm), rem(out.at[both], both, 2, cm)]

    def start(self):
        self.out[0].start()
        self.out[1].start()

    def forward(self):
        self.come[0].wait_recv()
        self.out[2].start()

    def arrive(self):
        self.come[1].wait_recv()
        self.come[2].wait_recv()

    def sent(self):
        for v in self.out:
            v.wait_send()


def share_kernel(own, out, lsem, ssem, rsem):
    dp, blk, y, c, ym, cm = mates()
    meet(ym, cm)
    s = Share(own, out, ssem, rsem)
    s.start()
    local = pltpu.make_async_copy(own, out.at[blk], lsem)
    local.start()
    s.forward()
    s.arrive()
    s.sent()
    local.wait()


def share_rows(geo, ident, kv):
    if geo.n_blk != 4:
        return lax.all_gather(kv, "blk", axis=0, tiled=False)
    dma = pltpu.SemaphoreType.DMA
    return pl.pallas_call(
        share_kernel, out_shape=jax.ShapeDtypeStruct((4,) + kv.shape, kv.dtype),
        in_specs=[pl.BlockSpec(memory_space=pltpu.VMEM)], out_specs=pl.BlockSpec(memory_space=pl.ANY),
        scratch_shapes=[dma, dma((3,)), dma((3,))],
        compiler_params=pltpu.CompilerParams(collective_id=ident, has_side_effects=True), name="share_rows")(kv)


def give_kernel(dkv, out, got1, half, got2, ssem, rsem):
    dp, blk, y, c, ym, cm = mates()
    meet(ym, cm)

    def rem(src, dst, k, to):
        return pltpu.make_async_remote_copy(src_ref=src, dst_ref=dst, send_sem=ssem.at[k], recv_sem=rsem.at[k],
                                            device_id=to, device_id_type=MESH)
    first = [rem(dkv.at[yy, 1 - c], got1.at[yy], yy, cm) for yy in range(2)]
    for f in first:
        f.start()
    for f in first:
        f.wait_recv()
    half[...] = (got1[1 - y].astype(F32) + dkv[1 - y, c].astype(F32)).astype(BF)
    second = rem(half, got2, 2, ym)
    second.start()
    mine = got1[y].astype(F32) + dkv[y, c].astype(F32)
    second.wait_recv()
    out[...] = mine + got2[...].astype(F32)
    for f in first + [second]:
        f.wait_send()


def give_rows(geo, ident, dkv):
    if geo.n_blk != 4:
        return lax.psum_scatter(dkv, "blk", scatter_dimension=0, tiled=False).astype(F32)
    dma = pltpu.SemaphoreType.DMA
    piece = dkv.shape[1:]
    vm = pl.BlockSpec(memory_space=pltpu.VMEM)
    return pl.pallas_call(
        give_kernel, out_shape=jax.ShapeDtypeStruct(piece, F32), in_specs=[vm], out_specs=vm,
        scratch_shapes=[pltpu.VMEM((2,) + piece, BF), pltpu.VMEM(piece, BF), pltpu.VMEM(piece, BF), dma((3,)), dma((3,))],
        compiler_params=pltpu.CompilerParams(collective_id=ident, has_side_effects=True, vmem_limit_bytes=40 << 20),
        name="give_rows")(dkv.reshape((2, 2) + piece))


def per_device(block_input, cotangent, seq_lengths, routes_two, routes_three, query_weight, key_weight, value_weight, output_weight,
               gate_weight, up_weight, down_weight, first_gain, second_gain, router_weight):
    micro, seqs, bl, d = block_input.shape
    n_dp, n_blk = lax.axis_size("dp"), lax.axis_size("blk")
    count = micro * seqs
    geo = Geo(count, bl, n_dp, n_blk, d, gate_weight.shape[1], (None, routes_two.shape[2], routes_three.shape[2]))
    slabs = pack(geo, query_weight, key_weight, value_weight, output_weight, gate_weight, up_weight, down_weight, first_gain,
                 second_gain, router_weight)
    ids = iter(range(10, 30))
    out, grad, shards = block(geo, block_input.reshape(count * bl, d), cotangent.reshape(count * bl, d), seq_lengths.reshape(count),
                (routes_two.reshape(count, -1), routes_three.reshape(count, -1)), slabs,
                lambda kv: share_rows(geo, next(ids), kv), lambda dkv: give_rows(geo, next(ids), dkv))
    return (out.reshape(block_input.shape), grad.reshape(block_input.shape)) + unpack(geo, shards)


def solution(mesh):
    in_specs = (
        P(None, "dp", "blk", None),
        P(None, "dp", "blk", None),
        P(None, "dp"),
        P(None, "dp", None),
        P(None, "dp", None),
        P("dp", None),
        P("dp", None),
        P("dp", None),
        P("dp", None),
        P("dp", None),
        P("dp", None),
        P("dp", None),
        P("dp"),
        P("dp"),
        P("dp", None),
    )
    out_specs = (
        P(None, "dp", "blk", None),
        P(None, "dp", "blk", None),
        P("dp", None),
        P("dp", None),
        P("dp", None),
        P("dp", None),
        P("dp", None),
        P("dp", None),
        P("dp", None),
        P("dp"),
        P("dp"),
        P("dp", None),
    )
    return jax.shard_map(
        per_device, mesh=mesh, in_specs=in_specs, out_specs=out_specs, check_vma=False
    )
```

```python
import functools
import math
import types

import jax
import jax.numpy as jnp
import numpy as np
from jax import lax
from jax.experimental import pallas as pl
from jax.experimental.pallas import tpu as pltpu
from jax.sharding import PartitionSpec as P

HEADS, KV_HEADS, HEAD_DIM, RECUR = 15, 5, 64, 3
GROUP = HEADS // KV_HEADS
eps = 1e-05
rope_base = 10000.0
masked_fill = -1e30
BF, F32 = jnp.bfloat16, jnp.float32
COLS_A = 1664
FT = 512


def dot(a, b):
    return lax.dot_general(a, b, (((1,), (0,)), ((), ())), preferred_element_type=F32)


def dot_nt(a, b):
    return lax.dot_general(a, b, (((1,), (1,)), ((), ())), preferred_element_type=F32)


def dot_tn(a, b):
    return lax.dot_general(a, b, (((0,), (0,)), ((), ())), preferred_element_type=F32)


def halves(v):
    high = v.astype(BF)
    return high, (v - high.astype(F32)).astype(BF)


def pick(choice, v):
    high, low = halves(v)
    return dot(choice, high) + dot(choice, low)


def put_back(choice, v):
    high, low = halves(v)
    return dot_tn(choice, high) + dot_tn(choice, low)


def lanes(shape):
    return lax.broadcasted_iota(jnp.int32, shape, len(shape) - 1)


def rowid(shape):
    return lax.broadcasted_iota(jnp.int32, shape, len(shape) - 2)


def swapped(x):
    first = lax.rem(lanes(x.shape), 64) < 32
    return jnp.where(first, pltpu.roll(x, 96, 1), pltpu.roll(x, 32, 1))


class Far:
    def __init__(self, value):
        self.value = value


class Words:
    def __init__(self, value):
        self.value = value


class Out:
    def __init__(self, shape, dtype=F32, far=False):
        self.shape, self.dtype, self.far = shape, dtype, far


def join(*parts, **more):
    got = types.SimpleNamespace()
    for p in parts + (more,):
        vars(got).update(p if isinstance(p, dict) else vars(p))
    return got


def call(name, body, ins, outs, scratch=None, limit=63, **params):
    flat_in, tree_in = jax.tree.flatten(ins)
    flat_out, tree_out = jax.tree.flatten(outs)
    flat_scratch, tree_scratch = jax.tree.flatten(scratch or {})
    n_in, n_out = len(flat_in), len(flat_out)

    def kernel(*refs):
        body(join(tree_in.unflatten(refs[:n_in]), tree_out.unflatten(refs[n_in:n_in + n_out]),
                  tree_scratch.unflatten(refs[n_in + n_out:])))

    vm, far = pl.BlockSpec(memory_space=pltpu.VMEM), pl.BlockSpec(memory_space=pl.ANY)
    words = pl.BlockSpec(memory_space=pltpu.SMEM)
    got = pl.pallas_call(
        kernel,
        out_shape=[jax.ShapeDtypeStruct(o.shape, o.dtype) for o in flat_out],
        in_specs=[far if isinstance(v, Far) else words if isinstance(v, Words) else vm for v in flat_in],
        out_specs=[far if o.far else vm for o in flat_out],
        scratch_shapes=flat_scratch,
        compiler_params=pltpu.CompilerParams(vmem_limit_bytes=limit << 20, **params),
        name=name,
    )(*[v.value if isinstance(v, (Far, Words)) else v for v in flat_in])
    return types.SimpleNamespace(**tree_out.unflatten(got))


class Geo:
    def __init__(self, ns, bl, n_dp, n_blk, d, ff, tops):
        self.ns, self.bl, self.n_dp, self.n_blk, self.d, self.ff = ns, bl, n_dp, n_blk, d, ff
        self.gw = d // n_dp
        self.gp = -(-self.gw // 16) * 16
        self.dp = n_dp * self.gp
        self.slots = (bl, bl // 2, bl // 4)
        self.tops = tops

    def rows(self, r):
        return self.ns * self.slots[r]

    def keys(self, r):
        return self.n_blk * self.slots[r]

    def spread(self):
        e = np.zeros((1024, self.dp), np.float32)
        f = np.arange(self.d)
        e[f, f // self.gw * self.gp + f % self.gw] = 1
        return jnp.asarray(e, BF)

    def tables(self):
        f = rope_base ** (-(np.arange(32, dtype=np.float64) * 2.0) / 64)
        f32 = np.asarray(f, np.float32)
        ph = (np.arange(self.bl * self.n_blk, dtype=np.float32)[:, None] * f32).astype(np.float32).astype(np.float64)
        c, s = np.cos(ph), np.sin(ph)
        cos = np.concatenate([c, c, c, c], 1).astype(np.float32)
        sin = np.concatenate([-s, s, -s, s], 1).astype(np.float32)
        return jnp.asarray(cos), jnp.asarray(sin)


def gains(wa):
    sel = (lanes((8, 128)) == rowid((8, 128)) + 64).astype(BF)
    return dot_nt(sel, wa[:, 896:1024])


def choose(geo, r, routes, blk):
    s, t, bl = geo.slots[r], geo.tops[r], geo.bl
    before = jnp.sum((routes < blk * bl).astype(F32), axis=1, keepdims=True).astype(jnp.int32)
    shift = ((lanes((s, t)) - rowid((s, t))) == before).astype(BF)
    here = (routes == rowid((bl, t)) + blk * bl).astype(BF)
    return dot_nt(shift, here).astype(BF)


def allowed(geo, r, routes, blk, turned, heads=GROUP):
    s, kn, bl = geo.slots[r], geo.keys(r), geo.bl
    shape = (kn, heads * s) if turned else (heads * s, kn)
    key = rowid(shape) if turned else lanes(shape)
    query = lax.rem(lanes(shape) if turned else rowid(shape), s)
    ok = key <= blk * s + query
    if r > 0:
        t = geo.tops[r]
        inside = (routes // bl == rowid((kn, t)) // s)
        if turned:
            count = jnp.sum(inside.astype(F32), axis=1, keepdims=True)
        else:
            count = dot_nt(jnp.ones((8, t), BF), inside.astype(BF))[0:1]
        ok = ok & (lax.rem(key, s).astype(F32) < count)
    return jnp.where(ok, 0.0, masked_fill)


def project_kv(geo, r, k):
    a = k.a[...].astype(F32)
    n1 = lax.rsqrt(jnp.sum(a * a, axis=-1, keepdims=True) * (1.0 / geo.d) + eps)
    k.u[...] = (a * n1 * k.gn[0:1]).astype(BF)
    k.st[...] = jnp.where(lanes(k.st.shape) == 0, n1, 0.0)
    u = k.u[...]
    cos, sin = k.cos[...], k.sin[...]
    left = lanes(cos.shape) < 64
    ckv, skv = jnp.where(left, cos, 1.0), jnp.where(left, sin, 0.0)
    for c0, n in ((1024, 256), (1280, 256), (1536, 128)):
        some = dot(u, k.wa[:, c0:c0 + n])
        for j in range(n // 128):
            x = some[:, 128 * j:128 * j + 128]
            k.kv[:, c0 - 1024 + 128 * j:c0 - 1024 + 128 * j + 128] = (x * ckv + swapped(x) * skv).astype(BF)


def project_q(geo, r, k):
    u = k.u[...]
    cos, sin = k.cos[...], k.sin[...]
    left = lanes(cos.shape) < 64
    for t in range(4):
        both = dot(u, k.wa[:, 256 * t:256 * t + 256])
        for j in range(2):
            x = both[:, 128 * j:128 * j + 128]
            x = (x * cos + swapped(x) * sin).astype(BF).astype(F32) * 0.125
            h = 4 * t + 2 * j
            k.q16[h] = jnp.where(left, x, 0.0).astype(BF)
            if h + 1 < HEADS:
                k.q16[h + 1] = jnp.where(left, pltpu.roll(x, 64, 1), 0.0).astype(BF)


def project(geo, r, k):
    project_kv(geo, r, k)
    project_q(geo, r, k)


def select_rows(geo, r, k, blk):
    s, bl = geo.slots[r], geo.bl
    for m in range(geo.ns):
        ch = choose(geo, r, k.routes[m:m + 1], blk)
        k.choice[m] = ch
        k.a[m * s:m * s + s] = pick(ch, k.h[m * bl:m * bl + bl])
        k.cos[m * s:m * s + s] = pick(ch, k.cosb[...])
        k.sin[m * s:m * s + s] = pick(ch, k.sinb[...])


def attend(geo, r, k, blk, pause=None):
    s, kn = geo.slots[r], geo.keys(r)

    def seq(m, _):
        row0 = m * s if isinstance(m, int) else pl.multiple_of(m * s, s)
        k.kvg[...] = k.kvall[:, m].reshape(kn, KV_HEADS * 128)
        k.bias[...] = allowed(geo, r, k.routes[pl.ds(m, 1)] if r else None, blk, False)
        k.col[...] = jnp.zeros(k.col.shape, F32)

        def group(g, _):
            kvh = k.kvg[:, pl.ds(pl.multiple_of(g * 128, 128), 128)]
            sc = dot_nt(k.q16[pl.ds(g * GROUP, GROUP), pl.ds(row0, s)].reshape(GROUP * s, 128), kvh) + k.bias[...]
            top = jnp.max(sc, axis=-1, keepdims=True)
            p = jnp.exp(sc - top)
            total = jnp.sum(p, axis=-1, keepdims=True)
            k.o16[pl.ds(g * GROUP, GROUP)] = (dot(p.astype(BF), kvh) * (1.0 / total)).reshape(GROUP, s, 128)
            k.col[...] = jnp.where(lanes(k.col.shape) == g, top + jnp.log(total), k.col[...])
            return 0
        if pause is None:
            lax.fori_loop(0, KV_HEADS, group, 0)
        else:
            lax.fori_loop(0, 3, group, 0)
            pause()
            lax.fori_loop(3, KV_HEADS, group, 0)
        left = lanes((s, 128)) < 64
        for t in range(8):
            odd = k.o16[2 * t + 1] if 2 * t + 1 < HEADS else 0.0
            k.o[pl.ds(row0, s), 128 * t:128 * t + 128] = jnp.where(left, pltpu.roll(k.o16[2 * t], 64, 1), odd).astype(BF)
        k.lse[m] = k.col[...].T[0:8]
        return 0
    if pause is None:
        lax.fori_loop(0, geo.ns, seq, 0)
    else:
        for m in range(geo.ns):
            seq(m, 0)
            pause()


class Tiles:
    def __init__(self, geo, k, pre=None):
        self.k, self.n, self.ff, self.pre = k, geo.ff // FT, geo.ff, pre

    def parts(self, t, slot):
        k, c0 = self.k, t * FT
        if not isinstance(t, int):
            c0 = pl.multiple_of(c0, FT)
        cu = c0 + self.ff
        return [pltpu.make_async_copy(k.gu.at[:, pl.ds(c0, FT)], k.gbuf.at[slot], k.tsem.at[slot, 0]),
                pltpu.make_async_copy(k.gu.at[:, pl.ds(cu, FT)], k.ubuf.at[slot], k.tsem.at[slot, 1]),
                pltpu.make_async_copy(k.wd.at[pl.ds(c0, FT)], k.dbuf.at[slot], k.tsem.at[slot, 2])] + [
                    pltpu.make_async_copy(v.at[:, pl.ds(c0, FT)], k.pre.at[slot, j], k.tsem.at[slot, 3 + j])
                    for j, v in enumerate(self.pre or ())]

    def start(self, t, slot):
        for c in self.parts(t, slot):
            c.start()

    def loop(self, step):
        def body(t, _):
            slot = lax.rem(t, 2)

            @pl.when(t + 1 < self.n)
            def _():
                self.start(t + 1, 1 - slot)
            for c in self.parts(t, slot):
                c.wait()
            step(t, slot)
            return 0
        lax.fori_loop(0, self.n, body, 0)

    @staticmethod
    def scratch(geo):
        return dict(gbuf=pltpu.VMEM((2, geo.dp, FT), BF), ubuf=pltpu.VMEM((2, geo.dp, FT), BF),
                    dbuf=pltpu.VMEM((2, FT, geo.dp), BF), tsem=pltpu.SemaphoreType.DMA((2, 5)))


def feed(geo, r, k, blk, tiles):
    s, bl = geo.slots[r], geo.bl
    y = dot(k.o[...], k.wou[...])
    a = k.a[...].astype(F32)
    b = a + y
    n2 = lax.rsqrt(jnp.sum(b * b, axis=-1, keepdims=True) * (1.0 / geo.d) + eps)
    gate = jax.nn.sigmoid(jnp.sum(a * k.gn[2 + r:3 + r], axis=-1, keepdims=True))
    k.b[...] = b.astype(BF)
    k.w[...] = (b * n2 * k.gn[1:2]).astype(BF)
    lane = lanes((geo.rows(r), 128))
    k.sx[...] = jnp.where(lane == 0, n2, jnp.where(lane == 1, gate, 0.0))
    k.acc[...] = y

    def wide(t, slot):
        c0 = t * FT if isinstance(t, int) else pl.multiple_of(t * FT, FT)
        return [pltpu.make_async_copy(k.keep.at[slot, j], ref.at[:, pl.ds(c0, FT)], k.ksem.at[slot, j])
                for j, ref in enumerate((k.gp, k.up))]

    def step(t, slot):
        @pl.when(t >= 2)
        def _():
            for c in wide(t - 2, slot):
                c.wait()
        gp = dot(k.w[...], k.gbuf[slot])
        up = dot(k.w[...], k.ubuf[slot])
        k.keep[slot, 0] = gp.astype(BF)
        k.keep[slot, 1] = up.astype(BF)
        z = (gp * jax.nn.sigmoid(gp) * up).astype(BF)
        k.acc[...] += dot(z, k.dbuf[slot])
        for c in wide(t, slot):
            c.start()
    tiles.loop(step)
    for t in range(max(tiles.n - 2, 0), tiles.n):
        for c in wide(t, t % 2):
            c.wait()
    yf = k.acc[...]
    k.yf[...] = yf.astype(BF)
    delta = yf * k.sx[:, 1:2]
    for m in range(geo.ns):
        if r == 0:
            here = rowid((bl, 1)) + blk * bl < k.lens[m]
            rows = slice(m * bl, m * bl + bl)
            k.h2[rows] = k.a[rows].astype(F32) + jnp.where(here, delta[rows], 0.0)
        else:
            k.h2[m * bl:m * bl + bl] = k.h[m * bl:m * bl + bl] + put_back(k.choice[m], delta[m * s:m * s + s])


def back_feed(geo, r, k, blk, tiles):
    s, bl, rows = geo.slots[r], geo.bl, geo.rows(r)
    k.small[...] = jnp.zeros(k.small.shape, F32)

    def incoming(m):
        here = slice(m * s, m * s + s)
        if r == 0:
            return jnp.where(rowid((bl, 1)) + blk * bl < k.lens[m], k.dh[here], 0.0)
        return k.inc[here]
    for m in range(geo.ns):
        here = slice(m * s, m * s + s)
        if r > 0:
            k.inc[here] = pick(k.choice[m], k.dh[m * bl:m * bl + bl])
        inc = incoming(m)
        gate = k.sx[here, 1:2]
        dg = jnp.sum(inc * k.yf[here].astype(F32), axis=-1, keepdims=True)
        dl = dg * gate * (1.0 - gate)
        k.tok[here] = inc + dl * k.gn[2 + r:3 + r]
        k.small[2 + r:3 + r] += jnp.sum(k.a[here].astype(F32) * dl, axis=0, keepdims=True)
        k.df[here] = (gate * inc).astype(BF)
    k.acc[...] = jnp.zeros(k.acc.shape, F32)

    def wide(t, slot):
        c0 = t * FT if isinstance(t, int) else pl.multiple_of(t * FT, FT)
        return [pltpu.make_async_copy(k.wide.at[slot, j], ref.at[:, pl.ds(c0, FT)], k.wsem.at[slot, j])
                for j, ref in enumerate((k.dgp, k.dup, k.z))]

    def step(t, slot):
        @pl.when(t >= 2)
        def _():
            for c in wide(t - 2, slot):
                c.wait()
        dz = dot_nt(k.df[...], k.dbuf[slot])
        gp = k.pre[slot, 0].astype(F32)
        up = k.pre[slot, 1].astype(F32)
        sig = jax.nn.sigmoid(gp)
        silu = gp * sig
        k.wide[slot, 2] = (silu * up).astype(BF)
        dup = (dz * silu).astype(BF)
        dgp = (dz * up * (sig * (1.0 + gp * (1.0 - sig)))).astype(BF)
        k.wide[slot, 1] = dup
        k.wide[slot, 0] = dgp
        k.acc[...] += dot_nt(dgp, k.gbuf[slot]) + dot_nt(dup, k.ubuf[slot])
        for c in wide(t, slot):
            c.start()
    tiles.loop(step)
    for t in range(max(tiles.n - 2, 0), tiles.n):
        for c in wide(t, t % 2):
            c.wait()
    for m in range(geo.ns):
        here = slice(m * s, m * s + s)
        n2, gate = k.sx[here, 0:1], k.sx[here, 1:2]
        dw = k.acc[here]
        b = k.b[here].astype(F32)
        k.small[1:2] += jnp.sum(dw * (b * n2), axis=0, keepdims=True)
        t = dw * k.gn[1:2]
        db = n2 * t - n2 * n2 * n2 * b * (jnp.sum(t * b, axis=-1, keepdims=True) * (1.0 / geo.d))
        k.tok[here] += db
        k.dy[here] = (gate * incoming(m) + db).astype(BF)


def back_out(geo, r, k):
    s, kn = geo.slots[r], geo.keys(r)
    rows = geo.rows(r)
    left = lanes((rows, 128)) < 64
    lane = lanes((rows, 128))
    dcol = jnp.zeros((rows, 128), F32)
    for t in range(8):
        x = dot_nt(k.dy[...], k.wou[128 * t:128 * t + 128])
        x = x.astype(BF).astype(F32)
        prod = x * k.o[:, 128 * t:128 * t + 128].astype(F32)
        even = jnp.sum(jnp.where(left, prod, 0.0), axis=-1, keepdims=True)
        dcol = jnp.where(lane == 2 * t, even, dcol)
        k.do16[2 * t] = jnp.where(left, 0.0, pltpu.roll(x, 64, 1)).astype(BF)
        if 2 * t + 1 < HEADS:
            odd = jnp.sum(jnp.where(left, 0.0, prod), axis=-1, keepdims=True)
            dcol = jnp.where(lane == 2 * t + 1, odd, dcol)
            k.do16[2 * t + 1] = jnp.where(left, 0.0, x).astype(BF)
    k.dcol[...] = dcol


def back_attend(geo, r, k, blk, pause=None):
    s, kn = geo.slots[r], geo.keys(r)
    batch = GROUP if pause is None else 1

    def seq(m, _):
        row0 = m * s if isinstance(m, int) else pl.multiple_of(m * s, s)
        if pause is None:
            k.kvg[...] = k.kvall[:, m].reshape(kn, KV_HEADS * 128)
        else:
            loads = [pltpu.make_async_copy(k.kvall.at[b, m], k.kvg.at[pl.ds(b * s, s)], k.lsem.at[b]) for b in range(geo.n_blk)]
            for v in loads:
                v.start()
            for v in loads:
                v.wait()
        for g in range(KV_HEADS):
            k.kvt[g] = k.kvg[:, 128 * g:128 * g + 128].astype(F32).T.astype(BF)
        k.bias[...] = allowed(geo, r, k.routes[pl.ds(m, 1)] if r else None, blk, True, batch)
        dt = k.dcol[pl.ds(row0, s)].T
        for h in range(HEADS):
            k.dt[h // GROUP:h // GROUP + 1, h % GROUP * s:(h % GROUP + 1) * s] = dt[h:h + 1]
        k.ct[0] = k.cos[pl.ds(row0, s)].T[0:32] * 0.125
        k.ct[1] = k.sin[pl.ds(row0, s)].T[32:64] * 0.125

        def group(g, _):
            lane0 = pl.multiple_of(g * 128, 128)
            kvh = k.kvg[:, pl.ds(lane0, 128)]
            total = None
            for j0 in range(0, GROUP, batch):
                heads = (pl.ds(g * GROUP + j0, batch), pl.ds(row0, s))
                cols = slice(j0 * s, (j0 + batch) * s)
                qh, doh = k.q16[heads].reshape(batch * s, 128), k.do16[heads].reshape(batch * s, 128)
                p = jnp.exp(dot_nt(kvh, qh) + k.bias[...] - k.lse[m, pl.ds(g, 1), cols])
                ds = (p * (dot_nt(kvh, doh) - k.dt[pl.ds(g, 1), cols])).astype(BF)
                part = dot(ds, qh) + dot(p.astype(BF), doh)
                total = part if total is None else total + part
                dqt = dot(k.kvt[g], ds)
                c, sn = k.ct[0], k.ct[1]
                for j in range(batch):
                    y1, y2 = dqt[0:32, j * s:j * s + s], dqt[32:64, j * s:j * s + s]
                    k.dqt[g * GROUP + j0 + j, 0:32] = (y1 * c + y2 * sn)
                    k.dqt[g * GROUP + j0 + j, 32:64] = (y2 * c - y1 * sn)
            total = total.astype(BF).reshape(geo.n_blk, s, 128)
            if pause is None:
                k.dkv[:, m, :, pl.ds(lane0, 128)] = total
            else:
                k.dkvm[:, :, pl.ds(lane0, 128)] = total
            return 0
        if pause is None:
            lax.fori_loop(0, KV_HEADS, group, 0)
        else:
            lax.fori_loop(0, 3, group, 0)
            pause()
            lax.fori_loop(3, KV_HEADS, group, 0)
            store = pltpu.make_async_copy(k.dkvm, k.dkv.at[:, m], k.lsem.at[0])
            store.start()
        for t in range(8):
            if 2 * t + 1 < HEADS:
                x = k.dqt[2 * t:2 * t + 2].reshape(128, s).T
            else:
                x = jnp.concatenate([k.dqt[2 * t], jnp.zeros((64, s), F32)], axis=0).T
            k.da[pl.ds(row0, s), 128 * t:128 * t + 128] = x.astype(BF)
        if pause is not None:
            store.wait()
        return 0
    if pause is None:
        lax.fori_loop(0, geo.ns, seq, 0)
    else:
        for m in range(geo.ns):
            seq(m, 0)
            pause()


def back_project(geo, r, k, blk):
    s, bl, rows = geo.slots[r], geo.bl, geo.rows(r)
    cos, sin = k.cos[...], k.sin[...]
    left = lanes(cos.shape) < 64
    ckv, skv = jnp.where(left, cos, 1.0), jnp.where(left, sin, 0.0)
    k.da2[:, 0:1024] = k.da[...]
    for g in range(KV_HEADS):
        x = k.dkvown[:, 128 * g:128 * g + 128].astype(F32)
        k.da2[:, 1024 + 128 * g:1152 + 128 * g] = (x * ckv - swapped(x) * skv).astype(BF)
    for m in range(geo.ns):
        here = slice(m * bl, m * bl + bl)
        mine = slice(m * s, m * s + s)
        du = dot_nt(k.da2[mine], k.wa[...])
        a = k.a[mine].astype(F32)
        n1 = k.st[mine, 0:1]
        k.first[0:1] += jnp.sum(du * (a * n1), axis=0, keepdims=True)
        t1 = du * k.gn[0:1]
        tok = k.tok[mine] + n1 * t1 - n1 * n1 * n1 * a * (jnp.sum(t1 * a, axis=-1, keepdims=True) * (1.0 / geo.d))
        if r == 0:
            ok = rowid((bl, 1)) + blk * bl < k.lens[m]
            k.dh2[here] = jnp.where(ok, tok, k.dh[here])
        else:
            k.dh2[here] = k.dh[here] + put_back(k.choice[m], tok - k.inc[mine])


def block(geo, x, cot, lens, routes, slabs, share, give_back):
    blk_of = lambda: lax.axis_index("blk")
    bl, d, dp, ff, nsq, nb = geo.bl, geo.d, geo.dp, geo.ff, geo.ns, geo.n_blk
    full = nsq * bl
    cos_all, sin_all = geo.tables()
    b0 = lax.axis_index("blk") * bl
    cosb = lax.dynamic_slice_in_dim(cos_all, b0, bl, 0)
    sinb = lax.dynamic_slice_in_dim(sin_all, b0, bl, 0)
    spread = geo.spread()
    R, S, KN = [geo.rows(r) for r in range(3)], geo.slots, [geo.keys(r) for r in range(3)]
    V, dma = pltpu.VMEM, pltpu.SemaphoreType.DMA
    lens = Words(lens)

    def proj_outs(r, kv=True):
        more = dict(choice=Out((nsq, S[r], bl), BF)) if r else {}
        more = dict(kv=Out((R[r], 640), BF), **more) if kv else more
        return dict(a=Out((R[r], dp), F32 if r else BF), u=Out((R[r], dp), BF), q16=Out((HEADS, R[r], 128), BF), st=Out((R[r], 128)), cos=Out((R[r], 128)), sin=Out((R[r], 128)), **more)

    def seen_outs(r):
        return dict(o=Out((R[r], 1024), BF), lse=Out((nsq, 8, GROUP * S[r])))

    def fore_outs(r):
        return dict(**(seen_outs(r) if r else {}), b=Out((R[r], dp), BF), w=Out((R[r], dp), BF),
                    gp=Out((R[r], ff), BF, True), up=Out((R[r], ff), BF, True), yf=Out((R[r], dp), BF), sx=Out((R[r], 128)))

    def seen_scratch(r):
        return dict(kvg=V((KN[r], 640), BF), bias=V((GROUP * S[r], KN[r]), F32), col=V((GROUP * S[r], 128), F32),
                    o16=V((HEADS, S[r], 128), F32))

    def fore_scratch(r):
        return dict(acc=V((R[r], dp), F32), keep=V((2, 2, R[r], FT), BF), ksem=dma((2, 2)), **(seen_scratch(r) if r else {}))

    def feed_outs(r):
        more = dict(inc=Out((R[r], dp))) if r else {}
        return dict(tok=Out((R[r], dp)), df=Out((R[r], dp), BF), dgp=Out((R[r], ff), BF, True), dup=Out((R[r], ff), BF, True),
                    z=Out((R[r], ff), BF, True), dy=Out((R[r], dp), BF), small=Out((8, dp)), **more)

    def feed_scratch(r):
        return dict(acc=V((R[r], dp), F32), pre=V((2, 2, R[r], FT), BF), wide=V((2, 3, R[r], FT), BF), wsem=dma((2, 3)))

    def turned_outs(r):
        piece = (nsq, S[r], 640)
        last = dict(dkvown=Out(piece)) if near and r else dict(dkv=Out((nb,) + piece, BF))
        return dict(da=Out((R[r], 1024), BF), **last)

    def out_parts(make, r=0):
        return dict(do16=make((HEADS, R[r], 128), BF), dcol=make((R[r], 128), F32))

    def turned_scratch(r, batch=GROUP):
        return dict(kvg=V((KN[r], 640), BF), kvt=V((KV_HEADS, 128, KN[r]), BF), bias=V((KN[r], batch * S[r]), F32), dt=V((8, GROUP * S[r]), F32), ct=V((2, 32, S[r]), F32),
                    dqt=V((HEADS, 64, S[r]), F32), **(out_parts(V, r) if r else {}))

    near = (geo.n_dp, geo.n_blk) == (G, 4)

    def share_scratch(r):
        return dict(kv=V((R[r], 640), BF), own=V((nsq, S[r], 640), BF), ssem=dma((3,)), rsem=dma((3,)))

    def give_scratch(r):
        piece = (nsq, S[r], 640)
        return dict(dkv=V((nb,) + piece, BF), got1=V((2,) + piece, BF), half=V(piece, BF), got2=V(piece, BF), ssem=dma((3,)),
                    rsem=dma((3,)))

    P, F, B, T, L = [None] * 3, [None] * 3, [None] * 3, [None] * 3, [None] * 3
    rt = [None] + list(routes)

    def begin(k):
        k.a[...] = dot(k.x[...], k.spread[0:d]).astype(BF)
        for m in range(nsq):
            k.cos[m * bl:m * bl + bl] = k.cosb[...]
            k.sin[m * bl:m * bl + bl] = k.sinb[...]

    ins = dict(x=x, spread=spread, cosb=cosb, sinb=sinb)
    afters = seen_outs(0)
    if not near:
        wa, wo, gu, wd = (lax.all_gather(w, "dp", axis=0, tiled=True) for w in slabs)

        def k_first(k):
            k = join(k, k.p)
            begin(k)
            k.gn = gains(k.wa)
            project(geo, 0, k)
        P[0] = join(call("first_project", k_first, dict(wa=wa, **ins), dict(p=proj_outs(0))).p)
        P[0].kvall = share(P[0].kv.reshape(nsq, S[0], 640))
        F[0] = call("attend", lambda k: attend(geo, 0, k, blk_of()), dict(q16=P[0].q16, kvall=P[0].kvall), afters, seen_scratch(0))
    else:
        def k_head(k):
            dp_, blk, y, c, ym, cm = mates()
            z, x_ = dp_ // NX, lax.rem(dp_, NX)
            k = join(k, k.p, k.f, k.fs)
            ticks = gather_ticks(AG_CHUNKS, k.shards, k.slabs, k.sems)
            meet((dp_ + 1 - 2 * x_, blk), ym, cm, z=z)

            def tick(n=1):
                for _ in range(min(n, len(ticks))):
                    ticks.pop(0)()
            tick(2)
            begin(k)
            tick(A_TICKS - 2)
            load = pltpu.make_async_copy(k.slabs[0], k.wa, k.wsem)
            load.start()
            load.wait()
            k.gn = gains(k.wa)
            project_kv(geo, 0, k)
            sharing = Share(k.own, k.kvall, k.ssem, k.rsem)
            k.own[...] = k.kv[...].reshape(nsq, S[0], 640)
            k.kvall[blk] = k.own[...]
            sharing.start()
            tick()
            project_q(geo, 0, k)
            tick()
            sharing.forward()
            tick()
            sharing.arrive()
            attend(geo, 0, k, blk, tick)
            tick(len(ticks))
            sharing.sent()
        got = call("head", k_head, dict(shards=list(slabs), **ins),
                   dict(slabs=[Out((v.shape[0] * geo.n_dp, v.shape[1]), BF, True) for v in slabs], p=proj_outs(0, False), f=afters,
                        kvall=Out((nb, nsq, S[0], 640), BF)),
                   dict(fs=seen_scratch(0), wa=V((dp, COLS_A), BF), kv=V((R[0], 640), BF), own=V((nsq, S[0], 640), BF),
                        wsem=dma, ssem=dma((3,)), rsem=dma((3,)), sems=gather_sems(4, len(AG_CHUNKS))),
                   collective_id=1, has_side_effects=True)
        wa, wo, gu, wd = got.slabs
        P[0], F[0] = join(got.p, kvall=got.kvall), join(got.f)
    gu, wd = Far(gu), Far(wd)
    wou = h = None

    def remote(ident):
        return dict(collective_id=ident, has_side_effects=True) if near else {}

    def k_fore(r, k):
        blk = blk_of()
        if near:
            meet(*mates()[4:])
        k = join(k, k.s, k.tl)
        tiles = Tiles(geo, k)
        tiles.start(0, 0)
        k.gn = gains(k.wa)
        if r == 0:
            k.wou[...] = dot(k.spread[...], k.wo[...]).astype(BF)
        v = join(k, k.p, k.f, k.fs)
        if r:
            attend(geo, r, v, blk)
        feed(geo, r, v, blk, tiles)
        n = join(k, k.n, h=k.h2, routes=k.routes2)
        select_rows(geo, r + 1, n, blk)
        if not near:
            project(geo, r + 1, n)
            return
        n = join(n, k.sh, k.sh_)
        project_kv(geo, r + 1, n)
        n.own[...] = n.kv[...].reshape(n.own.shape)
        n.kvall[blk] = n.own[...]
        sharing = Share(n.own, n.kvall, n.ssem, n.rsem)
        sharing.start()
        project_q(geo, r + 1, n)
        sharing.forward()
        sharing.arrive()
        sharing.sent()

    for r in range(2):
        p = dict(a=P[r].a, q16=P[r].q16, kvall=P[r].kvall) if r else dict(a=P[0].a, o=F[0].o)
        more = dict(choice=P[r].choice, h=h, routes=rt[r], wou=wou) if r else dict(wo=wo, spread=spread, lens=lens)
        got = call("forward", functools.partial(k_fore, r),
                   dict(wa=wa, gu=gu, wd=wd, p=p, cosb=cosb, sinb=sinb, routes2=rt[r + 1], s=more),
                   dict(f=fore_outs(r), n=proj_outs(r + 1, not near), h2=Out((full, dp)), **({} if r else dict(wou=Out((1024, dp), BF))),
                        **(dict(sh=dict(kvall=Out((nb, nsq, S[r + 1], 640), BF))) if near else {})),
                   dict(fs=fore_scratch(r), tl=Tiles.scratch(geo), **(dict(sh_=share_scratch(r + 1)) if near else {})), **remote(3 + r))
        h, F[r], P[r + 1] = got.h2, join(F[r] or {}, got.f), join(got.n)
        wou = wou if r else got.wou
        P[r + 1].kvall = join(got.sh).kvall if near else share(P[r + 1].kv.reshape(nsq, S[r + 1], 640))

    def k_turn(k):
        blk = blk_of()
        if near:
            meet(*mates()[4:])
        k = join(k, k.tl)
        tiles = Tiles(geo, k)
        tiles.start(0, 0)
        k.gn = gains(k.wa)
        v = join(k, k.p, k.f, k.fs, h2=k.h3)
        attend(geo, 2, v, blk)
        feed(geo, 2, v, blk, tiles)
        tiles = Tiles(geo, join(k, k.bs), (v.gp, v.up))
        tiles.start(0, 0)
        k.out[...] = dot_nt(k.h3[...].astype(BF), k.spread[0:d]).astype(BF)
        k.dh[...] = dot(k.cot[...], k.spread[0:d])
        v = join(v, k.bs, k.ts, k.b, k.t, k.gv if near else {})
        back_feed(geo, 2, v, blk, tiles)
        back_out(geo, 2, v)
        back_attend(geo, 2, v, blk)
        if near:
            give(v.dkv, v.dkvown, v.got1, v.half, v.got2, v.ssem, v.rsem)

    p = P[2]
    got = call("turn", k_turn,
               dict(wa=wa, gu=gu, wd=wd, wou=wou, h=h, spread=spread, cot=cot, routes=rt[2],
                    p=dict(a=p.a, q16=p.q16, kvall=p.kvall, choice=p.choice, cos=p.cos, sin=p.sin)),
               dict(f=fore_outs(2), b=feed_outs(2), t=turned_outs(2), out=Out((full, d), BF), dh=Out((full, dp))),
               dict(fs=fore_scratch(2), bs=feed_scratch(2), ts=turned_scratch(2), tl=Tiles.scratch(geo), h3=V((full, dp), F32),
                    **(dict(gv=give_scratch(2)) if near else {})), **remote(5))
    F[2], B[2], T[2], out, dh = join(got.f), join(got.b), join(got.t), got.out, got.dh

    def k_back(r, k):
        blk = blk_of()
        if near and r:
            meet(*mates()[4:])
        v = join(k, k.p, k.f, k.b, k.bs, k.tl)
        tiles = Tiles(geo, v, (v.gp, v.up))
        tiles.start(0, 0)
        v.gn = k.gn = gains(k.wa)
        k.first[...] = jnp.zeros(k.first.shape, F32)
        back_project(geo, r + 1, join(k, k.n), blk)
        v.dh = k.dh2
        back_feed(geo, r, v, blk, tiles)
        if r > 0:
            v = join(v, k.t, k.ts, k.gv if near else {})
        back_out(geo, r, v)
        if r > 0:
            back_attend(geo, r, v, blk)
            if near:
                give(v.dkv, v.dkvown, v.got1, v.half, v.got2, v.ssem, v.rsem)

    for r in (1, 0):
        n, q, p, f = r + 1, P[r + 1], P[r], F[r]
        mine = (T[n].dkvown if near else give_back(T[n].dkv)).reshape(R[n], 640)
        late = dict(q16=p.q16, kvall=p.kvall, cos=p.cos, sin=p.sin, choice=p.choice) if r else {}
        more = dict(lse=f.lse) if r else {}
        rest = dict(wou=wou, routes=rt[r]) if r else dict(wou=wou, lens=lens)
        got = call("backward", functools.partial(k_back, r),
                   dict(wa=wa, gu=gu, wd=wd, dh=dh, **rest,
                        n=dict(dkvown=mine, da=T[n].da, tok=B[n].tok, inc=B[n].inc, choice=q.choice, st=q.st, a=q.a,
                               cos=q.cos, sin=q.sin),
                        p=dict(a=p.a, **late),
                        f=dict(o=f.o, b=f.b, gp=Far(f.gp), up=Far(f.up), yf=f.yf, sx=f.sx, **more)),
                   dict(b=feed_outs(r), da2=Out((R[n], COLS_A), BF), first=Out((8, dp)), dh2=Out((full, dp)),
                        **(dict(t=turned_outs(r)) if r else out_parts(Out))),
                   dict(bs=feed_scratch(r), tl=Tiles.scratch(geo), **(dict(ts=turned_scratch(r)) if r else {}),
                        **(dict(gv=give_scratch(r)) if r and near else {})), **(remote(6) if r else {}))
        dh, B[r], L[n] = got.dh2, join(got.b), join(da2=got.da2, first=got.first)
        if r:
            T[r] = join(got.t)
    p, f = P[0], F[0]
    saved = [join(P[r], F[r], B[r], L[r] or {}) for r in range(3)]
    if near:
        gu_d = gate_up_grads(geo, saved), down_grads(geo, saved)
        grad, shards = tail(geo, join(p, f, B[0], got, wa=wa, dh=dh, lens=lens.value, spread=spread), saved, gu_d,
                            turned_scratch(0, 1))
        return out, grad, shards
    T[0] = call("backward_attend", lambda k: back_attend(geo, 0, k, blk_of()),
                dict(do16=got.do16, dcol=got.dcol, q16=p.q16, kvall=p.kvall, lse=f.lse, cos=p.cos, sin=p.sin),
                turned_outs(0), turned_scratch(0))
    mine = give_back(T[0].dkv).reshape(R[0], 640)

    def k_last(k):
        blk = blk_of()
        k.gn = gains(k.wa)
        k.first[...] = jnp.zeros(k.first.shape, F32)
        back_project(geo, 0, k, blk)
        high, low = halves(k.dh2[...])
        k.grad[...] = dot_nt(high, k.spread[0:d]) + dot_nt(low, k.spread[0:d])
    L[0] = call("last_project", k_last,
                dict(wa=wa, dkvown=mine, da=T[0].da, tok=B[0].tok, dh=dh, lens=lens, st=p.st, a=p.a, cos=p.cos, sin=p.sin,
                     spread=spread),
                dict(da2=Out((R[0], COLS_A), BF), first=Out((8, dp)), grad=Out((full, d))), dict(dh2=V((full, dp), F32)))
    saved[0] = join(saved[0], L[0])
    slabs = [products(geo, saved, QKV), products(geo, saved, OUT, spread), gate_up_grads(geo, saved), down_grads(geo, saved)]
    shards = [lax.psum(lax.psum_scatter(v, "dp", scatter_dimension=0, tiled=True), "blk") for v in slabs]
    return out, L[0].grad, shards


QKV, OUT = range(2)


def product_parts(geo, saved, kind, spread=None):
    dp = geo.dp
    if kind == QKV:
        ins = dict(lefts=[v.u for v in saved], rights=[[v.da2 for v in saved]], small=[v.small for v in saved],
                   first=[v.first for v in saved])
        return ins, (dp, COLS_A), 512
    return dict(lefts=[v.o for v in saved], rights=[[v.dy for v in saved]], spread=spread), (dp, dp), 512


def product_body(geo, kind, shape, tile, k):
    R = [geo.rows(r) for r in range(3)]
    rows, dp = shape[0], geo.dp
    at = 0
    for i in range(3):
        for c in range(0, rows, 256):
            v = dot(k.lefts[i][...], k.spread[:, c:c + 256]).astype(BF) if kind == OUT else k.lefts[i][:, c:c + 256]
            k.left[c:c + 256, at:at + R[i]] = v.T
        at += R[i]
    c0 = 0
    for refs in k.rights:
        n = refs[0].shape[1]
        for t in range(0, n, tile):
            w = min(tile, n - t)
            right = jnp.concatenate([v[:, t:t + w] for v in refs], axis=0)
            k.res[:, c0 + t:c0 + t + w] = dot(k.left[...], right).astype(BF)
        c0 += n
    if kind == QKV:
        small = k.small[0][...] + k.small[1][...] + k.small[2][...]
        f = k.first[0][...] + k.first[1][...] + k.first[2][...]
        small = jnp.where(rowid(small.shape) == 0, f, small)
        cols = jnp.concatenate([small, jnp.zeros((120, dp), F32)], axis=0).T
        cols = pltpu.roll(cols, 64, 1)
        k.res[:, 896:1024] = jnp.where(lanes(cols.shape) < 64, k.res[:, 896:1024].astype(F32), cols).astype(BF)


def products(geo, saved, kind, spread=None):
    ins, shape, tile = product_parts(geo, saved, kind, spread)
    total = sum(geo.rows(r) for r in range(3))
    return call("weight_grads", functools.partial(product_body, geo, kind, shape, tile), ins, dict(res=Out(shape, BF)),
                dict(left=pltpu.VMEM((shape[0], total), BF))).res


def gate_up_grads(geo, saved):
    R = [geo.rows(r) for r in range(3)]
    total, dp, n = sum(R), geo.dp, geo.ff // FT

    def body(w0, w1, w2, g0, g1, g2, u0, u1, u2, out, left):
        t = pl.program_id(0)

        @pl.when(t == 0)
        def _():
            at = 0
            for i, w in enumerate((w0, w1, w2)):
                for c in range(0, dp, 256):
                    left[c:c + 256, at:at + R[i]] = w[:, c:c + 256].T
                at += R[i]

        def put(parts):
            out[...] = dot(left[...], jnp.concatenate([v[...] for v in parts], axis=0)).astype(BF)
        pl.when(t < n)(lambda: put((g0, g1, g2)))
        pl.when(t >= n)(lambda: put((u0, u1, u2)))
    held = [pl.BlockSpec((rows, dp), lambda t: (0, 0)) for rows in R]
    gate = [pl.BlockSpec((rows, FT), lambda t: (0, jnp.minimum(t, n - 1))) for rows in R]
    up = [pl.BlockSpec((rows, FT), lambda t: (0, jnp.maximum(t - n, 0))) for rows in R]
    return pl.pallas_call(
        body, grid=(2 * n,), out_shape=jax.ShapeDtypeStruct((dp, 2 * geo.ff), BF), in_specs=held + gate + up,
        out_specs=pl.BlockSpec((dp, FT), lambda t: (0, t)), scratch_shapes=[pltpu.VMEM((dp, total), BF)],
        compiler_params=pltpu.CompilerParams(vmem_limit_bytes=63 << 20), name="gate_up_grads",
    )(*[v.w for v in saved], *[v.dgp for v in saved], *[v.dup for v in saved])


def down_grads(geo, saved, tile=512):
    R = [geo.rows(r) for r in range(3)]
    dp = geo.dp

    def body(z0, z1, z2, d0, d1, d2, out):
        left = jnp.concatenate([v[...] for v in (z0, z1, z2)], axis=0)
        right = jnp.concatenate([v[...] for v in (d0, d1, d2)], axis=0)
        out[...] = dot_tn(left, right).astype(BF)
    return pl.pallas_call(
        body, grid=(geo.ff // tile,), out_shape=jax.ShapeDtypeStruct((geo.ff, dp), BF),
        in_specs=[pl.BlockSpec((rows, tile), lambda t: (0, t)) for rows in R]
        + [pl.BlockSpec((rows, dp), lambda t: (0, 0)) for rows in R],
        out_specs=pl.BlockSpec((tile, dp), lambda t: (t, 0)),
        compiler_params=pltpu.CompilerParams(vmem_limit_bytes=63 << 20), name="down_grads",
    )(*[v.z for v in saved], *[v.df for v in saved])


def phase(body, ins, outs, scratch=None):
    leaf = lambda v: not isinstance(v, (dict, list, tuple))
    fi, ti = jax.tree.flatten(ins, is_leaf=leaf)
    fo, to = jax.tree.flatten(outs, is_leaf=leaf)

    def run(vi, vo, sc, sems):
        loads = [pltpu.make_async_copy(far, near, sems.at[i]) for i, (far, near) in enumerate(zip(fi, vi))]
        for v in loads:
            v.start()
        for v in loads:
            v.wait()
        body(join(ti.unflatten(vi), to.unflatten(vo), sc))
        stores = [pltpu.make_async_copy(near, far, sems.at[i]) for i, (far, near) in enumerate(zip(fo, vo))]
        for v in stores:
            v.start()
        for v in stores:
            v.wait()
    near = lambda refs: [pltpu.VMEM(v.shape, v.dtype) for v in refs]
    pl.run_scoped(run, near(fi), near(fo), scratch or {}, pltpu.SemaphoreType.DMA((max(len(fi), len(fo)),)))


def tail(geo, v, saved, gu_d, turned):
    dp, d, bl, nsq, s = geo.dp, geo.d, geo.bl, geo.ns, geo.slots[0]
    full = nsq * bl
    V, dma = pltpu.VMEM, pltpu.SemaphoreType.DMA
    total = sum(geo.rows(r) for r in range(3))
    one = Geo(1, bl, geo.n_dp, geo.n_blk, d, geo.ff, geo.tops)
    part = (nsq, s, 640)

    def body(k):
        dp_, blk, y, c, ym, cm = mates()
        z, x_ = dp_ // NX, lax.rem(dp_, NX)
        meet((dp_ + 1 - 2 * x_, blk), ym, cm, z=z)
        slabs = [k.ga, k.go, k.gu, k.gd]
        ticks = reduce_ticks(RS_CHUNKS, [slab_view(geo, i, w) for i, w in enumerate(slabs)], k.shards, k.bufs, k.sems)
        ready = RS_CHUNKS_READY

        def tick(n=1):
            nonlocal ready
            for _ in range(n):
                if ready > 0:
                    ready -= 1
                    ticks.pop(0)()
        tick(2)
        a = k.at
        phase(lambda q: back_attend(geo, 0, join(q, kvall=k.kvall, dkv=k.dkv), blk, tick),
              dict(do16=a.do16, dcol=a.dcol, q16=a.q16, lse=a.lse, cos=a.cos, sin=a.sin), dict(da=k.da),
              dict(dkvm=V((geo.n_blk, s, 640), BF), lsem=dma((geo.n_blk,)), **turned))

        def rem(src, dst, i, to):
            return pltpu.make_async_remote_copy(src_ref=src, dst_ref=dst, send_sem=k.gs.at[i], recv_sem=k.gr.at[i],
                                                device_id=to, device_id_type=MESH)
        first = [rem(k.dkv.at[2 * yy + 1 - c], k.got1.at[yy], yy, cm) for yy in range(2)]
        for f in first:
            f.start()
        tick()
        for f in first:
            f.wait_recv()

        def add(q):
            for yy, mine in enumerate((q.p0, q.p1)):
                k.got1[yy] = (k.got1[yy].astype(F32) + mine[...].astype(F32)).astype(BF)
        phase(add, dict(p0=k.dkv.at[c], p1=k.dkv.at[2 + c]), {})
        second = rem(k.got1.at[1 - y], k.got2, 2, ym)
        second.start()
        tick()
        second.wait_recv()
        tick()
        k.first[...] = jnp.zeros(k.first.shape, F32)
        for m in range(nsq):
            rows = pl.ds(m * bl, bl)

            def last(q):
                q.gn = gains(q.wa)
                q.dkvown[...] = k.got1[y, m].astype(F32) + k.got2[m].astype(F32)
                back_project(one, 0, join(q, lens=[k.lens[m]], first=k.first), blk)
                high, low = halves(q.dh2[...])
                q.grad[...] = dot_nt(high, q.spread[0:d]) + dot_nt(low, q.spread[0:d])
            phase(last, dict(wa=k.wa, da=k.da.at[rows], tok=a.tok.at[rows], dh=a.dh.at[rows], st=a.st.at[rows], a=a.a.at[rows],
                             cos=a.cos.at[rows], sin=a.sin.at[rows], spread=k.spread),
                  dict(da2=k.da2.at[rows], grad=k.grad.at[rows]),
                  dict(dkvown=V((bl, 640), F32), dh2=V((bl, dp), F32)))
            tick()
        for kind, res in ((QKV, k.ga), (OUT, k.go)):
            ins, shape, tile = product_parts(geo, [types.SimpleNamespace(**q) for q in k.saved], kind, k.spread)
            if kind == QKV:
                ins[FIRST] = ins[FIRST][1:]
                ins[RIGHTS] = [[k.da2] + ins[RIGHTS][0][1:]]

            def make(q, kind=kind, shape=shape, tile=tile):
                if kind == QKV:
                    q.first = [k.first] + q.first
                product_body(geo, kind, shape, tile, q)
            phase(make, ins, dict(res=res), dict(left=V((shape[0], total), BF)))
            tick()
        for t in ticks:
            t()
        for f in first + [second]:
            f.wait_send()

    FIRST, RIGHTS = tuple(dict(first=0, rights=0))
    keep = [dict(u=Far(q.u), o=Far(q.o), dy=Far(q.dy), small=Far(q.small),
                 **(dict(da2=Far(q.da2), first=Far(q.first)) if i else dict(da2=Far(q.u), first=Far(q.small))))
            for i, q in enumerate(saved)]
    bufs, sems = reduce_scratch(geo, RS_CHUNKS)
    got = call("tail", lambda k: body(join(k, at=join(k.at))),
               dict(at=dict(do16=Far(v.do16), dcol=Far(v.dcol), q16=Far(v.q16), lse=Far(v.lse), cos=Far(v.cos), sin=Far(v.sin),
                            tok=Far(v.tok), dh=Far(v.dh), st=Far(v.st), a=Far(v.a)),
                    kvall=Far(v.kvall), lens=Words(v.lens), wa=Far(v.wa), spread=Far(v.spread), gu=Far(gu_d[0]), gd=Far(gu_d[1]),
                    saved=keep),
               dict(shards=reduce_outs(geo), grad=Out((full, d), F32, True), ga=Out((dp, COLS_A), BF, True),
                    go=Out((dp, dp), BF, True), da=Out((full, 1024), BF, True), da2=Out((full, COLS_A), BF, True),
                    dkv=Out((geo.n_blk,) + part, BF, True)),
               dict(bufs=bufs, sems=sems, got1=V((2,) + part, BF), got2=V(part, BF), first=V((8, dp), F32),
                    gs=dma((3,)), gr=dma((3,))),
               collective_id=2, has_side_effects=True)
    return got.grad, got.shards


MESH = pl.DeviceIdType.MESH

NZ, NX = 4, 2
AHEAD = 2
OFFSETS = (0, 2, 4, 6, 8, 10, 12, 13, 14)
G = NZ * NX


def meet(*others, z=None):
    dp, blk = lax.axis_index("dp"), lax.axis_index("blk")
    bar = pltpu.get_barrier_semaphore()
    for t in others:
        pl.semaphore_signal(bar, inc=1, device_id=t, device_id_type=MESH)
    count = len(others)
    if z is not None:
        @pl.when(z > 0)
        def _():
            pl.semaphore_signal(bar, inc=1, device_id=(dp - NX, blk), device_id_type=MESH)

        @pl.when(z < NZ - 1)
        def _():
            pl.semaphore_signal(bar, inc=1, device_id=(dp + NX, blk), device_id_type=MESH)
        count = count + jnp.where(z > 0, 1, 0) + jnp.where(z < NZ - 1, 1, 0)
    pl.semaphore_wait(bar, count)


def gather_ticks(chunks, ins, outs, sems):
    ls, zs, zr, xs, xr, ys, yr, cs, cr = sems
    nslab = len(ins)
    dp, blk = lax.axis_index("dp"), lax.axis_index("blk")
    z, x = dp // NX, lax.rem(dp, NX)
    y, c = blk // 2, lax.rem(blk, 2)
    left, right = (dp - NX, blk), (dp + NX, blk)
    xm, ym, cm = (dp + 1 - 2 * x, blk), (dp, lax.rem(blk + 2, 4)), (dp, blk + 1 - 2 * c)

    locs = [pltpu.make_async_copy(ins[s], outs[s].at[pl.ds(pl.multiple_of(dp * ins[s].shape[0], 16), ins[s].shape[0])], ls.at[s])
            for s in range(nslab)]

    def piece(i, g, q):
        s, c0, n, split = chunks[i]
        rows = ins[s].shape[0]
        h = rows // split
        return outs[s].at[pl.ds(pl.multiple_of(g * rows + q * h, 16), h), pl.ds(c0, n)]

    def myq(i):
        return blk if chunks[i][3] == 4 else c

    def rem(src, dst, a, b, to):
        return pltpu.make_async_remote_copy(src_ref=src, dst_ref=dst, send_sem=a, recv_sem=b, device_id=to, device_id_type=MESH)

    def own(i):
        s, c0, n, split = chunks[i]
        h = ins[s].shape[0] // split
        return ins[s].at[pl.ds(pl.multiple_of(myq(i) * h, 16), h), pl.ds(c0, n)]

    def zcopy(i, d, s, src_own):
        zz = z - s if d == 0 else z + s
        p = piece(i, zz * NX + x, myq(i))
        return rem(own(i) if src_own else p, p, zs.at[i, d, s], zr.at[i, d, s], right if d == 0 else left)

    def zrecv(i, d, s):
        zz = z - 1 - s if d == 0 else z + 1 + s
        p = piece(i, zz * NX + x, myq(i))
        return rem(p, p, zs.at[i, d, s], zr.at[i, d, s], right if d == 0 else left)

    def xcopy(i, zz, src_own=False):
        p = piece(i, zz * NX + x, myq(i))
        return rem(own(i) if src_own else p, p, xs.at[i, zz], xr.at[i, zz], xm)

    def xrecv(i, zz):
        p = piece(i, zz * NX + 1 - x, myq(i))
        return rem(p, p, xs.at[i, zz], xr.at[i, zz], xm)

    def ycopy(i, g):
        p = piece(i, g, blk)
        return rem(p, p, ys.at[i, g], yr.at[i, g], ym)

    def yrecv(i, g):
        p = piece(i, g, lax.rem(blk + 2, 4))
        return rem(p, p, ys.at[i, g], yr.at[i, g], ym)

    def ccopy(i, k, g):
        q = myq(i) if k == 0 else lax.rem(blk + 2, 4)
        p = piece(i, g, q)
        return rem(p, p, cs.at[i, k, g], cr.at[i, k, g], cm)

    def crecv(i, k, g):
        if chunks[i][3] == 4:
            mate = blk + 1 - 2 * c
            q = mate if k == 0 else lax.rem(mate + 2, 4)
        else:
            q = 1 - c
        p = piece(i, g, q)
        return rem(p, p, cs.at[i, k, g], cr.at[i, k, g], cm)

    def spread(i, g):
        if chunks[i][3] == 4:
            ycopy(i, g).start()
        ccopy(i, 0, g).start()

    def begin(i):
        @pl.when(z < NZ - 1)
        def _():
            zcopy(i, 0, 0, True).start()

        @pl.when(z > 0)
        def _():
            zcopy(i, 1, 0, True).start()
        xcopy(i, z, True).start()

    def zstep(i, s):
        @pl.when(z - 1 - s >= 0)
        def _():
            zrecv(i, 0, s).wait_recv()
            if s < NZ - 2:
                @pl.when(z < NZ - 1)
                def _():
                    zcopy(i, 0, s + 1, False).start()
            xcopy(i, z - 1 - s).start()
            spread(i, (z - 1 - s) * NX + x)

        @pl.when(z + 1 + s < NZ)
        def _():
            zrecv(i, 1, s).wait_recv()
            if s < NZ - 2:
                @pl.when(z > 0)
                def _():
                    zcopy(i, 1, s + 1, False).start()
            xcopy(i, z + 1 + s).start()
            spread(i, (z + 1 + s) * NX + x)

    def xstep(i, k):
        def one(zz):
            xrecv(i, zz).wait_recv()
            spread(i, zz * NX + 1 - x)
        if k == 0:
            one(z)
        else:
            pl.when(z - k >= 0)(lambda: one(z - k))
            pl.when(z + k < NZ)(lambda: one(z + k))

    def ystep(i, k):
        g = lax.rem(dp + k, G)
        yrecv(i, g).wait_recv()
        ccopy(i, 1, g).start()

    def cstep(i, k):
        g = lax.rem(dp + k, G)
        crecv(i, 0, g).wait_recv()
        if chunks[i][3] == 4:
            crecv(i, 1, g).wait_recv()

    def sent(i):
        @pl.when(z < NZ - 1)
        def _():
            zcopy(i, 0, 0, True).wait_send()

        @pl.when(z > 0)
        def _():
            zcopy(i, 1, 0, True).wait_send()
        for s in range(NZ - 1):
            if s < NZ - 2:
                @pl.when((z - 1 - s >= 0) & (z < NZ - 1))
                def _():
                    zcopy(i, 0, s + 1, False).wait_send()

                @pl.when((z + 1 + s < NZ) & (z > 0))
                def _():
                    zcopy(i, 1, s + 1, False).wait_send()
        xcopy(i, z, True).wait_send()
        for k in range(1, NZ):
            xcopy(i, lax.rem(z + k, NZ)).wait_send()
        for k in range(1, G):
            g = lax.rem(dp + k, G)
            ccopy(i, 0, g).wait_send()
            if chunks[i][3] == 4:
                ycopy(i, g).wait_send()
                ccopy(i, 1, g).wait_send()

    nch = len(chunks)
    stages = [begin] + [functools.partial(lambda i, s: (zstep(i, s), xstep(i, s)), s=s) for s in range(NZ - 1)]
    stages.append(lambda i: xstep(i, NZ - 1))
    stages.append(lambda i: [ystep(i, k) for k in range(1, G)] if chunks[i][3] == 4 else None)
    stages.append(lambda i: [cstep(i, k) for k in range(1, G)])
    stages.append(sent)

    def first():
        for l in locs:
            l.start()

    def tick(t):
        if t == 6:
            locs[0].wait()
        for s in reversed(range(len(stages))):
            for i in range(nch):
                if AG_STARTS[i] + s == t:
                    stages[s](i)
        if t == AG_STARTS[-1] + len(stages) - 1:
            for l in locs[1:]:
                l.wait()
    return [first] + [functools.partial(tick, t) for t in range(AG_STARTS[-1] + len(stages))]


def gather_sems(n, nch):
    dma = pltpu.SemaphoreType.DMA
    return [dma((n,)), dma((nch, 2, NZ - 1)), dma((nch, 2, NZ - 1)), dma((nch, NZ)), dma((nch, NZ)),
            dma((nch, G)), dma((nch, G)), dma((nch, 2, G)), dma((nch, 2, G))]


def add_into(dst, other, n):
    def body(k, _):
        dst[k] = (dst[k].astype(jnp.float32) + other(k).astype(jnp.float32)).astype(dst.dtype)
        return 0
    lax.fori_loop(0, n, body, 0)


def reduce_ticks(chunks, ins, outs, bufs, sems):
    nch = len(chunks)
    own, crv, yrv, xrv, zrv, fin, s4b = bufs
    ls, cs, cr, ys, yr, xs, xr, zs, zr, fs, fr = sems
    dp, blk = lax.axis_index("dp"), lax.axis_index("blk")
    z, x = dp // NX, lax.rem(dp, NX)
    y, c = blk // 2, lax.rem(blk, 2)
    left, right = (dp - NX, blk), (dp + NX, blk)
    xm, ym, cm = (dp + 1 - 2 * x, blk), (dp, lax.rem(blk + 2, 4)), (dp, blk + 1 - 2 * c)

    def rem(src, dst, a, b, to):
        return pltpu.make_async_remote_copy(src_ref=src, dst_ref=dst, send_sem=a, recv_sem=b, device_id=to, device_id_type=MESH)

    def four(i):
        return chunks[i][3] == 4

    def part(i, core):
        s, c0, n, split = chunks[i]
        cols = pl.ds(c0, n)
        return ins[s].at[:, :, :, core, :, cols] if split == 4 else ins[s].at[:, :, core, :, cols]

    def load(i):
        return pltpu.make_async_copy(part(i, c), own[i], ls.at[i])

    def core_send(i):
        return rem(part(i, 1 - c), crv[i], cs.at[i, 0], cr.at[i, 0], cm)

    def y_send(i):
        return rem(own[i].at[:, :, 1 - y], yrv[i], ys.at[i], yr.at[i], ym)

    def s2(i):
        return yrv[i] if four(i) else own[i]

    def x_send(i):
        return rem(s2(i).at[:, 1 - x], xrv[i], xs.at[i], xr.at[i], xm)

    def z_copy(i, d, lo, hi, first, to):
        src = xrv[i].at[pl.ds(lo, hi - lo)] if first else zrv[i].at[d, pl.ds(lo, hi - lo)]
        return rem(src, zrv[i].at[d, pl.ds(lo, hi - lo)], zs.at[i, d], zr.at[i, d], to)

    def right_send(i, k):
        return z_copy(i, 0, k + 1, NZ, k == 0, right)

    def left_send(i, k):
        return z_copy(i, 1, 0, k, k == NZ - 1, left)

    def st0(i):
        load(i).start()
        core_send(i).start()

    def st1(i):
        load(i).wait()
        core_send(i).wait_recv()

        def body(g, _):
            zz, xx = g // NX, lax.rem(g, NX)
            for yy in ((0, 1) if four(i) else (None,)):
                at = (zz, xx) if yy is None else (zz, xx, yy)
                own[i][at] = (own[i][at].astype(jnp.float32) + crv[i][at].astype(jnp.float32)).astype(jnp.bfloat16)
            return 0
        lax.fori_loop(0, G, body, 0)
        if four(i):
            y_send(i).start()

    def st2(i):
        if four(i):
            y_send(i).wait_recv()

            def body(g, _):
                zz, xx = g // NX, lax.rem(g, NX)
                yrv[i][zz, xx] = (yrv[i][zz, xx].astype(jnp.float32) + own[i][zz, xx, y].astype(jnp.float32)).astype(jnp.bfloat16)
                return 0
            lax.fori_loop(0, G, body, 0)
        x_send(i).start()

    def zstep(i, s):
        if s < NZ - 1:
            @pl.when(z == s)
            def _():
                if s > 0:
                    z_copy(i, 0, s, NZ, False, right).wait_recv()
                    for k in range(s + 1, NZ):
                        zrv[i][0, k] = (zrv[i][0, k].astype(jnp.float32) + xrv[i][k].astype(jnp.float32)).astype(jnp.bfloat16)
                right_send(i, s).start()

            @pl.when(z == NZ - 1 - s)
            def _():
                k0 = NZ - 1 - s
                if s > 0:
                    z_copy(i, 1, 0, k0 + 1, False, left).wait_recv()
                    for k in range(k0):
                        zrv[i][1, k] = (zrv[i][1, k].astype(jnp.float32) + xrv[i][k].astype(jnp.float32)).astype(jnp.bfloat16)
                left_send(i, k0).start()

    def st3(i):
        x_send(i).wait_recv()
        add_into(xrv[i], lambda k: s2(i)[k, x], NZ)
        zstep(i, 0)

    def finish(i):
        q = blk if four(i) else c
        dst = fin[i].at[q] if four(i) else s4b[i]

        def put(v):
            if four(i):
                fin[i][blk] = v.astype(jnp.bfloat16)
            else:
                s4b[i][...] = v.astype(jnp.bfloat16)

        @pl.when(z == 0)
        def _():
            z_copy(i, 1, 0, 1, False, left).wait_recv()
            put(xrv[i][0].astype(jnp.float32) + zrv[i][1, 0].astype(jnp.float32))

        @pl.when(z == NZ - 1)
        def _():
            z_copy(i, 0, NZ - 1, NZ, False, right).wait_recv()
            put(xrv[i][NZ - 1].astype(jnp.float32) + zrv[i][0, NZ - 1].astype(jnp.float32))

        @pl.when((z > 0) & (z < NZ - 1))
        def _():
            put(xrv[i][z].astype(jnp.float32) + zrv[i][0, z].astype(jnp.float32) + zrv[i][1, z].astype(jnp.float32))
        if four(i):
            fin_send(i, 0).start()
            fin_send(i, 1).start()
        else:
            fin_send(i, 0).start()

    def fin_send(i, k):
        if four(i):
            q = blk if k < 2 else lax.rem(blk + 2, 4)
            return rem(fin[i].at[q], fin[i].at[q], fs.at[i, k], fr.at[i, k], ym if k == 0 else cm)
        if k == 0:
            return rem(s4b[i], fin[i].at[2], fs.at[i, 0], fr.at[i, 0], ym)
        return rem(fin[i].at[c], fin[i].at[c], fs.at[i, 1], fr.at[i, 1], cm)

    def fin_recv(i, k):
        if four(i):
            mate = blk + 1 - 2 * c
            q = lax.rem(blk + 2, 4) if k == 0 else mate if k == 1 else lax.rem(mate + 2, 4)
            return rem(fin[i].at[q], fin[i].at[q], fs.at[i, k], fr.at[i, k], cm)
        if k == 0:
            return fin_send(i, 0)
        return rem(fin[i].at[1 - c], fin[i].at[1 - c], fs.at[i, 1], fr.at[i, 1], cm)

    def st8(i):
        fin_recv(i, 0).wait_recv()
        if four(i):
            fin_send(i, 2).start()
        else:
            fin[i][c] = (fin[i][2].astype(jnp.float32) + s4b[i][...].astype(jnp.float32)).astype(jnp.bfloat16)
            fin_send(i, 1).start()

    def st9(i):
        s, c0, n, split = chunks[i]
        for k in ((1, 2) if four(i) else (1,)):
            fin_recv(i, k).wait_recv()
        for q in range(split):
            outs[s][q, :, pl.ds(c0, n)] = fin[i][q]

    def sent(i):
        core_send(i).wait_send()
        if four(i):
            y_send(i).wait_send()
        x_send(i).wait_send()
        for k in range(NZ - 1):
            pl.when(z == k)(lambda k=k: right_send(i, k).wait_send())
            pl.when(z == k + 1)(lambda k=k: left_send(i, k + 1).wait_send())
        for k in range(3 if four(i) else 2):
            fin_send(i, k).wait_send()

    stages = [st1, st2, st3] + [functools.partial(lambda i, s: zstep(i, s), s=s) for s in range(1, NZ - 1)] + [finish, st8, st9, sent]
    def tick(t):
        if t < 0:
            for i in range(min(AHEAD, nch)):
                st0(i)
            return
        if t + AHEAD < nch:
            st0(t + AHEAD)
        for s in reversed(range(len(stages))):
            i = t - OFFSETS[s]
            if 0 <= i < nch:
                stages[s](i)
    return [functools.partial(tick, t) for t in range(-1, nch + max(OFFSETS))]


def slab_split(k):
    return next(ch[3] for ch in RS_CHUNKS if ch[0] == k)


def slab_rows(geo, k):
    return (geo.ff // geo.n_dp if k == 3 else geo.gp) // slab_split(k)


def slab_view(geo, k, ref):
    lead = (NZ, NX, 2, 2) if slab_split(k) == 4 else (NZ, NX, 2)
    return ref.reshape(*lead, slab_rows(geo, k), ref.shape[1])


def reduce_scratch(geo, chunks):
    nch = len(chunks)
    dma = pltpu.SemaphoreType.DMA

    def shapes(kind):
        out = []
        for s, c0, nc, split in chunks:
            h = slab_rows(geo, s)
            lead = (NZ, NX, 2) if split == 4 else (NZ, NX)
            tiny = (1, 16, 128)
            shape = (lead + (h, nc), lead + (h, nc), (NZ, NX, h, nc) if split == 4 else tiny, (NZ, h, nc), (2, NZ, h, nc),
                     (4 if split == 4 else 3, h, nc), (h, nc) if split == 2 else tiny)[kind]
            out.append(pltpu.VMEM(shape, jnp.bfloat16))
        return out
    sems = [dma((nch,)), dma((nch, 1)), dma((nch, 1)), dma((nch,)), dma((nch,)), dma((nch,)), dma((nch,)),
            dma((nch, 2)), dma((nch, 2)), dma((nch, 3)), dma((nch, 3))]
    return [shapes(k) for k in range(7)], sems


def reduce_outs(geo):
    cols = (COLS_A, geo.dp, 2 * geo.ff, geo.dp)
    return [Out((slab_split(k), slab_rows(geo, k), cols[k]), BF) for k in range(4)]


A_TICKS = 8
AG_STARTS = (0, 1, 2, 3, 4)
AG_CHUNKS = [(0, 0, 1664, 4), (1, 0, 1024, 2), (2, 0, 2560, 4), (2, 2560, 2560, 4), (3, 0, 1024, 2)]
RS_CHUNKS = [(2, 0, 640, 4), (3, 0, 256, 2), (2, 640, 640, 4), (2, 1280, 640, 4), (3, 256, 256, 2), (2, 1920, 640, 4),
             (2, 2560, 640, 4), (3, 512, 256, 2), (2, 3200, 640, 4), (2, 3840, 640, 4), (3, 768, 256, 2), (2, 4480, 640, 4),
             (0, 0, 896, 4), (1, 0, 512, 2), (0, 896, 768, 4), (1, 512, 512, 2)]
RS_CHUNKS_READY = 12 - AHEAD + 1


def pad_to(v, shape):
    return jnp.pad(v, [(0, b - a) for a, b in zip(v.shape, shape)])


def pad_cols(v, geo):
    v = v.reshape(v.shape[0], geo.n_dp, geo.gw)
    return jnp.pad(v, ((0, 0), (0, 0), (0, geo.gp - geo.gw))).reshape(v.shape[0], geo.dp)


def unpad_cols(v, geo):
    return v.reshape(v.shape[0], geo.n_dp, geo.gp)[:, :, :geo.gw].reshape(v.shape[0], geo.d)


def pack(geo, q, k, v, o, g, u, d, g1, g2, rt):
    rows = q.shape[0]
    kv = jnp.concatenate([k.reshape(rows, KV_HEADS, 64), v.reshape(rows, KV_HEADS, 64)], axis=2).reshape(rows, 640)
    small = pad_to(jnp.concatenate([g1[:, None], g2[:, None], rt], axis=1), (rows, 64))
    a = pad_to(jnp.concatenate([q, small, kv], axis=1), (geo.gp, COLS_A))
    gu = pad_to(jnp.concatenate([g, u], axis=1), (geo.gp, 2 * geo.ff))
    return a, pad_to(pad_cols(o, geo), (geo.gp, geo.dp)), gu, pad_cols(d, geo)


def unpack(geo, slabs):
    a, o, gu, d = (w.reshape(-1, w.shape[-1]) for w in slabs)
    a, o, gu = a[:geo.gw], o[:geo.gw], gu[:geo.gw]
    kv = a[:, 1024:].reshape(geo.gw, KV_HEADS, 128)
    return tuple(w.astype(F32) for w in (a[:, :960], kv[:, :, :64].reshape(geo.gw, 320), kv[:, :, 64:].reshape(geo.gw, 320), unpad_cols(o, geo),
            gu[:, :geo.ff], gu[:, geo.ff:], unpad_cols(d, geo), a[:, 960], a[:, 961], a[:, 962:965]))


def mates():
    dp, blk = lax.axis_index("dp"), lax.axis_index("blk")
    y, c = blk // 2, lax.rem(blk, 2)
    return dp, blk, y, c, (dp, lax.rem(blk + 2, 4)), (dp, blk + 1 - 2 * c)


class Share:
    def __init__(self, own, out, ssem, rsem):
        dp, blk, y, c, ym, cm = mates()

        def rem(src, b, k, to):
            return pltpu.make_async_remote_copy(src_ref=src, dst_ref=out.at[b], send_sem=ssem.at[k], recv_sem=rsem.at[k],
                                                device_id=to, device_id_type=MESH)
        far, near = lax.rem(blk + 2, 4), blk + 1 - 2 * c
        both = lax.rem(near + 2, 4)
        self.out = [rem(own, blk, 0, ym), rem(own, blk, 1, cm), rem(out.at[far], far, 2, cm)]
        self.come = [rem(out.at[far], far, 0, ym), rem(out.at[near], near, 1, cm), rem(out.at[both], both, 2, cm)]

    def start(self):
        self.out[0].start()
        self.out[1].start()

    def forward(self):
        self.come[0].wait_recv()
        self.out[2].start()

    def arrive(self):
        self.come[1].wait_recv()
        self.come[2].wait_recv()

    def sent(self):
        for v in self.out:
            v.wait_send()


def give(dkv, out, got1, half, got2, ssem, rsem):
    dp, blk, y, c, ym, cm = mates()

    def rem(src, dst, k, to):
        return pltpu.make_async_remote_copy(src_ref=src, dst_ref=dst, send_sem=ssem.at[k], recv_sem=rsem.at[k],
                                            device_id=to, device_id_type=MESH)
    first = [rem(dkv.at[2 * yy + 1 - c], got1.at[yy], yy, cm) for yy in range(2)]
    for f in first:
        f.start()
    for f in first:
        f.wait_recv()
    half[...] = (got1[1 - y].astype(F32) + dkv[2 * (1 - y) + c].astype(F32)).astype(BF)
    second = rem(half, got2, 2, ym)
    second.start()
    mine = got1[y].astype(F32) + dkv[2 * y + c].astype(F32)
    second.wait_recv()
    out[...] = mine + got2[...].astype(F32)
    for f in first + [second]:
        f.wait_send()


def per_device(block_input, cotangent, seq_lengths, routes_two, routes_three, query_weight, key_weight, value_weight, output_weight,
               gate_weight, up_weight, down_weight, first_gain, second_gain, router_weight):
    micro, seqs, bl, d = block_input.shape
    n_dp, n_blk = lax.axis_size("dp"), lax.axis_size("blk")
    count = micro * seqs
    geo = Geo(count, bl, n_dp, n_blk, d, gate_weight.shape[1], (None, routes_two.shape[2], routes_three.shape[2]))
    slabs = pack(geo, query_weight, key_weight, value_weight, output_weight, gate_weight, up_weight, down_weight, first_gain,
                 second_gain, router_weight)
    out, grad, shards = block(geo, block_input.reshape(count * bl, d), cotangent.reshape(count * bl, d), seq_lengths.reshape(count),
                (routes_two.reshape(count, -1), routes_three.reshape(count, -1)), slabs,
                lambda kv: lax.all_gather(kv, "blk", axis=0, tiled=False),
                              lambda dkv: lax.psum_scatter(dkv, "blk", scatter_dimension=0, tiled=False).astype(F32))
    return (out.reshape(block_input.shape), grad.reshape(block_input.shape)) + unpack(geo, shards)


def solution(mesh):
    in_specs = (
        P(None, "dp", "blk", None),
        P(None, "dp", "blk", None),
        P(None, "dp"),
        P(None, "dp", None),
        P(None, "dp", None),
        P("dp", None),
        P("dp", None),
        P("dp", None),
        P("dp", None),
        P("dp", None),
        P("dp", None),
        P("dp", None),
        P("dp"),
        P("dp"),
        P("dp", None),
    )
    out_specs = (
        P(None, "dp", "blk", None),
        P(None, "dp", "blk", None),
        P("dp", None),
        P("dp", None),
        P("dp", None),
        P("dp", None),
        P("dp", None),
        P("dp", None),
        P("dp", None),
        P("dp"),
        P("dp"),
        P("dp", None),
    )
    return jax.shard_map(
        per_device, mesh=mesh, in_specs=in_specs, out_specs=out_specs, check_vma=False
    )
```

```python
import functools
import math
import types

import jax
import jax.numpy as jnp
import numpy as np
from jax import lax
from jax.experimental import pallas as pl
from jax.experimental.pallas import tpu as pltpu
from jax.sharding import PartitionSpec as P

HEADS, KV_HEADS, HEAD_DIM, RECUR = 15, 5, 64, 3
GROUP = HEADS // KV_HEADS
eps = 1e-05
rope_base = 10000.0
masked_fill = -1e30
BF, F32 = jnp.bfloat16, jnp.float32
COLS_A = 1664
FT = 512


def dot(a, b):
    return lax.dot_general(a, b, (((1,), (0,)), ((), ())), preferred_element_type=F32)


def dot_nt(a, b):
    return lax.dot_general(a, b, (((1,), (1,)), ((), ())), preferred_element_type=F32)


def dot_tn(a, b):
    return lax.dot_general(a, b, (((0,), (0,)), ((), ())), preferred_element_type=F32)


def halves(v):
    high = v.astype(BF)
    return high, (v - high.astype(F32)).astype(BF)


def pick(choice, v):
    high, low = halves(v)
    return dot(choice, high) + dot(choice, low)


def put_back(choice, v):
    high, low = halves(v)
    return dot_tn(choice, high) + dot_tn(choice, low)


def lanes(shape):
    return lax.broadcasted_iota(jnp.int32, shape, len(shape) - 1)


def rowid(shape):
    return lax.broadcasted_iota(jnp.int32, shape, len(shape) - 2)


def swapped(x):
    first = lax.rem(lanes(x.shape), 64) < 32
    return jnp.where(first, pltpu.roll(x, 96, 1), pltpu.roll(x, 32, 1))


class Far:
    def __init__(self, value):
        self.value = value


class Words:
    def __init__(self, value):
        self.value = value


class Out:
    def __init__(self, shape, dtype=F32, far=False):
        self.shape, self.dtype, self.far = shape, dtype, far


def join(*parts, **more):
    got = types.SimpleNamespace()
    for p in parts + (more,):
        vars(got).update(p if isinstance(p, dict) else vars(p))
    return got


def call(name, body, ins, outs, scratch=None, limit=63, **params):
    flat_in, tree_in = jax.tree.flatten(ins)
    flat_out, tree_out = jax.tree.flatten(outs)
    flat_scratch, tree_scratch = jax.tree.flatten(scratch or {})
    n_in, n_out = len(flat_in), len(flat_out)

    def kernel(*refs):
        body(join(tree_in.unflatten(refs[:n_in]), tree_out.unflatten(refs[n_in:n_in + n_out]),
                  tree_scratch.unflatten(refs[n_in + n_out:])))

    vm, far = pl.BlockSpec(memory_space=pltpu.VMEM), pl.BlockSpec(memory_space=pl.ANY)
    words = pl.BlockSpec(memory_space=pltpu.SMEM)
    got = pl.pallas_call(
        kernel,
        out_shape=[jax.ShapeDtypeStruct(o.shape, o.dtype) for o in flat_out],
        in_specs=[far if isinstance(v, Far) else words if isinstance(v, Words) else vm for v in flat_in],
        out_specs=[far if o.far else vm for o in flat_out],
        scratch_shapes=flat_scratch,
        compiler_params=pltpu.CompilerParams(vmem_limit_bytes=limit << 20, **params),
        name=name,
    )(*[v.value if isinstance(v, (Far, Words)) else v for v in flat_in])
    return types.SimpleNamespace(**tree_out.unflatten(got))


class Geo:
    def __init__(self, ns, bl, n_dp, n_blk, d, ff, tops):
        self.ns, self.bl, self.n_dp, self.n_blk, self.d, self.ff = ns, bl, n_dp, n_blk, d, ff
        self.gw = d // n_dp
        self.gp = -(-self.gw // 16) * 16
        self.dp = n_dp * self.gp
        self.slots = (bl, bl // 2, bl // 4)
        self.tops = tops

    def rows(self, r):
        return self.ns * self.slots[r]

    def keys(self, r):
        return self.n_blk * self.slots[r]

    def spread(self):
        e = np.zeros((1024, self.dp), np.float32)
        f = np.arange(self.d)
        e[f, f // self.gw * self.gp + f % self.gw] = 1
        return jnp.asarray(e, BF)

    def tables(self):
        f = rope_base ** (-(np.arange(32, dtype=np.float64) * 2.0) / 64)
        f32 = np.asarray(f, np.float32)
        ph = (np.arange(self.bl * self.n_blk, dtype=np.float32)[:, None] * f32).astype(np.float32).astype(np.float64)
        c, s = np.cos(ph), np.sin(ph)
        cos = np.concatenate([c, c, c, c], 1).astype(np.float32)
        sin = np.concatenate([-s, s, -s, s], 1).astype(np.float32)
        return jnp.asarray(cos), jnp.asarray(sin)


def gains(wa):
    sel = (lanes((8, 128)) == rowid((8, 128)) + 64).astype(BF)
    return dot_nt(sel, wa[:, 896:1024])


def choose(geo, r, routes, blk):
    s, t, bl = geo.slots[r], geo.tops[r], geo.bl
    before = jnp.sum((routes < blk * bl).astype(F32), axis=1, keepdims=True).astype(jnp.int32)
    shift = ((lanes((s, t)) - rowid((s, t))) == before).astype(BF)
    here = (routes == rowid((bl, t)) + blk * bl).astype(BF)
    return dot_nt(shift, here).astype(BF)


def allowed(geo, r, routes, blk, turned, heads=GROUP):
    s, kn, bl = geo.slots[r], geo.keys(r), geo.bl
    shape = (kn, heads * s) if turned else (heads * s, kn)
    key = rowid(shape) if turned else lanes(shape)
    query = lax.rem(lanes(shape) if turned else rowid(shape), s)
    ok = key <= blk * s + query
    if r > 0:
        t = geo.tops[r]
        inside = (routes // bl == rowid((kn, t)) // s)
        if turned:
            count = jnp.sum(inside.astype(F32), axis=1, keepdims=True)
        else:
            count = dot_nt(jnp.ones((8, t), BF), inside.astype(BF))[0:1]
        ok = ok & (lax.rem(key, s).astype(F32) < count)
    return jnp.where(ok, 0.0, masked_fill)


def project_kv(geo, r, k):
    a = k.a[...].astype(F32)
    n1 = lax.rsqrt(jnp.sum(a * a, axis=-1, keepdims=True) * (1.0 / geo.d) + eps)
    k.u[...] = (a * n1 * k.gn[0:1]).astype(BF)
    k.st[...] = jnp.where(lanes(k.st.shape) == 0, n1, 0.0)
    u = k.u[...]
    cos, sin = k.cos[...], k.sin[...]
    left = lanes(cos.shape) < 64
    ckv, skv = jnp.where(left, cos, 1.0), jnp.where(left, sin, 0.0)
    for c0, n in ((1024, 256), (1280, 256), (1536, 128)):
        some = dot(u, k.wa[:, c0:c0 + n])
        for j in range(n // 128):
            x = some[:, 128 * j:128 * j + 128]
            k.kv[:, c0 - 1024 + 128 * j:c0 - 1024 + 128 * j + 128] = (x * ckv + swapped(x) * skv).astype(BF)


def project_q(geo, r, k):
    u = k.u[...]
    cos, sin = k.cos[...], k.sin[...]
    left = lanes(cos.shape) < 64
    for t in range(4):
        both = dot(u, k.wa[:, 256 * t:256 * t + 256])
        for j in range(2):
            x = both[:, 128 * j:128 * j + 128]
            x = (x * cos + swapped(x) * sin).astype(BF).astype(F32) * 0.125
            h = 4 * t + 2 * j
            k.q16[h] = jnp.where(left, x, 0.0).astype(BF)
            if h + 1 < HEADS:
                k.q16[h + 1] = jnp.where(left, pltpu.roll(x, 64, 1), 0.0).astype(BF)


def project(geo, r, k):
    project_kv(geo, r, k)
    project_q(geo, r, k)


def select_rows(geo, r, k, blk):
    s, bl = geo.slots[r], geo.bl
    for m in range(geo.ns):
        ch = choose(geo, r, k.routes[m:m + 1], blk)
        k.choice[m] = ch
        k.a[m * s:m * s + s] = pick(ch, k.h[m * bl:m * bl + bl])
        k.cos[m * s:m * s + s] = pick(ch, k.cosb[...])
        k.sin[m * s:m * s + s] = pick(ch, k.sinb[...])


def attend(geo, r, k, blk, pause=None):
    s, kn = geo.slots[r], geo.keys(r)

    def seq(m, _):
        row0 = m * s if isinstance(m, int) else pl.multiple_of(m * s, s)
        k.kvg[...] = k.kvall[:, m].reshape(kn, KV_HEADS * 128)
        k.bias[...] = allowed(geo, r, k.routes[pl.ds(m, 1)] if r else None, blk, False)
        k.col[...] = jnp.zeros(k.col.shape, F32)

        def group(g, _):
            kvh = k.kvg[:, pl.ds(pl.multiple_of(g * 128, 128), 128)]
            sc = dot_nt(k.q16[pl.ds(g * GROUP, GROUP), pl.ds(row0, s)].reshape(GROUP * s, 128), kvh) + k.bias[...]
            top = jnp.max(sc, axis=-1, keepdims=True)
            p = jnp.exp(sc - top)
            total = jnp.sum(p, axis=-1, keepdims=True)
            k.o16[pl.ds(g * GROUP, GROUP)] = (dot(p.astype(BF), kvh) * (1.0 / total)).reshape(GROUP, s, 128)
            k.col[...] = jnp.where(lanes(k.col.shape) == g, top + jnp.log(total), k.col[...])
            return 0
        if pause is None:
            lax.fori_loop(0, KV_HEADS, group, 0)
        else:
            lax.fori_loop(0, 3, group, 0)
            pause()
            lax.fori_loop(3, KV_HEADS, group, 0)
        left = lanes((s, 128)) < 64
        for t in range(8):
            odd = k.o16[2 * t + 1] if 2 * t + 1 < HEADS else 0.0
            k.o[pl.ds(row0, s), 128 * t:128 * t + 128] = jnp.where(left, pltpu.roll(k.o16[2 * t], 64, 1), odd).astype(BF)
        k.lse[m] = k.col[...].T[0:8]
        return 0
    if pause is None:
        lax.fori_loop(0, geo.ns, seq, 0)
    else:
        for m in range(geo.ns):
            seq(m, 0)
            pause()


class Tiles:
    def __init__(self, geo, k, pre=None):
        self.k, self.n, self.ff, self.pre = k, geo.ff // FT, geo.ff, pre

    def parts(self, t, slot):
        k, c0 = self.k, t * FT
        if not isinstance(t, int):
            c0 = pl.multiple_of(c0, FT)
        cu = c0 + self.ff
        return [pltpu.make_async_copy(k.gu.at[:, pl.ds(c0, FT)], k.gbuf.at[slot], k.tsem.at[slot, 0]),
                pltpu.make_async_copy(k.gu.at[:, pl.ds(cu, FT)], k.ubuf.at[slot], k.tsem.at[slot, 1]),
                pltpu.make_async_copy(k.wd.at[pl.ds(c0, FT)], k.dbuf.at[slot], k.tsem.at[slot, 2])] + [
                    pltpu.make_async_copy(v.at[:, pl.ds(c0, FT)], k.pre.at[slot, j], k.tsem.at[slot, 3 + j])
                    for j, v in enumerate(self.pre or ())]

    def start(self, t, slot):
        for c in self.parts(t, slot):
            c.start()

    def loop(self, step):
        def body(t, _):
            slot = lax.rem(t, 2)

            @pl.when(t + 1 < self.n)
            def _():
                self.start(t + 1, 1 - slot)
            for c in self.parts(t, slot):
                c.wait()
            step(t, slot)
            return 0
        lax.fori_loop(0, self.n, body, 0)

    @staticmethod
    def scratch(geo):
        return dict(gbuf=pltpu.VMEM((2, geo.dp, FT), BF), ubuf=pltpu.VMEM((2, geo.dp, FT), BF),
                    dbuf=pltpu.VMEM((2, FT, geo.dp), BF), tsem=pltpu.SemaphoreType.DMA((2, 5)))


def feed(geo, r, k, blk, tiles):
    s, bl = geo.slots[r], geo.bl
    y = dot(k.o[...], k.wou[...])
    a = k.a[...].astype(F32)
    b = a + y
    n2 = lax.rsqrt(jnp.sum(b * b, axis=-1, keepdims=True) * (1.0 / geo.d) + eps)
    gate = jax.nn.sigmoid(jnp.sum(a * k.gn[2 + r:3 + r], axis=-1, keepdims=True))
    k.b[...] = b.astype(BF)
    k.w[...] = (b * n2 * k.gn[1:2]).astype(BF)
    lane = lanes((geo.rows(r), 128))
    k.sx[...] = jnp.where(lane == 0, n2, jnp.where(lane == 1, gate, 0.0))
    k.acc[...] = y

    def wide(t, slot):
        c0 = t * FT if isinstance(t, int) else pl.multiple_of(t * FT, FT)
        return [pltpu.make_async_copy(k.keep.at[slot, j], ref.at[:, pl.ds(c0, FT)], k.ksem.at[slot, j])
                for j, ref in enumerate((k.gp, k.up))]

    def step(t, slot):
        @pl.when(t >= 2)
        def _():
            for c in wide(t - 2, slot):
                c.wait()
        gp = dot(k.w[...], k.gbuf[slot])
        up = dot(k.w[...], k.ubuf[slot])
        k.keep[slot, 0] = gp.astype(BF)
        k.keep[slot, 1] = up.astype(BF)
        z = (gp * jax.nn.sigmoid(gp) * up).astype(BF)
        k.acc[...] += dot(z, k.dbuf[slot])
        for c in wide(t, slot):
            c.start()
    tiles.loop(step)
    for t in range(max(tiles.n - 2, 0), tiles.n):
        for c in wide(t, t % 2):
            c.wait()
    yf = k.acc[...]
    k.yf[...] = yf.astype(BF)
    delta = yf * k.sx[:, 1:2]
    for m in range(geo.ns):
        if r == 0:
            here = rowid((bl, 1)) + blk * bl < k.lens[m]
            rows = slice(m * bl, m * bl + bl)
            k.h2[rows] = k.a[rows].astype(F32) + jnp.where(here, delta[rows], 0.0)
        else:
            k.h2[m * bl:m * bl + bl] = k.h[m * bl:m * bl + bl] + put_back(k.choice[m], delta[m * s:m * s + s])


def back_feed(geo, r, k, blk, tiles):
    s, bl, rows = geo.slots[r], geo.bl, geo.rows(r)
    k.small[...] = jnp.zeros(k.small.shape, F32)

    def incoming(m):
        here = slice(m * s, m * s + s)
        if r == 0:
            return jnp.where(rowid((bl, 1)) + blk * bl < k.lens[m], k.dh[here], 0.0)
        return k.inc[here]
    for m in range(geo.ns):
        here = slice(m * s, m * s + s)
        if r > 0:
            k.inc[here] = pick(k.choice[m], k.dh[m * bl:m * bl + bl])
        inc = incoming(m)
        gate = k.sx[here, 1:2]
        dg = jnp.sum(inc * k.yf[here].astype(F32), axis=-1, keepdims=True)
        dl = dg * gate * (1.0 - gate)
        k.tok[here] = inc + dl * k.gn[2 + r:3 + r]
        k.small[2 + r:3 + r] += jnp.sum(k.a[here].astype(F32) * dl, axis=0, keepdims=True)
        k.df[here] = (gate * inc).astype(BF)
    k.acc[...] = jnp.zeros(k.acc.shape, F32)

    def wide(t, slot):
        c0 = t * FT if isinstance(t, int) else pl.multiple_of(t * FT, FT)
        return [pltpu.make_async_copy(k.wide.at[slot, j], ref.at[:, pl.ds(c0, FT)], k.wsem.at[slot, j])
                for j, ref in enumerate((k.dgp, k.dup, k.z))]

    def step(t, slot):
        @pl.when(t >= 2)
        def _():
            for c in wide(t - 2, slot):
                c.wait()
        dz = dot_nt(k.df[...], k.dbuf[slot])
        gp = k.pre[slot, 0].astype(F32)
        up = k.pre[slot, 1].astype(F32)
        sig = jax.nn.sigmoid(gp)
        silu = gp * sig
        k.wide[slot, 2] = (silu * up).astype(BF)
        dup = (dz * silu).astype(BF)
        dgp = (dz * up * (sig * (1.0 + gp * (1.0 - sig)))).astype(BF)
        k.wide[slot, 1] = dup
        k.wide[slot, 0] = dgp
        k.acc[...] += dot_nt(dgp, k.gbuf[slot]) + dot_nt(dup, k.ubuf[slot])
        for c in wide(t, slot):
            c.start()
    tiles.loop(step)
    for t in range(max(tiles.n - 2, 0), tiles.n):
        for c in wide(t, t % 2):
            c.wait()
    for m in range(geo.ns):
        here = slice(m * s, m * s + s)
        n2, gate = k.sx[here, 0:1], k.sx[here, 1:2]
        dw = k.acc[here]
        b = k.b[here].astype(F32)
        k.small[1:2] += jnp.sum(dw * (b * n2), axis=0, keepdims=True)
        t = dw * k.gn[1:2]
        db = n2 * t - n2 * n2 * n2 * b * (jnp.sum(t * b, axis=-1, keepdims=True) * (1.0 / geo.d))
        k.tok[here] += db
        k.dy[here] = (gate * incoming(m) + db).astype(BF)


def back_out(geo, r, k):
    s, kn = geo.slots[r], geo.keys(r)
    rows = geo.rows(r)
    left = lanes((rows, 128)) < 64
    lane = lanes((rows, 128))
    dcol = jnp.zeros((rows, 128), F32)
    for t in range(8):
        x = dot_nt(k.dy[...], k.wou[128 * t:128 * t + 128])
        x = x.astype(BF).astype(F32)
        prod = x * k.o[:, 128 * t:128 * t + 128].astype(F32)
        even = jnp.sum(jnp.where(left, prod, 0.0), axis=-1, keepdims=True)
        dcol = jnp.where(lane == 2 * t, even, dcol)
        k.do16[2 * t] = jnp.where(left, 0.0, pltpu.roll(x, 64, 1)).astype(BF)
        if 2 * t + 1 < HEADS:
            odd = jnp.sum(jnp.where(left, 0.0, prod), axis=-1, keepdims=True)
            dcol = jnp.where(lane == 2 * t + 1, odd, dcol)
            k.do16[2 * t + 1] = jnp.where(left, 0.0, x).astype(BF)
    k.dcol[...] = dcol


def back_attend(geo, r, k, blk, pause=None):
    s, kn = geo.slots[r], geo.keys(r)
    batch = GROUP if pause is None else 1

    def seq(m, _):
        row0 = m * s if isinstance(m, int) else pl.multiple_of(m * s, s)
        if pause is None:
            k.kvg[...] = k.kvall[:, m].reshape(kn, KV_HEADS * 128)
        else:
            loads = [pltpu.make_async_copy(k.kvall.at[b, m], k.kvg.at[pl.ds(b * s, s)], k.lsem.at[b]) for b in range(geo.n_blk)]
            for v in loads:
                v.start()
            for v in loads:
                v.wait()
        for g in range(KV_HEADS):
            k.kvt[g] = k.kvg[:, 128 * g:128 * g + 128].astype(F32).T.astype(BF)
        k.bias[...] = allowed(geo, r, k.routes[pl.ds(m, 1)] if r else None, blk, True, batch)
        dt = k.dcol[pl.ds(row0, s)].T
        for h in range(HEADS):
            k.dt[h // GROUP:h // GROUP + 1, h % GROUP * s:(h % GROUP + 1) * s] = dt[h:h + 1]
        k.ct[0] = k.cos[pl.ds(row0, s)].T[0:32] * 0.125
        k.ct[1] = k.sin[pl.ds(row0, s)].T[32:64] * 0.125

        def group(g, _):
            lane0 = pl.multiple_of(g * 128, 128)
            kvh = k.kvg[:, pl.ds(lane0, 128)]
            total = None
            for j0 in range(0, GROUP, batch):
                heads = (pl.ds(g * GROUP + j0, batch), pl.ds(row0, s))
                cols = slice(j0 * s, (j0 + batch) * s)
                qh, doh = k.q16[heads].reshape(batch * s, 128), k.do16[heads].reshape(batch * s, 128)
                p = jnp.exp(dot_nt(kvh, qh) + k.bias[...] - k.lse[m, pl.ds(g, 1), cols])
                ds = (p * (dot_nt(kvh, doh) - k.dt[pl.ds(g, 1), cols])).astype(BF)
                part = dot(ds, qh) + dot(p.astype(BF), doh)
                total = part if total is None else total + part
                dqt = dot(k.kvt[g], ds)
                c, sn = k.ct[0], k.ct[1]
                for j in range(batch):
                    y1, y2 = dqt[0:32, j * s:j * s + s], dqt[32:64, j * s:j * s + s]
                    k.dqt[g * GROUP + j0 + j, 0:32] = (y1 * c + y2 * sn)
                    k.dqt[g * GROUP + j0 + j, 32:64] = (y2 * c - y1 * sn)
            total = total.astype(BF).reshape(geo.n_blk, s, 128)
            if pause is None:
                k.dkv[:, m, :, pl.ds(lane0, 128)] = total
            else:
                k.dkvm[:, :, pl.ds(lane0, 128)] = total
            return 0
        if pause is None:
            lax.fori_loop(0, KV_HEADS, group, 0)
        else:
            lax.fori_loop(0, 3, group, 0)
            pause()
            lax.fori_loop(3, KV_HEADS, group, 0)
            store = pltpu.make_async_copy(k.dkvm, k.dkv.at[:, m], k.lsem.at[0])
            store.start()
        for t in range(8):
            if 2 * t + 1 < HEADS:
                x = k.dqt[2 * t:2 * t + 2].reshape(128, s).T
            else:
                x = jnp.concatenate([k.dqt[2 * t], jnp.zeros((64, s), F32)], axis=0).T
            k.da[pl.ds(row0, s), 128 * t:128 * t + 128] = x.astype(BF)
        if pause is not None:
            store.wait()
        return 0
    if pause is None:
        lax.fori_loop(0, geo.ns, seq, 0)
    else:
        for m in range(geo.ns):
            seq(m, 0)
            pause()


def back_project(geo, r, k, blk):
    s, bl, rows = geo.slots[r], geo.bl, geo.rows(r)
    cos, sin = k.cos[...], k.sin[...]
    left = lanes(cos.shape) < 64
    ckv, skv = jnp.where(left, cos, 1.0), jnp.where(left, sin, 0.0)
    k.da2[:, 0:1024] = k.da[...]
    for g in range(KV_HEADS):
        x = k.dkvown[:, 128 * g:128 * g + 128].astype(F32)
        k.da2[:, 1024 + 128 * g:1152 + 128 * g] = (x * ckv - swapped(x) * skv).astype(BF)
    for m in range(geo.ns):
        here = slice(m * bl, m * bl + bl)
        mine = slice(m * s, m * s + s)
        du = dot_nt(k.da2[mine], k.wa[...])
        a = k.a[mine].astype(F32)
        n1 = k.st[mine, 0:1]
        k.first[0:1] += jnp.sum(du * (a * n1), axis=0, keepdims=True)
        t1 = du * k.gn[0:1]
        tok = k.tok[mine] + n1 * t1 - n1 * n1 * n1 * a * (jnp.sum(t1 * a, axis=-1, keepdims=True) * (1.0 / geo.d))
        if r == 0:
            ok = rowid((bl, 1)) + blk * bl < k.lens[m]
            k.dh2[here] = jnp.where(ok, tok, k.dh[here])
        else:
            k.dh2[here] = k.dh[here] + put_back(k.choice[m], tok - k.inc[mine])


def block(geo, x, cot, lens, routes, slabs, share, give_back):
    blk_of = lambda: lax.axis_index("blk")
    bl, d, dp, ff, nsq, nb = geo.bl, geo.d, geo.dp, geo.ff, geo.ns, geo.n_blk
    full = nsq * bl
    cos_all, sin_all = geo.tables()
    b0 = lax.axis_index("blk") * bl
    cosb = lax.dynamic_slice_in_dim(cos_all, b0, bl, 0)
    sinb = lax.dynamic_slice_in_dim(sin_all, b0, bl, 0)
    spread = geo.spread()
    R, S, KN = [geo.rows(r) for r in range(3)], geo.slots, [geo.keys(r) for r in range(3)]
    V, dma = pltpu.VMEM, pltpu.SemaphoreType.DMA
    lens = Words(lens)

    def proj_outs(r, kv=True):
        more = dict(choice=Out((nsq, S[r], bl), BF)) if r else {}
        more = dict(kv=Out((R[r], 640), BF), **more) if kv else more
        return dict(a=Out((R[r], dp), F32 if r else BF), u=Out((R[r], dp), BF), q16=Out((HEADS, R[r], 128), BF), st=Out((R[r], 128)), cos=Out((R[r], 128)), sin=Out((R[r], 128)), **more)

    def seen_outs(r):
        return dict(o=Out((R[r], 1024), BF), lse=Out((nsq, 8, GROUP * S[r])))

    def fore_outs(r):
        return dict(**(seen_outs(r) if r else {}), b=Out((R[r], dp), BF), w=Out((R[r], dp), BF),
                    gp=Out((R[r], ff), BF, True), up=Out((R[r], ff), BF, True), yf=Out((R[r], dp), BF), sx=Out((R[r], 128)))

    def seen_scratch(r):
        return dict(kvg=V((KN[r], 640), BF), bias=V((GROUP * S[r], KN[r]), F32), col=V((GROUP * S[r], 128), F32),
                    o16=V((HEADS, S[r], 128), F32))

    def fore_scratch(r):
        return dict(acc=V((R[r], dp), F32), keep=V((2, 2, R[r], FT), BF), ksem=dma((2, 2)), **(seen_scratch(r) if r else {}))

    def feed_outs(r):
        more = dict(inc=Out((R[r], dp))) if r else {}
        return dict(tok=Out((R[r], dp)), df=Out((R[r], dp), BF), dgp=Out((R[r], ff), BF, True), dup=Out((R[r], ff), BF, True),
                    z=Out((R[r], ff), BF, True), dy=Out((R[r], dp), BF), small=Out((8, dp)), **more)

    def feed_scratch(r):
        return dict(acc=V((R[r], dp), F32), pre=V((2, 2, R[r], FT), BF), wide=V((2, 3, R[r], FT), BF), wsem=dma((2, 3)))

    def turned_outs(r):
        piece = (nsq, S[r], 640)
        last = dict(dkvown=Out(piece)) if near and r else dict(dkv=Out((nb,) + piece, BF))
        return dict(da=Out((R[r], 1024), BF), **last)

    def out_parts(make, r=0):
        return dict(do16=make((HEADS, R[r], 128), BF), dcol=make((R[r], 128), F32))

    def turned_scratch(r, batch=GROUP):
        return dict(kvg=V((KN[r], 640), BF), kvt=V((KV_HEADS, 128, KN[r]), BF), bias=V((KN[r], batch * S[r]), F32), dt=V((8, GROUP * S[r]), F32), ct=V((2, 32, S[r]), F32),
                    dqt=V((HEADS, 64, S[r]), F32), **(out_parts(V, r) if r else {}))

    near = (geo.n_dp, geo.n_blk) == (G, 4)

    def share_scratch(r):
        return dict(kv=V((R[r], 640), BF), own=V((nsq, S[r], 640), BF), ssem=dma((3,)), rsem=dma((3,)))

    def give_scratch(r):
        piece = (nsq, S[r], 640)
        return dict(dkv=V((nb,) + piece, BF), got1=V((2,) + piece, BF), half=V(piece, BF), got2=V(piece, BF), ssem=dma((3,)),
                    rsem=dma((3,)))

    P, F, B, T, L = [None] * 3, [None] * 3, [None] * 3, [None] * 3, [None] * 3
    rt = [None] + list(routes)

    def begin(k):
        k.a[...] = dot(k.x[...], k.spread[0:d]).astype(BF)
        for m in range(nsq):
            k.cos[m * bl:m * bl + bl] = k.cosb[...]
            k.sin[m * bl:m * bl + bl] = k.sinb[...]

    ins = dict(x=x, spread=spread, cosb=cosb, sinb=sinb)
    afters = seen_outs(0)
    if not near:
        wa, wo, gu, wd = (lax.all_gather(w, "dp", axis=0, tiled=True) for w in slabs)

        def k_first(k):
            k = join(k, k.p)
            begin(k)
            k.gn = gains(k.wa)
            project(geo, 0, k)
        P[0] = join(call("first_project", k_first, dict(wa=wa, **ins), dict(p=proj_outs(0))).p)
        P[0].kvall = share(P[0].kv.reshape(nsq, S[0], 640))
        F[0] = call("attend", lambda k: attend(geo, 0, k, blk_of()), dict(q16=P[0].q16, kvall=P[0].kvall), afters, seen_scratch(0))
    else:
        def k_head(k):
            dp_, blk, y, c, ym, cm = mates()
            z, x_ = dp_ // NX, lax.rem(dp_, NX)
            k = join(k, k.p, k.f, k.fs)
            ticks = gather_ticks(AG_CHUNKS, k.shards, k.slabs, k.sems)
            meet((dp_ + 1 - 2 * x_, blk), ym, cm, z=z)

            def tick(n=1):
                for _ in range(min(n, len(ticks))):
                    ticks.pop(0)()
            tick(2)
            begin(k)
            tick(A_TICKS - 2)
            load = pltpu.make_async_copy(k.slabs[0], k.wa, k.wsem)
            load.start()
            load.wait()
            k.gn = gains(k.wa)
            project_kv(geo, 0, k)
            sharing = Share(k.own, k.kvall, k.ssem, k.rsem)
            k.own[...] = k.kv[...].reshape(nsq, S[0], 640)
            k.kvall[blk] = k.own[...]
            sharing.start()
            tick()
            project_q(geo, 0, k)
            tick()
            sharing.forward()
            tick()
            sharing.arrive()
            attend(geo, 0, k, blk, tick)
            tick(len(ticks))
            sharing.sent()
        got = call("head", k_head, dict(shards=list(slabs), **ins),
                   dict(slabs=[Out((v.shape[0] * geo.n_dp, v.shape[1]), BF, True) for v in slabs], p=proj_outs(0, False), f=afters,
                        kvall=Out((nb, nsq, S[0], 640), BF)),
                   dict(fs=seen_scratch(0), wa=V((dp, COLS_A), BF), kv=V((R[0], 640), BF), own=V((nsq, S[0], 640), BF),
                        wsem=dma, ssem=dma((3,)), rsem=dma((3,)), sems=gather_sems(4, len(AG_CHUNKS))),
                   collective_id=1, has_side_effects=True)
        wa, wo, gu, wd = got.slabs
        P[0], F[0] = join(got.p, kvall=got.kvall), join(got.f)
    gu, wd = Far(gu), Far(wd)
    wou = h = None

    def remote(ident):
        return dict(collective_id=ident, has_side_effects=True) if near else {}

    def k_fore(r, k):
        blk = blk_of()
        if near:
            meet(*mates()[4:])
        k = join(k, k.s, k.tl)
        tiles = Tiles(geo, k)
        tiles.start(0, 0)
        k.gn = gains(k.wa)
        if r == 0:
            k.wou[...] = dot(k.spread[...], k.wo[...]).astype(BF)
        v = join(k, k.p, k.f, k.fs)
        if r:
            attend(geo, r, v, blk)
        feed(geo, r, v, blk, tiles)
        n = join(k, k.n, h=k.h2, routes=k.routes2)
        select_rows(geo, r + 1, n, blk)
        if not near:
            project(geo, r + 1, n)
            return
        n = join(n, k.sh, k.sh_)
        project_kv(geo, r + 1, n)
        n.own[...] = n.kv[...].reshape(n.own.shape)
        n.kvall[blk] = n.own[...]
        sharing = Share(n.own, n.kvall, n.ssem, n.rsem)
        sharing.start()
        project_q(geo, r + 1, n)
        sharing.forward()
        sharing.arrive()
        sharing.sent()

    for r in range(2):
        p = dict(a=P[r].a, q16=P[r].q16, kvall=P[r].kvall) if r else dict(a=P[0].a, o=F[0].o)
        more = dict(choice=P[r].choice, h=h, routes=rt[r], wou=wou) if r else dict(wo=wo, spread=spread, lens=lens)
        got = call("forward", functools.partial(k_fore, r),
                   dict(wa=wa, gu=gu, wd=wd, p=p, cosb=cosb, sinb=sinb, routes2=rt[r + 1], s=more),
                   dict(f=fore_outs(r), n=proj_outs(r + 1, not near), h2=Out((full, dp)), **({} if r else dict(wou=Out((1024, dp), BF))),
                        **(dict(sh=dict(kvall=Out((nb, nsq, S[r + 1], 640), BF))) if near else {})),
                   dict(fs=fore_scratch(r), tl=Tiles.scratch(geo), **(dict(sh_=share_scratch(r + 1)) if near else {})), **remote(3 + r))
        h, F[r], P[r + 1] = got.h2, join(F[r] or {}, got.f), join(got.n)
        wou = wou if r else got.wou
        P[r + 1].kvall = join(got.sh).kvall if near else share(P[r + 1].kv.reshape(nsq, S[r + 1], 640))

    def k_turn(k):
        blk = blk_of()
        if near:
            meet(*mates()[4:])
        k = join(k, k.tl)
        tiles = Tiles(geo, k)
        tiles.start(0, 0)
        k.gn = gains(k.wa)
        v = join(k, k.p, k.f, k.fs, h2=k.h3)
        attend(geo, 2, v, blk)
        feed(geo, 2, v, blk, tiles)
        tiles = Tiles(geo, join(k, k.bs), (v.gp, v.up))
        tiles.start(0, 0)
        k.out[...] = dot_nt(k.h3[...].astype(BF), k.spread[0:d]).astype(BF)
        k.dh[...] = dot(k.cot[...], k.spread[0:d])
        v = join(v, k.bs, k.ts, k.b, k.t, k.gv if near else {})
        back_feed(geo, 2, v, blk, tiles)
        back_out(geo, 2, v)
        back_attend(geo, 2, v, blk)
        if near:
            give(v.dkv, v.dkvown, v.got1, v.half, v.got2, v.ssem, v.rsem)

    p = P[2]
    got = call("turn", k_turn,
               dict(wa=wa, gu=gu, wd=wd, wou=wou, h=h, spread=spread, cot=cot, routes=rt[2],
                    p=dict(a=p.a, q16=p.q16, kvall=p.kvall, choice=p.choice, cos=p.cos, sin=p.sin)),
               dict(f=fore_outs(2), b=feed_outs(2), t=turned_outs(2), out=Out((full, d), BF), dh=Out((full, dp))),
               dict(fs=fore_scratch(2), bs=feed_scratch(2), ts=turned_scratch(2), tl=Tiles.scratch(geo), h3=V((full, dp), F32),
                    **(dict(gv=give_scratch(2)) if near else {})), **remote(5))
    F[2], B[2], T[2], out, dh = join(got.f), join(got.b), join(got.t), got.out, got.dh

    def k_back(r, k):
        blk = blk_of()
        if near and r:
            meet(*mates()[4:])
        v = join(k, k.p, k.f, k.b, k.bs, k.tl)
        tiles = Tiles(geo, v, (v.gp, v.up))
        tiles.start(0, 0)
        v.gn = k.gn = gains(k.wa)
        k.first[...] = jnp.zeros(k.first.shape, F32)
        back_project(geo, r + 1, join(k, k.n), blk)
        v.dh = k.dh2
        back_feed(geo, r, v, blk, tiles)
        if r > 0:
            v = join(v, k.t, k.ts, k.gv if near else {})
        back_out(geo, r, v)
        if r > 0:
            back_attend(geo, r, v, blk)
            if near:
                give(v.dkv, v.dkvown, v.got1, v.half, v.got2, v.ssem, v.rsem)

    for r in (1, 0):
        n, q, p, f = r + 1, P[r + 1], P[r], F[r]
        mine = (T[n].dkvown if near else give_back(T[n].dkv)).reshape(R[n], 640)
        late = dict(q16=p.q16, kvall=p.kvall, cos=p.cos, sin=p.sin, choice=p.choice) if r else {}
        more = dict(lse=f.lse) if r else {}
        rest = dict(wou=wou, routes=rt[r]) if r else dict(wou=wou, lens=lens)
        got = call("backward", functools.partial(k_back, r),
                   dict(wa=wa, gu=gu, wd=wd, dh=dh, **rest,
                        n=dict(dkvown=mine, da=T[n].da, tok=B[n].tok, inc=B[n].inc, choice=q.choice, st=q.st, a=q.a,
                               cos=q.cos, sin=q.sin),
                        p=dict(a=p.a, **late),
                        f=dict(o=f.o, b=f.b, gp=Far(f.gp), up=Far(f.up), yf=f.yf, sx=f.sx, **more)),
                   dict(b=feed_outs(r), da2=Out((R[n], COLS_A), BF), first=Out((8, dp)), dh2=Out((full, dp)),
                        **(dict(t=turned_outs(r)) if r else out_parts(Out))),
                   dict(bs=feed_scratch(r), tl=Tiles.scratch(geo), **(dict(ts=turned_scratch(r)) if r else {}),
                        **(dict(gv=give_scratch(r)) if r and near else {})), **(remote(6) if r else {}))
        dh, B[r], L[n] = got.dh2, join(got.b), join(da2=got.da2, first=got.first)
        if r:
            T[r] = join(got.t)
    p, f = P[0], F[0]
    saved = [join(P[r], F[r], B[r], L[r] or {}) for r in range(3)]
    if near:
        gu_d = gate_up_grads(geo, saved), down_grads(geo, saved)
        grad, shards = tail(geo, join(p, f, B[0], got, wa=wa, dh=dh, lens=lens.value, spread=spread), saved, gu_d,
                            turned_scratch(0, 1))
        return out, grad, shards
    T[0] = call("backward_attend", lambda k: back_attend(geo, 0, k, blk_of()),
                dict(do16=got.do16, dcol=got.dcol, q16=p.q16, kvall=p.kvall, lse=f.lse, cos=p.cos, sin=p.sin),
                turned_outs(0), turned_scratch(0))
    mine = give_back(T[0].dkv).reshape(R[0], 640)

    def k_last(k):
        blk = blk_of()
        k.gn = gains(k.wa)
        k.first[...] = jnp.zeros(k.first.shape, F32)
        back_project(geo, 0, k, blk)
        high, low = halves(k.dh2[...])
        k.grad[...] = dot_nt(high, k.spread[0:d]) + dot_nt(low, k.spread[0:d])
    L[0] = call("last_project", k_last,
                dict(wa=wa, dkvown=mine, da=T[0].da, tok=B[0].tok, dh=dh, lens=lens, st=p.st, a=p.a, cos=p.cos, sin=p.sin,
                     spread=spread),
                dict(da2=Out((R[0], COLS_A), BF), first=Out((8, dp)), grad=Out((full, d))), dict(dh2=V((full, dp), F32)))
    saved[0] = join(saved[0], L[0])
    slabs = [products(geo, saved, QKV), products(geo, saved, OUT, spread), gate_up_grads(geo, saved), down_grads(geo, saved)]
    shards = [lax.psum(lax.psum_scatter(v, "dp", scatter_dimension=0, tiled=True), "blk") for v in slabs]
    return out, L[0].grad, shards


QKV, OUT = range(2)


def product_parts(geo, saved, kind, spread=None):
    dp = geo.dp
    if kind == QKV:
        ins = dict(lefts=[v.u for v in saved], rights=[[v.da2 for v in saved]], small=[v.small for v in saved],
                   first=[v.first for v in saved])
        return ins, (dp, COLS_A), 512
    return dict(lefts=[v.o for v in saved], rights=[[v.dy for v in saved]], spread=spread), (dp, dp), 512


def product_body(geo, kind, shape, tile, k):
    R = [geo.rows(r) for r in range(3)]
    rows, dp = shape[0], geo.dp
    at = 0
    for i in range(3):
        for c in range(0, rows, 256):
            v = dot(k.lefts[i][...], k.spread[:, c:c + 256]).astype(BF) if kind == OUT else k.lefts[i][:, c:c + 256]
            k.left[c:c + 256, at:at + R[i]] = v.T
        at += R[i]
    c0 = 0
    for refs in k.rights:
        n = refs[0].shape[1]
        for t in range(0, n, tile):
            w = min(tile, n - t)
            right = jnp.concatenate([v[:, t:t + w] for v in refs], axis=0)
            k.res[:, c0 + t:c0 + t + w] = dot(k.left[...], right).astype(BF)
        c0 += n
    if kind == QKV:
        small = k.small[0][...] + k.small[1][...] + k.small[2][...]
        f = k.first[0][...] + k.first[1][...] + k.first[2][...]
        small = jnp.where(rowid(small.shape) == 0, f, small)
        cols = jnp.concatenate([small, jnp.zeros((120, dp), F32)], axis=0).T
        cols = pltpu.roll(cols, 64, 1)
        k.res[:, 896:1024] = jnp.where(lanes(cols.shape) < 64, k.res[:, 896:1024].astype(F32), cols).astype(BF)


def products(geo, saved, kind, spread=None):
    ins, shape, tile = product_parts(geo, saved, kind, spread)
    total = sum(geo.rows(r) for r in range(3))
    return call("weight_grads", functools.partial(product_body, geo, kind, shape, tile), ins, dict(res=Out(shape, BF)),
                dict(left=pltpu.VMEM((shape[0], total), BF))).res


def gate_up_grads(geo, saved):
    R = [geo.rows(r) for r in range(3)]
    total, dp, n = sum(R), geo.dp, geo.ff // FT

    def body(w0, w1, w2, g0, g1, g2, u0, u1, u2, out, left):
        t = pl.program_id(0)

        @pl.when(t == 0)
        def _():
            at = 0
            for i, w in enumerate((w0, w1, w2)):
                for c in range(0, dp, 256):
                    left[c:c + 256, at:at + R[i]] = w[:, c:c + 256].T
                at += R[i]

        def put(parts):
            out[...] = dot(left[...], jnp.concatenate([v[...] for v in parts], axis=0)).astype(BF)
        pl.when(t < n)(lambda: put((g0, g1, g2)))
        pl.when(t >= n)(lambda: put((u0, u1, u2)))
    held = [pl.BlockSpec((rows, dp), lambda t: (0, 0)) for rows in R]
    gate = [pl.BlockSpec((rows, FT), lambda t: (0, jnp.minimum(t, n - 1))) for rows in R]
    up = [pl.BlockSpec((rows, FT), lambda t: (0, jnp.maximum(t - n, 0))) for rows in R]
    return pl.pallas_call(
        body, grid=(2 * n,), out_shape=jax.ShapeDtypeStruct((dp, 2 * geo.ff), BF), in_specs=held + gate + up,
        out_specs=pl.BlockSpec((dp, FT), lambda t: (0, t)), scratch_shapes=[pltpu.VMEM((dp, total), BF)],
        compiler_params=pltpu.CompilerParams(vmem_limit_bytes=63 << 20), name="gate_up_grads",
    )(*[v.w for v in saved], *[v.dgp for v in saved], *[v.dup for v in saved])


def down_grads(geo, saved, tile=512):
    R = [geo.rows(r) for r in range(3)]
    dp = geo.dp

    def body(z0, z1, z2, d0, d1, d2, out):
        left = jnp.concatenate([v[...] for v in (z0, z1, z2)], axis=0)
        right = jnp.concatenate([v[...] for v in (d0, d1, d2)], axis=0)
        out[...] = dot_tn(left, right).astype(BF)
    return pl.pallas_call(
        body, grid=(geo.ff // tile,), out_shape=jax.ShapeDtypeStruct((geo.ff, dp), BF),
        in_specs=[pl.BlockSpec((rows, tile), lambda t: (0, t)) for rows in R]
        + [pl.BlockSpec((rows, dp), lambda t: (0, 0)) for rows in R],
        out_specs=pl.BlockSpec((tile, dp), lambda t: (t, 0)),
        compiler_params=pltpu.CompilerParams(vmem_limit_bytes=63 << 20), name="down_grads",
    )(*[v.z for v in saved], *[v.df for v in saved])


def phase(body, ins, outs, scratch=None):
    leaf = lambda v: not isinstance(v, (dict, list, tuple))
    fi, ti = jax.tree.flatten(ins, is_leaf=leaf)
    fo, to = jax.tree.flatten(outs, is_leaf=leaf)

    def run(vi, vo, sc, sems):
        loads = [pltpu.make_async_copy(far, near, sems.at[i]) for i, (far, near) in enumerate(zip(fi, vi))]
        for v in loads:
            v.start()
        for v in loads:
            v.wait()
        body(join(ti.unflatten(vi), to.unflatten(vo), sc))
        stores = [pltpu.make_async_copy(near, far, sems.at[i]) for i, (far, near) in enumerate(zip(fo, vo))]
        for v in stores:
            v.start()
        for v in stores:
            v.wait()
    near = lambda refs: [pltpu.VMEM(v.shape, v.dtype) for v in refs]
    pl.run_scoped(run, near(fi), near(fo), scratch or {}, pltpu.SemaphoreType.DMA((max(len(fi), len(fo)),)))


def tail(geo, v, saved, gu_d, turned):
    dp, d, bl, nsq, s = geo.dp, geo.d, geo.bl, geo.ns, geo.slots[0]
    full = nsq * bl
    V, dma = pltpu.VMEM, pltpu.SemaphoreType.DMA
    total = sum(geo.rows(r) for r in range(3))
    one = Geo(1, bl, geo.n_dp, geo.n_blk, d, geo.ff, geo.tops)
    part = (nsq, s, 640)

    def body(k):
        dp_, blk, y, c, ym, cm = mates()
        z, x_ = dp_ // NX, lax.rem(dp_, NX)
        meet((dp_ + 1 - 2 * x_, blk), ym, cm, z=z)
        slabs = [k.ga, k.go, k.gu, k.gd]
        ticks = reduce_ticks(RS_CHUNKS, [slab_view(geo, i, w) for i, w in enumerate(slabs)], k.shards, k.bufs, k.sems)
        ready = RS_CHUNKS_READY

        def tick(n=1):
            nonlocal ready
            for _ in range(n):
                if ready > 0:
                    ready -= 1
                    ticks.pop(0)()
        tick(2)
        a = k.at
        phase(lambda q: back_attend(geo, 0, join(q, kvall=k.kvall, dkv=k.dkv), blk, tick),
              dict(do16=a.do16, dcol=a.dcol, q16=a.q16, lse=a.lse, cos=a.cos, sin=a.sin), dict(da=k.da),
              dict(dkvm=V((geo.n_blk, s, 640), BF), lsem=dma((geo.n_blk,)), **turned))

        def rem(src, dst, i, to):
            return pltpu.make_async_remote_copy(src_ref=src, dst_ref=dst, send_sem=k.gs.at[i], recv_sem=k.gr.at[i],
                                                device_id=to, device_id_type=MESH)
        first = [rem(k.dkv.at[2 * yy + 1 - c], k.got1.at[yy], yy, cm) for yy in range(2)]
        for f in first:
            f.start()
        tick()
        for f in first:
            f.wait_recv()

        def add(q):
            for yy, mine in enumerate((q.p0, q.p1)):
                k.got1[yy] = (k.got1[yy].astype(F32) + mine[...].astype(F32)).astype(BF)
        phase(add, dict(p0=k.dkv.at[c], p1=k.dkv.at[2 + c]), {})
        second = rem(k.got1.at[1 - y], k.got2, 2, ym)
        second.start()
        tick()
        second.wait_recv()
        tick()
        k.first[...] = jnp.zeros(k.first.shape, F32)
        for m in range(nsq):
            rows = pl.ds(m * bl, bl)

            def last(q):
                q.gn = gains(q.wa)
                q.dkvown[...] = k.got1[y, m].astype(F32) + k.got2[m].astype(F32)
                back_project(one, 0, join(q, lens=[k.lens[m]], first=k.first), blk)
                high, low = halves(q.dh2[...])
                q.grad[...] = dot_nt(high, q.spread[0:d]) + dot_nt(low, q.spread[0:d])
            phase(last, dict(wa=k.wa, da=k.da.at[rows], tok=a.tok.at[rows], dh=a.dh.at[rows], st=a.st.at[rows], a=a.a.at[rows],
                             cos=a.cos.at[rows], sin=a.sin.at[rows], spread=k.spread),
                  dict(da2=k.da2.at[rows], grad=k.grad.at[rows]),
                  dict(dkvown=V((bl, 640), F32), dh2=V((bl, dp), F32)))
            tick()
        for kind, res in ((QKV, k.ga), (OUT, k.go)):
            ins, shape, tile = product_parts(geo, [types.SimpleNamespace(**q) for q in k.saved], kind, k.spread)
            if kind == QKV:
                ins[FIRST] = ins[FIRST][1:]
                ins[RIGHTS] = [[k.da2] + ins[RIGHTS][0][1:]]

            def make(q, kind=kind, shape=shape, tile=tile):
                if kind == QKV:
                    q.first = [k.first] + q.first
                product_body(geo, kind, shape, tile, q)
            phase(make, ins, dict(res=res), dict(left=V((shape[0], total), BF)))
            tick()
        for t in ticks:
            t()
        for f in first + [second]:
            f.wait_send()

    FIRST, RIGHTS = tuple(dict(first=0, rights=0))
    keep = [dict(u=Far(q.u), o=Far(q.o), dy=Far(q.dy), small=Far(q.small),
                 **(dict(da2=Far(q.da2), first=Far(q.first)) if i else dict(da2=Far(q.u), first=Far(q.small))))
            for i, q in enumerate(saved)]
    bufs, sems = reduce_scratch(geo, RS_CHUNKS)
    got = call("tail", lambda k: body(join(k, at=join(k.at))),
               dict(at=dict(do16=Far(v.do16), dcol=Far(v.dcol), q16=Far(v.q16), lse=Far(v.lse), cos=Far(v.cos), sin=Far(v.sin),
                            tok=Far(v.tok), dh=Far(v.dh), st=Far(v.st), a=Far(v.a)),
                    kvall=Far(v.kvall), lens=Words(v.lens), wa=Far(v.wa), spread=Far(v.spread), gu=Far(gu_d[0]), gd=Far(gu_d[1]),
                    saved=keep),
               dict(shards=reduce_outs(geo), grad=Out((full, d), F32, True), ga=Out((dp, COLS_A), BF, True),
                    go=Out((dp, dp), BF, True), da=Out((full, 1024), BF, True), da2=Out((full, COLS_A), BF, True),
                    dkv=Out((geo.n_blk,) + part, BF, True)),
               dict(bufs=bufs, sems=sems, got1=V((2,) + part, BF), got2=V(part, BF), first=V((8, dp), F32),
                    gs=dma((3,)), gr=dma((3,))),
               collective_id=2, has_side_effects=True)
    return got.grad, got.shards


MESH = pl.DeviceIdType.MESH

NZ, NX = 4, 2
AHEAD = 2
OFFSETS = (0, 2, 4, 6, 8, 10, 12, 13, 14)
G = NZ * NX


def meet(*others, z=None):
    dp, blk = lax.axis_index("dp"), lax.axis_index("blk")
    bar = pltpu.get_barrier_semaphore()
    for t in others:
        pl.semaphore_signal(bar, inc=1, device_id=t, device_id_type=MESH)
    count = len(others)
    if z is not None:
        @pl.when(z > 0)
        def _():
            pl.semaphore_signal(bar, inc=1, device_id=(dp - NX, blk), device_id_type=MESH)

        @pl.when(z < NZ - 1)
        def _():
            pl.semaphore_signal(bar, inc=1, device_id=(dp + NX, blk), device_id_type=MESH)
        count = count + jnp.where(z > 0, 1, 0) + jnp.where(z < NZ - 1, 1, 0)
    pl.semaphore_wait(bar, count)


def gather_ticks(chunks, ins, outs, sems):
    ls, zs, zr, xs, xr, ys, yr, cs, cr = sems
    nslab = len(ins)
    dp, blk = lax.axis_index("dp"), lax.axis_index("blk")
    z, x = dp // NX, lax.rem(dp, NX)
    y, c = blk // 2, lax.rem(blk, 2)
    left, right = (dp - NX, blk), (dp + NX, blk)
    xm, ym, cm = (dp + 1 - 2 * x, blk), (dp, lax.rem(blk + 2, 4)), (dp, blk + 1 - 2 * c)

    locs = [pltpu.make_async_copy(ins[s], outs[s].at[pl.ds(pl.multiple_of(dp * ins[s].shape[0], 16), ins[s].shape[0])], ls.at[s])
            for s in range(nslab)]

    def piece(i, g, q):
        s, c0, n, split = chunks[i]
        rows = ins[s].shape[0]
        h = rows // split
        return outs[s].at[pl.ds(pl.multiple_of(g * rows + q * h, 16), h), pl.ds(c0, n)]

    def myq(i):
        return blk if chunks[i][3] == 4 else c

    def rem(src, dst, a, b, to):
        return pltpu.make_async_remote_copy(src_ref=src, dst_ref=dst, send_sem=a, recv_sem=b, device_id=to, device_id_type=MESH)

    def own(i):
        s, c0, n, split = chunks[i]
        h = ins[s].shape[0] // split
        return ins[s].at[pl.ds(pl.multiple_of(myq(i) * h, 16), h), pl.ds(c0, n)]

    def zcopy(i, d, s, src_own):
        zz = z - s if d == 0 else z + s
        p = piece(i, zz * NX + x, myq(i))
        return rem(own(i) if src_own else p, p, zs.at[i, d, s], zr.at[i, d, s], right if d == 0 else left)

    def zrecv(i, d, s):
        zz = z - 1 - s if d == 0 else z + 1 + s
        p = piece(i, zz * NX + x, myq(i))
        return rem(p, p, zs.at[i, d, s], zr.at[i, d, s], right if d == 0 else left)

    def xcopy(i, zz, src_own=False):
        p = piece(i, zz * NX + x, myq(i))
        return rem(own(i) if src_own else p, p, xs.at[i, zz], xr.at[i, zz], xm)

    def xrecv(i, zz):
        p = piece(i, zz * NX + 1 - x, myq(i))
        return rem(p, p, xs.at[i, zz], xr.at[i, zz], xm)

    def ycopy(i, g):
        p = piece(i, g, blk)
        return rem(p, p, ys.at[i, g], yr.at[i, g], ym)

    def yrecv(i, g):
        p = piece(i, g, lax.rem(blk + 2, 4))
        return rem(p, p, ys.at[i, g], yr.at[i, g], ym)

    def ccopy(i, k, g):
        q = myq(i) if k == 0 else lax.rem(blk + 2, 4)
        p = piece(i, g, q)
        return rem(p, p, cs.at[i, k, g], cr.at[i, k, g], cm)

    def crecv(i, k, g):
        if chunks[i][3] == 4:
            mate = blk + 1 - 2 * c
            q = mate if k == 0 else lax.rem(mate + 2, 4)
        else:
            q = 1 - c
        p = piece(i, g, q)
        return rem(p, p, cs.at[i, k, g], cr.at[i, k, g], cm)

    def spread(i, g):
        if chunks[i][3] == 4:
            ycopy(i, g).start()
        ccopy(i, 0, g).start()

    def begin(i):
        @pl.when(z < NZ - 1)
        def _():
            zcopy(i, 0, 0, True).start()

        @pl.when(z > 0)
        def _():
            zcopy(i, 1, 0, True).start()
        xcopy(i, z, True).start()

    def zstep(i, s):
        @pl.when(z - 1 - s >= 0)
        def _():
            zrecv(i, 0, s).wait_recv()
            if s < NZ - 2:
                @pl.when(z < NZ - 1)
                def _():
                    zcopy(i, 0, s + 1, False).start()
            xcopy(i, z - 1 - s).start()
            spread(i, (z - 1 - s) * NX + x)

        @pl.when(z + 1 + s < NZ)
        def _():
            zrecv(i, 1, s).wait_recv()
            if s < NZ - 2:
                @pl.when(z > 0)
                def _():
                    zcopy(i, 1, s + 1, False).start()
            xcopy(i, z + 1 + s).start()
            spread(i, (z + 1 + s) * NX + x)

    def xstep(i, k):
        def one(zz):
            xrecv(i, zz).wait_recv()
            spread(i, zz * NX + 1 - x)
        if k == 0:
            one(z)
        else:
            pl.when(z - k >= 0)(lambda: one(z - k))
            pl.when(z + k < NZ)(lambda: one(z + k))

    def ystep(i, k):
        g = lax.rem(dp + k, G)
        yrecv(i, g).wait_recv()
        ccopy(i, 1, g).start()

    def cstep(i, k):
        g = lax.rem(dp + k, G)
        crecv(i, 0, g).wait_recv()
        if chunks[i][3] == 4:
            crecv(i, 1, g).wait_recv()

    def sent(i):
        @pl.when(z < NZ - 1)
        def _():
            zcopy(i, 0, 0, True).wait_send()

        @pl.when(z > 0)
        def _():
            zcopy(i, 1, 0, True).wait_send()
        for s in range(NZ - 1):
            if s < NZ - 2:
                @pl.when((z - 1 - s >= 0) & (z < NZ - 1))
                def _():
                    zcopy(i, 0, s + 1, False).wait_send()

                @pl.when((z + 1 + s < NZ) & (z > 0))
                def _():
                    zcopy(i, 1, s + 1, False).wait_send()
        xcopy(i, z, True).wait_send()
        for k in range(1, NZ):
            xcopy(i, lax.rem(z + k, NZ)).wait_send()
        for k in range(1, G):
            g = lax.rem(dp + k, G)
            ccopy(i, 0, g).wait_send()
            if chunks[i][3] == 4:
                ycopy(i, g).wait_send()
                ccopy(i, 1, g).wait_send()

    nch = len(chunks)
    stages = [begin] + [functools.partial(lambda i, s: (zstep(i, s), xstep(i, s)), s=s) for s in range(NZ - 1)]
    stages.append(lambda i: xstep(i, NZ - 1))
    stages.append(lambda i: [ystep(i, k) for k in range(1, G)] if chunks[i][3] == 4 else None)
    stages.append(lambda i: [cstep(i, k) for k in range(1, G)])
    stages.append(sent)

    def first():
        for l in locs:
            l.start()

    def tick(t):
        if t == 6:
            locs[0].wait()
        for s in reversed(range(len(stages))):
            for i in range(nch):
                if AG_STARTS[i] + s == t:
                    stages[s](i)
        if t == AG_STARTS[-1] + len(stages) - 1:
            for l in locs[1:]:
                l.wait()
    return [first] + [functools.partial(tick, t) for t in range(AG_STARTS[-1] + len(stages))]


def gather_sems(n, nch):
    dma = pltpu.SemaphoreType.DMA
    return [dma((n,)), dma((nch, 2, NZ - 1)), dma((nch, 2, NZ - 1)), dma((nch, NZ)), dma((nch, NZ)),
            dma((nch, G)), dma((nch, G)), dma((nch, 2, G)), dma((nch, 2, G))]


def add_into(dst, other, n):
    def body(k, _):
        dst[k] = (dst[k].astype(jnp.float32) + other(k).astype(jnp.float32)).astype(dst.dtype)
        return 0
    lax.fori_loop(0, n, body, 0)


def reduce_ticks(chunks, ins, outs, bufs, sems):
    nch = len(chunks)
    own, crv, yrv, xrv, zrv, fin, s4b = bufs
    ls, cs, cr, ys, yr, xs, xr, zs, zr, fs, fr = sems
    dp, blk = lax.axis_index("dp"), lax.axis_index("blk")
    z, x = dp // NX, lax.rem(dp, NX)
    y, c = blk // 2, lax.rem(blk, 2)
    left, right = (dp - NX, blk), (dp + NX, blk)
    xm, ym, cm = (dp + 1 - 2 * x, blk), (dp, lax.rem(blk + 2, 4)), (dp, blk + 1 - 2 * c)

    def rem(src, dst, a, b, to):
        return pltpu.make_async_remote_copy(src_ref=src, dst_ref=dst, send_sem=a, recv_sem=b, device_id=to, device_id_type=MESH)

    def four(i):
        return chunks[i][3] == 4

    def part(i, core):
        s, c0, n, split = chunks[i]
        cols = pl.ds(c0, n)
        return ins[s].at[:, :, :, core, :, cols] if split == 4 else ins[s].at[:, :, core, :, cols]

    def load(i):
        return pltpu.make_async_copy(part(i, c), own[i], ls.at[i])

    def core_send(i):
        return rem(part(i, 1 - c), crv[i], cs.at[i, 0], cr.at[i, 0], cm)

    def y_send(i):
        return rem(own[i].at[:, :, 1 - y], yrv[i], ys.at[i], yr.at[i], ym)

    def s2(i):
        return yrv[i] if four(i) else own[i]

    def x_send(i):
        return rem(s2(i).at[:, 1 - x], xrv[i], xs.at[i], xr.at[i], xm)

    def z_copy(i, d, lo, hi, first, to):
        src = xrv[i].at[pl.ds(lo, hi - lo)] if first else zrv[i].at[d, pl.ds(lo, hi - lo)]
        return rem(src, zrv[i].at[d, pl.ds(lo, hi - lo)], zs.at[i, d], zr.at[i, d], to)

    def right_send(i, k):
        return z_copy(i, 0, k + 1, NZ, k == 0, right)

    def left_send(i, k):
        return z_copy(i, 1, 0, k, k == NZ - 1, left)

    def st0(i):
        load(i).start()
        core_send(i).start()

    def st1(i):
        load(i).wait()
        core_send(i).wait_recv()

        def body(g, _):
            zz, xx = g // NX, lax.rem(g, NX)
            for yy in ((0, 1) if four(i) else (None,)):
                at = (zz, xx) if yy is None else (zz, xx, yy)
                own[i][at] = (own[i][at].astype(jnp.float32) + crv[i][at].astype(jnp.float32)).astype(jnp.bfloat16)
            return 0
        lax.fori_loop(0, G, body, 0)
        if four(i):
            y_send(i).start()

    def st2(i):
        if four(i):
            y_send(i).wait_recv()

            def body(g, _):
                zz, xx = g // NX, lax.rem(g, NX)
                yrv[i][zz, xx] = (yrv[i][zz, xx].astype(jnp.float32) + own[i][zz, xx, y].astype(jnp.float32)).astype(jnp.bfloat16)
                return 0
            lax.fori_loop(0, G, body, 0)
        x_send(i).start()

    def zstep(i, s):
        if s < NZ - 1:
            @pl.when(z == s)
            def _():
                if s > 0:
                    z_copy(i, 0, s, NZ, False, right).wait_recv()
                    for k in range(s + 1, NZ):
                        zrv[i][0, k] = (zrv[i][0, k].astype(jnp.float32) + xrv[i][k].astype(jnp.float32)).astype(jnp.bfloat16)
                right_send(i, s).start()

            @pl.when(z == NZ - 1 - s)
            def _():
                k0 = NZ - 1 - s
                if s > 0:
                    z_copy(i, 1, 0, k0 + 1, False, left).wait_recv()
                    for k in range(k0):
                        zrv[i][1, k] = (zrv[i][1, k].astype(jnp.float32) + xrv[i][k].astype(jnp.float32)).astype(jnp.bfloat16)
                left_send(i, k0).start()

    def st3(i):
        x_send(i).wait_recv()
        add_into(xrv[i], lambda k: s2(i)[k, x], NZ)
        zstep(i, 0)

    def finish(i):
        q = blk if four(i) else c
        dst = fin[i].at[q] if four(i) else s4b[i]

        def put(v):
            if four(i):
                fin[i][blk] = v.astype(jnp.bfloat16)
            else:
                s4b[i][...] = v.astype(jnp.bfloat16)

        @pl.when(z == 0)
        def _():
            z_copy(i, 1, 0, 1, False, left).wait_recv()
            put(xrv[i][0].astype(jnp.float32) + zrv[i][1, 0].astype(jnp.float32))

        @pl.when(z == NZ - 1)
        def _():
            z_copy(i, 0, NZ - 1, NZ, False, right).wait_recv()
            put(xrv[i][NZ - 1].astype(jnp.float32) + zrv[i][0, NZ - 1].astype(jnp.float32))

        @pl.when((z > 0) & (z < NZ - 1))
        def _():
            put(xrv[i][z].astype(jnp.float32) + zrv[i][0, z].astype(jnp.float32) + zrv[i][1, z].astype(jnp.float32))
        if four(i):
            fin_send(i, 0).start()
            fin_send(i, 1).start()
        else:
            fin_send(i, 0).start()

    def fin_send(i, k):
        if four(i):
            q = blk if k < 2 else lax.rem(blk + 2, 4)
            return rem(fin[i].at[q], fin[i].at[q], fs.at[i, k], fr.at[i, k], ym if k == 0 else cm)
        if k == 0:
            return rem(s4b[i], fin[i].at[2], fs.at[i, 0], fr.at[i, 0], ym)
        return rem(fin[i].at[c], fin[i].at[c], fs.at[i, 1], fr.at[i, 1], cm)

    def fin_recv(i, k):
        if four(i):
            mate = blk + 1 - 2 * c
            q = lax.rem(blk + 2, 4) if k == 0 else mate if k == 1 else lax.rem(mate + 2, 4)
            return rem(fin[i].at[q], fin[i].at[q], fs.at[i, k], fr.at[i, k], cm)
        if k == 0:
            return fin_send(i, 0)
        return rem(fin[i].at[1 - c], fin[i].at[1 - c], fs.at[i, 1], fr.at[i, 1], cm)

    def st8(i):
        fin_recv(i, 0).wait_recv()
        if four(i):
            fin_send(i, 2).start()
        else:
            fin[i][c] = (fin[i][2].astype(jnp.float32) + s4b[i][...].astype(jnp.float32)).astype(jnp.bfloat16)
            fin_send(i, 1).start()

    def st9(i):
        s, c0, n, split = chunks[i]
        for k in ((1, 2) if four(i) else (1,)):
            fin_recv(i, k).wait_recv()
        for q in range(split):
            outs[s][q, :, pl.ds(c0, n)] = fin[i][q]

    def sent(i):
        core_send(i).wait_send()
        if four(i):
            y_send(i).wait_send()
        x_send(i).wait_send()
        for k in range(NZ - 1):
            pl.when(z == k)(lambda k=k: right_send(i, k).wait_send())
            pl.when(z == k + 1)(lambda k=k: left_send(i, k + 1).wait_send())
        for k in range(3 if four(i) else 2):
            fin_send(i, k).wait_send()

    stages = [st1, st2, st3] + [functools.partial(lambda i, s: zstep(i, s), s=s) for s in range(1, NZ - 1)] + [finish, st8, st9, sent]
    def tick(t):
        if t < 0:
            for i in range(min(AHEAD, nch)):
                st0(i)
            return
        if t + AHEAD < nch:
            st0(t + AHEAD)
        for s in reversed(range(len(stages))):
            i = t - OFFSETS[s]
            if 0 <= i < nch:
                stages[s](i)
    return [functools.partial(tick, t) for t in range(-1, nch + max(OFFSETS))]


def slab_split(k):
    return next(ch[3] for ch in RS_CHUNKS if ch[0] == k)


def slab_rows(geo, k):
    return (geo.ff // geo.n_dp if k == 3 else geo.gp) // slab_split(k)


def slab_view(geo, k, ref):
    lead = (NZ, NX, 2, 2) if slab_split(k) == 4 else (NZ, NX, 2)
    return ref.reshape(*lead, slab_rows(geo, k), ref.shape[1])


def reduce_scratch(geo, chunks):
    nch = len(chunks)
    dma = pltpu.SemaphoreType.DMA

    def shapes(kind):
        out = []
        for s, c0, nc, split in chunks:
            h = slab_rows(geo, s)
            lead = (NZ, NX, 2) if split == 4 else (NZ, NX)
            tiny = (1, 16, 128)
            shape = (lead + (h, nc), lead + (h, nc), (NZ, NX, h, nc) if split == 4 else tiny, (NZ, h, nc), (2, NZ, h, nc),
                     (4 if split == 4 else 3, h, nc), (h, nc) if split == 2 else tiny)[kind]
            out.append(pltpu.VMEM(shape, jnp.bfloat16))
        return out
    sems = [dma((nch,)), dma((nch, 1)), dma((nch, 1)), dma((nch,)), dma((nch,)), dma((nch,)), dma((nch,)),
            dma((nch, 2)), dma((nch, 2)), dma((nch, 3)), dma((nch, 3))]
    return [shapes(k) for k in range(7)], sems


def reduce_outs(geo):
    cols = (COLS_A, geo.dp, 2 * geo.ff, geo.dp)
    return [Out((slab_split(k), slab_rows(geo, k), cols[k]), BF) for k in range(4)]


A_TICKS = 8
AG_STARTS = (0, 1, 2, 3, 4)
AG_CHUNKS = [(0, 0, 1664, 4), (1, 0, 1024, 2), (2, 0, 2560, 4), (2, 2560, 2560, 4), (3, 0, 1024, 2)]
RS_CHUNKS = [(2, 0, 640, 4), (3, 0, 256, 2), (2, 640, 640, 4), (2, 1280, 640, 4), (3, 256, 256, 2), (2, 1920, 640, 4),
             (2, 2560, 640, 4), (3, 512, 256, 2), (2, 3200, 640, 4), (2, 3840, 640, 4), (3, 768, 256, 2), (2, 4480, 640, 4),
             (1, 0, 512, 2), (0, 0, 896, 4), (1, 512, 512, 2), (0, 896, 768, 4)]
RS_CHUNKS_READY = 12 - AHEAD + 1


def pad_to(v, shape):
    return jnp.pad(v, [(0, b - a) for a, b in zip(v.shape, shape)])


def pad_cols(v, geo):
    v = v.reshape(v.shape[0], geo.n_dp, geo.gw)
    return jnp.pad(v, ((0, 0), (0, 0), (0, geo.gp - geo.gw))).reshape(v.shape[0], geo.dp)


def unpad_cols(v, geo):
    return v.reshape(v.shape[0], geo.n_dp, geo.gp)[:, :, :geo.gw].reshape(v.shape[0], geo.d)


def pack(geo, q, k, v, o, g, u, d, g1, g2, rt):
    rows = q.shape[0]
    kv = jnp.concatenate([k.reshape(rows, KV_HEADS, 64), v.reshape(rows, KV_HEADS, 64)], axis=2).reshape(rows, 640)
    small = pad_to(jnp.concatenate([g1[:, None], g2[:, None], rt], axis=1), (rows, 64))
    a = pad_to(jnp.concatenate([q, small, kv], axis=1), (geo.gp, COLS_A))
    gu = pad_to(jnp.concatenate([g, u], axis=1), (geo.gp, 2 * geo.ff))
    return a, pad_to(pad_cols(o, geo), (geo.gp, geo.dp)), gu, pad_cols(d, geo)


def unpack(geo, slabs):
    a, o, gu, d = (w.reshape(-1, w.shape[-1]) for w in slabs)
    a, o, gu = a[:geo.gw], o[:geo.gw], gu[:geo.gw]
    kv = a[:, 1024:].reshape(geo.gw, KV_HEADS, 128)
    return tuple(w.astype(F32) for w in (a[:, :960], kv[:, :, :64].reshape(geo.gw, 320), kv[:, :, 64:].reshape(geo.gw, 320), unpad_cols(o, geo),
            gu[:, :geo.ff], gu[:, geo.ff:], unpad_cols(d, geo), a[:, 960], a[:, 961], a[:, 962:965]))


def mates():
    dp, blk = lax.axis_index("dp"), lax.axis_index("blk")
    y, c = blk // 2, lax.rem(blk, 2)
    return dp, blk, y, c, (dp, lax.rem(blk + 2, 4)), (dp, blk + 1 - 2 * c)


class Share:
    def __init__(self, own, out, ssem, rsem):
        dp, blk, y, c, ym, cm = mates()

        def rem(src, b, k, to):
            return pltpu.make_async_remote_copy(src_ref=src, dst_ref=out.at[b], send_sem=ssem.at[k], recv_sem=rsem.at[k],
                                                device_id=to, device_id_type=MESH)
        far, near = lax.rem(blk + 2, 4), blk + 1 - 2 * c
        both = lax.rem(near + 2, 4)
        self.out = [rem(own, blk, 0, ym), rem(own, blk, 1, cm), rem(out.at[far], far, 2, cm)]
        self.come = [rem(out.at[far], far, 0, ym), rem(out.at[near], near, 1, cm), rem(out.at[both], both, 2, cm)]

    def start(self):
        self.out[0].start()
        self.out[1].start()

    def forward(self):
        self.come[0].wait_recv()
        self.out[2].start()

    def arrive(self):
        self.come[1].wait_recv()
        self.come[2].wait_recv()

    def sent(self):
        for v in self.out:
            v.wait_send()


def give(dkv, out, got1, half, got2, ssem, rsem):
    dp, blk, y, c, ym, cm = mates()

    def rem(src, dst, k, to):
        return pltpu.make_async_remote_copy(src_ref=src, dst_ref=dst, send_sem=ssem.at[k], recv_sem=rsem.at[k],
                                            device_id=to, device_id_type=MESH)
    first = [rem(dkv.at[2 * yy + 1 - c], got1.at[yy], yy, cm) for yy in range(2)]
    for f in first:
        f.start()
    for f in first:
        f.wait_recv()
    half[...] = (got1[1 - y].astype(F32) + dkv[2 * (1 - y) + c].astype(F32)).astype(BF)
    second = rem(half, got2, 2, ym)
    second.start()
    mine = got1[y].astype(F32) + dkv[2 * y + c].astype(F32)
    second.wait_recv()
    out[...] = mine + got2[...].astype(F32)
    for f in first + [second]:
        f.wait_send()


def per_device(block_input, cotangent, seq_lengths, routes_two, routes_three, query_weight, key_weight, value_weight, output_weight,
               gate_weight, up_weight, down_weight, first_gain, second_gain, router_weight):
    micro, seqs, bl, d = block_input.shape
    n_dp, n_blk = lax.axis_size("dp"), lax.axis_size("blk")
    count = micro * seqs
    geo = Geo(count, bl, n_dp, n_blk, d, gate_weight.shape[1], (None, routes_two.shape[2], routes_three.shape[2]))
    slabs = pack(geo, query_weight, key_weight, value_weight, output_weight, gate_weight, up_weight, down_weight, first_gain,
                 second_gain, router_weight)
    out, grad, shards = block(geo, block_input.reshape(count * bl, d), cotangent.reshape(count * bl, d), seq_lengths.reshape(count),
                (routes_two.reshape(count, -1), routes_three.reshape(count, -1)), slabs,
                lambda kv: lax.all_gather(kv, "blk", axis=0, tiled=False),
                              lambda dkv: lax.psum_scatter(dkv, "blk", scatter_dimension=0, tiled=False).astype(F32))
    return (out.reshape(block_input.shape), grad.reshape(block_input.shape)) + unpack(geo, shards)


def solution(mesh):
    in_specs = (
        P(None, "dp", "blk", None),
        P(None, "dp", "blk", None),
        P(None, "dp"),
        P(None, "dp", None),
        P(None, "dp", None),
        P("dp", None),
        P("dp", None),
        P("dp", None),
        P("dp", None),
        P("dp", None),
        P("dp", None),
        P("dp", None),
        P("dp"),
        P("dp"),
        P("dp", None),
    )
    out_specs = (
        P(None, "dp", "blk", None),
        P(None, "dp", "blk", None),
        P("dp", None),
        P("dp", None),
        P("dp", None),
        P("dp", None),
        P("dp", None),
        P("dp", None),
        P("dp", None),
        P("dp"),
        P("dp"),
        P("dp", None),
    )
    return jax.shard_map(
        per_device, mesh=mesh, in_specs=in_specs, out_specs=out_specs, check_vma=False
    )
```
